32 devices in a mesh: row: 8 (over z, x), col: 4 (over y, core).
Axes of the slice: x: 2, y: 2, z: 4, core: 2. Of those that a mesh axis runs over, the one named last changes fastest.
Arguments:
- layer_input: bfloat16 [16384, 896], P(('row', 'col')), may hold values from -40 to 40
- gain_attn: bfloat16 [896], replicated, may hold values from 0.099609375 to 1.8984375
- qkv_weight: bfloat16 [896, 1152], P('row', 'col'), may hold values from -0.1875 to 0.1875
- qkv_bias: bfloat16 [1152], P('col'), may hold values from -3 to 3
- out_weight: bfloat16 [896, 896], P('col', 'row'), may hold values from -1 to 1
- gain_mlp: bfloat16 [896], replicated, may hold values from 0.099609375 to 1.8984375
- gate_weight: bfloat16 [896, 4864], P('row', 'col'), may hold values from -0.1875 to 0.1875
- up_weight: bfloat16 [896, 4864], P('row', 'col'), may hold values from -0.1875 to 0.1875
- down_weight: bfloat16 [4864, 896], P('col', 'row'), may hold values from -0.078125 to 0.078125
- cotangent: bfloat16 [16384, 896], P(('row', 'col')), may hold values from -6 to 6
Outputs:
- layer_output: bfloat16 [16384, 896], P(('row', 'col'))
- input_grad: bfloat16 [16384, 896], P(('row', 'col'))
- gain_attn_grad: float32 [896], replicated
- qkv_weight_grad: float32 [896, 1152], P('row', 'col')
- qkv_bias_grad: float32 [1152], P('col')
- out_weight_grad: float32 [896, 896], P('col', 'row')
- gain_mlp_grad: float32 [896], replicated
- gate_weight_grad: float32 [896, 4864], P('row', 'col')
- up_weight_grad: float32 [896, 4864], P('row', 'col')
- down_weight_grad: float32 [4864, 896], P('col', 'row')
The draws below stay inside these ranges and needn't reach their ends.
All inputs are finite; a program needn't handle non-finite values.
Results may differ from the reference program's by a relative error of at most 0.02.
Values may be sent and summed in bfloat16 or wider, within the bound.
No kernel may reach another device: no remote copies, remote signals or barrier semaphores. Data moves between devices by JAX's collectives and lax.ppermute only.
A program may use at most 192 MiB of HBM per device.

```python
import jax
import jax.numpy as jnp
from jax import lax

D = 896
KV = 2
HD = 64
FF = 4864
SEQ_LEN = 1024
QPG = 7
GROUP_W = 576
QKV_W = 1152
ATT = 896
TOK_ROW = 2048
TOKENS = 16384
BLOCK = 512


def draw_layer_input(key, part):
    key = jax.random.fold_in(key, 11)
    key_base, key_cols, key_rows = jax.random.split(key, 3)
    col_ramp = 0.55 * jnp.arange(D, dtype=jnp.float32) / D
    row_ramp = 0.4 * jnp.arange(TOKENS, dtype=jnp.float32) / TOKENS
    col_scale = jnp.exp(jax.random.uniform(key_cols, (D,), minval=-1.15, maxval=1.15) + col_ramp - 0.3)
    row_scale = jnp.exp(jax.random.uniform(key_rows, (TOKENS, 1), minval=-0.6, maxval=0.6) + row_ramp[:, None] - 0.2)
    base_draw = jax.random.truncated_normal(key_base, -4.0, 4.0, (TOKENS, D))
    return (base_draw * row_scale * col_scale[None, :]).astype(jnp.bfloat16)


def steps_of(rng, dims, pieces, least, largest):
    gain, own = 1.0, jax.random.fold_in(rng, 6)
    for dim, parts in pieces:
        heights = jnp.exp(jax.random.uniform(jax.random.fold_in(own, dim), (parts,), jnp.float32, least / len(pieces), largest / len(pieces)))
        gain = gain * jnp.repeat(heights, dims[dim] // parts).reshape([-1 if axis == dim else 1 for axis in range(len(dims))])
    return gain


def centred(own_key, extent, spread, most, cuts=(), kind=jnp.bfloat16):
    drawn = spread * jax.random.normal(own_key, extent, jnp.float32)
    if cuts:
        drawn = drawn * steps_of(own_key, extent, cuts, -0.22, 0.18)
    return jnp.clip(drawn, -most, most).astype(kind)


def setup_inputs(seed: int = 0) -> dict:
    seeds = jax.random.split(jax.random.key(seed), 11)
    return {
        "layer_input": draw_layer_input(jax.random.fold_in(seeds[10], 71), 0),
        "gain_attn": jnp.clip(1.0 + 0.18 * jax.random.normal(seeds[1], (D,), jnp.float32), 0.099609375, 1.8984375).astype(jnp.bfloat16),
        "qkv_weight": centred(seeds[2], (D, QKV_W), D ** -0.5, 0.1875, ((0, 8), (1, 4))),
        "qkv_bias": centred(seeds[3], (QKV_W,), 0.5, 3.0, ((0, 4),)),
        "out_weight": centred(seeds[4], (ATT, D), (ATT // 32) ** -0.5, 1.0, ((0, 4), (1, 8))),
        "gain_mlp": jnp.clip(1.0 + 0.18 * jax.random.normal(seeds[5], (D,), jnp.float32), 0.099609375, 1.8984375).astype(jnp.bfloat16),
        "gate_weight": centred(seeds[6], (D, FF), D ** -0.5, 0.1875, ((0, 8), (1, 4))),
        "up_weight": centred(seeds[7], (D, FF), D ** -0.5, 0.1875, ((0, 8), (1, 4))),
        "down_weight": centred(seeds[8], (FF, D), FF ** -0.5, 0.078125, ((0, 4), (1, 8))),
        "cotangent": centred(seeds[9], (TOKENS, D), 1.0, 6.0, ((0, 32),)),
    }


eps = 1e-06
theta_base = 1000000.0
highest = lax.Precision.HIGHEST

@jax.custom_vjp
def low(v):
    return lax.optimization_barrier(v.astype(jnp.bfloat16)).astype(jnp.float32)

@jax.custom_vjp
def low_back(v):
    return v

def low_keep(v):
    return (low(v), None)

def low_pass(kept, grad):
    return (grad,)

def back_keep(v):
    return (v, None)

def back_low(kept, grad):
    return (low(grad),)
low.defvjp(low_keep, low_pass)
low_back.defvjp(back_keep, back_low)

def tables(length):
    half_width = HD // 2
    inverse = theta_base ** (-(jnp.arange(half_width, dtype=jnp.float32) * 2.0 / HD))
    angles = jnp.arange(length, dtype=jnp.float32)[:, None] * inverse[None, :]
    return (jnp.cos(angles), jnp.sin(angles))

def rotate(value_in, cosine, sine_part):
    half_width = value_in.shape[-1] // 2
    first_half = value_in[..., :half_width]
    second = value_in[..., half_width:]
    return jnp.concatenate([first_half * cosine - second * sine_part, second * cosine + first_half * sine_part], axis=-1)

def attend(query_rows, key_rows, value_rows):
    block_count = SEQ_LEN // BLOCK
    score_scale = HD ** (-0.5)

    def one_block(block_index):
        query_block = lax.dynamic_slice_in_dim(query_rows, block_index * BLOCK, BLOCK, 1)
        raw_scores = low_back(jnp.einsum('sqgjd,skgd->sgjqk', query_block, key_rows, precision=highest))
        scores = raw_scores * score_scale
        query_pos = block_index * BLOCK + jnp.arange(BLOCK, dtype=jnp.int32)
        key_pos = jnp.arange(SEQ_LEN, dtype=jnp.int32)
        scores = jnp.where(key_pos[None, :] <= query_pos[:, None], scores, -1e+30)
        weights = jax.nn.softmax(scores, axis=-1)
        return jnp.einsum('sgjqk,skgd->sqgjd', low(weights), value_rows, precision=highest)
    blocks = lax.map(jax.checkpoint(one_block), jnp.arange(block_count, dtype=jnp.int32))
    return jnp.moveaxis(blocks, 0, 1).reshape(2, SEQ_LEN, KV, QPG, HD)

def layer_forward(input_rows, gain_attn, qkv_weight, qkv_bias, out_weight, gain_mlp, gate_weight, up_weight, down_weight):
    scale_one = lax.rsqrt(lax.optimization_barrier(jnp.mean(input_rows * input_rows, axis=-1, keepdims=True)) + eps)
    normed_one = low(input_rows * scale_one * gain_attn)
    mixed_rows = low(low_back(jnp.dot(normed_one, qkv_weight, precision=highest) + qkv_bias))
    mixed_rows = mixed_rows.reshape(2, SEQ_LEN, KV, GROUP_W)
    cosine, sine_part = tables(SEQ_LEN)
    query_rows = mixed_rows[..., :QPG * HD].reshape(2, SEQ_LEN, KV, QPG, HD)
    query_rows = low(rotate(query_rows, cosine[None, :, None, None, :], sine_part[None, :, None, None, :]))
    key_rows = low(rotate(mixed_rows[..., QPG * HD:(QPG + 1) * HD], cosine[None, :, None, :], sine_part[None, :, None, :]))
    value_rows = mixed_rows[..., (QPG + 1) * HD:]
    attended = low(low_back(attend(query_rows, key_rows, value_rows))).reshape(2 * SEQ_LEN, ATT)
    middle = input_rows + low_back(jnp.dot(attended, out_weight, precision=highest))
    scale_two = lax.rsqrt(lax.optimization_barrier(jnp.mean(middle * middle, axis=-1, keepdims=True)) + eps)
    normed_two = low(middle * scale_two * gain_mlp)
    gate_lin = low_back(jnp.dot(normed_two, gate_weight, precision=highest))
    up_lin = low_back(jnp.dot(normed_two, up_weight, precision=highest))
    hidden = low(jax.nn.silu(gate_lin) * up_lin)
    return middle + jnp.dot(hidden, down_weight, precision=highest)

def reference(layer_input, gain_attn, qkv_weight, qkv_bias, out_weight, gain_mlp, gate_weight, up_weight, down_weight, cotangent):
    params = tuple((weight_item.astype(jnp.float32) for weight_item in (gain_attn, qkv_weight, qkv_bias, out_weight, gain_mlp, gate_weight, up_weight, down_weight)))
    input_groups = layer_input.astype(jnp.float32).reshape(TOKENS // TOK_ROW, TOK_ROW, D)
    cot_groups = cotangent.astype(jnp.float32).reshape(TOKENS // TOK_ROW, TOK_ROW, D)

    def group_step(totals, pair_rows):
        rows_in, rows_cot = pair_rows
        result, pullback = jax.vjp(layer_forward, rows_in, *params)
        gradients = pullback(rows_cot)
        totals = tuple((total_item + grad_item for total_item, grad_item in zip(totals, gradients[1:])))
        return (totals, (result.astype(jnp.bfloat16), gradients[0].astype(jnp.bfloat16)))
    zero_grads = tuple((jnp.zeros_like(weight_item) for weight_item in params))
    totals, (outputs, input_grads) = lax.scan(group_step, zero_grads, (input_groups, cot_groups))
    return (outputs.reshape(TOKENS, D), input_grads.reshape(TOKENS, D), totals[0], totals[1], totals[2], totals[3], totals[4], totals[5], totals[6], totals[7])
```

```python
import jax
import jax.numpy as jnp
from jax import lax
from jax.sharding import PartitionSpec as P

HD = 64


eps = 1e-06
theta_base = 1000000.0
bf16 = jnp.bfloat16
f32 = jnp.float32


def flip(block, axis, bit):
    count = lax.axis_size(axis)
    return lax.ppermute(block, axis, [(i, i ^ 1 << bit) for i in range(count)])


def bit_reversed(value, bits):
    return sum((value >> b & 1) << (bits - 1 - b) for b in range(bits))


def tables(length):
    half_width = HD // 2
    inverse = theta_base ** (-(jnp.arange(half_width, dtype=jnp.float32) * 2.0 / HD))
    angles = jnp.arange(length, dtype=jnp.float32)[:, None] * inverse[None, :]
    return (jnp.cos(angles), jnp.sin(angles))


def rotate(value_in, cosine, sine_part):
    half_width = value_in.shape[-1] // 2
    first_half = value_in[..., :half_width]
    second = value_in[..., half_width:]
    return jnp.concatenate(
        [first_half * cosine - second * sine_part, second * cosine + first_half * sine_part],
        axis=-1,
    )


def causal(row_start, block_rows, row_stop):
    query_pos = row_start + jnp.arange(block_rows, dtype=jnp.int32)
    key_pos = jnp.arange(row_stop, dtype=jnp.int32)
    return key_pos[None, :] <= query_pos[:, None]


def gather_rows(block, bits):
    if bits > 3:
        for bit in reversed(range(bits)):
            block = jnp.concatenate([block, flip(block, "row", bit)], 0)
        return block
    held = [block]
    for bit in reversed(range(bits)):
        held = held + [flip(piece, "row", bit) for piece in held]
    return jnp.concatenate(held, 0)


def scatter_rows(total, bits):
    for bit in range(bits):
        half = total.shape[0] // 2
        got = flip(total[half:].astype(bf16), "row", bit)
        total = total[:half] + got.astype(f32)
    return total


def in_order(first, second, parity, axis=0):
    return jnp.where(
        parity == 0,
        jnp.concatenate([first, second], axis),
        jnp.concatenate([second, first], axis),
    )


def pair(block, parity):
    return in_order(block, flip(block, "col", 0), parity)


def keep_half(partial, parity):
    half = partial.shape[0] // 2
    outgoing = lax.dynamic_slice_in_dim(partial, (1 - parity) * half, half, 0).astype(bf16)
    staying = lax.dynamic_slice_in_dim(partial, parity * half, half, 0)
    return staying + flip(outgoing, "col", 0).astype(f32)


def to_pairs(block):
    first = lax.ppermute(block, "col", [(2 * a + b, 2 * b + a) for a in range(2) for b in range(2)])
    second = lax.ppermute(
        block, "col", [(2 * a + b, 2 * (1 - b) + a) for a in range(2) for b in range(2)]
    )
    return first, second


def from_pairs(same, other):
    first = lax.ppermute(same, "col", [(2 * a + b, 2 * b + a) for a in range(2) for b in range(2)])
    second = lax.ppermute(
        other, "col", [(2 * a + b, 2 * b + 1 - a) for a in range(2) for b in range(2)]
    )
    return first, second


def head_forward(query_rows, key_rows, value_rows, block_rows):
    length = query_rows.shape[0]
    score_scale = HD ** (-0.5)
    outputs = []
    log_parts = []
    for row_start in range(0, length, block_rows):
        row_stop = row_start + block_rows
        scores = (
            jnp.einsum(
                "qd,kd->qk",
                query_rows[row_start:row_stop],
                key_rows[:row_stop],
                preferred_element_type=jnp.float32,
            )
            * score_scale
        )
        scores = jnp.where(causal(row_start, block_rows, row_stop), scores, -1e30)
        largest = jnp.max(scores, axis=1, keepdims=True)
        exponent = jnp.exp(scores - largest)
        summed = jnp.sum(exponent, axis=1, keepdims=True)
        probability = (exponent / summed).astype(jnp.bfloat16)
        outputs.append(
            jnp.dot(probability, value_rows[:row_stop], preferred_element_type=jnp.float32)
        )
        log_parts.append((largest + jnp.log(summed))[:, 0])
    return (jnp.concatenate(outputs, 0), jnp.concatenate(log_parts, 0))


def attention_forward(query_heads, key_rows, value_rows, block_rows):
    return lax.map(
        lambda query_one: head_forward(query_one, key_rows, value_rows, block_rows), query_heads
    )


def attention_backward(query_heads, key_rows, value_rows, grad_heads, log_totals, block_rows):
    length = key_rows.shape[0]
    score_scale = HD ** (-0.5)

    def head_backward(carry, head_inputs):
        key_grad, value_grad = carry
        query_rows, head_grad, log_total = head_inputs
        query_parts = []
        for row_start in range(0, length, block_rows):
            row_stop = row_start + block_rows
            query_block = query_rows[row_start:row_stop]
            grad_block = head_grad[row_start:row_stop]
            scores = (
                jnp.einsum(
                    "qd,kd->qk",
                    query_block,
                    key_rows[:row_stop],
                    preferred_element_type=jnp.float32,
                )
                * score_scale
            )
            scores = jnp.where(causal(row_start, block_rows, row_stop), scores, -1e30)
            probability = jnp.exp(scores - log_total[row_start:row_stop, None])
            prob_grad = jnp.einsum(
                "qd,kd->qk", grad_block, value_rows[:row_stop], preferred_element_type=jnp.float32
            )
            row_inner = jnp.sum(probability * prob_grad, axis=1, keepdims=True)
            score_grad = (probability * (prob_grad - row_inner) * score_scale).astype(jnp.bfloat16)
            query_parts.append(
                jnp.dot(score_grad, key_rows[:row_stop], preferred_element_type=jnp.float32)
            )
            padding = ((0, length - row_stop), (0, 0))
            key_grad = key_grad + jnp.pad(
                jnp.einsum(
                    "qk,qd->kd", score_grad, query_block, preferred_element_type=jnp.float32
                ),
                padding,
            )
            value_grad = value_grad + jnp.pad(
                jnp.einsum(
                    "qk,qd->kd",
                    probability.astype(jnp.bfloat16),
                    grad_block,
                    preferred_element_type=jnp.float32,
                ),
                padding,
            )
        return ((key_grad, value_grad), jnp.concatenate(query_parts, 0))

    zero_rows = jnp.zeros((length, HD), jnp.float32)
    (key_grad, value_grad), query_grad = lax.scan(
        head_backward, (zero_rows, zero_rows), (query_heads, grad_heads, log_totals)
    )
    return query_grad, key_grad, value_grad


def cuts(width, count):
    step = -(-width // count // 128) * 128
    return [(start, min(start + step, width)) for start in range(0, width, step)]


def shards(
    layer_input,
    gain_attn,
    qkv_weight,
    qkv_bias,
    out_weight,
    gain_mlp,
    gate_weight,
    up_weight,
    down_weight,
    cotangent,
):
    row = lax.axis_index("row")
    column = lax.axis_index("col")
    row_count = lax.axis_size("row")
    bits = row_count.bit_length() - 1
    core = column % 2
    sequence = column // 2
    tok_local, model_width = layer_input.shape
    length = tok_local * 2
    deep = model_width // row_count
    ff_cols = gate_weight.shape[1]
    qkv_cols = qkv_weight.shape[1]
    out_cols = out_weight.shape[0]
    group_width = 2 * qkv_cols
    query_width = group_width - 2 * HD
    head_count = query_width // HD
    block_rows = min(512, length)
    score_scale = HD ** (-0.5)

    first, second = to_pairs(jnp.concatenate([qkv_weight, out_weight.T], 1))
    low = jnp.where(sequence == 0, first, second)
    high = jnp.where(sequence == 0, second, first)
    qkv_full = gather_rows(jnp.concatenate([low[:, :qkv_cols], high[:, :qkv_cols]], 1), bits)
    out_full = gather_rows(jnp.concatenate([low[:, qkv_cols:], high[:, qkv_cols:]], 1), bits)
    first, second = to_pairs(qkv_bias[None, :])
    bias_full = in_order(first, second, sequence, 1).astype(f32)

    place = jnp.arange(model_width, dtype=jnp.int32)
    masks = jnp.array([bit_reversed(p, bits) for p in range(row_count)], jnp.int32)
    source = jnp.repeat(masks ^ row, deep) * deep + place % deep
    to_stored = (place[:, None] == source[None, :]).astype(bf16)

    def stored(block):
        return jnp.dot(block, to_stored, preferred_element_type=f32)

    def unstored(block):
        return jnp.einsum("ts,fs->tf", block, to_stored, preferred_element_type=f32).astype(bf16)

    def unstored_row(vector):
        blocks = vector.reshape(row_count, deep)
        blocks = jnp.concatenate(
            [blocks[bit_reversed(m, bits)][None] for m in range(row_count)], 0
        )
        for bit in range(bits):
            wide = blocks.reshape(-1, 2, 1 << bit, deep)
            turned = jnp.concatenate([wide[:, 1:], wide[:, :1]], 1).reshape(row_count, deep)
            blocks = jnp.where((row >> bit) % 2 == 1, turned, blocks)
        return blocks.reshape(model_width)

    input_rows = stored(layer_input)
    grad_out = stored(cotangent)
    gain_one = stored(gain_attn[None, :])
    gain_two = stored(gain_mlp[None, :])

    scale_one = lax.rsqrt(jnp.mean(input_rows * input_rows, axis=1) + eps)
    normed_one_blk = (input_rows * scale_one[:, None] * gain_one).astype(bf16)
    normed_one = pair(normed_one_blk, core)
    grouped = (jnp.dot(normed_one, qkv_full, preferred_element_type=f32) + bias_full).astype(bf16)
    cosine, sine_part = tables(length)
    query_heads = (
        grouped[:, :query_width].astype(f32).reshape(length, head_count, HD).transpose(1, 0, 2)
    )
    query_heads = rotate(query_heads, cosine[None], sine_part[None]).astype(bf16)
    key_rows = rotate(
        grouped[:, query_width : query_width + HD].astype(f32), cosine, sine_part
    ).astype(bf16)
    value_rows = grouped[:, query_width + HD :]
    head_outputs, log_totals = attention_forward(query_heads, key_rows, value_rows, block_rows)
    att_group = head_outputs.transpose(1, 0, 2).reshape(length, query_width).astype(bf16)
    attn_partial = jnp.einsum("ta,da->td", att_group, out_full, preferred_element_type=f32)
    middle = input_rows + keep_half(attn_partial, core)
    scale_two = lax.rsqrt(jnp.mean(middle * middle, axis=1) + eps)
    normed_two_blk = (middle * scale_two[:, None] * gain_two).astype(bf16)

    def widen(block):
        beside = flip(block, "col", 0)
        across = flip(block, "col", 1)
        return jnp.concatenate([block, beside, across, flip(across, "col", 0)], 0)

    def narrow(partial):
        own, beside, across, far = jnp.split(partial, 4, 0)
        across = across + flip(far.astype(bf16), "col", 0).astype(f32)
        return (
            own
            + flip(beside.astype(bf16), "col", 0).astype(f32)
            + flip(across.astype(bf16), "col", 1).astype(f32)
        )

    normed_two = widen(normed_two_blk)
    grad_full = widen(grad_out.astype(bf16))
    down_flipped = down_weight.T
    down_sum = 0.0
    normed_sum = 0.0
    gate_total = []
    up_total = []
    down_total = []
    for start, stop in cuts(ff_cols, 2):
        width = stop - start
        joined = gather_rows(
            jnp.concatenate(
                [gate_weight[:, start:stop], up_weight[:, start:stop], down_flipped[:, start:stop]],
                1,
            ),
            bits,
        )
        gate_full = joined[:, :width]
        up_full = joined[:, width : 2 * width]
        down_full = joined[:, 2 * width :]
        gate_lin = jnp.dot(normed_two, gate_full, preferred_element_type=f32)
        up_lin = jnp.dot(normed_two, up_full, preferred_element_type=f32)
        grad_hidden = jnp.dot(grad_full, down_full, preferred_element_type=f32)
        sigmoid_gate = jax.nn.sigmoid(gate_lin)
        silu_gate = gate_lin * sigmoid_gate
        hidden = (silu_gate * up_lin).astype(bf16)
        grad_gate = (
            grad_hidden * up_lin * sigmoid_gate * (1.0 + gate_lin * (1.0 - sigmoid_gate))
        ).astype(bf16)
        grad_up = (grad_hidden * silu_gate).astype(bf16)
        down_sum = down_sum + jnp.einsum(
            "tf,df->td", hidden, down_full, preferred_element_type=f32
        )
        normed_sum = (
            normed_sum
            + jnp.einsum("tf,df->td", grad_gate, gate_full, preferred_element_type=f32)
            + jnp.einsum("tf,df->td", grad_up, up_full, preferred_element_type=f32)
        )
        gate_total.append(
            scatter_rows(
                jnp.einsum("td,tf->df", normed_two, grad_gate, preferred_element_type=f32), bits
            )
        )
        up_total.append(
            scatter_rows(
                jnp.einsum("td,tf->df", normed_two, grad_up, preferred_element_type=f32), bits
            )
        )
        down_total.append(
            scatter_rows(
                jnp.einsum("td,tf->df", grad_full, hidden, preferred_element_type=f32), bits
            )
        )
    grad_normed_two = narrow(normed_sum)
    layer_output = unstored((middle + narrow(down_sum)).astype(bf16))
    scaled_two = gain_two * grad_normed_two
    inner_two = jnp.sum(scaled_two * middle, axis=1)
    grad_middle = (
        grad_out
        + scale_two[:, None] * scaled_two
        - middle * (scale_two**3 * inner_two / model_width)[:, None]
    )
    gain_two_grad = jnp.sum(grad_normed_two * middle * scale_two[:, None], axis=0)
    grad_branch = pair(grad_middle.astype(bf16), core)
    grad_att = jnp.dot(grad_branch, out_full, preferred_element_type=f32).astype(bf16)
    out_grad = jnp.einsum("td,ta->da", grad_branch, att_group, preferred_element_type=f32)
    grad_att_heads = grad_att.reshape(length, head_count, HD).transpose(1, 0, 2)
    query_grad, key_grad, value_grad = attention_backward(
        query_heads, key_rows, value_rows, grad_att_heads, log_totals, block_rows
    )
    query_grad = rotate(query_grad, cosine[None], -sine_part[None])
    key_grad = rotate(key_grad, cosine, -sine_part)
    grad_mixed = jnp.concatenate(
        [query_grad.transpose(1, 0, 2).reshape(length, query_width), key_grad, value_grad], 1
    ).astype(bf16)
    bias_grad = jnp.sum(grad_mixed, axis=0, dtype=f32)
    qkv_grad = jnp.einsum("td,tc->dc", normed_one, grad_mixed, preferred_element_type=f32)
    grad_normed_one = keep_half(
        jnp.einsum("tc,dc->td", grad_mixed, qkv_full, preferred_element_type=f32), core
    )
    scaled_one = gain_one * grad_normed_one
    inner_one = jnp.sum(scaled_one * input_rows, axis=1)
    input_grad = unstored(
        (
            grad_middle
            + scale_one[:, None] * scaled_one
            - input_rows * (scale_one**3 * inner_one / model_width)[:, None]
        ).astype(bf16)
    )
    gain_one_grad = jnp.sum(grad_normed_one * input_rows * scale_one[:, None], axis=0)

    def to_columns(total):
        half = total.shape[1] // 2
        low, high = total[:, :half].astype(bf16), total[:, half:].astype(bf16)
        first, second = from_pairs(
            jnp.where(sequence == 0, low, high), jnp.where(sequence == 0, high, low)
        )
        return first.astype(f32) + second.astype(f32)

    out_total = to_columns(scatter_rows(out_grad, bits))
    qkv_total = to_columns(scatter_rows(qkv_grad, bits))
    bias_row = lax.dynamic_update_slice_in_dim(
        jnp.zeros((group_width * 2,), f32), bias_grad, core * group_width, 0
    )
    small = jnp.concatenate([unstored_row(gain_one_grad), unstored_row(gain_two_grad), bias_row])
    small = jnp.pad(small, (0, -small.shape[0] % 128)).reshape(-1, 128)
    for bit in range(2):
        small = small + flip(small, "col", bit)
    for bit in range(bits):
        small = small + flip(small, "row", bit)
    small = small.reshape(-1)
    gain_one_total = small[:model_width]
    gain_two_total = small[model_width : 2 * model_width]
    bias_total = lax.dynamic_slice_in_dim(small, 2 * model_width + column * qkv_cols, qkv_cols, 0)
    return (
        layer_output,
        input_grad,
        gain_one_total,
        qkv_total,
        bias_total,
        out_total.T,
        gain_two_total,
        jnp.concatenate(gate_total, 1),
        jnp.concatenate(up_total, 1),
        jnp.concatenate(down_total, 1).T,
    )


def solution(mesh):
    in_specs = (
        P(("row", "col"), None),
        P(),
        P("row", "col"),
        P("col"),
        P("col", "row"),
        P(),
        P("row", "col"),
        P("row", "col"),
        P("col", "row"),
        P(("row", "col"), None),
    )
    out_specs = (
        P(("row", "col"), None),
        P(("row", "col"), None),
        P(),
        P("row", "col"),
        P("col"),
        P("col", "row"),
        P(),
        P("row", "col"),
        P("row", "col"),
        P("col", "row"),
    )
    return jax.shard_map(shards, mesh=mesh, in_specs=in_specs, out_specs=out_specs, check_vma=False)
```

```python
import functools
import math

import jax
import jax.numpy as jnp
from jax import lax
from jax.experimental import pallas as pl
from jax.experimental.pallas import tpu as pltpu
from jax.sharding import PartitionSpec as P

HD = 64
eps = 1e-06
theta_base = 1000000.0
bf16 = jnp.bfloat16
f32 = jnp.float32
NT = (((1,), (1,)), ((), ()))
TN = (((0,), (0,)), ((), ()))


def flip(block, axis, bit):
    count = lax.axis_size(axis)
    return lax.ppermute(block, axis, [(i, i ^ 1 << bit) for i in range(count)])


def bit_reversed(value, bits):
    return sum((value >> b & 1) << (bits - 1 - b) for b in range(bits))


def halves_turned(block):
    lane = lax.broadcasted_iota(jnp.int32, block.shape, 1)
    return jnp.where(lane % HD < HD // 2, pltpu.roll(block, 128 - HD // 2, 1), pltpu.roll(block, HD // 2, 1))

def attend_kernel(norm_ref, w_ref, bias_ref, cos_ref, sin_ref, qk_ref, v_ref, att_ref, lse_ref, kpad, vpad, lse_cols, *, block):
    step = pl.program_id(0)
    length = norm_ref.shape[0]
    wide = qk_ref.shape[1]
    pairs = wide // 128
    lane = lax.broadcasted_iota(jnp.int32, (1, 128), 1)
    @pl.when(step == 0)
    def _():
        for r in range(0, length, block):
            rows = pl.ds(r, block)
            mixed = (jnp.dot(norm_ref[rows, :], w_ref[...], preferred_element_type=f32) + bias_ref[...]).astype(bf16).astype(f32)
            cos, sin = cos_ref[rows, :], sin_ref[rows, :]
            for p in range(pairs):
                u = mixed[:, p * 128:(p + 1) * 128]
                turned = (u * cos + halves_turned(u) * sin).astype(bf16)
                qk_ref[rows, p * 128:(p + 1) * 128] = turned
            value = mixed[:, wide:]
            v_ref[rows, :] = value.astype(bf16)
            zero = jnp.zeros_like(value)
            vpad[0, rows, :] = jnp.concatenate([value, zero], 1).astype(bf16)
            vpad[1, rows, :] = jnp.concatenate([zero, value], 1).astype(bf16)
            last = turned.astype(f32)
            kpad[1, rows, :] = jnp.where(lane >= HD, last, 0.0).astype(bf16)
            kpad[0, rows, :] = jnp.where(lane < HD, pltpu.roll(last, HD, 1), 0.0).astype(bf16)
        lse_cols[...] = jnp.zeros_like(lse_cols)

    factor = HD ** -0.5 * math.log2(math.e)
    cols = pl.ds(pl.multiple_of(step * 128, 128), 128)
    row_i = lax.broadcasted_iota(jnp.int32, (block, block), 0)
    col_i = lax.broadcasted_iota(jnp.int32, (block, block), 1)
    for r in range(0, length, block):
        rows = pl.ds(r, block)
        q = qk_ref[rows, cols]

        def head(odd):
            scores = lax.dot_general(q, kpad[odd, :r + block, :], (((1,), (1,)), ((), ())), preferred_element_type=f32)
            diag = jnp.where(col_i <= row_i, scores[:, r:], -1e30)
            scores = jnp.concatenate([scores[:, :r], diag], 1) if r else diag
            top = jnp.max(scores, 1, keepdims=True)
            e = jnp.exp2((scores - top) * factor)
            total = jnp.sum(e, 1, keepdims=True)
            out = jnp.dot(e.astype(bf16), vpad[odd, :r + block, :], preferred_element_type=f32)
            lse = top * factor + jnp.log2(total)
            at = lax.broadcasted_iota(jnp.int32, (1, 128), 1) == 2 * step + odd
            lse_cols[rows, :] = jnp.where(at, lse, lse_cols[rows, :])
            return out / total

        even = head(0)

        @pl.when(step < pairs - 1)
        def _():
            att_ref[rows, :] = (even + head(1)).astype(bf16)

        @pl.when(step == pairs - 1)
        def _():
            att_ref[rows, :] = even.astype(bf16)

    @pl.when(step == pairs - 1)
    def _():
        lse_ref[...] = lse_cols[...].T[:lse_ref.shape[0], :]

def attend(normed, weight, bias, cos, sin):
    length, depth = normed.shape
    group = weight.shape[1]
    wide = group - HD
    pairs = wide // 128
    block = min(256, length)
    whole = lambda shape: pl.BlockSpec(shape, lambda p: (0, 0))
    return pl.pallas_call(
        functools.partial(attend_kernel, block=block),
        grid=(pairs,),
        in_specs=[whole(normed.shape), whole(weight.shape), whole(bias.shape), whole(cos.shape), whole(sin.shape)],
        out_specs=[whole((length, wide)), whole((length, HD)), pl.BlockSpec((length, 128), lambda p: (0, p)), whole((8, length))],
        out_shape=[jax.ShapeDtypeStruct((length, wide), bf16), jax.ShapeDtypeStruct((length, HD), bf16),
                   jax.ShapeDtypeStruct((length, wide), bf16), jax.ShapeDtypeStruct((8, length), f32)],
        scratch_shapes=[pltpu.VMEM((2, length, 128), bf16), pltpu.VMEM((2, length, 128), bf16), pltpu.VMEM((length, 128), f32)],
        compiler_params=pltpu.CompilerParams(vmem_limit_bytes=50*1024*1024),
        cost_estimate=pl.CostEstimate(flops=6*10**9, bytes_accessed=6*10**6, transcendentals=5*10**6),
    )(normed, weight, bias, cos, sin)

def attend_back_kernel(grad_ref, w_ref, qk_ref, v_ref, lse_ref, cos_ref, sin_ref, mixed_ref, bias_ref, kpad, vpad, gatt, dq_acc, dk, dv, *, block):
    step = pl.program_id(0)
    length = grad_ref.shape[0]
    wide = qk_ref.shape[1]
    pairs = wide // 128
    lane = lax.broadcasted_iota(jnp.int32, (1, 128), 1)
    @pl.when(step == 0)
    def _():
        for r in range(0, length, block):
            rows = pl.ds(r, block)
            got = jnp.dot(grad_ref[rows, :], w_ref[...], preferred_element_type=f32)
            gatt[rows, :wide - HD] = got.astype(bf16)
            gatt[rows, wide - HD:] = jnp.zeros((block, HD), bf16)
            value = v_ref[rows, :].astype(f32)
            zero = jnp.zeros_like(value)
            vpad[0, rows, :] = jnp.concatenate([value, zero], 1).astype(bf16)
            vpad[1, rows, :] = jnp.concatenate([zero, value], 1).astype(bf16)
            last = qk_ref[rows, wide - 128:].astype(f32)
            kpad[1, rows, :] = jnp.where(lane >= HD, last, 0.0).astype(bf16)
            kpad[0, rows, :] = jnp.where(lane < HD, pltpu.roll(last, HD, 1), 0.0).astype(bf16)
        dk[...] = jnp.zeros_like(dk)
        dv[...] = jnp.zeros_like(dv)

    factor = HD ** -0.5 * math.log2(math.e)
    cols = pl.ds(pl.multiple_of(step * 128, 128), 128)
    key_i = lax.broadcasted_iota(jnp.int32, (block, block), 0)
    query_i = lax.broadcasted_iota(jnp.int32, (block, block), 1)
    for r in range(0, length, block):
        rows = pl.ds(r, block)
        q = qk_ref[rows, cols]
        g = gatt[rows, cols]

        def head(odd):
            lse = lse_ref[pl.ds(2 * step + odd, 1), rows]
            probs, grads = [], []
            inner = jnp.zeros((1, block), f32)
            for c in range(0, r + block, block):
                scores = lax.dot_general(kpad[odd, c:c + block, :], q, NT, preferred_element_type=f32)
                p = jnp.exp2(scores * factor - lse)
                if c == r:
                    p = jnp.where(key_i <= query_i, p, 0.0)
                dp = lax.dot_general(vpad[odd, c:c + block, :], g, NT, preferred_element_type=f32)
                inner = inner + jnp.sum(p * dp, 0, keepdims=True)
                probs.append(p)
                grads.append(dp)
            dq = 0.0
            for i, c in enumerate(range(0, r + block, block)):
                keys = pl.ds(c, block)
                ds = (probs[i] * (grads[i] - inner)).astype(bf16)
                half = lane >= HD if odd else lane < HD
                dk[keys, :] += jnp.where(half, jnp.dot(ds, q, preferred_element_type=f32), 0.0)
                dv[keys, :] += jnp.where(half, jnp.dot(probs[i].astype(bf16), g, preferred_element_type=f32), 0.0)
                dq = dq + lax.dot_general(ds, kpad[odd, c:c + block, :], TN, preferred_element_type=f32)
            return dq

        dq_acc[rows, :] = head(0)

        @pl.when(step < pairs - 1)
        def _():
            dq_acc[rows, :] += head(1)

    def back(u, rows):
        return u * cos_ref[rows, :] - halves_turned(u) * sin_ref[rows, :]
    scale = HD ** -0.5
    for r in range(0, length, block):
        rows = pl.ds(r, block)
        @pl.when(step < pairs - 1)
        def _():
            mixed_ref[rows, cols] = back(dq_acc[rows, :] * scale, rows).astype(bf16)
        @pl.when(step == pairs - 1)
        def _():
            k = dk[rows, :]
            k = jnp.where(lane >= HD, k + pltpu.roll(k, HD, 1), dq_acc[rows, :]) * scale
            mixed_ref[rows, wide - 128:wide] = back(k, rows).astype(bf16)
            v = dv[rows, :]
            v = v + pltpu.roll(v, HD, 1)
            mixed_ref[rows, wide:] = v[:, :HD].astype(bf16)
    @pl.when(step == pairs - 1)
    def _():
        total = jnp.zeros((1, mixed_ref.shape[1]), f32)
        for r in range(0, length, block):
            total = total + jnp.sum(mixed_ref[pl.ds(r, block), :].astype(f32), 0, keepdims=True)
        bias_ref[...] = total

def attend_back(grad, weight, qk, v, lse, cos, sin):
    length, depth = grad.shape
    wide = qk.shape[1]
    group = wide + HD
    pairs = wide // 128
    block = min(256, length)
    whole = lambda shape: pl.BlockSpec(shape, lambda p: (0, 0))
    ins = (grad, weight, qk, v, lse, cos, sin)
    return pl.pallas_call(
        functools.partial(attend_back_kernel, block=block),
        grid=(pairs,),
        in_specs=[whole(a.shape) for a in ins],
        out_specs=[whole((length, group)), whole((1, group))],
        out_shape=[jax.ShapeDtypeStruct((length, group), bf16), jax.ShapeDtypeStruct((1, group), f32)],
        scratch_shapes=[pltpu.VMEM((2, length, 128), bf16), pltpu.VMEM((2, length, 128), bf16), pltpu.VMEM((length, wide), bf16),
                        pltpu.VMEM((length, 128), f32), pltpu.VMEM((length, 128), f32), pltpu.VMEM((length, 128), f32)],
        compiler_params=pltpu.CompilerParams(vmem_limit_bytes=50*1024*1024),
        cost_estimate=pl.CostEstimate(flops=12*10**9, bytes_accessed=8*10**6, transcendentals=5*10**6),
    )(*ins)

def rope_tables(length):
    inverse = theta_base ** (-(jnp.arange(HD // 2, dtype=f32) * 2.0 / HD))
    angles = jnp.arange(length, dtype=f32)[:, None] * inverse[None, :]
    c, s = jnp.cos(angles), jnp.sin(angles)
    return jnp.concatenate([c] * 4, 1), jnp.concatenate([-s, s, -s, s], 1)


def mlp_kernel(x_ref, g_ref, wg_ref, wu_ref, wd_ref, *rest, add):
    if add: down_in, ngrad_in, hid_ref, gg_ref, gu_ref, down_ref, ngrad_ref = rest
    else: hid_ref, gg_ref, gu_ref, down_ref, ngrad_ref = rest
    x, g = x_ref[...], g_ref[...]
    gate = jnp.dot(x, wg_ref[...], preferred_element_type=f32)
    up = jnp.dot(x, wu_ref[...], preferred_element_type=f32)
    gh = jnp.dot(g, wd_ref[...], preferred_element_type=f32)
    sig = 1.0 / (1.0 + jnp.exp(-gate))
    silu = gate * sig
    hid = (silu * up).astype(bf16)
    ghs = gh * sig
    gg = (ghs * up * (1.0 + gate - silu)).astype(bf16)
    gu = (ghs * gate).astype(bf16)
    hid_ref[...] = hid[:, :hid_ref.shape[1]]
    gg_ref[...] = gg[:, :gg_ref.shape[1]]
    gu_ref[...] = gu[:, :gu_ref.shape[1]]
    down = lax.dot_general(hid, wd_ref[...], NT, preferred_element_type=f32)
    ngrad = lax.dot_general(gg, wg_ref[...], NT, preferred_element_type=f32) + lax.dot_general(gu, wu_ref[...], NT, preferred_element_type=f32)
    if add:
        down = down + down_in[...].astype(f32); ngrad = ngrad + ngrad_in[...].astype(f32)
    down_ref[...] = down.astype(bf16)
    ngrad_ref[...] = ngrad.astype(bf16)

def mlp(x, g, joined, width, sums=None, tile=512):
    t, d = x.shape
    n = joined.shape[1] // 3
    tile = min(tile, t)
    tok = pl.BlockSpec((tile, d), lambda i: (i, 0)); tn = pl.BlockSpec((tile, width), lambda i: (i, 0))
    w = [pl.BlockSpec((d, n), lambda i, k=k: (0, k)) for k in range(3)]
    add = sums is not None
    return pl.pallas_call(functools.partial(mlp_kernel, add=add), grid=(t // tile,),
        in_specs=[tok, tok, *w] + [tok, tok] * add, out_specs=[tn, tn, tn, tok, tok],
        out_shape=[jax.ShapeDtypeStruct((t, width), bf16)] * 3 + [jax.ShapeDtypeStruct((t, d), bf16)] * 2,
        compiler_params=pltpu.CompilerParams(vmem_limit_bytes=56*1024*1024),
        cost_estimate=pl.CostEstimate(flops=12 * t * d * n, bytes_accessed=2 * (3 * d * n + 3 * t * n + 4 * t * d), transcendentals=2 * t * n),
    )(x, g, joined, joined, joined, *(sums or ()))


def gather_rows(block, bits):
    pieces = [block]
    beside = [flip(block, "row", 0)]
    for bit in reversed(range(1, bits)):
        got = flip(jnp.concatenate(pieces, 0), "row", bit)
        beside.append(flip(got, "row", 0))
        pieces.append(got)
    return jnp.concatenate(pieces + beside, 0)


def scatter_rows(total, first, bits):
    for bit in range(first, bits):
        half = total.shape[0] // 2
        got = flip(total[half:].astype(bf16), "row", bit)
        total = total[:half] + got.astype(f32)
    return total


def in_order(first, second, parity, axis=0):
    return jnp.where(
        parity == 0,
        jnp.concatenate([first, second], axis),
        jnp.concatenate([second, first], axis),
    )


def pair(block, parity):
    return in_order(block, flip(block, "col", 0), parity)


def keep_half(partial, parity):
    half = partial.shape[0] // 2
    outgoing = lax.dynamic_slice_in_dim(partial, (1 - parity) * half, half, 0).astype(bf16)
    staying = lax.dynamic_slice_in_dim(partial, parity * half, half, 0)
    return staying + flip(outgoing, "col", 0).astype(f32)


def to_pairs(block):
    first = lax.ppermute(block, "col", [(2 * a + b, 2 * b + a) for a in range(2) for b in range(2)])
    second = lax.ppermute(
        block, "col", [(2 * a + b, 2 * (1 - b) + a) for a in range(2) for b in range(2)]
    )
    return first, second


def from_pairs(same, other):
    first = lax.ppermute(same, "col", [(2 * a + b, 2 * b + a) for a in range(2) for b in range(2)])
    second = lax.ppermute(
        other, "col", [(2 * a + b, 2 * b + 1 - a) for a in range(2) for b in range(2)]
    )
    return first, second


def cuts(width):
    first = min(512, width)
    return [(0, first), (first, width)] if first < width else [(0, width)]


def shards(
    layer_input,
    gain_attn,
    qkv_weight,
    qkv_bias,
    out_weight,
    gain_mlp,
    gate_weight,
    up_weight,
    down_weight,
    cotangent,
):
    row = lax.axis_index("row")
    column = lax.axis_index("col")
    row_count = lax.axis_size("row")
    bits = row_count.bit_length() - 1
    core = column % 2
    sequence = column // 2
    tok_local, model_width = layer_input.shape
    length = tok_local * 2
    deep = model_width // row_count
    ff_cols = gate_weight.shape[1]
    qkv_cols = qkv_weight.shape[1]
    out_cols = out_weight.shape[0]
    group_width = 2 * qkv_cols
    query_width = group_width - 2 * HD

    first, second = to_pairs(jnp.concatenate([qkv_weight, out_weight.T], 1))
    low = jnp.where(sequence == 0, first, second)
    high = jnp.where(sequence == 0, second, first)
    qkv_full = gather_rows(jnp.concatenate([low[:, :qkv_cols], high[:, :qkv_cols]], 1), bits)
    out_full = gather_rows(jnp.concatenate([low[:, qkv_cols:], high[:, qkv_cols:]], 1), bits)
    first, second = to_pairs(qkv_bias[None, :])
    bias_full = in_order(first, second, sequence, 1).astype(f32)

    place = jnp.arange(model_width, dtype=jnp.int32)
    masks = jnp.array([bit_reversed(p, bits) for p in range(row_count)], jnp.int32)
    source = jnp.repeat(masks ^ row, deep) * deep + place % deep
    to_stored = (place[:, None] == source[None, :]).astype(bf16)

    def stored(block):
        return jnp.dot(block, to_stored, preferred_element_type=f32)

    def unstored(block):
        return jnp.einsum("ts,fs->tf", block, to_stored, preferred_element_type=f32).astype(bf16)

    def unstored_row(vector):
        blocks = vector.reshape(row_count, deep)
        blocks = jnp.concatenate(
            [blocks[bit_reversed(m, bits)][None] for m in range(row_count)], 0
        )
        for bit in range(bits):
            wide = blocks.reshape(-1, 2, 1 << bit, deep)
            turned = jnp.concatenate([wide[:, 1:], wide[:, :1]], 1).reshape(row_count, deep)
            blocks = jnp.where((row >> bit) % 2 == 1, turned, blocks)
        return blocks.reshape(model_width)

    input_rows = stored(layer_input)
    grad_out = stored(cotangent)
    gain_one = stored(gain_attn[None, :])
    gain_two = stored(gain_mlp[None, :])

    scale_one = lax.rsqrt(jnp.mean(input_rows * input_rows, axis=1) + eps)
    normed_one_blk = (input_rows * scale_one[:, None] * gain_one).astype(bf16)
    normed_one = pair(normed_one_blk, core)
    cosine, sine_part = rope_tables(length)
    qk_rows, value_rows, att_group, log_totals = attend(
        normed_one, qkv_full, bias_full, cosine, sine_part
    )
    att_group = att_group[:, :query_width]
    attn_partial = jnp.einsum("ta,da->td", att_group, out_full, preferred_element_type=f32)
    middle = input_rows + keep_half(attn_partial, core)
    scale_two = lax.rsqrt(jnp.mean(middle * middle, axis=1) + eps)
    normed_two_blk = (middle * scale_two[:, None] * gain_two).astype(bf16)

    def widen(block):
        beside = flip(block, "col", 0)
        across = flip(block, "col", 1)
        return jnp.concatenate([block, beside, across, flip(across, "col", 0)], 0)

    def narrow(partial):
        own, beside, across, far = jnp.split(partial, 4, 0)
        across = across.astype(f32) + flip(far, "col", 0).astype(f32)
        return (
            own.astype(f32)
            + flip(beside, "col", 0).astype(f32)
            + flip(across.astype(bf16), "col", 1).astype(f32)
        )

    normed_two = widen(normed_two_blk)
    grad_full = widen(grad_out.astype(bf16))
    down_flipped = down_weight.T
    sums = None
    totals = []
    for start, stop in cuts(ff_cols):
        width = stop - start
        padded = -(-width // 256) * 256
        pieces = [
            jnp.pad(part[:, start:stop], ((0, 0), (0, padded - width)))
            for part in (gate_weight, up_weight, down_flipped)
        ]
        joined = gather_rows(jnp.concatenate(pieces, 1), bits)
        hidden, grad_gate, grad_up, *sums = mlp(normed_two, grad_full, joined, width, sums)
        half = model_width // 2

        def products(columns):
            return [
                jnp.einsum("td,tf->df", rows[:, columns], right, preferred_element_type=f32)
                for rows, right in (
                    (normed_two, grad_gate),
                    (normed_two, grad_up),
                    (grad_full, hidden),
                )
            ]

        sent = jnp.concatenate([part.astype(bf16) for part in products(slice(half, None))], 1)
        kept = jnp.concatenate(products(slice(0, half)), 1)
        total = kept + flip(sent, "row", 0).astype(f32)
        total = scatter_rows(total, 1, bits)
        totals.append([total[:, :width], total[:, width : 2 * width], total[:, 2 * width :]])
    down_sum, normed_sum = sums
    gate_total, up_total, down_total = zip(*totals)
    grad_normed_two = narrow(normed_sum)
    layer_output = unstored((middle + narrow(down_sum)).astype(bf16))
    scaled_two = gain_two * grad_normed_two
    inner_two = jnp.sum(scaled_two * middle, axis=1)
    grad_middle = (
        grad_out
        + scale_two[:, None] * scaled_two
        - middle * (scale_two**3 * inner_two / model_width)[:, None]
    )
    gain_two_grad = jnp.sum(grad_normed_two * middle * scale_two[:, None], axis=0)
    grad_branch = pair(grad_middle.astype(bf16), core)
    out_grad = jnp.einsum("td,ta->da", grad_branch, att_group, preferred_element_type=f32)
    grad_mixed, bias_grad = attend_back(
        grad_branch, out_full, qk_rows, value_rows, log_totals, cosine, sine_part
    )
    bias_grad = bias_grad[0]
    qkv_grad = jnp.einsum("td,tc->dc", normed_one, grad_mixed, preferred_element_type=f32)
    grad_normed_one = keep_half(
        jnp.einsum("tc,dc->td", grad_mixed, qkv_full, preferred_element_type=f32), core
    )
    scaled_one = gain_one * grad_normed_one
    inner_one = jnp.sum(scaled_one * input_rows, axis=1)
    input_grad = unstored(
        (
            grad_middle
            + scale_one[:, None] * scaled_one
            - input_rows * (scale_one**3 * inner_one / model_width)[:, None]
        ).astype(bf16)
    )
    gain_one_grad = jnp.sum(grad_normed_one * input_rows * scale_one[:, None], axis=0)

    def to_columns(total):
        half = total.shape[1] // 2
        low, high = total[:, :half].astype(bf16), total[:, half:].astype(bf16)
        first, second = from_pairs(
            jnp.where(sequence == 0, low, high), jnp.where(sequence == 0, high, low)
        )
        return first.astype(f32) + second.astype(f32)

    out_total = to_columns(scatter_rows(out_grad, 0, bits))
    qkv_total = to_columns(scatter_rows(qkv_grad, 0, bits))
    bias_row = lax.dynamic_update_slice_in_dim(
        jnp.zeros((group_width * 2,), f32), bias_grad, core * group_width, 0
    )
    small = jnp.concatenate([unstored_row(gain_one_grad), unstored_row(gain_two_grad), bias_row])
    small = jnp.pad(small, (0, -small.shape[0] % 128)).reshape(-1, 128)
    for bit in range(2):
        small = small + flip(small, "col", bit)
    for bit in range(bits):
        small = small + flip(small, "row", bit)
    small = small.reshape(-1)
    gain_one_total = small[:model_width]
    gain_two_total = small[model_width : 2 * model_width]
    bias_total = lax.dynamic_slice_in_dim(small, 2 * model_width + column * qkv_cols, qkv_cols, 0)
    return (
        layer_output,
        input_grad,
        gain_one_total,
        qkv_total,
        bias_total,
        out_total.T,
        gain_two_total,
        jnp.concatenate(gate_total, 1),
        jnp.concatenate(up_total, 1),
        jnp.concatenate(down_total, 1).T,
    )


def solution(mesh):
    in_specs = (
        P(("row", "col"), None),
        P(),
        P("row", "col"),
        P("col"),
        P("col", "row"),
        P(),
        P("row", "col"),
        P("row", "col"),
        P("col", "row"),
        P(("row", "col"), None),
    )
    out_specs = (
        P(("row", "col"), None),
        P(("row", "col"), None),
        P(),
        P("row", "col"),
        P("col"),
        P("col", "row"),
        P(),
        P("row", "col"),
        P("row", "col"),
        P("col", "row"),
    )
    return jax.shard_map(shards, mesh=mesh, in_specs=in_specs, out_specs=out_specs, check_vma=False)
```

```python
import functools
import math

import jax
import jax.numpy as jnp
from jax import lax
from jax.experimental import pallas as pl
from jax.experimental.pallas import tpu as pltpu
from jax.sharding import PartitionSpec as P

HD = 64
eps = 1e-06
theta_base = 1000000.0
bf16 = jnp.bfloat16
f32 = jnp.float32
NT = (((1,), (1,)), ((), ()))
TN = (((0,), (0,)), ((), ()))
MIB = 1024 * 1024


def flip(block, axis, bit):
    count = lax.axis_size(axis)
    return lax.ppermute(block, axis, [(i, i ^ 1 << bit) for i in range(count)])


def bit_reversed(value, bits):
    return sum((value >> b & 1) << (bits - 1 - b) for b in range(bits))


def after(value, *earlier):
    return lax.optimization_barrier((value, *earlier))[0]


def kernel_params(mib):
    return pltpu.CompilerParams(vmem_limit_bytes=mib * MIB)


def cost(flops, nbytes, exps=0):
    return pl.CostEstimate(flops=int(flops), bytes_accessed=int(nbytes), transcendentals=int(exps))


def whole(array):
    return pl.BlockSpec(array.shape, lambda *_: (0,) * len(array.shape))


def in_place(block):
    return pl.BlockSpec(memory_space=pl.ANY)


def assemble(pieces, held, sems):
    copies = []
    at = 0
    for i, piece in enumerate(pieces):
        rows = piece.shape[0]
        copies.append(pltpu.make_async_copy(piece, held.at[pl.ds(at, rows)], sems.at[i]))
        at += rows
    for copy in copies:
        copy.start()
    for copy in copies:
        copy.wait()


def halves_turned(block):
    lane = lax.broadcasted_iota(jnp.int32, block.shape, 1)
    up = pltpu.roll(block, 128 - HD // 2, 1)
    return jnp.where(lane % HD < HD // 2, up, pltpu.roll(block, HD // 2, 1))


def side_rows(r, block, half, parity):
    side = (r // half) ^ parity
    return pl.ds(pl.multiple_of(side * half + r % half, block), block)


def pad_heads(key_value, rows, value, last):
    lane = lax.broadcasted_iota(jnp.int32, (1, 128), 1)
    kpad, vpad = key_value
    zero = jnp.zeros_like(value)
    vpad[0, rows, :] = jnp.concatenate([value, zero], 1).astype(bf16)
    vpad[1, rows, :] = jnp.concatenate([zero, value], 1).astype(bf16)
    kpad[1, rows, :] = jnp.where(lane >= HD, last, 0.0).astype(bf16)
    kpad[0, rows, :] = jnp.where(lane < HD, pltpu.roll(last, HD, 1), 0.0).astype(bf16)


def attend_kernel(parity_ref, own_ref, other_ref, bias_ref, cos_ref, sin_ref, *rest, block, count):
    pieces = rest[:count]
    qk_ref, v_ref, att_ref, lse_ref, held, kpad, vpad, lse_cols, sems = rest[count:]
    step = pl.program_id(0)
    half = own_ref.shape[0]
    length = 2 * half
    wide = qk_ref.shape[1]
    pairs = wide // 128
    parity = parity_ref[0]

    @pl.when(step == 0)
    def _():
        assemble(pieces, held, sems)
        for side, rows_ref in enumerate((own_ref, other_ref)):
            for r in range(0, half, block):
                at = pl.multiple_of((side ^ parity) * half + r, block)
                rows = pl.ds(at, block)
                mixed = jnp.dot(rows_ref[r : r + block, :], held[...], preferred_element_type=f32)
                mixed = (mixed + bias_ref[...]).astype(bf16).astype(f32)
                cos, sin = cos_ref[rows, :], sin_ref[rows, :]
                for p in range(pairs):
                    u = mixed[:, p * 128 : (p + 1) * 128]
                    turned = (u * cos + halves_turned(u) * sin).astype(bf16)
                    qk_ref[rows, p * 128 : (p + 1) * 128] = turned
                v_ref[rows, :] = mixed[:, wide:].astype(bf16)
                pad_heads((kpad, vpad), rows, mixed[:, wide:], turned.astype(f32))
        lse_cols[...] = jnp.zeros_like(lse_cols)

    factor = HD**-0.5 * math.log2(math.e)
    cols = pl.ds(pl.multiple_of(step * 128, 128), 128)
    row_i = lax.broadcasted_iota(jnp.int32, (block, block), 0)
    col_i = lax.broadcasted_iota(jnp.int32, (block, block), 1)
    for r in range(0, length, block):
        rows = pl.ds(r, block)
        to = side_rows(r, block, half, parity)
        q = qk_ref[rows, cols]

        def head(odd):
            keys = kpad[odd, : r + block, :]
            scores = lax.dot_general(q, keys, NT, preferred_element_type=f32)
            diag = jnp.where(col_i <= row_i, scores[:, r:], -1e30)
            scores = jnp.concatenate([scores[:, :r], diag], 1) if r else diag
            top = jnp.max(scores, 1, keepdims=True)
            e = jnp.exp2((scores - top) * factor)
            total = jnp.sum(e, 1, keepdims=True)
            out = jnp.dot(e.astype(bf16), vpad[odd, : r + block, :], preferred_element_type=f32)
            lse = top * factor + jnp.log2(total)
            at = lax.broadcasted_iota(jnp.int32, (1, 128), 1) == 2 * step + odd
            lse_cols[rows, :] = jnp.where(at, lse, lse_cols[rows, :])
            return out / total

        even = head(0)

        @pl.when(step < pairs - 1)
        def _():
            att_ref[to, :] = (even + head(1)).astype(bf16)

        @pl.when(step == pairs - 1)
        def _():
            att_ref[to, :] = even.astype(bf16)

    @pl.when(step == pairs - 1)
    def _():
        lse_ref[...] = lse_cols[...].T[: lse_ref.shape[0], :]


def attend(parity, own, other, pieces, bias, cos, sin):
    half, depth = own.shape
    length = 2 * half
    group = bias.shape[1]
    wide = group - HD
    pairs = wide // 128
    block = min(256, half)
    return pl.pallas_call(
        functools.partial(attend_kernel, block=block, count=len(pieces)),
        grid=(pairs,),
        in_specs=[pl.BlockSpec(memory_space=pltpu.SMEM)]
        + [whole(a) for a in (own, other, bias, cos, sin)]
        + [in_place(piece) for piece in pieces],
        out_specs=[
            pl.BlockSpec((length, wide), lambda p: (0, 0)),
            pl.BlockSpec((length, HD), lambda p: (0, 0)),
            pl.BlockSpec((length, 128), lambda p: (0, p)),
            pl.BlockSpec((8, length), lambda p: (0, 0)),
        ],
        out_shape=[
            jax.ShapeDtypeStruct((length, wide), bf16),
            jax.ShapeDtypeStruct((length, HD), bf16),
            jax.ShapeDtypeStruct((length, wide), bf16),
            jax.ShapeDtypeStruct((8, length), f32),
        ],
        scratch_shapes=[
            pltpu.VMEM((depth, group), bf16),
            pltpu.VMEM((2, length, 128), bf16),
            pltpu.VMEM((2, length, 128), bf16),
            pltpu.VMEM((length, 128), f32),
            pltpu.SemaphoreType.DMA((len(pieces),)),
        ],
        compiler_params=kernel_params(40),
        cost_estimate=cost(12e9, 8e6, 5e6),
    )(parity, own, other, bias, cos, sin, *pieces)


def project_kernel(att_ref, *rest, count):
    pieces = rest[:count]
    own_ref, other_ref, held, sems = rest[count:]
    half = own_ref.shape[0]
    assemble(pieces, held, sems)
    for side, ref in enumerate((own_ref, other_ref)):
        rows = att_ref[side * half : (side + 1) * half, :]
        ref[...] = lax.dot_general(rows, held[...], NT, preferred_element_type=f32).astype(ref.dtype)


def project(att, pieces):
    length, wide = att.shape
    depth = sum(piece.shape[0] for piece in pieces)
    return pl.pallas_call(
        functools.partial(project_kernel, count=len(pieces)),
        in_specs=[pl.BlockSpec(memory_space=pltpu.VMEM)] + [in_place(piece) for piece in pieces],
        out_specs=[pl.BlockSpec(memory_space=pltpu.VMEM)] * 2,
        out_shape=[
            jax.ShapeDtypeStruct((length // 2, depth), f32),
            jax.ShapeDtypeStruct((length // 2, depth), bf16),
        ],
        scratch_shapes=[
            pltpu.VMEM((depth, wide), bf16),
            pltpu.SemaphoreType.DMA((len(pieces),)),
        ],
        compiler_params=kernel_params(40),
        cost_estimate=cost(2 * length * depth * wide, 6e6),
    )(att, *pieces)


def attend_back_kernel(
    parity_ref, own_ref, other_ref, qk_ref, v_ref, lse_ref, cos_ref, sin_ref, *rest, block, count
):
    pieces = rest[:count]
    mixed_ref, bias_ref, held, kpad, vpad, gatt, dq_acc, dk, dv, sems = rest[count:]
    step = pl.program_id(0)
    half_rows = own_ref.shape[0]
    length = 2 * half_rows
    wide = qk_ref.shape[1]
    pairs = wide // 128
    parity = parity_ref[0]
    lane = lax.broadcasted_iota(jnp.int32, (1, 128), 1)

    @pl.when(step == 0)
    def _():
        assemble(pieces, held, sems)
        for side, rows_ref in enumerate((own_ref, other_ref)):
            for r in range(0, half_rows, block):
                rows = pl.ds(pl.multiple_of((side ^ parity) * half_rows + r, block), block)
                got = jnp.dot(rows_ref[r : r + block, :], held[...], preferred_element_type=f32)
                gatt[rows, :] = got.astype(bf16)
        for r in range(0, length, block):
            rows = pl.ds(r, block)
            last = qk_ref[rows, wide - 128 :].astype(f32)
            pad_heads((kpad, vpad), rows, v_ref[rows, :].astype(f32), last)
        dk[...] = jnp.zeros_like(dk)
        dv[...] = jnp.zeros_like(dv)

    factor = HD**-0.5 * math.log2(math.e)
    cols = pl.ds(pl.multiple_of(step * 128, 128), 128)
    key_i = lax.broadcasted_iota(jnp.int32, (block, block), 0)
    query_i = lax.broadcasted_iota(jnp.int32, (block, block), 1)
    for r in range(0, length, block):
        rows = pl.ds(r, block)
        q = qk_ref[rows, cols]
        g = gatt[rows, cols]

        def head(odd):
            lse = lse_ref[pl.ds(2 * step + odd, 1), rows]
            probs, grads = [], []
            inner = jnp.zeros((1, block), f32)
            for c in range(0, r + block, block):
                scores = lax.dot_general(
                    kpad[odd, c : c + block, :], q, NT, preferred_element_type=f32
                )
                p = jnp.exp2(scores * factor - lse)
                if c == r:
                    p = jnp.where(key_i <= query_i, p, 0.0)
                dp = lax.dot_general(vpad[odd, c : c + block, :], g, NT, preferred_element_type=f32)
                inner = inner + jnp.sum(p * dp, 0, keepdims=True)
                probs.append(p)
                grads.append(dp)
            dq = 0.0
            half = lane >= HD if odd else lane < HD
            for i, c in enumerate(range(0, r + block, block)):
                keys = pl.ds(c, block)
                ds = (probs[i] * (grads[i] - inner)).astype(bf16)
                p = probs[i].astype(bf16)
                dk[keys, :] += jnp.where(half, jnp.dot(ds, q, preferred_element_type=f32), 0.0)
                dv[keys, :] += jnp.where(half, jnp.dot(p, g, preferred_element_type=f32), 0.0)
                dq = dq + lax.dot_general(
                    ds, kpad[odd, c : c + block, :], TN, preferred_element_type=f32
                )
            return dq

        dq_acc[rows, :] = head(0)

        @pl.when(step < pairs - 1)
        def _():
            dq_acc[rows, :] += head(1)

    def back(u, rows):
        return u * cos_ref[rows, :] - halves_turned(u) * sin_ref[rows, :]

    scale = HD**-0.5
    for r in range(0, length, block):
        rows = pl.ds(r, block)
        to = side_rows(r, block, half_rows, parity)

        @pl.when(step < pairs - 1)
        def _():
            mixed_ref[to, cols] = back(dq_acc[rows, :] * scale, rows).astype(bf16)

        @pl.when(step == pairs - 1)
        def _():
            k = dk[rows, :]
            k = jnp.where(lane >= HD, k + pltpu.roll(k, HD, 1), dq_acc[rows, :]) * scale
            mixed_ref[to, wide - 128 : wide] = back(k, rows).astype(bf16)
            v = dv[rows, :]
            v = v + pltpu.roll(v, HD, 1)
            mixed_ref[to, wide:] = v[:, :HD].astype(bf16)

    @pl.when(step == pairs - 1)
    def _():
        total = jnp.zeros((1, mixed_ref.shape[1]), f32)
        for r in range(0, length, block):
            part = mixed_ref[pl.ds(r, block), :].astype(f32)
            total = total + jnp.sum(part, 0, keepdims=True)
        bias_ref[...] = total


def attend_back(parity, own, other, pieces, qk, v, lse, cos, sin):
    half, depth = own.shape
    length = 2 * half
    wide = qk.shape[1]
    group = wide + HD
    pairs = wide // 128
    block = min(256, half)
    ins = (own, other, qk, v, lse, cos, sin)
    return pl.pallas_call(
        functools.partial(attend_back_kernel, block=block, count=len(pieces)),
        grid=(pairs,),
        in_specs=[pl.BlockSpec(memory_space=pltpu.SMEM)]
        + [whole(a) for a in ins]
        + [in_place(piece) for piece in pieces],
        out_specs=[
            pl.BlockSpec((length, group), lambda p: (0, 0)),
            pl.BlockSpec((1, group), lambda p: (0, 0)),
        ],
        out_shape=[
            jax.ShapeDtypeStruct((length, group), bf16),
            jax.ShapeDtypeStruct((1, group), f32),
        ],
        scratch_shapes=[
            pltpu.VMEM((depth, wide), bf16),
            pltpu.VMEM((2, length, 128), bf16),
            pltpu.VMEM((2, length, 128), bf16),
            pltpu.VMEM((length, wide), bf16),
            pltpu.VMEM((length, 128), f32),
            pltpu.VMEM((length, 128), f32),
            pltpu.VMEM((length, 128), f32),
            pltpu.SemaphoreType.DMA((len(pieces),)),
        ],
        compiler_params=kernel_params(50),
        cost_estimate=cost(25e9, 8e6, 5e6),
    )(parity, *ins, *pieces)


def mlp_kernel(x0_ref, x1_ref, g0_ref, g1_ref, *rest, count, add):
    pieces = rest[:count]
    rest = rest[count:]
    if add:
        near_in, far_in, act_ref, near_ref, far_ref, held, sems = rest
    else:
        act_ref, near_ref, far_ref, held, sems = rest
    n = held.shape[1] // 3
    step = pl.program_id(0)

    @pl.when(step == 0)
    def _():
        assemble(pieces, held, sems)

    wg, wu, wd = (held[:, k * n : (k + 1) * n] for k in range(3))
    x = jnp.where(step == 0, x0_ref[...], x1_ref[...])
    g = jnp.where(step == 0, g0_ref[...], g1_ref[...])
    gate = jnp.dot(x, wg, preferred_element_type=f32)
    up = jnp.dot(x, wu, preferred_element_type=f32)
    gh = jnp.dot(g, wd, preferred_element_type=f32)
    sig = 1.0 / (1.0 + jnp.exp(-gate))
    silu = gate * sig
    hid = (silu * up).astype(bf16)
    ghs = gh * sig
    gg = (ghs * up * (1.0 + gate - silu)).astype(bf16)
    gu = (ghs * gate).astype(bf16)
    act_ref[:, :n] = gg
    act_ref[:, n : 2 * n] = gu
    act_ref[:, 2 * n :] = hid
    ngrad = lax.dot_general(gg, wg, NT, preferred_element_type=f32)
    ngrad = ngrad + lax.dot_general(gu, wu, NT, preferred_element_type=f32)
    down = lax.dot_general(hid, wd, NT, preferred_element_type=f32)

    @pl.when(step == 0)
    def _():
        near_ref[0] = (ngrad + near_in[0].astype(f32) if add else ngrad).astype(bf16)
        near_ref[1] = (down + near_in[1].astype(f32) if add else down).astype(bf16)

    @pl.when(step == 1)
    def _():
        far_ref[0] = (ngrad + far_in[0].astype(f32) if add else ngrad).astype(bf16)
        far_ref[1] = (down + far_in[1].astype(f32) if add else down).astype(bf16)


def mlp(rows, grads, pieces, sums=None):
    t, d = rows[0].shape
    columns = pieces[0].shape[1]
    add = sums is not None
    ins = (*rows, *grads)
    sums = tuple(sums or ())
    both = pl.BlockSpec((2, t, d), lambda i: (0, 0, 0))
    return pl.pallas_call(
        functools.partial(mlp_kernel, count=len(pieces), add=add),
        grid=(2,),
        in_specs=[whole(a) for a in ins] + [in_place(p) for p in pieces] + [both] * len(sums),
        out_specs=[pl.BlockSpec((t, columns), lambda i: (i, 0)), both, both],
        out_shape=[
            jax.ShapeDtypeStruct((2 * t, columns), bf16),
            jax.ShapeDtypeStruct((2, t, d), bf16),
            jax.ShapeDtypeStruct((2, t, d), bf16),
        ],
        scratch_shapes=[
            pltpu.VMEM((d, columns), bf16),
            pltpu.SemaphoreType.DMA((len(pieces),)),
        ],
        compiler_params=kernel_params(58),
        cost_estimate=cost(8 * t * d * columns, 30 * MIB, 2 * t * columns),
    )(*ins, *pieces, *sums)


def outer_kernel(*refs, groups, blocks):
    rights = refs[groups * blocks : -2]
    sent_ref, kept_ref = refs[-2:]
    half = kept_ref.shape[0]
    t = refs[0].shape[0]

    def fill(lefts):
        for part, ref in ((slice(half, 2 * half), sent_ref), (slice(0, half), kept_ref)):
            total = 0.0
            for i, left in enumerate(lefts):
                right = rights[i * t // rights[0].shape[0]]
                at = i * t % right.shape[0]
                total = total + lax.dot_general(
                    left[:, part], right[at : at + t, :], TN, preferred_element_type=f32
                )
            ref[...] = total.astype(ref.dtype)

    step = pl.program_id(0)
    if groups == 1:
        fill(refs[:blocks])
    else:
        @pl.when(step < 2)
        def _():
            fill(refs[:blocks])

        @pl.when(step == 2)
        def _():
            fill(refs[blocks : 2 * blocks])


def outer(lefts, rights):
    groups, blocks = len(lefts), len(lefts[0])
    steps = 1 if groups == 1 else 3
    t, d = lefts[0][0].shape
    rows = rights[0].shape[0]
    columns = rights[0].shape[1]
    n = columns // steps
    flat = [left for group in lefts for left in group]
    out = pl.BlockSpec((d // 2, n), lambda k: (0, k))
    return pl.pallas_call(
        functools.partial(outer_kernel, groups=groups, blocks=blocks),
        grid=(steps,),
        in_specs=[whole(left) for left in flat]
        + [pl.BlockSpec((rows, n), lambda k: (0, k)) for _ in rights],
        out_specs=[out, out],
        out_shape=[
            jax.ShapeDtypeStruct((d // 2, columns), bf16),
            jax.ShapeDtypeStruct((d // 2, columns), f32),
        ],
        compiler_params=kernel_params(58),
        cost_estimate=cost(2 * t * blocks * d * columns, 20 * MIB),
    )(*flat, *rights)


def rope_tables(length):
    inverse = theta_base ** (-(jnp.arange(HD // 2, dtype=f32) * 2.0 / HD))
    angles = jnp.arange(length, dtype=f32)[:, None] * inverse[None, :]
    c, s = jnp.cos(angles), jnp.sin(angles)
    return jnp.concatenate([c] * 4, 1), jnp.concatenate([-s, s, -s, s], 1)


class Gather:
    def __init__(self, block, bits):
        self.bits = bits
        self.left = bits - 1
        self.pieces = [block]
        self.beside = []
        self.fresh = block

    def ready(self, *earlier):
        self.fresh = after(self.fresh, *earlier)
        self.pieces[-1] = self.fresh

    def step(self):
        self.beside.append(flip(self.fresh, "row", 0))
        if self.left > 0:
            held = jnp.concatenate(self.pieces, 0) if len(self.pieces) > 1 else self.pieces[0]
            self.fresh = flip(held, "row", self.left)
            self.pieces.append(self.fresh)
            self.left -= 1

    def all(self):
        while len(self.beside) < self.bits:
            self.step()
        out = self.pieces + self.beside
        return out if out[0].shape[0] % 16 == 0 else [jnp.concatenate(out, 0)]


def halve(kept, got, bits, bit):
    half = kept.shape[0] // 2
    sent = (kept[half:] + got[half:].astype(f32)).astype(bf16)
    return sent, kept[:half] + got[:half].astype(f32)


class Scatter:
    def __init__(self, sent, kept, bits):
        self.bits, self.bit = bits, 0
        self.kept = kept
        self.got = flip(sent, "row", 0)

    def step(self):
        if self.bit == self.bits - 1:
            return
        self.bit += 1
        sent, self.kept = halve(self.kept, self.got, self.bits, self.bit)
        self.got = flip(sent, "row", self.bit)

    def total(self):
        while self.bit < self.bits - 1:
            self.step()
        return self.kept + self.got.astype(f32)


def turned_pairs(block):
    first = [(2 * a + b, 2 * b + a) for a in range(2) for b in range(2)]
    second = [(2 * a + b, 2 * (1 - b) + a) for a in range(2) for b in range(2)]
    return lax.ppermute(block, "col", first), lax.ppermute(block, "col", second)


def from_pairs(same, other):
    first = [(2 * a + b, 2 * b + a) for a in range(2) for b in range(2)]
    second = [(2 * a + b, 2 * b + 1 - a) for a in range(2) for b in range(2)]
    return lax.ppermute(same, "col", first), lax.ppermute(other, "col", second)


def cuts(width):
    first = min(512, width)
    return [(0, first), (first, width)] if first < width else [(0, width)]


def shards(
    layer_input,
    gain_attn,
    qkv_weight,
    qkv_bias,
    out_weight,
    gain_mlp,
    gate_weight,
    up_weight,
    down_weight,
    cotangent,
):
    row = lax.axis_index("row")
    column = lax.axis_index("col")
    row_count = lax.axis_size("row")
    bits = row_count.bit_length() - 1
    core = column % 2
    sequence = column // 2
    parity = core.astype(jnp.int32).reshape(1)
    tok_local, model_width = layer_input.shape
    length = tok_local * 2
    deep = model_width // row_count
    ff_cols = gate_weight.shape[1]
    qkv_cols = qkv_weight.shape[1]
    out_cols = out_weight.shape[0]
    group_width = 2 * qkv_cols
    query_width = group_width - 2 * HD

    bias_rows = jnp.pad(qkv_bias[None, :], ((0, 15), (0, 0)))
    first, second = turned_pairs(
        jnp.concatenate(
            [
                jnp.concatenate([qkv_weight, bias_rows], 0),
                jnp.pad(out_weight.T, ((0, 16), (0, 0))),
            ],
            1,
        )
    )
    low = jnp.where(sequence == 0, first, second)
    high = jnp.where(sequence == 0, second, first)
    qkv_own = jnp.concatenate([low[:, :qkv_cols], high[:, :qkv_cols]], 1)
    bias_full = qkv_own[deep : deep + 1].astype(f32)
    out_own = jnp.concatenate([low[:deep, qkv_cols:], high[:deep, qkv_cols:]], 1)
    out_own = jnp.pad(out_own, ((0, 0), (0, HD)))
    qkv_gather = Gather(qkv_own[:deep], bits)
    out_gather = Gather(out_own, bits)
    down_flipped = down_weight.T
    mlp_gathers = []
    for start, stop in cuts(ff_cols):
        padded = -(-(stop - start) // 256) * 256
        pieces = [
            jnp.pad(part[:, start:stop], ((0, 0), (0, padded - (stop - start))))
            for part in (gate_weight, up_weight, down_flipped)
        ]
        mlp_gathers.append(Gather(jnp.concatenate(pieces, 1), bits))
    qkv_gather.step()
    out_gather.ready(qkv_gather.fresh)
    qkv_gather.step()
    out_gather.step()
    mlp_gathers[0].ready(qkv_gather.fresh, out_gather.fresh)
    qkv_pieces = qkv_gather.all()
    out_gather.step()
    mlp_gathers[0].step()
    mlp_gathers[1].ready(qkv_pieces[-1], out_gather.fresh)
    out_pieces = out_gather.all()
    mlp_gathers[1].step()

    place = jnp.arange(model_width, dtype=jnp.int32)
    masks = jnp.array([bit_reversed(p, bits) for p in range(row_count)], jnp.int32)
    source = jnp.repeat(masks ^ row, deep) * deep + place % deep
    to_stored = (place[:, None] == source[None, :]).astype(bf16)

    def stored(block):
        return jnp.dot(block, to_stored, preferred_element_type=f32)

    def unstored(block):
        return jnp.einsum("ts,fs->tf", block, to_stored, preferred_element_type=f32).astype(bf16)

    def unstored_row(vector):
        blocks = vector.reshape(row_count, deep)
        blocks = jnp.concatenate(
            [blocks[bit_reversed(m, bits)][None] for m in range(row_count)], 0
        )
        for bit in range(bits):
            wide = blocks.reshape(-1, 2, 1 << bit, deep)
            turned = jnp.concatenate([wide[:, 1:], wide[:, :1]], 1).reshape(row_count, deep)
            blocks = jnp.where((row >> bit) % 2 == 1, turned, blocks)
        return blocks.reshape(model_width)

    input_rows = stored(layer_input)
    grad_out = stored(cotangent)
    gain_one = stored(gain_attn[None, :])
    gain_two = stored(gain_mlp[None, :])

    scale_one = lax.rsqrt(jnp.mean(input_rows * input_rows, axis=1) + eps)
    normed_own = (input_rows * scale_one[:, None] * gain_one).astype(bf16)
    normed_other = flip(normed_own, "col", 0)
    grad_blocks = [grad_out.astype(bf16)]
    grad_blocks.append(flip(grad_blocks[0], "col", 0))
    across = flip(grad_blocks[0], "col", 1)
    grad_blocks += [across, flip(across, "col", 0)]
    cosine, sine_part = rope_tables(length)
    qk_rows, value_rows, att_rows, log_totals = attend(
        parity,
        normed_own,
        normed_other,
        qkv_pieces,
        bias_full,
        cosine,
        sine_part,
    )
    att_own, att_other = project(att_rows, out_pieces)
    middle = input_rows + att_own + flip(att_other, "col", 0).astype(f32)
    scale_two = lax.rsqrt(jnp.mean(middle * middle, axis=1) + eps)
    blocks = [(middle * scale_two[:, None] * gain_two).astype(bf16)]
    across = flip(blocks[0], "col", 1)
    blocks.append(flip(blocks[0], "col", 0))
    blocks += [across, flip(across, "col", 0)]

    first_pieces, second_pieces = (gather.all() for gather in mlp_gathers)
    act_own, *sums_own = mlp(blocks[:2], grad_blocks[:2], first_pieces)
    act_far, *sums_far = mlp(blocks[2:], grad_blocks[2:], first_pieces)
    first_scatter = Scatter(*outer([blocks, grad_blocks], [act_own, act_far]), bits)
    start_far = after(blocks[2], first_scatter.kept)
    act_far, near_far, far_far = mlp(
        [start_far, blocks[3]], grad_blocks[2:], second_pieces, sums_far
    )
    across = near_far.astype(f32) + flip(far_far, "col", 0).astype(f32)
    across = across.astype(bf16)
    normed_back = flip(across[0], "col", 1)
    act_own, near_own, far_own = mlp(
        [after(blocks[0], across), blocks[1]], grad_blocks[:2], second_pieces, sums_own
    )
    beside = flip(far_own, "col", 0)
    first_scatter.step()
    second_scatter = Scatter(*outer([blocks, grad_blocks], [act_own, act_far]), bits)
    down_back = flip(after(across[1], normed_back), "col", 1)

    def summed(k, back):
        return near_own[k].astype(f32) + beside[k].astype(f32) + back.astype(f32)

    grad_normed_two = summed(0, normed_back)
    scaled_two = gain_two * grad_normed_two
    inner_two = jnp.sum(scaled_two * middle, axis=1)
    grad_middle = (
        grad_out
        + scale_two[:, None] * scaled_two
        - middle * (scale_two**3 * inner_two / model_width)[:, None]
    )
    gain_two_grad = jnp.sum(grad_normed_two * middle * scale_two[:, None], axis=0)
    branch_own = grad_middle.astype(bf16)
    branch_other = flip(branch_own, "col", 0)
    out_scatter = Scatter(*outer([[branch_own, branch_other]], [att_rows]), bits)
    layer_output = unstored((middle + summed(1, down_back)).astype(bf16))
    grad_mixed, bias_grad = attend_back(
        parity,
        branch_own,
        branch_other,
        out_pieces,
        qk_rows,
        value_rows,
        log_totals,
        cosine,
        sine_part,
    )
    bias_grad = bias_grad[0]
    qkv_scatter = Scatter(*outer([[normed_own, normed_other]], [grad_mixed]), bits)
    qkv_full = jnp.concatenate(qkv_pieces, 0)
    partial = jnp.einsum("tc,dc->td", grad_mixed, qkv_full, preferred_element_type=f32)
    grad_normed_one = partial[:tok_local] + flip(
        partial[tok_local:].astype(bf16), "col", 0
    ).astype(f32)
    scaled_one = gain_one * grad_normed_one
    inner_one = jnp.sum(scaled_one * input_rows, axis=1)
    input_grad = unstored(
        (
            grad_middle
            + scale_one[:, None] * scaled_one
            - input_rows * (scale_one**3 * inner_one / model_width)[:, None]
        ).astype(bf16)
    )
    gain_one_grad = jnp.sum(grad_normed_one * input_rows * scale_one[:, None], axis=0)

    def to_columns(total, width):
        low, high = total[:, :width].astype(bf16), total[:, width : 2 * width].astype(bf16)
        first, second = from_pairs(
            jnp.where(sequence == 0, low, high), jnp.where(sequence == 0, high, low)
        )
        return first.astype(f32) + second.astype(f32)

    qkv_total = to_columns(qkv_scatter.total(), qkv_cols)
    out_total = to_columns(out_scatter.total(), out_cols)
    mlp_totals = []
    for scatter, (start, stop) in zip((first_scatter, second_scatter), cuts(ff_cols)):
        total = scatter.total()
        padded = total.shape[1] // 3
        mlp_totals.append(
            [total[:, k * padded : k * padded + stop - start] for k in range(3)]
        )
    gate_total, up_total, down_total = (jnp.concatenate(parts, 1) for parts in zip(*mlp_totals))
    bias_row = lax.dynamic_update_slice_in_dim(
        jnp.zeros((group_width * 2,), f32), bias_grad, core * group_width, 0
    )
    small = jnp.concatenate([unstored_row(gain_one_grad), unstored_row(gain_two_grad), bias_row])
    small = jnp.pad(small, (0, -small.shape[0] % 128)).reshape(-1, 128)
    for bit in range(2):
        small = small + flip(small, "col", bit)
    for bit in range(bits):
        small = small + flip(small, "row", bit)
    small = small.reshape(-1)
    gain_one_total = small[:model_width]
    gain_two_total = small[model_width : 2 * model_width]
    bias_total = lax.dynamic_slice_in_dim(small, 2 * model_width + column * qkv_cols, qkv_cols, 0)
    return (
        layer_output,
        input_grad,
        gain_one_total,
        qkv_total,
        bias_total,
        out_total.T,
        gain_two_total,
        gate_total,
        up_total,
        down_total.T,
    )


def solution(mesh):
    in_specs = (
        P(("row", "col"), None),
        P(),
        P("row", "col"),
        P("col"),
        P("col", "row"),
        P(),
        P("row", "col"),
        P("row", "col"),
        P("col", "row"),
        P(("row", "col"), None),
    )
    out_specs = (
        P(("row", "col"), None),
        P(("row", "col"), None),
        P(),
        P("row", "col"),
        P("col"),
        P("col", "row"),
        P(),
        P("row", "col"),
        P("row", "col"),
        P("col", "row"),
    )
    return jax.shard_map(shards, mesh=mesh, in_specs=in_specs, out_specs=out_specs, check_vma=False)
```

```python
import functools
import math

import jax
import jax.numpy as jnp
from jax import lax
from jax.experimental import pallas as pl
from jax.experimental.pallas import tpu as pltpu
from jax.sharding import PartitionSpec as P

HD = 64
eps = 1e-06
theta_base = 1000000.0
bf16 = jnp.bfloat16
f32 = jnp.float32
NT = (((1,), (1,)), ((), ()))
TN = (((0,), (0,)), ((), ()))
MIB = 1024 * 1024


def flip(block, axis, bit):
    count = lax.axis_size(axis)
    return lax.ppermute(block, axis, [(i, i ^ 1 << bit) for i in range(count)])


def bit_reversed(value, bits):
    return sum((value >> b & 1) << (bits - 1 - b) for b in range(bits))


def after(value, *earlier):
    return lax.optimization_barrier((value, *earlier))[0]


def kernel_params(mib):
    return pltpu.CompilerParams(vmem_limit_bytes=mib * MIB)


def cost(flops, nbytes, exps=0):
    return pl.CostEstimate(
        flops=int(flops), bytes_accessed=int(nbytes), transcendentals=int(exps)
    )


def whole(array):
    return pl.BlockSpec(array.shape, lambda *_: (0,) * len(array.shape))


def in_place(block):
    return pl.BlockSpec(memory_space=pl.ANY)


def assemble(pieces, held, sems):
    copies = []
    at = 0
    for i, piece in enumerate(pieces):
        rows = piece.shape[0]
        copies.append(pltpu.make_async_copy(piece, held.at[pl.ds(at, rows)], sems.at[i]))
        at += rows
    for copy in copies:
        copy.start()
    for copy in copies:
        copy.wait()


def halves_turned(block):
    lane = lax.broadcasted_iota(jnp.int32, block.shape, 1)
    up = pltpu.roll(block, 128 - HD // 2, 1)
    return jnp.where(lane % HD < HD // 2, up, pltpu.roll(block, HD // 2, 1))


def side_rows(r, block, half, parity):
    side = (r // half) ^ parity
    return pl.ds(pl.multiple_of(side * half + r % half, block), block)


def pad_heads(key_value, rows, value, last):
    lane = lax.broadcasted_iota(jnp.int32, (1, 128), 1)
    kpad, vpad = key_value
    zero = jnp.zeros_like(value)
    vpad[0, rows, :] = jnp.concatenate([value, zero], 1).astype(bf16)
    vpad[1, rows, :] = jnp.concatenate([zero, value], 1).astype(bf16)
    kpad[1, rows, :] = jnp.where(lane >= HD, last, 0.0).astype(bf16)
    kpad[0, rows, :] = jnp.where(lane < HD, pltpu.roll(last, HD, 1), 0.0).astype(bf16)


def attend_kernel(parity_ref, own_ref, other_ref, bias_ref, cos_ref, sin_ref, *rest, block, count):
    pieces = rest[:count]
    qk_ref, v_ref, att_ref, lse_ref, held, kpad, vpad, lse_cols, sems = rest[count:]
    step = pl.program_id(0)
    half = own_ref.shape[0]
    length = 2 * half
    wide = qk_ref.shape[1]
    pairs = wide // 128
    parity = parity_ref[0]

    @pl.when(step == 0)
    def _():
        assemble(pieces, held, sems)
        for side, rows_ref in enumerate((own_ref, other_ref)):
            for r in range(0, half, block):
                at = pl.multiple_of((side ^ parity) * half + r, block)
                rows = pl.ds(at, block)
                mixed = jnp.dot(rows_ref[r : r + block, :], held[...], preferred_element_type=f32)
                mixed = (mixed + bias_ref[...]).astype(bf16).astype(f32)
                cos, sin = cos_ref[rows, :], sin_ref[rows, :]
                for p in range(pairs):
                    u = mixed[:, p * 128 : (p + 1) * 128]
                    turned = (u * cos + halves_turned(u) * sin).astype(bf16)
                    qk_ref[rows, p * 128 : (p + 1) * 128] = turned
                v_ref[rows, :] = mixed[:, wide:].astype(bf16)
                pad_heads((kpad, vpad), rows, mixed[:, wide:], turned.astype(f32))
        lse_cols[...] = jnp.zeros_like(lse_cols)

    factor = HD**-0.5 * math.log2(math.e)
    cols = pl.ds(pl.multiple_of(step * 128, 128), 128)
    row_i = lax.broadcasted_iota(jnp.int32, (block, block), 0)
    col_i = lax.broadcasted_iota(jnp.int32, (block, block), 1)
    for r in range(0, length, block):
        rows = pl.ds(r, block)
        to = side_rows(r, block, half, parity)
        q = qk_ref[rows, cols]

        def head(odd):
            keys = kpad[odd, : r + block, :]
            scores = lax.dot_general(q, keys, NT, preferred_element_type=f32)
            diag = jnp.where(col_i <= row_i, scores[:, r:], -1e30)
            scores = jnp.concatenate([scores[:, :r], diag], 1) if r else diag
            top = jnp.max(scores, 1, keepdims=True)
            e = jnp.exp2((scores - top) * factor)
            total = jnp.sum(e, 1, keepdims=True)
            out = jnp.dot(e.astype(bf16), vpad[odd, : r + block, :], preferred_element_type=f32)
            lse = top * factor + jnp.log2(total)
            at = lax.broadcasted_iota(jnp.int32, (1, 128), 1) == 2 * step + odd
            lse_cols[rows, :] = jnp.where(at, lse, lse_cols[rows, :])
            return out / total

        even = head(0)

        @pl.when(step < pairs - 1)
        def _():
            att_ref[to, :] = (even + head(1)).astype(bf16)

        @pl.when(step == pairs - 1)
        def _():
            att_ref[to, :] = even.astype(bf16)

    @pl.when(step == pairs - 1)
    def _():
        lse_ref[...] = lse_cols[...].T[: lse_ref.shape[0], :]


def attend(parity, own, other, pieces, bias, cos, sin):
    half, depth = own.shape
    length = 2 * half
    group = bias.shape[1]
    wide = group - HD
    pairs = wide // 128
    block = min(256, half)
    return pl.pallas_call(
        functools.partial(attend_kernel, block=block, count=len(pieces)),
        grid=(pairs,),
        in_specs=[pl.BlockSpec(memory_space=pltpu.SMEM)]
        + [whole(a) for a in (own, other, bias, cos, sin)]
        + [in_place(piece) for piece in pieces],
        out_specs=[
            pl.BlockSpec((length, wide), lambda p: (0, 0)),
            pl.BlockSpec((length, HD), lambda p: (0, 0)),
            pl.BlockSpec((length, 128), lambda p: (0, p)),
            pl.BlockSpec((8, length), lambda p: (0, 0)),
        ],
        out_shape=[
            jax.ShapeDtypeStruct((length, wide), bf16),
            jax.ShapeDtypeStruct((length, HD), bf16),
            jax.ShapeDtypeStruct((length, wide), bf16),
            jax.ShapeDtypeStruct((8, length), f32),
        ],
        scratch_shapes=[
            pltpu.VMEM((depth, group), bf16),
            pltpu.VMEM((2, length, 128), bf16),
            pltpu.VMEM((2, length, 128), bf16),
            pltpu.VMEM((length, 128), f32),
            pltpu.SemaphoreType.DMA((len(pieces),)),
        ],
        compiler_params=kernel_params(40),
        cost_estimate=cost(12e9, 8e6, 5e6),
    )(parity, own, other, bias, cos, sin, *pieces)


def project_kernel(att_ref, *rest, count):
    pieces = rest[:count]
    own_ref, other_ref, held, sems = rest[count:]
    half = own_ref.shape[0]
    assemble(pieces, held, sems)
    for side, ref in enumerate((own_ref, other_ref)):
        rows = att_ref[side * half : (side + 1) * half, :]
        ref[...] = lax.dot_general(rows, held[...], NT, preferred_element_type=f32).astype(ref.dtype)


def project(att, pieces):
    length, wide = att.shape
    depth = sum(piece.shape[0] for piece in pieces)
    return pl.pallas_call(
        functools.partial(project_kernel, count=len(pieces)),
        in_specs=[pl.BlockSpec(memory_space=pltpu.VMEM)] + [in_place(piece) for piece in pieces],
        out_specs=[pl.BlockSpec(memory_space=pltpu.VMEM)] * 2,
        out_shape=[
            jax.ShapeDtypeStruct((length // 2, depth), f32),
            jax.ShapeDtypeStruct((length // 2, depth), bf16),
        ],
        scratch_shapes=[
            pltpu.VMEM((depth, wide), bf16),
            pltpu.SemaphoreType.DMA((len(pieces),)),
        ],
        compiler_params=kernel_params(40),
        cost_estimate=cost(2 * length * depth * wide, 6e6),
    )(att, *pieces)


def attend_back_kernel(
    parity_ref,
    own_ref,
    other_ref,
    qk_ref,
    v_ref,
    lse_ref,
    cos_ref,
    sin_ref,
    *rest,
    block,
    count,
    first,
    last,
):
    pieces = rest[:count]
    if first == 0:
        mixed_ref, bias_ref, dk, dv, held, kpad, vpad, gatt, dq_acc, sems = rest[count:]
    else:
        dk_in, dv_in, mixed_ref, bias_ref, held, kpad, vpad, gatt, dq_acc, dk, dv, sems = rest[count:]
    step = pl.program_id(0) + first
    half_rows = own_ref.shape[0]
    length = 2 * half_rows
    wide = qk_ref.shape[1]
    pairs = wide // 128
    used = slice(first * 128, last * 128)
    parity = parity_ref[0]
    lane = lax.broadcasted_iota(jnp.int32, (1, 128), 1)

    @pl.when(step == first)
    def _():
        assemble(pieces, held, sems)
        for side, rows_ref in enumerate((own_ref, other_ref)):
            for r in range(0, half_rows, block):
                rows = pl.ds(pl.multiple_of((side ^ parity) * half_rows + r, block), block)
                got = jnp.dot(
                    rows_ref[r : r + block, :], held[:, used], preferred_element_type=f32
                )
                gatt[rows, :] = got.astype(bf16)
        for r in range(0, length, block):
            rows = pl.ds(r, block)
            keys = qk_ref[rows, wide - 128 :].astype(f32)
            pad_heads((kpad, vpad), rows, v_ref[rows, :].astype(f32), keys)
        dk[...] = dk_in[...] if first else jnp.zeros_like(dk)
        dv[...] = dv_in[...] if first else jnp.zeros_like(dv)

    factor = HD**-0.5 * math.log2(math.e)
    cols = pl.ds(pl.multiple_of(step * 128, 128), 128)
    here = pl.ds(pl.multiple_of((step - first) * 128, 128), 128)
    key_i = lax.broadcasted_iota(jnp.int32, (block, block), 0)
    query_i = lax.broadcasted_iota(jnp.int32, (block, block), 1)
    for r in range(0, length, block):
        rows = pl.ds(r, block)
        q = qk_ref[rows, cols]
        g = gatt[rows, here]

        def head(odd):
            lse = lse_ref[pl.ds(2 * step + odd, 1), rows]
            probs, grads = [], []
            inner = jnp.zeros((1, block), f32)
            for c in range(0, r + block, block):
                scores = lax.dot_general(
                    kpad[odd, c : c + block, :], q, NT, preferred_element_type=f32
                )
                p = jnp.exp2(scores * factor - lse)
                if c == r:
                    p = jnp.where(key_i <= query_i, p, 0.0)
                dp = lax.dot_general(vpad[odd, c : c + block, :], g, NT, preferred_element_type=f32)
                inner = inner + jnp.sum(p * dp, 0, keepdims=True)
                probs.append(p)
                grads.append(dp)
            dq = 0.0
            half = lane >= HD if odd else lane < HD
            for i, c in enumerate(range(0, r + block, block)):
                keys = pl.ds(c, block)
                ds = (probs[i] * (grads[i] - inner)).astype(bf16)
                p = probs[i].astype(bf16)
                dk[keys, :] += jnp.where(half, jnp.dot(ds, q, preferred_element_type=f32), 0.0)
                dv[keys, :] += jnp.where(half, jnp.dot(p, g, preferred_element_type=f32), 0.0)
                dq = dq + lax.dot_general(
                    ds, kpad[odd, c : c + block, :], TN, preferred_element_type=f32
                )
            return dq

        dq_acc[rows, :] = head(0)

        @pl.when(step < pairs - 1)
        def _():
            dq_acc[rows, :] += head(1)

    def back(u, rows):
        return u * cos_ref[rows, :] - halves_turned(u) * sin_ref[rows, :]

    scale = HD**-0.5
    for r in range(0, length, block):
        rows = pl.ds(r, block)
        to = side_rows(r, block, half_rows, parity)

        @pl.when(step < pairs - 1)
        def _():
            mixed_ref[to, here] = back(dq_acc[rows, :] * scale, rows).astype(bf16)

        if last == pairs:
            end = (last - first) * 128

            @pl.when(step == pairs - 1)
            def _():
                k = dk[rows, :]
                k = jnp.where(lane >= HD, k + pltpu.roll(k, HD, 1), dq_acc[rows, :]) * scale
                mixed_ref[to, end - 128 : end] = back(k, rows).astype(bf16)
                v = dv[rows, :]
                v = v + pltpu.roll(v, HD, 1)
                mixed_ref[to, end:] = v[:, :HD].astype(bf16)

    @pl.when(step == last - 1)
    def _():
        total = jnp.zeros((1, mixed_ref.shape[1]), f32)
        for r in range(0, length, block):
            part = mixed_ref[pl.ds(r, block), :].astype(f32)
            total = total + jnp.sum(part, 0, keepdims=True)
        bias_ref[...] = total


def attend_back(parity, own, other, pieces, qk, v, lse, cos, sin, first, last, earlier=()):
    half, depth = own.shape
    length = 2 * half
    wide = qk.shape[1]
    pairs = wide // 128
    group = (last - first) * 128 + (HD if last == pairs else 0)
    block = min(256, half)
    ins = (own, other, qk, v, lse, cos, sin)
    carried = pl.BlockSpec((length, 128), lambda p: (0, 0))
    carry = [jax.ShapeDtypeStruct((length, 128), f32)] * 2
    return pl.pallas_call(
        functools.partial(
            attend_back_kernel, block=block, count=len(pieces), first=first, last=last
        ),
        grid=(last - first,),
        in_specs=[pl.BlockSpec(memory_space=pltpu.SMEM)]
        + [whole(a) for a in ins]
        + [in_place(piece) for piece in pieces]
        + [carried] * len(earlier),
        out_specs=[
            pl.BlockSpec((length, group), lambda p: (0, 0)),
            pl.BlockSpec((1, group), lambda p: (0, 0)),
        ]
        + ([] if first else [carried] * 2),
        out_shape=[
            jax.ShapeDtypeStruct((length, group), bf16),
            jax.ShapeDtypeStruct((1, group), f32),
        ]
        + ([] if first else carry),
        scratch_shapes=[
            pltpu.VMEM((depth, wide), bf16),
            pltpu.VMEM((2, length, 128), bf16),
            pltpu.VMEM((2, length, 128), bf16),
            pltpu.VMEM((length, (last - first) * 128), bf16),
            pltpu.VMEM((length, 128), f32),
        ]
        + ([pltpu.VMEM((length, 128), f32)] * 2 if first else [])
        + [pltpu.SemaphoreType.DMA((len(pieces),))],
        compiler_params=kernel_params(50),
        cost_estimate=cost(12e9, 6e6, 3e6),
    )(parity, *ins, *pieces, *earlier)


def mlp_kernel(x0_ref, x1_ref, g0_ref, g1_ref, *rest, count, add):
    pieces = rest[:count]
    rest = rest[count:]
    if add:
        near_in, far_in, act_ref, near_ref, far_ref, held, sems = rest
    else:
        act_ref, near_ref, far_ref, held, sems = rest
    n = held.shape[1] // 3
    step = pl.program_id(0)

    @pl.when(step == 0)
    def _():
        assemble(pieces, held, sems)

    wg, wu, wd = (held[:, k * n : (k + 1) * n] for k in range(3))
    x = jnp.where(step == 0, x0_ref[...], x1_ref[...])
    g = jnp.where(step == 0, g0_ref[...], g1_ref[...])
    gate = jnp.dot(x, wg, preferred_element_type=f32)
    up = jnp.dot(x, wu, preferred_element_type=f32)
    gh = jnp.dot(g, wd, preferred_element_type=f32)
    sig = 1.0 / (1.0 + jnp.exp(-gate))
    silu = gate * sig
    hid = (silu * up).astype(bf16)
    ghs = gh * sig
    gg = (ghs * up * (1.0 + gate - silu)).astype(bf16)
    gu = (ghs * gate).astype(bf16)
    act_ref[:, :n] = gg
    act_ref[:, n : 2 * n] = gu
    act_ref[:, 2 * n :] = hid
    ngrad = lax.dot_general(gg, wg, NT, preferred_element_type=f32)
    ngrad = ngrad + lax.dot_general(gu, wu, NT, preferred_element_type=f32)
    down = lax.dot_general(hid, wd, NT, preferred_element_type=f32)

    @pl.when(step == 0)
    def _():
        near_ref[0] = (ngrad + near_in[0].astype(f32) if add else ngrad).astype(bf16)
        near_ref[1] = (down + near_in[1].astype(f32) if add else down).astype(bf16)

    @pl.when(step == 1)
    def _():
        far_ref[0] = (ngrad + far_in[0].astype(f32) if add else ngrad).astype(bf16)
        far_ref[1] = (down + far_in[1].astype(f32) if add else down).astype(bf16)


def mlp(rows, grads, pieces, sums=None):
    t, d = rows[0].shape
    columns = pieces[0].shape[1]
    add = sums is not None
    ins = (*rows, *grads)
    sums = tuple(sums or ())
    both = pl.BlockSpec((2, t, d), lambda i: (0, 0, 0))
    return pl.pallas_call(
        functools.partial(mlp_kernel, count=len(pieces), add=add),
        grid=(2,),
        in_specs=[whole(a) for a in ins] + [in_place(p) for p in pieces] + [both] * len(sums),
        out_specs=[pl.BlockSpec((t, columns), lambda i: (i, 0)), both, both],
        out_shape=[
            jax.ShapeDtypeStruct((2 * t, columns), bf16),
            jax.ShapeDtypeStruct((2, t, d), bf16),
            jax.ShapeDtypeStruct((2, t, d), bf16),
        ],
        scratch_shapes=[
            pltpu.VMEM((d, columns), bf16),
            pltpu.SemaphoreType.DMA((len(pieces),)),
        ],
        compiler_params=kernel_params(58),
        cost_estimate=cost(8 * t * d * columns, 30 * MIB, 2 * t * columns),
    )(*ins, *pieces, *sums)


def fill(sent_ref, kept_ref, lefts, rights, second):
    half = kept_ref.shape[0]
    t = lefts[0].shape[0]
    q = half // 2
    if second:
        parts = ((sent_ref, 0, q), (sent_ref, q, 3 * q), (kept_ref, 0, 0), (kept_ref, q, 2 * q))
        size = q
    else:
        parts = ((sent_ref, 0, half), (kept_ref, 0, 0))
        size = half
    for ref, to, start in parts:
        total = 0.0
        for i, left in enumerate(lefts):
            right = rights[i * t // rights[0].shape[0]]
            at = i * t % right.shape[0]
            total = total + lax.dot_general(
                left[:, start : start + size],
                right[at : at + t, :],
                TN,
                preferred_element_type=f32,
            )
        ref[to : to + size, :] = total.astype(ref.dtype)


def outer_kernel(*refs, blocks):
    rows, grads, rights = refs[:blocks], refs[blocks : 2 * blocks], refs[2 * blocks : -4]
    sent_one, kept_one, sent_two, kept_two = refs[-4:]
    step = pl.program_id(0)

    @pl.when(step < 2)
    def _():
        fill(sent_one, kept_one, rows, rights, False)

    @pl.when(step == 2)
    def _():
        fill(sent_two, kept_two, grads, rights, True)


def outer(rows, grads, acts):
    t, d = rows[0].shape
    tall, columns = acts[0].shape
    n = columns // 3
    flat = [*rows, *grads]
    one = pl.BlockSpec((d // 2, n), lambda k: (0, jnp.minimum(k, 1)))
    two = pl.BlockSpec((d // 2, n), lambda k: (0, 0))
    return pl.pallas_call(
        functools.partial(outer_kernel, blocks=len(rows)),
        grid=(3,),
        in_specs=[whole(left) for left in flat]
        + [pl.BlockSpec((tall, n), lambda k: (0, k)) for _ in acts],
        out_specs=[one, one, two, two],
        out_shape=[
            jax.ShapeDtypeStruct((d // 2, 2 * n), bf16),
            jax.ShapeDtypeStruct((d // 2, 2 * n), f32),
            jax.ShapeDtypeStruct((d // 2, n), bf16),
            jax.ShapeDtypeStruct((d // 2, n), f32),
        ],
        compiler_params=kernel_params(58),
        cost_estimate=cost(2 * t * len(rows) * d * columns, 20 * MIB),
    )(*flat, *acts)


def outer_one_kernel(*refs):
    fill(refs[-2], refs[-1], refs[:-3], refs[-3:-2], False)


def outer_one(lefts, right):
    t, d = lefts[0].shape
    columns = right.shape[1]
    vmem = pl.BlockSpec(memory_space=pltpu.VMEM)
    return pl.pallas_call(
        outer_one_kernel,
        in_specs=[vmem] * (len(lefts) + 1),
        out_specs=[vmem] * 2,
        out_shape=[
            jax.ShapeDtypeStruct((d // 2, columns), bf16),
            jax.ShapeDtypeStruct((d // 2, columns), f32),
        ],
        compiler_params=kernel_params(40),
        cost_estimate=cost(2 * t * len(lefts) * d * columns, 6 * MIB),
    )(*lefts, right)


def rope_tables(length):
    inverse = theta_base ** (-(jnp.arange(HD // 2, dtype=f32) * 2.0 / HD))
    angles = jnp.arange(length, dtype=f32)[:, None] * inverse[None, :]
    c, s = jnp.cos(angles), jnp.sin(angles)
    return jnp.concatenate([c] * 4, 1), jnp.concatenate([-s, s, -s, s], 1)


class Gather:
    def __init__(self, block, bits):
        self.bits = bits
        self.left = bits - 1
        self.pieces = [block]
        self.beside = []

    def ready(self, *earlier):
        self.pieces[-1] = after(self.pieces[-1], *earlier)

    def double(self, *earlier):
        held = jnp.concatenate(self.pieces, 0) if len(self.pieces) > 1 else self.pieces[0]
        self.pieces.append(flip(after(held, *earlier) if earlier else held, "row", self.left))
        self.left -= 1
        return self.pieces[-1]

    def send(self, *earlier):
        piece = self.pieces[len(self.beside)]
        self.beside.append(flip(after(piece, *earlier) if earlier else piece, "row", 0))
        return self.beside[-1]

    def finish(self, *earlier):
        while self.left > 0:
            self.double()
        rest = jnp.concatenate(self.pieces[len(self.beside) :], 0)
        self.beside.append(flip(after(rest, *earlier), "row", 0))
        out = self.pieces + self.beside
        return out if out[0].shape[0] % 16 == 0 else [jnp.concatenate(out, 0)]

    def all(self):
        while self.left > 0:
            self.double()
        while len(self.beside) < self.bits:
            self.send()
        out = self.pieces + self.beside
        return out if out[0].shape[0] % 16 == 0 else [jnp.concatenate(out, 0)]


class Scatter:
    def __init__(self, parts, bits):
        self.bits = bits
        self.orders = [[0, 1], [1, 0]][: len(parts)]
        self.kept = [kept for _, kept in parts]
        self.done = 0
        self.start([sent for sent, _ in parts])

    def start(self, sents):
        bits = [order[self.done] if self.done < 2 else self.done for order in self.orders]
        self.got = [flip(sent, "row", bit) for sent, bit in zip(sents, bits)]

    def wait(self, *earlier):
        self.got = [after(got, *earlier) for got in self.got]

    def step(self):
        if self.done == self.bits - 1:
            return
        self.done += 1
        half = self.kept[0].shape[0] // 2
        sents = [
            (kept[half:] + got[half:].astype(f32)).astype(bf16)
            for kept, got in zip(self.kept, self.got)
        ]
        self.kept = [kept[:half] + got[:half].astype(f32) for kept, got in zip(self.kept, self.got)]
        if self.done == 2:
            sents = [jnp.concatenate(sents, 1)]
            self.kept = [jnp.concatenate(self.kept, 1)]
        self.start(sents)

    def total(self):
        while self.done < self.bits - 1:
            self.step()
        totals = [kept + got.astype(f32) for kept, got in zip(self.kept, self.got)]
        return jnp.concatenate(totals, 1)


def turned_pairs(block):
    first = [(2 * a + b, 2 * b + a) for a in range(2) for b in range(2)]
    second = [(2 * a + b, 2 * (1 - b) + a) for a in range(2) for b in range(2)]
    return lax.ppermute(block, "col", first), lax.ppermute(block, "col", second)


def from_pairs(same, other):
    first = [(2 * a + b, 2 * b + a) for a in range(2) for b in range(2)]
    second = [(2 * a + b, 2 * b + 1 - a) for a in range(2) for b in range(2)]
    return lax.ppermute(same, "col", first), lax.ppermute(other, "col", second)


def cuts(width):
    first = min(512, width)
    return [(0, first), (first, width)] if first < width else [(0, width)]


def shards(
    layer_input,
    gain_attn,
    qkv_weight,
    qkv_bias,
    out_weight,
    gain_mlp,
    gate_weight,
    up_weight,
    down_weight,
    cotangent,
):
    row = lax.axis_index("row")
    column = lax.axis_index("col")
    row_count = lax.axis_size("row")
    bits = row_count.bit_length() - 1
    core = column % 2
    sequence = column // 2
    parity = core.astype(jnp.int32).reshape(1)
    tok_local, model_width = layer_input.shape
    length = tok_local * 2
    deep = model_width // row_count
    ff_cols = gate_weight.shape[1]
    qkv_cols = qkv_weight.shape[1]
    out_cols = out_weight.shape[0]
    group_width = 2 * qkv_cols
    query_width = group_width - 2 * HD

    bias_rows = jnp.pad(qkv_bias[None, :], ((0, 15), (0, 0)))
    first, second = turned_pairs(
        jnp.concatenate(
            [
                jnp.concatenate([qkv_weight, bias_rows], 0),
                jnp.pad(out_weight.T, ((0, 16), (0, 0))),
            ],
            1,
        )
    )
    low = jnp.where(sequence == 0, first, second)
    high = jnp.where(sequence == 0, second, first)
    qkv_own = jnp.concatenate([low[:, :qkv_cols], high[:, :qkv_cols]], 1)
    bias_full = qkv_own[deep : deep + 1].astype(f32)
    out_own = jnp.concatenate([low[:deep, qkv_cols:], high[:deep, qkv_cols:]], 1)
    out_own = jnp.pad(out_own, ((0, 0), (0, HD)))
    qkv_gather = Gather(qkv_own[:deep], bits)
    out_gather = Gather(out_own, bits)
    down_flipped = down_weight.T
    mlp_gathers = []
    for start, stop in cuts(ff_cols):
        padded = -(-(stop - start) // 256) * 256
        pieces = [
            jnp.pad(part[:, start:stop], ((0, 0), (0, padded - (stop - start))))
            for part in (gate_weight, up_weight, down_flipped)
        ]
        mlp_gathers.append(Gather(jnp.concatenate(pieces, 1), bits))
    place = jnp.arange(model_width, dtype=jnp.int32)
    masks = jnp.array([bit_reversed(p, bits) for p in range(row_count)], jnp.int32)
    source = jnp.repeat(masks ^ row, deep) * deep + place % deep
    to_stored = (place[:, None] == source[None, :]).astype(bf16)

    def stored(block):
        return jnp.dot(block, to_stored, preferred_element_type=f32)

    def unstored(block):
        return jnp.einsum("ts,fs->tf", block, to_stored, preferred_element_type=f32).astype(bf16)

    def unstored_row(vector):
        blocks = vector.reshape(row_count, deep)
        blocks = jnp.concatenate(
            [blocks[bit_reversed(m, bits)][None] for m in range(row_count)], 0
        )
        for bit in range(bits):
            wide = blocks.reshape(-1, 2, 1 << bit, deep)
            turned = jnp.concatenate([wide[:, 1:], wide[:, :1]], 1).reshape(row_count, deep)
            blocks = jnp.where((row >> bit) % 2 == 1, turned, blocks)
        return blocks.reshape(model_width)

    input_rows = stored(layer_input)
    grad_out = stored(cotangent)
    gain_one = stored(gain_attn[None, :])
    gain_two = stored(gain_mlp[None, :])

    scale_one = lax.rsqrt(jnp.mean(input_rows * input_rows, axis=1) + eps)
    normed_own = (input_rows * scale_one[:, None] * gain_one).astype(bf16)
    normed_other = flip(normed_own, "col", 0)
    cosine, sine_part = rope_tables(length)
    grad_blocks = [grad_out.astype(bf16)]

    near, far = mlp_gathers
    n_four = near.double()
    n_own = near.send()
    a_own = qkv_gather.send(n_own)
    a_four = qkv_gather.double(n_own)
    a_two = qkv_gather.double(a_own, n_four)
    a_beside = qkv_gather.send(a_own)
    o_four = out_gather.double(a_four)
    a_last = qkv_gather.send(a_beside)
    qkv_pieces = qkv_gather.all()
    far.ready(a_two, o_four)
    f_four = far.double()
    o_two = out_gather.double(a_two)
    across = flip(after(grad_blocks[0], a_four), "col", 1)
    out_pieces = out_gather.finish(a_last, o_two)
    n_two = near.double(o_two)
    n_beside = near.send(a_last)
    qk_rows, value_rows, att_rows, log_totals = attend(
        parity,
        normed_own,
        normed_other,
        qkv_pieces,
        bias_full,
        cosine,
        sine_part,
    )
    n_last = near.send(att_rows)
    att_own, att_other = project(after(att_rows, n_beside, n_two, across, f_four), out_pieces)
    att_got = flip(att_other, "col", 0)
    grad_blocks.append(flip(after(grad_blocks[0], att_got), "col", 0))
    grad_blocks += [across, flip(after(across, att_got), "col", 0)]
    middle = input_rows + att_own + att_got.astype(f32)
    scale_two = lax.rsqrt(jnp.mean(middle * middle, axis=1) + eps)
    blocks = [(middle * scale_two[:, None] * gain_two).astype(bf16)]
    across = flip(blocks[0], "col", 1)
    blocks.append(flip(after(blocks[0], n_last), "col", 0))
    blocks += [across, flip(across, "col", 0)]

    f_own = far.send(n_last)
    f_two = far.double(blocks[0])
    f_beside = far.send(f_own)
    f_last = far.send(f_beside)
    first_pieces, second_pieces = (gather.all() for gather in mlp_gathers)
    act_own, *sums_own = mlp([after(blocks[0], blocks[2]), blocks[1]], grad_blocks[:2], first_pieces)
    act_far, *sums_far = mlp(blocks[2:], grad_blocks[2:], first_pieces)
    sent_one, kept_one, sent_two, kept_two = outer(blocks, grad_blocks, [act_own, act_far])
    first_scatter = Scatter([(sent_one, kept_one), (sent_two, kept_two)], bits)
    start_far = after(blocks[2], kept_one)
    act_far, near_far, far_far = mlp(
        [start_far, blocks[3]], grad_blocks[2:], second_pieces, sums_far
    )
    far_far = after(far_far, *first_scatter.got)
    across = near_far.astype(f32) + flip(far_far, "col", 0).astype(f32)
    across = across.astype(bf16)
    normed_back = flip(across[0], "col", 1)
    act_own, near_own, far_own = mlp(
        [after(blocks[0], across), blocks[1]],
        grad_blocks[:2],
        second_pieces,
        sums_own,
    )
    first_scatter.step()
    beside = flip(after(far_own, normed_back, *first_scatter.got), "col", 0)
    first_scatter.step()
    down_back = flip(after(across[1], normed_back), "col", 1)

    def summed(k, back):
        return near_own[k].astype(f32) + beside[k].astype(f32) + back.astype(f32)

    grad_normed_two = summed(0, normed_back)
    scaled_two = gain_two * grad_normed_two
    inner_two = jnp.sum(scaled_two * middle, axis=1)
    grad_middle = (
        grad_out
        + scale_two[:, None] * scaled_two
        - middle * (scale_two**3 * inner_two / model_width)[:, None]
    )
    gain_two_grad = jnp.sum(grad_normed_two * middle * scale_two[:, None], axis=0)
    branch_own = grad_middle.astype(bf16)
    branch_other = flip(branch_own, "col", 0)
    sent_one, kept_one, sent_two, kept_two = outer(
        [after(blocks[0], branch_own, *first_scatter.kept), *blocks[1:]],
        grad_blocks,
        [act_own, act_far],
    )
    second_scatter = Scatter([(sent_one, kept_one), (sent_two, kept_two)], bits)
    out_scatter = Scatter([outer_one([after(branch_own, kept_one), branch_other], att_rows)], bits)
    split = qk_rows.shape[1] // 256
    mixed_first, bias_first, *carry = attend_back(
        parity,
        after(branch_own, out_scatter.kept[0]),
        branch_other,
        out_pieces,
        qk_rows,
        value_rows,
        log_totals,
        cosine,
        sine_part,
        0,
        split,
    )
    second_scatter.wait(mixed_first)
    out_scatter.wait(mixed_first)
    second_scatter.step()
    out_scatter.step()
    mixed_last, bias_last = attend_back(
        parity,
        after(branch_own, *second_scatter.kept, out_scatter.kept[0]),
        branch_other,
        out_pieces,
        qk_rows,
        value_rows,
        log_totals,
        cosine,
        sine_part,
        split,
        2 * split,
        carry,
    )
    bias_grad = jnp.concatenate([bias_first, bias_last], 1)[0]
    first_scatter.wait(mixed_last)
    second_scatter.wait(mixed_last)
    out_scatter.wait(mixed_last)
    grad_mixed = jnp.concatenate([mixed_first, mixed_last], 1)
    passed = [*second_scatter.got, *out_scatter.got]
    second_scatter.step()
    out_scatter.step()
    layer_output = unstored((middle + summed(1, after(down_back, grad_mixed))).astype(bf16))
    qkv_scatter = Scatter([outer_one([normed_own, normed_other], grad_mixed)], bits)
    qkv_full = jnp.concatenate(qkv_pieces, 0)
    grad_mixed = after(grad_mixed, qkv_scatter.kept[0], *passed)
    partial = jnp.einsum("tc,dc->td", grad_mixed, qkv_full, preferred_element_type=f32)
    grad_normed_one = partial[:tok_local] + flip(
        partial[tok_local:].astype(bf16), "col", 0
    ).astype(f32)
    scaled_one = gain_one * grad_normed_one
    inner_one = jnp.sum(scaled_one * input_rows, axis=1)
    input_grad = unstored(
        (
            grad_middle
            + scale_one[:, None] * scaled_one
            - input_rows * (scale_one**3 * inner_one / model_width)[:, None]
        ).astype(bf16)
    )
    gain_one_grad = jnp.sum(grad_normed_one * input_rows * scale_one[:, None], axis=0)

    def to_columns(total, width):
        low, high = total[:, :width].astype(bf16), total[:, width : 2 * width].astype(bf16)
        first, second = from_pairs(
            jnp.where(sequence == 0, low, high), jnp.where(sequence == 0, high, low)
        )
        return first.astype(f32) + second.astype(f32)

    qkv_total = to_columns(qkv_scatter.total(), qkv_cols)
    out_total = to_columns(out_scatter.total(), out_cols)
    mlp_totals = []
    for scatter, (start, stop) in zip((first_scatter, second_scatter), cuts(ff_cols)):
        total = scatter.total()
        padded = total.shape[1] // 3
        mlp_totals.append(
            [total[:, k * padded : k * padded + stop - start] for k in range(3)]
        )
    gate_total, up_total, down_total = (jnp.concatenate(parts, 1) for parts in zip(*mlp_totals))
    bias_row = lax.dynamic_update_slice_in_dim(
        jnp.zeros((group_width * 2,), f32), bias_grad, core * group_width, 0
    )
    small = jnp.concatenate([unstored_row(gain_one_grad), unstored_row(gain_two_grad), bias_row])
    small = jnp.pad(small, (0, -small.shape[0] % 128)).reshape(-1, 128)
    for bit in range(2):
        small = small + flip(small, "col", bit)
    for bit in range(bits):
        small = small + flip(small, "row", bit)
    small = small.reshape(-1)
    gain_one_total = small[:model_width]
    gain_two_total = small[model_width : 2 * model_width]
    bias_total = lax.dynamic_slice_in_dim(small, 2 * model_width + column * qkv_cols, qkv_cols, 0)
    return (
        layer_output,
        input_grad,
        gain_one_total,
        qkv_total,
        bias_total,
        out_total.T,
        gain_two_total,
        gate_total,
        up_total,
        down_total.T,
    )


def solution(mesh):
    in_specs = (
        P(("row", "col"), None),
        P(),
        P("row", "col"),
        P("col"),
        P("col", "row"),
        P(),
        P("row", "col"),
        P("row", "col"),
        P("col", "row"),
        P(("row", "col"), None),
    )
    out_specs = (
        P(("row", "col"), None),
        P(("row", "col"), None),
        P(),
        P("row", "col"),
        P("col"),
        P("col", "row"),
        P(),
        P("row", "col"),
        P("row", "col"),
        P("col", "row"),
    )
    return jax.shard_map(shards, mesh=mesh, in_specs=in_specs, out_specs=out_specs, check_vma=False)
```

```python
import functools
import math

import jax
import jax.numpy as jnp
from jax import lax
from jax.experimental import pallas as pl
from jax.experimental.pallas import tpu as pltpu
from jax.sharding import PartitionSpec as P

HD = 64
eps = 1e-06
theta_base = 1000000.0
bf16 = jnp.bfloat16
f32 = jnp.float32
NT = (((1,), (1,)), ((), ()))
TN = (((0,), (0,)), ((), ()))
MIB = 1024 * 1024


def flip(block, axis, bit):
    count = lax.axis_size(axis)
    return lax.ppermute(block, axis, [(i, i ^ 1 << bit) for i in range(count)])


def bit_reversed(value, bits):
    return sum((value >> b & 1) << (bits - 1 - b) for b in range(bits))


def after(value, *earlier):
    return lax.optimization_barrier((value, *earlier))[0]


def kernel_params(mib):
    return pltpu.CompilerParams(vmem_limit_bytes=mib * MIB)


def cost(flops, nbytes, exps=0):
    return pl.CostEstimate(
        flops=int(flops), bytes_accessed=int(nbytes), transcendentals=int(exps)
    )


def whole(array):
    return pl.BlockSpec(array.shape, lambda *_: (0,) * len(array.shape))


def in_place(block):
    return pl.BlockSpec(memory_space=pl.ANY)


def assemble(pieces, held, sems):
    copies = []
    at = 0
    for i, piece in enumerate(pieces):
        rows = piece.shape[0]
        copies.append(pltpu.make_async_copy(piece, held.at[pl.ds(at, rows)], sems.at[i]))
        at += rows
    for copy in copies:
        copy.start()
    for copy in copies:
        copy.wait()


def halves_turned(block):
    lane = lax.broadcasted_iota(jnp.int32, block.shape, 1)
    up = pltpu.roll(block, 128 - HD // 2, 1)
    return jnp.where(lane % HD < HD // 2, up, pltpu.roll(block, HD // 2, 1))


def side_rows(r, block, half, parity):
    side = (r // half) ^ parity
    return pl.ds(pl.multiple_of(side * half + r % half, block), block)


def pad_heads(key_value, rows, value, last):
    lane = lax.broadcasted_iota(jnp.int32, (1, 128), 1)
    kpad, vpad = key_value
    zero = jnp.zeros_like(value)
    vpad[0, rows, :] = jnp.concatenate([value, zero], 1).astype(bf16)
    vpad[1, rows, :] = jnp.concatenate([zero, value], 1).astype(bf16)
    kpad[1, rows, :] = jnp.where(lane >= HD, last, 0.0).astype(bf16)
    kpad[0, rows, :] = jnp.where(lane < HD, pltpu.roll(last, HD, 1), 0.0).astype(bf16)


def attend_kernel(parity_ref, own_ref, other_ref, bias_ref, cos_ref, sin_ref, *rest, block, count):
    pieces = rest[:count]
    qk_ref, v_ref, att_ref, lse_ref, held, kpad, vpad, lse_cols, sems = rest[count:]
    step = pl.program_id(0)
    half = own_ref.shape[0]
    length = 2 * half
    wide = qk_ref.shape[1]
    pairs = wide // 128
    parity = parity_ref[0]

    @pl.when(step == 0)
    def _():
        assemble(pieces, held, sems)
        for side, rows_ref in enumerate((own_ref, other_ref)):
            for r in range(0, half, block):
                at = pl.multiple_of((side ^ parity) * half + r, block)
                rows = pl.ds(at, block)
                mixed = jnp.dot(rows_ref[r : r + block, :], held[...], preferred_element_type=f32)
                mixed = (mixed + bias_ref[...]).astype(bf16).astype(f32)
                cos, sin = cos_ref[rows, :], sin_ref[rows, :]
                for p in range(pairs):
                    u = mixed[:, p * 128 : (p + 1) * 128]
                    turned = (u * cos + halves_turned(u) * sin).astype(bf16)
                    qk_ref[rows, p * 128 : (p + 1) * 128] = turned
                v_ref[rows, :] = mixed[:, wide:].astype(bf16)
                pad_heads((kpad, vpad), rows, mixed[:, wide:], turned.astype(f32))
        lse_cols[...] = jnp.zeros_like(lse_cols)

    factor = HD**-0.5 * math.log2(math.e)
    cols = pl.ds(pl.multiple_of(step * 128, 128), 128)
    row_i = lax.broadcasted_iota(jnp.int32, (block, block), 0)
    col_i = lax.broadcasted_iota(jnp.int32, (block, block), 1)
    for r in range(0, length, block):
        rows = pl.ds(r, block)
        to = side_rows(r, block, half, parity)
        q = qk_ref[rows, cols]

        def head(odd):
            keys = kpad[odd, : r + block, :]
            scores = lax.dot_general(q, keys, NT, preferred_element_type=f32)
            diag = jnp.where(col_i <= row_i, scores[:, r:], -1e30)
            scores = jnp.concatenate([scores[:, :r], diag], 1) if r else diag
            top = jnp.max(scores, 1, keepdims=True)
            e = jnp.exp2((scores - top) * factor)
            total = jnp.sum(e, 1, keepdims=True)
            out = jnp.dot(e.astype(bf16), vpad[odd, : r + block, :], preferred_element_type=f32)
            lse = top * factor + jnp.log2(total)
            at = lax.broadcasted_iota(jnp.int32, (1, 128), 1) == 2 * step + odd
            lse_cols[rows, :] = jnp.where(at, lse, lse_cols[rows, :])
            return out / total

        even = head(0)

        @pl.when(step < pairs - 1)
        def _():
            att_ref[to, :] = (even + head(1)).astype(bf16)

        @pl.when(step == pairs - 1)
        def _():
            att_ref[to, :] = even.astype(bf16)

    @pl.when(step == pairs - 1)
    def _():
        lse_ref[...] = lse_cols[...].T[: lse_ref.shape[0], :]


def attend(parity, own, other, pieces, bias, cos, sin):
    half, depth = own.shape
    length = 2 * half
    group = bias.shape[1]
    wide = group - HD
    pairs = wide // 128
    block = min(256, half)
    return pl.pallas_call(
        functools.partial(attend_kernel, block=block, count=len(pieces)),
        grid=(pairs,),
        in_specs=[pl.BlockSpec(memory_space=pltpu.SMEM)]
        + [whole(a) for a in (own, other, bias, cos, sin)]
        + [in_place(piece) for piece in pieces],
        out_specs=[
            pl.BlockSpec((length, wide), lambda p: (0, 0)),
            pl.BlockSpec((length, HD), lambda p: (0, 0)),
            pl.BlockSpec((length, 128), lambda p: (0, p)),
            pl.BlockSpec((8, length), lambda p: (0, 0)),
        ],
        out_shape=[
            jax.ShapeDtypeStruct((length, wide), bf16),
            jax.ShapeDtypeStruct((length, HD), bf16),
            jax.ShapeDtypeStruct((length, wide), bf16),
            jax.ShapeDtypeStruct((8, length), f32),
        ],
        scratch_shapes=[
            pltpu.VMEM((depth, group), bf16),
            pltpu.VMEM((2, length, 128), bf16),
            pltpu.VMEM((2, length, 128), bf16),
            pltpu.VMEM((length, 128), f32),
            pltpu.SemaphoreType.DMA((len(pieces),)),
        ],
        compiler_params=kernel_params(40),
        cost_estimate=cost(12e9, 8e6, 5e6),
    )(parity, own, other, bias, cos, sin, *pieces)


def project_kernel(att_ref, *rest, count):
    pieces = rest[:count]
    own_ref, other_ref, held, sems = rest[count:]
    half = own_ref.shape[0]
    assemble(pieces, held, sems)
    for side, ref in enumerate((own_ref, other_ref)):
        rows = att_ref[side * half : (side + 1) * half, :]
        ref[...] = lax.dot_general(rows, held[...], NT, preferred_element_type=f32).astype(ref.dtype)


def project(att, pieces):
    length, wide = att.shape
    depth = sum(piece.shape[0] for piece in pieces)
    return pl.pallas_call(
        functools.partial(project_kernel, count=len(pieces)),
        in_specs=[pl.BlockSpec(memory_space=pltpu.VMEM)] + [in_place(piece) for piece in pieces],
        out_specs=[pl.BlockSpec(memory_space=pltpu.VMEM)] * 2,
        out_shape=[
            jax.ShapeDtypeStruct((length // 2, depth), f32),
            jax.ShapeDtypeStruct((length // 2, depth), bf16),
        ],
        scratch_shapes=[
            pltpu.VMEM((depth, wide), bf16),
            pltpu.SemaphoreType.DMA((len(pieces),)),
        ],
        compiler_params=kernel_params(40),
        cost_estimate=cost(2 * length * depth * wide, 6e6),
    )(att, *pieces)


def attend_back_kernel(
    parity_ref,
    own_ref,
    other_ref,
    qk_ref,
    v_ref,
    lse_ref,
    cos_ref,
    sin_ref,
    *rest,
    block,
    count,
    first,
    last,
):
    pieces = rest[:count]
    if first == 0:
        mixed_ref, bias_ref, dk, dv, held, kpad, vpad, gatt, dq_acc, sems = rest[count:]
    else:
        dk_in, dv_in, mixed_ref, bias_ref, held, kpad, vpad, gatt, dq_acc, dk, dv, sems = rest[count:]
    step = pl.program_id(0) + first
    half_rows = own_ref.shape[0]
    length = 2 * half_rows
    wide = qk_ref.shape[1]
    pairs = wide // 128
    used = slice(first * 128, last * 128)
    parity = parity_ref[0]
    lane = lax.broadcasted_iota(jnp.int32, (1, 128), 1)

    @pl.when(step == first)
    def _():
        assemble(pieces, held, sems)
        for side, rows_ref in enumerate((own_ref, other_ref)):
            for r in range(0, half_rows, block):
                rows = pl.ds(pl.multiple_of((side ^ parity) * half_rows + r, block), block)
                got = jnp.dot(
                    rows_ref[r : r + block, :], held[:, used], preferred_element_type=f32
                )
                gatt[rows, :] = got.astype(bf16)
        for r in range(0, length, block):
            rows = pl.ds(r, block)
            keys = qk_ref[rows, wide - 128 :].astype(f32)
            pad_heads((kpad, vpad), rows, v_ref[rows, :].astype(f32), keys)
        dk[...] = dk_in[...] if first else jnp.zeros_like(dk)
        dv[...] = dv_in[...] if first else jnp.zeros_like(dv)

    factor = HD**-0.5 * math.log2(math.e)
    cols = pl.ds(pl.multiple_of(step * 128, 128), 128)
    here = pl.ds(pl.multiple_of((step - first) * 128, 128), 128)
    key_i = lax.broadcasted_iota(jnp.int32, (block, block), 0)
    query_i = lax.broadcasted_iota(jnp.int32, (block, block), 1)
    for r in range(0, length, block):
        rows = pl.ds(r, block)
        q = qk_ref[rows, cols]
        g = gatt[rows, here]

        def head(odd):
            lse = lse_ref[pl.ds(2 * step + odd, 1), rows]
            probs, grads = [], []
            inner = jnp.zeros((1, block), f32)
            for c in range(0, r + block, block):
                scores = lax.dot_general(
                    kpad[odd, c : c + block, :], q, NT, preferred_element_type=f32
                )
                p = jnp.exp2(scores * factor - lse)
                if c == r:
                    p = jnp.where(key_i <= query_i, p, 0.0)
                dp = lax.dot_general(vpad[odd, c : c + block, :], g, NT, preferred_element_type=f32)
                inner = inner + jnp.sum(p * dp, 0, keepdims=True)
                probs.append(p)
                grads.append(dp)
            dq = 0.0
            half = lane >= HD if odd else lane < HD
            for i, c in enumerate(range(0, r + block, block)):
                keys = pl.ds(c, block)
                ds = (probs[i] * (grads[i] - inner)).astype(bf16)
                p = probs[i].astype(bf16)
                dk[keys, :] += jnp.where(half, jnp.dot(ds, q, preferred_element_type=f32), 0.0)
                dv[keys, :] += jnp.where(half, jnp.dot(p, g, preferred_element_type=f32), 0.0)
                dq = dq + lax.dot_general(
                    ds, kpad[odd, c : c + block, :], TN, preferred_element_type=f32
                )
            return dq

        dq_acc[rows, :] = head(0)

        @pl.when(step < pairs - 1)
        def _():
            dq_acc[rows, :] += head(1)

    def back(u, rows):
        return u * cos_ref[rows, :] - halves_turned(u) * sin_ref[rows, :]

    scale = HD**-0.5
    for r in range(0, length, block):
        rows = pl.ds(r, block)
        to = side_rows(r, block, half_rows, parity)

        @pl.when(step < pairs - 1)
        def _():
            mixed_ref[to, here] = back(dq_acc[rows, :] * scale, rows).astype(bf16)

        if last == pairs:
            end = (last - first) * 128

            @pl.when(step == pairs - 1)
            def _():
                k = dk[rows, :]
                k = jnp.where(lane >= HD, k + pltpu.roll(k, HD, 1), dq_acc[rows, :]) * scale
                mixed_ref[to, end - 128 : end] = back(k, rows).astype(bf16)
                v = dv[rows, :]
                v = v + pltpu.roll(v, HD, 1)
                mixed_ref[to, end:] = v[:, :HD].astype(bf16)

    @pl.when(step == last - 1)
    def _():
        total = jnp.zeros((1, mixed_ref.shape[1]), f32)
        for r in range(0, length, block):
            part = mixed_ref[pl.ds(r, block), :].astype(f32)
            total = total + jnp.sum(part, 0, keepdims=True)
        bias_ref[...] = total


def attend_back(parity, own, other, pieces, qk, v, lse, cos, sin, first, last, earlier=()):
    half, depth = own.shape
    length = 2 * half
    wide = qk.shape[1]
    pairs = wide // 128
    group = (last - first) * 128 + (HD if last == pairs else 0)
    block = min(256, half)
    ins = (own, other, qk, v, lse, cos, sin)
    carried = pl.BlockSpec((length, 128), lambda p: (0, 0))
    carry = [jax.ShapeDtypeStruct((length, 128), f32)] * 2
    return pl.pallas_call(
        functools.partial(
            attend_back_kernel, block=block, count=len(pieces), first=first, last=last
        ),
        grid=(last - first,),
        in_specs=[pl.BlockSpec(memory_space=pltpu.SMEM)]
        + [whole(a) for a in ins]
        + [in_place(piece) for piece in pieces]
        + [carried] * len(earlier),
        out_specs=[
            pl.BlockSpec((length, group), lambda p: (0, 0)),
            pl.BlockSpec((1, group), lambda p: (0, 0)),
        ]
        + ([] if first else [carried] * 2),
        out_shape=[
            jax.ShapeDtypeStruct((length, group), bf16),
            jax.ShapeDtypeStruct((1, group), f32),
        ]
        + ([] if first else carry),
        scratch_shapes=[
            pltpu.VMEM((depth, wide), bf16),
            pltpu.VMEM((2, length, 128), bf16),
            pltpu.VMEM((2, length, 128), bf16),
            pltpu.VMEM((length, (last - first) * 128), bf16),
            pltpu.VMEM((length, 128), f32),
        ]
        + ([pltpu.VMEM((length, 128), f32)] * 2 if first else [])
        + [pltpu.SemaphoreType.DMA((len(pieces),))],
        compiler_params=kernel_params(50),
        cost_estimate=cost(12e9, 6e6, 3e6),
    )(parity, *ins, *pieces, *earlier)


def mlp_kernel(x0_ref, x1_ref, g0_ref, g1_ref, *rest, count, add):
    pieces = rest[:count]
    rest = rest[count:]
    if add:
        near_in, far_in, act_ref, near_ref, far_ref, held, sems = rest
    else:
        act_ref, near_ref, far_ref, held, sems = rest
    n = held.shape[1] // 3
    step = pl.program_id(0)

    @pl.when(step == 0)
    def _():
        assemble(pieces, held, sems)

    wg, wu, wd = (held[:, k * n : (k + 1) * n] for k in range(3))
    x = jnp.where(step == 0, x0_ref[...], x1_ref[...])
    g = jnp.where(step == 0, g0_ref[...], g1_ref[...])
    gate = jnp.dot(x, wg, preferred_element_type=f32)
    up = jnp.dot(x, wu, preferred_element_type=f32)
    gh = jnp.dot(g, wd, preferred_element_type=f32)
    sig = 1.0 / (1.0 + jnp.exp(-gate))
    silu = gate * sig
    hid = (silu * up).astype(bf16)
    ghs = gh * sig
    gg = (ghs * up * (1.0 + gate - silu)).astype(bf16)
    gu = (ghs * gate).astype(bf16)
    act_ref[:, :n] = gg
    act_ref[:, n : 2 * n] = gu
    act_ref[:, 2 * n :] = hid
    ngrad = lax.dot_general(gg, wg, NT, preferred_element_type=f32)
    ngrad = ngrad + lax.dot_general(gu, wu, NT, preferred_element_type=f32)
    down = lax.dot_general(hid, wd, NT, preferred_element_type=f32)

    @pl.when(step == 0)
    def _():
        near_ref[0] = (ngrad + near_in[0].astype(f32) if add else ngrad).astype(bf16)
        near_ref[1] = (down + near_in[1].astype(f32) if add else down).astype(bf16)

    @pl.when(step == 1)
    def _():
        far_ref[0] = (ngrad + far_in[0].astype(f32) if add else ngrad).astype(bf16)
        far_ref[1] = (down + far_in[1].astype(f32) if add else down).astype(bf16)


def mlp(rows, grads, pieces, sums=None):
    t, d = rows[0].shape
    columns = pieces[0].shape[1]
    add = sums is not None
    ins = (*rows, *grads)
    sums = tuple(sums or ())
    both = pl.BlockSpec((2, t, d), lambda i: (0, 0, 0))
    return pl.pallas_call(
        functools.partial(mlp_kernel, count=len(pieces), add=add),
        grid=(2,),
        in_specs=[whole(a) for a in ins] + [in_place(p) for p in pieces] + [both] * len(sums),
        out_specs=[pl.BlockSpec((t, columns), lambda i: (i, 0)), both, both],
        out_shape=[
            jax.ShapeDtypeStruct((2 * t, columns), bf16),
            jax.ShapeDtypeStruct((2, t, d), bf16),
            jax.ShapeDtypeStruct((2, t, d), bf16),
        ],
        scratch_shapes=[
            pltpu.VMEM((d, columns), bf16),
            pltpu.SemaphoreType.DMA((len(pieces),)),
        ],
        compiler_params=kernel_params(58),
        cost_estimate=cost(8 * t * d * columns, 30 * MIB, 2 * t * columns),
    )(*ins, *pieces, *sums)


def fill(sent_ref, kept_ref, lefts, rights, second):
    half = kept_ref.shape[0]
    t = lefts[0].shape[0]
    q = half // 2
    if second:
        parts = ((sent_ref, 0, q), (sent_ref, q, 3 * q), (kept_ref, 0, 0), (kept_ref, q, 2 * q))
        size = q
    else:
        parts = ((sent_ref, 0, half), (kept_ref, 0, 0))
        size = half
    for ref, to, start in parts:
        total = 0.0
        for i, left in enumerate(lefts):
            right = rights[i * t // rights[0].shape[0]]
            at = i * t % right.shape[0]
            total = total + lax.dot_general(
                left[:, start : start + size],
                right[at : at + t, :],
                TN,
                preferred_element_type=f32,
            )
        ref[to : to + size, :] = total.astype(ref.dtype)


def outer_kernel(*refs, blocks):
    rows, grads, rights = refs[:blocks], refs[blocks : 2 * blocks], refs[2 * blocks : -4]
    sent_one, kept_one, sent_two, kept_two = refs[-4:]
    step = pl.program_id(0)

    @pl.when(step < 2)
    def _():
        fill(sent_one, kept_one, rows, rights, False)

    @pl.when(step == 2)
    def _():
        fill(sent_two, kept_two, grads, rights, True)


def outer(rows, grads, acts):
    t, d = rows[0].shape
    tall, columns = acts[0].shape
    n = columns // 3
    flat = [*rows, *grads]
    one = pl.BlockSpec((d // 2, n), lambda k: (0, jnp.minimum(k, 1)))
    two = pl.BlockSpec((d // 2, n), lambda k: (0, 0))
    return pl.pallas_call(
        functools.partial(outer_kernel, blocks=len(rows)),
        grid=(3,),
        in_specs=[whole(left) for left in flat]
        + [pl.BlockSpec((tall, n), lambda k: (0, k)) for _ in acts],
        out_specs=[one, one, two, two],
        out_shape=[
            jax.ShapeDtypeStruct((d // 2, 2 * n), bf16),
            jax.ShapeDtypeStruct((d // 2, 2 * n), f32),
            jax.ShapeDtypeStruct((d // 2, n), bf16),
            jax.ShapeDtypeStruct((d // 2, n), f32),
        ],
        compiler_params=kernel_params(58),
        cost_estimate=cost(2 * t * len(rows) * d * columns, 20 * MIB),
    )(*flat, *acts)


def outer_one_kernel(*refs):
    fill(refs[-2], refs[-1], refs[:-3], refs[-3:-2], False)


def outer_one(lefts, right):
    t, d = lefts[0].shape
    columns = right.shape[1]
    vmem = pl.BlockSpec(memory_space=pltpu.VMEM)
    return pl.pallas_call(
        outer_one_kernel,
        in_specs=[vmem] * (len(lefts) + 1),
        out_specs=[vmem] * 2,
        out_shape=[
            jax.ShapeDtypeStruct((d // 2, columns), bf16),
            jax.ShapeDtypeStruct((d // 2, columns), f32),
        ],
        compiler_params=kernel_params(40),
        cost_estimate=cost(2 * t * len(lefts) * d * columns, 6 * MIB),
    )(*lefts, right)


def rope_tables(length):
    inverse = theta_base ** (-(jnp.arange(HD // 2, dtype=f32) * 2.0 / HD))
    angles = jnp.arange(length, dtype=f32)[:, None] * inverse[None, :]
    c, s = jnp.cos(angles), jnp.sin(angles)
    return jnp.concatenate([c] * 4, 1), jnp.concatenate([-s, s, -s, s], 1)


class Gather:
    def __init__(self, block, bits):
        self.bits = bits
        self.left = bits - 1
        self.pieces = [block]
        self.sent = 0
        self.beside = []

    def ready(self, *earlier):
        self.pieces[-1] = after(self.pieces[-1], *earlier)

    def double(self, *earlier):
        held = jnp.concatenate(self.pieces, 0) if len(self.pieces) > 1 else self.pieces[0]
        self.pieces.append(flip(after(held, *earlier) if earlier else held, "row", self.left))
        self.left -= 1
        return self.pieces[-1]

    def send(self, *earlier):
        piece = self.pieces[self.sent]
        self.sent += 1
        self.beside.append(flip(after(piece, *earlier) if earlier else piece, "row", 0))
        return self.beside[-1]

    def catch_up(self, *earlier):
        rest = jnp.concatenate(self.pieces[self.sent :], 0)
        self.sent = len(self.pieces)
        self.beside.append(flip(after(rest, *earlier), "row", 0))
        return self.beside[-1]

    def finish(self, *earlier):
        while self.left > 0:
            self.double()
        self.catch_up(*earlier)
        out = self.pieces + self.beside
        return out if out[0].shape[0] % 16 == 0 else [jnp.concatenate(out, 0)]

    def all(self):
        while self.left > 0:
            self.double()
        while self.sent < len(self.pieces):
            self.send()
        out = self.pieces + self.beside
        return out if out[0].shape[0] % 16 == 0 else [jnp.concatenate(out, 0)]


class Scatter:
    def __init__(self, parts, bits):
        self.bits = bits
        self.orders = [[0, 1], [1, 0]][: len(parts)]
        self.kept = [kept for _, kept in parts]
        self.done = 0
        self.start([sent for sent, _ in parts])

    def start(self, sents):
        bits = [order[self.done] if self.done < 2 else self.done for order in self.orders]
        self.got = [flip(sent, "row", bit) for sent, bit in zip(sents, bits)]

    def wait(self, *earlier):
        self.got = [after(got, *earlier) for got in self.got]

    def step(self):
        if self.done == self.bits - 1:
            return
        self.done += 1
        half = self.kept[0].shape[0] // 2
        sents = [
            (kept[half:] + got[half:].astype(f32)).astype(bf16)
            for kept, got in zip(self.kept, self.got)
        ]
        self.kept = [kept[:half] + got[:half].astype(f32) for kept, got in zip(self.kept, self.got)]
        if self.done == 2:
            sents = [jnp.concatenate(sents, 1)]
            self.kept = [jnp.concatenate(self.kept, 1)]
        self.start(sents)

    def total(self):
        while self.done < self.bits - 1:
            self.step()
        totals = [kept + got.astype(f32) for kept, got in zip(self.kept, self.got)]
        return jnp.concatenate(totals, 1)


def turned_pairs(block):
    first = [(2 * a + b, 2 * b + a) for a in range(2) for b in range(2)]
    second = [(2 * a + b, 2 * (1 - b) + a) for a in range(2) for b in range(2)]
    return lax.ppermute(block, "col", first), lax.ppermute(block, "col", second)


def from_pairs(same, other):
    first = [(2 * a + b, 2 * b + a) for a in range(2) for b in range(2)]
    second = [(2 * a + b, 2 * b + 1 - a) for a in range(2) for b in range(2)]
    return lax.ppermute(same, "col", first), lax.ppermute(other, "col", second)


def cuts(width):
    first = min(512, width)
    return [(0, first), (first, width)] if first < width else [(0, width)]


def shards(
    layer_input,
    gain_attn,
    qkv_weight,
    qkv_bias,
    out_weight,
    gain_mlp,
    gate_weight,
    up_weight,
    down_weight,
    cotangent,
):
    row = lax.axis_index("row")
    column = lax.axis_index("col")
    row_count = lax.axis_size("row")
    bits = row_count.bit_length() - 1
    core = column % 2
    sequence = column // 2
    parity = core.astype(jnp.int32).reshape(1)
    tok_local, model_width = layer_input.shape
    length = tok_local * 2
    deep = model_width // row_count
    ff_cols = gate_weight.shape[1]
    qkv_cols = qkv_weight.shape[1]
    out_cols = out_weight.shape[0]
    group_width = 2 * qkv_cols
    query_width = group_width - 2 * HD

    bias_rows = jnp.pad(qkv_bias[None, :], ((0, 15), (0, 0)))
    first, second = turned_pairs(
        jnp.concatenate(
            [
                jnp.concatenate([qkv_weight, bias_rows], 0),
                jnp.pad(out_weight.T, ((0, 16), (0, 0))),
            ],
            1,
        )
    )
    low = jnp.where(sequence == 0, first, second)
    high = jnp.where(sequence == 0, second, first)
    qkv_own = jnp.concatenate([low[:, :qkv_cols], high[:, :qkv_cols]], 1)
    bias_full = qkv_own[deep : deep + 1].astype(f32)
    out_own = jnp.concatenate([low[:deep, qkv_cols:], high[:deep, qkv_cols:]], 1)
    out_own = jnp.pad(out_own, ((0, 0), (0, HD)))
    qkv_gather = Gather(qkv_own[:deep], bits)
    out_gather = Gather(out_own, bits)
    down_flipped = down_weight.T
    mlp_gathers = []
    for start, stop in cuts(ff_cols):
        padded = -(-(stop - start) // 256) * 256
        pieces = [
            jnp.pad(part[:, start:stop], ((0, 0), (0, padded - (stop - start))))
            for part in (gate_weight, up_weight, down_flipped)
        ]
        mlp_gathers.append(Gather(jnp.concatenate(pieces, 1), bits))
    place = jnp.arange(model_width, dtype=jnp.int32)
    masks = jnp.array([bit_reversed(p, bits) for p in range(row_count)], jnp.int32)
    source = jnp.repeat(masks ^ row, deep) * deep + place % deep
    to_stored = (place[:, None] == source[None, :]).astype(bf16)
    from_stored = (source[:, None] == place[None, :]).astype(bf16)

    def stored(block):
        return jnp.dot(block, to_stored, preferred_element_type=f32)

    def unstored(block):
        return jnp.dot(block, from_stored, preferred_element_type=f32).astype(bf16)

    def unstored_row(vector):
        blocks = vector.reshape(row_count, deep)
        blocks = jnp.concatenate(
            [blocks[bit_reversed(m, bits)][None] for m in range(row_count)], 0
        )
        for bit in range(bits):
            wide = blocks.reshape(-1, 2, 1 << bit, deep)
            turned = jnp.concatenate([wide[:, 1:], wide[:, :1]], 1).reshape(row_count, deep)
            blocks = jnp.where((row >> bit) % 2 == 1, turned, blocks)
        return blocks.reshape(model_width)

    input_rows = stored(after(layer_input, first, second))
    grad_out = stored(cotangent)
    gain_one = stored(gain_attn[None, :])
    gain_two = stored(gain_mlp[None, :])

    scale_one = lax.rsqrt(jnp.mean(input_rows * input_rows, axis=1) + eps)
    normed_own = (input_rows * scale_one[:, None] * gain_one).astype(bf16)
    normed_other = flip(normed_own, "col", 0)
    cosine, sine_part = rope_tables(length)
    grad_blocks = [grad_out.astype(bf16)]

    near, far = mlp_gathers
    n_four = near.double()
    n_own = near.send()
    a_own = qkv_gather.send()
    a_four = qkv_gather.double()
    a_two = qkv_gather.double(a_own)
    a_beside = qkv_gather.send(a_own)
    o_four = out_gather.double(a_four)
    a_last = qkv_gather.send(a_beside, n_own)
    qkv_pieces = qkv_gather.all()
    far.ready(a_two, o_four)
    f_four = far.double()
    o_two = out_gather.double(a_two)
    across = flip(after(grad_blocks[0], a_four), "col", 1)
    out_pieces = out_gather.finish(a_last, o_two)
    n_two = near.double(o_two)
    n_beside = near.send(a_last)
    qk_rows, value_rows, att_rows, log_totals = attend(
        parity,
        normed_own,
        normed_other,
        qkv_pieces,
        bias_full,
        cosine,
        sine_part,
    )
    n_last = near.send(att_rows)
    att_own, att_other = project(after(att_rows, n_beside, n_two, across, f_four), out_pieces)
    att_got = flip(att_other, "col", 0)
    grad_blocks.append(flip(after(grad_blocks[0], att_got), "col", 0))
    grad_blocks += [across, flip(after(across, att_got), "col", 0)]
    middle = input_rows + att_own + att_got.astype(f32)
    scale_two = lax.rsqrt(jnp.mean(middle * middle, axis=1) + eps)
    blocks = [(middle * scale_two[:, None] * gain_two).astype(bf16)]
    across = flip(blocks[0], "col", 1)
    blocks.append(flip(after(blocks[0], n_last), "col", 0))
    blocks += [across, flip(across, "col", 0)]

    f_beside = far.catch_up(n_last)
    f_two = far.double(blocks[2])
    f_last = far.send(f_beside)
    first_pieces, second_pieces = (gather.all() for gather in mlp_gathers)
    act_own, *sums_own = mlp([after(blocks[0], blocks[2]), blocks[1]], grad_blocks[:2], first_pieces)
    act_far, *sums_far = mlp(blocks[2:], grad_blocks[2:], first_pieces)
    sent_one, kept_one, sent_two, kept_two = outer(blocks, grad_blocks, [act_own, act_far])
    first_scatter = Scatter([(sent_one, kept_one), (sent_two, kept_two)], bits)
    start_far = after(blocks[2], kept_one)
    act_far, near_far, far_far = mlp(
        [start_far, blocks[3]], grad_blocks[2:], second_pieces, sums_far
    )
    far_far = after(far_far, *first_scatter.got)
    across = near_far.astype(f32) + flip(far_far, "col", 0).astype(f32)
    across = across.astype(bf16)
    normed_back = flip(across[0], "col", 1)
    act_own, near_own, far_own = mlp(
        [after(blocks[0], across), blocks[1]],
        grad_blocks[:2],
        second_pieces,
        sums_own,
    )
    first_scatter.step()
    beside = flip(after(far_own, normed_back, *first_scatter.got), "col", 0)
    first_scatter.step()
    down_back = flip(after(across[1], normed_back), "col", 1)

    def summed(k, back):
        return near_own[k].astype(f32) + beside[k].astype(f32) + back.astype(f32)

    grad_normed_two = summed(0, normed_back)
    scaled_two = gain_two * grad_normed_two
    inner_two = jnp.sum(scaled_two * middle, axis=1)
    grad_middle = (
        grad_out
        + scale_two[:, None] * scaled_two
        - middle * (scale_two**3 * inner_two / model_width)[:, None]
    )
    gain_two_grad = jnp.sum(grad_normed_two * middle * scale_two[:, None], axis=0)
    branch_own = grad_middle.astype(bf16)
    branch_other = flip(branch_own, "col", 0)
    out_scatter = Scatter([outer_one([branch_own, branch_other], att_rows)], bits)
    sent_one, kept_one, sent_two, kept_two = outer(
        [after(blocks[0], out_scatter.kept[0], *first_scatter.kept), *blocks[1:]],
        grad_blocks,
        [act_own, act_far],
    )
    second_scatter = Scatter([(sent_one, kept_one), (sent_two, kept_two)], bits)
    out_scatter.wait(kept_one)
    out_scatter.step()
    split = qk_rows.shape[1] // 256
    mixed_first, bias_first, *carry = attend_back(
        parity,
        after(branch_own, kept_one, out_scatter.kept[0]),
        branch_other,
        out_pieces,
        qk_rows,
        value_rows,
        log_totals,
        cosine,
        sine_part,
        0,
        split,
    )
    out_scatter.wait(mixed_first)
    mixed_last, bias_last = attend_back(
        parity,
        after(branch_own, mixed_first),
        branch_other,
        out_pieces,
        qk_rows,
        value_rows,
        log_totals,
        cosine,
        sine_part,
        split,
        2 * split,
        carry,
    )
    bias_grad = jnp.concatenate([bias_first, bias_last], 1)[0]
    first_scatter.wait(mixed_last)
    second_scatter.wait(mixed_last)
    out_scatter.wait(mixed_last)
    grad_mixed = jnp.concatenate([mixed_first, mixed_last], 1)
    second_scatter.step()
    layer_output = unstored((middle + summed(1, after(down_back, grad_mixed))).astype(bf16))
    qkv_scatter = Scatter([outer_one([normed_own, normed_other], after(grad_mixed, second_scatter.kept[0]))], bits)
    qkv_full = jnp.concatenate(qkv_pieces, 0)
    grad_mixed = after(grad_mixed, qkv_scatter.kept[0])
    out_scatter.wait(qkv_scatter.kept[0])
    out_scatter.step()
    partial = jnp.einsum("tc,dc->td", grad_mixed, qkv_full, preferred_element_type=f32)
    grad_normed_one = partial[:tok_local] + flip(
        partial[tok_local:].astype(bf16), "col", 0
    ).astype(f32)
    scaled_one = gain_one * grad_normed_one
    inner_one = jnp.sum(scaled_one * input_rows, axis=1)
    input_grad = unstored(
        (
            grad_middle
            + scale_one[:, None] * scaled_one
            - input_rows * (scale_one**3 * inner_one / model_width)[:, None]
        ).astype(bf16)
    )
    gain_one_grad = jnp.sum(grad_normed_one * input_rows * scale_one[:, None], axis=0)

    def to_columns(total, width):
        low, high = total[:, :width].astype(bf16), total[:, width : 2 * width].astype(bf16)
        first, second = from_pairs(
            jnp.where(sequence == 0, low, high), jnp.where(sequence == 0, high, low)
        )
        return first.astype(f32) + second.astype(f32)

    bias_row = lax.dynamic_update_slice_in_dim(
        jnp.zeros((group_width * 2,), f32), bias_grad, core * group_width, 0
    )
    small = jnp.concatenate([unstored_row(gain_one_grad), unstored_row(gain_two_grad), bias_row])
    small = jnp.pad(small, (0, -small.shape[0] % 128)).reshape(-1, 128)
    small = after(small, *second_scatter.got)
    second_scatter.step()
    for bit in range(2):
        small = small + flip(small, "col", bit)
    for bit in range(bits):
        small = small + flip(small, "row", bit)
    qkv_total = to_columns(qkv_scatter.total(), qkv_cols)
    out_total = to_columns(out_scatter.total(), out_cols)
    mlp_totals = []
    for scatter, (start, stop) in zip((first_scatter, second_scatter), cuts(ff_cols)):
        total = scatter.total()
        padded = total.shape[1] // 3
        mlp_totals.append(
            [total[:, k * padded : k * padded + stop - start] for k in range(3)]
        )
    gate_total, up_total, down_total = (jnp.concatenate(parts, 1) for parts in zip(*mlp_totals))
    small = small.reshape(-1)
    gain_one_total = small[:model_width]
    gain_two_total = small[model_width : 2 * model_width]
    bias_total = lax.dynamic_slice_in_dim(small, 2 * model_width + column * qkv_cols, qkv_cols, 0)
    return (
        layer_output,
        input_grad,
        gain_one_total,
        qkv_total,
        bias_total,
        out_total.T,
        gain_two_total,
        gate_total,
        up_total,
        down_total.T,
    )


def solution(mesh):
    in_specs = (
        P(("row", "col"), None),
        P(),
        P("row", "col"),
        P("col"),
        P("col", "row"),
        P(),
        P("row", "col"),
        P("row", "col"),
        P("col", "row"),
        P(("row", "col"), None),
    )
    out_specs = (
        P(("row", "col"), None),
        P(("row", "col"), None),
        P(),
        P("row", "col"),
        P("col"),
        P("col", "row"),
        P(),
        P("row", "col"),
        P("row", "col"),
        P("col", "row"),
    )
    return jax.shard_map(shards, mesh=mesh, in_specs=in_specs, out_specs=out_specs, check_vma=False)
```

```python
import functools
import math

import jax
import jax.numpy as jnp
from jax import lax
from jax.experimental import pallas as pl
from jax.experimental.pallas import tpu as pltpu
from jax.sharding import PartitionSpec as P

HD = 64
eps = 1e-06
theta_base = 1000000.0
bf16 = jnp.bfloat16
f32 = jnp.float32
NT = (((1,), (1,)), ((), ()))
TN = (((0,), (0,)), ((), ()))
MIB = 1024 * 1024


def flip(block, axis, bit):
    count = lax.axis_size(axis)
    return lax.ppermute(block, axis, [(i, i ^ 1 << bit) for i in range(count)])


def bit_reversed(value, bits):
    return sum((value >> b & 1) << (bits - 1 - b) for b in range(bits))


def after(value, *earlier):
    return lax.optimization_barrier((value, *earlier))[0]


def kernel_params(mib):
    return pltpu.CompilerParams(vmem_limit_bytes=mib * MIB)


def cost(flops, nbytes, exps=0):
    return pl.CostEstimate(
        flops=int(flops), bytes_accessed=int(nbytes), transcendentals=int(exps)
    )


def whole(array):
    return pl.BlockSpec(array.shape, lambda *_: (0,) * len(array.shape))


def in_place(block):
    return pl.BlockSpec(memory_space=pl.ANY)


def assemble(pieces, held, sems):
    copies = []
    at = 0
    for i, piece in enumerate(pieces):
        rows = piece.shape[0]
        copies.append(pltpu.make_async_copy(piece, held.at[pl.ds(at, rows)], sems.at[i]))
        at += rows
    for copy in copies:
        copy.start()
    for copy in copies:
        copy.wait()


def halves_turned(block):
    lane = lax.broadcasted_iota(jnp.int32, block.shape, 1)
    up = pltpu.roll(block, 128 - HD // 2, 1)
    return jnp.where(lane % HD < HD // 2, up, pltpu.roll(block, HD // 2, 1))


def side_rows(r, block, half, parity):
    side = (r // half) ^ parity
    return pl.ds(pl.multiple_of(side * half + r % half, block), block)


def pad_heads(key_value, rows, value, last):
    lane = lax.broadcasted_iota(jnp.int32, (1, 128), 1)
    kpad, vpad = key_value
    zero = jnp.zeros_like(value)
    vpad[0, rows, :] = jnp.concatenate([value, zero], 1).astype(bf16)
    vpad[1, rows, :] = jnp.concatenate([zero, value], 1).astype(bf16)
    kpad[1, rows, :] = jnp.where(lane >= HD, last, 0.0).astype(bf16)
    kpad[0, rows, :] = jnp.where(lane < HD, pltpu.roll(last, HD, 1), 0.0).astype(bf16)


def attend_kernel(parity_ref, *rest, block, count, first, last):
    if first == 0:
        own_ref, other_ref, bias_ref, cos_ref, sin_ref = rest[:5]
        pieces = rest[5 : 5 + count]
        qk_ref, v_ref, att_ref, lse_ref, held, kpad, vpad, lse_cols, sems = rest[5 + count :]
    else:
        qk_ref, v_ref, att_ref, lse_ref, kpad, vpad, lse_cols = rest
    step = pl.program_id(0) + first
    length, wide = qk_ref.shape
    half = length // 2
    pairs = wide // 128
    parity = parity_ref[0]

    @pl.when(step == first)
    def _():
        lse_cols[...] = jnp.zeros_like(lse_cols)
        if first:
            for r in range(0, length, block):
                rows = pl.ds(r, block)
                keys = qk_ref[rows, wide - 128 :].astype(f32)
                pad_heads((kpad, vpad), rows, v_ref[rows, :].astype(f32), keys)
            return
        assemble(pieces, held, sems)
        for side, rows_ref in enumerate((own_ref, other_ref)):
            for r in range(0, half, block):
                at = pl.multiple_of((side ^ parity) * half + r, block)
                rows = pl.ds(at, block)
                mixed = jnp.dot(rows_ref[r : r + block, :], held[...], preferred_element_type=f32)
                mixed = (mixed + bias_ref[...]).astype(bf16).astype(f32)
                cos, sin = cos_ref[rows, :], sin_ref[rows, :]
                for p in range(pairs):
                    u = mixed[:, p * 128 : (p + 1) * 128]
                    turned = (u * cos + halves_turned(u) * sin).astype(bf16)
                    qk_ref[rows, p * 128 : (p + 1) * 128] = turned
                v_ref[rows, :] = mixed[:, wide:].astype(bf16)
                pad_heads((kpad, vpad), rows, mixed[:, wide:], turned.astype(f32))

    factor = HD**-0.5 * math.log2(math.e)
    cols = pl.ds(pl.multiple_of(step * 128, 128), 128)
    row_i = lax.broadcasted_iota(jnp.int32, (block, block), 0)
    col_i = lax.broadcasted_iota(jnp.int32, (block, block), 1)
    for r in range(0, length, block):
        rows = pl.ds(r, block)
        to = side_rows(r, block, half, parity)
        q = qk_ref[rows, cols]

        def head(odd):
            keys = kpad[odd, : r + block, :]
            scores = lax.dot_general(q, keys, NT, preferred_element_type=f32)
            diag = jnp.where(col_i <= row_i, scores[:, r:], -1e30)
            scores = jnp.concatenate([scores[:, :r], diag], 1) if r else diag
            top = jnp.max(scores, 1, keepdims=True)
            e = jnp.exp2((scores - top) * factor)
            total = jnp.sum(e, 1, keepdims=True)
            out = jnp.dot(e.astype(bf16), vpad[odd, : r + block, :], preferred_element_type=f32)
            lse = top * factor + jnp.log2(total)
            at = lax.broadcasted_iota(jnp.int32, (1, 128), 1) == 2 * step + odd
            lse_cols[rows, :] = jnp.where(at, lse, lse_cols[rows, :])
            return out / total

        even = head(0)

        @pl.when(step < pairs - 1)
        def _():
            att_ref[to, :] = (even + head(1)).astype(bf16)

        @pl.when(step == pairs - 1)
        def _():
            att_ref[to, :] = even.astype(bf16)

    @pl.when(step == last - 1)
    def _():
        lse_ref[...] = lse_cols[...].T[: lse_ref.shape[0], :]


def attend(parity, own, other, pieces, bias, cos, sin, last):
    half, depth = own.shape
    length = 2 * half
    group = bias.shape[1]
    wide = group - HD
    block = min(256, half)
    return pl.pallas_call(
        functools.partial(attend_kernel, block=block, count=len(pieces), first=0, last=last),
        grid=(last,),
        in_specs=[pl.BlockSpec(memory_space=pltpu.SMEM)]
        + [whole(a) for a in (own, other, bias, cos, sin)]
        + [in_place(piece) for piece in pieces],
        out_specs=[
            pl.BlockSpec((length, wide), lambda p: (0, 0)),
            pl.BlockSpec((length, HD), lambda p: (0, 0)),
            pl.BlockSpec((length, 128), lambda p: (0, p)),
            pl.BlockSpec((8, length), lambda p: (0, 0)),
        ],
        out_shape=[
            jax.ShapeDtypeStruct((length, wide), bf16),
            jax.ShapeDtypeStruct((length, HD), bf16),
            jax.ShapeDtypeStruct((length, last * 128), bf16),
            jax.ShapeDtypeStruct((8, length), f32),
        ],
        scratch_shapes=[
            pltpu.VMEM((depth, group), bf16),
            pltpu.VMEM((2, length, 128), bf16),
            pltpu.VMEM((2, length, 128), bf16),
            pltpu.VMEM((length, 128), f32),
            pltpu.SemaphoreType.DMA((len(pieces),)),
        ],
        compiler_params=kernel_params(40),
        cost_estimate=cost(8e9, 6e6, 3e6),
    )(parity, own, other, bias, cos, sin, *pieces)


def attend_rest(parity, qk, v, first):
    length, wide = qk.shape
    pairs = wide // 128
    block = min(256, length // 2)
    return pl.pallas_call(
        functools.partial(attend_kernel, block=block, count=0, first=first, last=pairs),
        grid=(pairs - first,),
        in_specs=[pl.BlockSpec(memory_space=pltpu.SMEM), whole(qk), whole(v)],
        out_specs=[
            pl.BlockSpec((length, 128), lambda p: (0, p)),
            pl.BlockSpec((8, length), lambda p: (0, 0)),
        ],
        out_shape=[
            jax.ShapeDtypeStruct((length, (pairs - first) * 128), bf16),
            jax.ShapeDtypeStruct((8, length), f32),
        ],
        scratch_shapes=[
            pltpu.VMEM((2, length, 128), bf16),
            pltpu.VMEM((2, length, 128), bf16),
            pltpu.VMEM((length, 128), f32),
        ],
        compiler_params=kernel_params(40),
        cost_estimate=cost(6e9, 4e6, 3e6),
    )(parity, qk, v)


def project_kernel(first_ref, last_ref, *rest, count):
    pieces = rest[:count]
    own_ref, other_ref, held, sems = rest[count:]
    half = own_ref.shape[0]
    assemble(pieces, held, sems)
    for side, ref in enumerate((own_ref, other_ref)):
        total = 0.0
        at = 0
        for part_ref in (first_ref, last_ref):
            rows = part_ref[side * half : (side + 1) * half, :]
            weight = held[:, at : at + rows.shape[1]]
            total = total + lax.dot_general(rows, weight, NT, preferred_element_type=f32)
            at += rows.shape[1]
        ref[...] = total.astype(ref.dtype)


def project(first, last, pieces):
    length = first.shape[0]
    wide = first.shape[1] + last.shape[1]
    depth = sum(piece.shape[0] for piece in pieces)
    return pl.pallas_call(
        functools.partial(project_kernel, count=len(pieces)),
        in_specs=[pl.BlockSpec(memory_space=pltpu.VMEM)] * 2
        + [in_place(piece) for piece in pieces],
        out_specs=[pl.BlockSpec(memory_space=pltpu.VMEM)] * 2,
        out_shape=[
            jax.ShapeDtypeStruct((length // 2, depth), f32),
            jax.ShapeDtypeStruct((length // 2, depth), bf16),
        ],
        scratch_shapes=[
            pltpu.VMEM((depth, wide), bf16),
            pltpu.SemaphoreType.DMA((len(pieces),)),
        ],
        compiler_params=kernel_params(40),
        cost_estimate=cost(2 * length * depth * wide, 6e6),
    )(first, last, *pieces)


def attend_back_kernel(
    parity_ref,
    own_ref,
    other_ref,
    qk_ref,
    v_ref,
    lse_ref,
    cos_ref,
    sin_ref,
    *rest,
    block,
    count,
    first,
    last,
):
    pieces = rest[:count]
    if first == 0:
        mixed_ref, bias_ref, dk, dv, held, kpad, vpad, gatt, dq_acc, sems = rest[count:]
    else:
        dk_in, dv_in, mixed_ref, bias_ref, held, kpad, vpad, gatt, dq_acc, dk, dv, sems = rest[count:]
    step = pl.program_id(0) + first
    half_rows = own_ref.shape[0]
    length = 2 * half_rows
    wide = qk_ref.shape[1]
    pairs = wide // 128
    used = slice(first * 128, last * 128)
    parity = parity_ref[0]
    lane = lax.broadcasted_iota(jnp.int32, (1, 128), 1)

    @pl.when(step == first)
    def _():
        assemble(pieces, held, sems)
        for side, rows_ref in enumerate((own_ref, other_ref)):
            for r in range(0, half_rows, block):
                rows = pl.ds(pl.multiple_of((side ^ parity) * half_rows + r, block), block)
                got = jnp.dot(
                    rows_ref[r : r + block, :], held[:, used], preferred_element_type=f32
                )
                gatt[rows, :] = got.astype(bf16)
        for r in range(0, length, block):
            rows = pl.ds(r, block)
            keys = qk_ref[rows, wide - 128 :].astype(f32)
            pad_heads((kpad, vpad), rows, v_ref[rows, :].astype(f32), keys)
        dk[...] = dk_in[...] if first else jnp.zeros_like(dk)
        dv[...] = dv_in[...] if first else jnp.zeros_like(dv)

    factor = HD**-0.5 * math.log2(math.e)
    cols = pl.ds(pl.multiple_of(step * 128, 128), 128)
    here = pl.ds(pl.multiple_of((step - first) * 128, 128), 128)
    key_i = lax.broadcasted_iota(jnp.int32, (block, block), 0)
    query_i = lax.broadcasted_iota(jnp.int32, (block, block), 1)
    for r in range(0, length, block):
        rows = pl.ds(r, block)
        q = qk_ref[rows, cols]
        g = gatt[rows, here]

        def head(odd):
            lse = lse_ref[pl.ds(2 * step + odd, 1), rows]
            probs, grads = [], []
            inner = jnp.zeros((1, block), f32)
            for c in range(0, r + block, block):
                scores = lax.dot_general(
                    kpad[odd, c : c + block, :], q, NT, preferred_element_type=f32
                )
                p = jnp.exp2(scores * factor - lse)
                if c == r:
                    p = jnp.where(key_i <= query_i, p, 0.0)
                dp = lax.dot_general(vpad[odd, c : c + block, :], g, NT, preferred_element_type=f32)
                inner = inner + jnp.sum(p * dp, 0, keepdims=True)
                probs.append(p)
                grads.append(dp)
            dq = 0.0
            half = lane >= HD if odd else lane < HD
            for i, c in enumerate(range(0, r + block, block)):
                keys = pl.ds(c, block)
                ds = (probs[i] * (grads[i] - inner)).astype(bf16)
                p = probs[i].astype(bf16)
                dk[keys, :] += jnp.where(half, jnp.dot(ds, q, preferred_element_type=f32), 0.0)
                dv[keys, :] += jnp.where(half, jnp.dot(p, g, preferred_element_type=f32), 0.0)
                dq = dq + lax.dot_general(
                    ds, kpad[odd, c : c + block, :], TN, preferred_element_type=f32
                )
            return dq

        dq_acc[rows, :] = head(0)

        @pl.when(step < pairs - 1)
        def _():
            dq_acc[rows, :] += head(1)

    def back(u, rows):
        return u * cos_ref[rows, :] - halves_turned(u) * sin_ref[rows, :]

    scale = HD**-0.5
    for r in range(0, length, block):
        rows = pl.ds(r, block)
        to = side_rows(r, block, half_rows, parity)

        @pl.when(step < pairs - 1)
        def _():
            mixed_ref[to, here] = back(dq_acc[rows, :] * scale, rows).astype(bf16)

        if last == pairs:
            end = (last - first) * 128

            @pl.when(step == pairs - 1)
            def _():
                k = dk[rows, :]
                k = jnp.where(lane >= HD, k + pltpu.roll(k, HD, 1), dq_acc[rows, :]) * scale
                mixed_ref[to, end - 128 : end] = back(k, rows).astype(bf16)
                v = dv[rows, :]
                v = v + pltpu.roll(v, HD, 1)
                mixed_ref[to, end:] = v[:, :HD].astype(bf16)

    @pl.when(step == last - 1)
    def _():
        total = jnp.zeros((1, mixed_ref.shape[1]), f32)
        for r in range(0, length, block):
            part = mixed_ref[pl.ds(r, block), :].astype(f32)
            total = total + jnp.sum(part, 0, keepdims=True)
        bias_ref[...] = total


def attend_back(parity, own, other, pieces, qk, v, lse, cos, sin, first, last, earlier=()):
    half, depth = own.shape
    length = 2 * half
    wide = qk.shape[1]
    pairs = wide // 128
    group = (last - first) * 128 + (HD if last == pairs else 0)
    block = min(256, half)
    ins = (own, other, qk, v, lse, cos, sin)
    carried = pl.BlockSpec((length, 128), lambda p: (0, 0))
    carry = [jax.ShapeDtypeStruct((length, 128), f32)] * 2
    return pl.pallas_call(
        functools.partial(
            attend_back_kernel, block=block, count=len(pieces), first=first, last=last
        ),
        grid=(last - first,),
        in_specs=[pl.BlockSpec(memory_space=pltpu.SMEM)]
        + [whole(a) for a in ins]
        + [in_place(piece) for piece in pieces]
        + [carried] * len(earlier),
        out_specs=[
            pl.BlockSpec((length, group), lambda p: (0, 0)),
            pl.BlockSpec((1, group), lambda p: (0, 0)),
        ]
        + ([] if first else [carried] * 2),
        out_shape=[
            jax.ShapeDtypeStruct((length, group), bf16),
            jax.ShapeDtypeStruct((1, group), f32),
        ]
        + ([] if first else carry),
        scratch_shapes=[
            pltpu.VMEM((depth, wide), bf16),
            pltpu.VMEM((2, length, 128), bf16),
            pltpu.VMEM((2, length, 128), bf16),
            pltpu.VMEM((length, (last - first) * 128), bf16),
            pltpu.VMEM((length, 128), f32),
        ]
        + ([pltpu.VMEM((length, 128), f32)] * 2 if first else [])
        + [pltpu.SemaphoreType.DMA((len(pieces),))],
        compiler_params=kernel_params(50),
        cost_estimate=cost(12e9, 6e6, 3e6),
    )(parity, *ins, *pieces, *earlier)


def mlp_kernel(x0_ref, x1_ref, g0_ref, g1_ref, *rest, count, add):
    pieces = rest[:count]
    rest = rest[count:]
    if add:
        near_in, far_in, act_ref, near_ref, far_ref, held, sems = rest
    else:
        act_ref, near_ref, far_ref, held, sems = rest
    n = held.shape[1] // 3
    step = pl.program_id(0)

    @pl.when(step == 0)
    def _():
        assemble(pieces, held, sems)

    wg, wu, wd = (held[:, k * n : (k + 1) * n] for k in range(3))
    x = jnp.where(step == 0, x0_ref[...], x1_ref[...])
    g = jnp.where(step == 0, g0_ref[...], g1_ref[...])
    gate = jnp.dot(x, wg, preferred_element_type=f32)
    up = jnp.dot(x, wu, preferred_element_type=f32)
    gh = jnp.dot(g, wd, preferred_element_type=f32)
    sig = 1.0 / (1.0 + jnp.exp(-gate))
    silu = gate * sig
    hid = (silu * up).astype(bf16)
    ghs = gh * sig
    gg = (ghs * up * (1.0 + gate - silu)).astype(bf16)
    gu = (ghs * gate).astype(bf16)
    act_ref[:, :n] = gg
    act_ref[:, n : 2 * n] = gu
    act_ref[:, 2 * n :] = hid
    ngrad = lax.dot_general(gg, wg, NT, preferred_element_type=f32)
    ngrad = ngrad + lax.dot_general(gu, wu, NT, preferred_element_type=f32)
    down = lax.dot_general(hid, wd, NT, preferred_element_type=f32)

    @pl.when(step == 0)
    def _():
        near_ref[0] = (ngrad + near_in[0].astype(f32) if add else ngrad).astype(bf16)
        near_ref[1] = (down + near_in[1].astype(f32) if add else down).astype(bf16)

    @pl.when(step == 1)
    def _():
        far_ref[0] = (ngrad + far_in[0].astype(f32) if add else ngrad).astype(bf16)
        far_ref[1] = (down + far_in[1].astype(f32) if add else down).astype(bf16)


def mlp(rows, grads, pieces, sums=None):
    t, d = rows[0].shape
    columns = pieces[0].shape[1]
    add = sums is not None
    ins = (*rows, *grads)
    sums = tuple(sums or ())
    both = pl.BlockSpec((2, t, d), lambda i: (0, 0, 0))
    return pl.pallas_call(
        functools.partial(mlp_kernel, count=len(pieces), add=add),
        grid=(2,),
        in_specs=[whole(a) for a in ins] + [in_place(p) for p in pieces] + [both] * len(sums),
        out_specs=[pl.BlockSpec((t, columns), lambda i: (i, 0)), both, both],
        out_shape=[
            jax.ShapeDtypeStruct((2 * t, columns), bf16),
            jax.ShapeDtypeStruct((2, t, d), bf16),
            jax.ShapeDtypeStruct((2, t, d), bf16),
        ],
        scratch_shapes=[
            pltpu.VMEM((d, columns), bf16),
            pltpu.SemaphoreType.DMA((len(pieces),)),
        ],
        compiler_params=kernel_params(58),
        cost_estimate=cost(8 * t * d * columns, 30 * MIB, 2 * t * columns),
    )(*ins, *pieces, *sums)


def fill(sent_ref, kept_ref, lefts, rights, second):
    half = kept_ref.shape[0]
    t = lefts[0].shape[0]
    q = half // 2
    if second:
        parts = ((sent_ref, 0, q), (sent_ref, q, 3 * q), (kept_ref, 0, 0), (kept_ref, q, 2 * q))
        size = q
    else:
        parts = ((sent_ref, 0, half), (kept_ref, 0, 0))
        size = half
    for ref, to, start in parts:
        total = 0.0
        for i, left in enumerate(lefts):
            right = rights[i * t // rights[0].shape[0]]
            at = i * t % right.shape[0]
            total = total + lax.dot_general(
                left[:, start : start + size],
                right[at : at + t, :],
                TN,
                preferred_element_type=f32,
            )
        ref[to : to + size, :] = total.astype(ref.dtype)


def outer_kernel(*refs, blocks):
    rows, grads, rights = refs[:blocks], refs[blocks : 2 * blocks], refs[2 * blocks : -4]
    sent_one, kept_one, sent_two, kept_two = refs[-4:]
    step = pl.program_id(0)

    @pl.when(step < 2)
    def _():
        fill(sent_one, kept_one, rows, rights, False)

    @pl.when(step == 2)
    def _():
        fill(sent_two, kept_two, grads, rights, True)


def outer(rows, grads, acts):
    t, d = rows[0].shape
    tall, columns = acts[0].shape
    n = columns // 3
    flat = [*rows, *grads]
    one = pl.BlockSpec((d // 2, n), lambda k: (0, jnp.minimum(k, 1)))
    two = pl.BlockSpec((d // 2, n), lambda k: (0, 0))
    return pl.pallas_call(
        functools.partial(outer_kernel, blocks=len(rows)),
        grid=(3,),
        in_specs=[whole(left) for left in flat]
        + [pl.BlockSpec((tall, n), lambda k: (0, k)) for _ in acts],
        out_specs=[one, one, two, two],
        out_shape=[
            jax.ShapeDtypeStruct((d // 2, 2 * n), bf16),
            jax.ShapeDtypeStruct((d // 2, 2 * n), f32),
            jax.ShapeDtypeStruct((d // 2, n), bf16),
            jax.ShapeDtypeStruct((d // 2, n), f32),
        ],
        compiler_params=kernel_params(58),
        cost_estimate=cost(2 * t * len(rows) * d * columns, 20 * MIB),
    )(*flat, *acts)


def outer_one_kernel(*refs):
    fill(refs[-2], refs[-1], refs[:-3], refs[-3:-2], False)


def outer_one(lefts, right):
    t, d = lefts[0].shape
    columns = right.shape[1]
    vmem = pl.BlockSpec(memory_space=pltpu.VMEM)
    return pl.pallas_call(
        outer_one_kernel,
        in_specs=[vmem] * (len(lefts) + 1),
        out_specs=[vmem] * 2,
        out_shape=[
            jax.ShapeDtypeStruct((d // 2, columns), bf16),
            jax.ShapeDtypeStruct((d // 2, columns), f32),
        ],
        compiler_params=kernel_params(40),
        cost_estimate=cost(2 * t * len(lefts) * d * columns, 6 * MIB),
    )(*lefts, right)


def rope_tables(length):
    inverse = theta_base ** (-(jnp.arange(HD // 2, dtype=f32) * 2.0 / HD))
    angles = jnp.arange(length, dtype=f32)[:, None] * inverse[None, :]
    c, s = jnp.cos(angles), jnp.sin(angles)
    return jnp.concatenate([c] * 4, 1), jnp.concatenate([-s, s, -s, s], 1)


class Gather:
    def __init__(self, block, bits):
        self.bits = bits
        self.left = bits - 1
        self.pieces = [block]
        self.sent = 0
        self.beside = []

    def ready(self, *earlier):
        self.pieces[-1] = after(self.pieces[-1], *earlier)

    def double(self, *earlier):
        held = jnp.concatenate(self.pieces, 0) if len(self.pieces) > 1 else self.pieces[0]
        self.pieces.append(flip(after(held, *earlier) if earlier else held, "row", self.left))
        self.left -= 1
        return self.pieces[-1]

    def double_all(self):
        while self.left > 0:
            self.double()
        return self.pieces[-1]

    def send(self, *earlier):
        piece = self.pieces[self.sent]
        self.sent += 1
        self.beside.append(flip(after(piece, *earlier) if earlier else piece, "row", 0))
        return self.beside[-1]

    def catch_up(self, *earlier):
        rest = jnp.concatenate(self.pieces[self.sent :], 0)
        self.sent = len(self.pieces)
        self.beside.append(flip(after(rest, *earlier), "row", 0))
        return self.beside[-1]

    def finish(self, *earlier):
        while self.left > 0:
            self.double()
        self.catch_up(*earlier)
        out = self.pieces + self.beside
        return out if out[0].shape[0] % 16 == 0 else [jnp.concatenate(out, 0)]

    def all(self):
        while self.left > 0:
            self.double()
        while self.sent < len(self.pieces):
            self.send()
        out = self.pieces + self.beside
        return out if out[0].shape[0] % 16 == 0 else [jnp.concatenate(out, 0)]


class Scatter:
    def __init__(self, parts, bits):
        self.bits = bits
        self.orders = [[0, 1], [1, 0]][: len(parts)]
        self.kept = [kept for _, kept in parts]
        self.done = 0
        self.start([sent for sent, _ in parts])

    def start(self, sents):
        bits = [order[self.done] if self.done < 2 else self.done for order in self.orders]
        self.got = [flip(sent, "row", bit) for sent, bit in zip(sents, bits)]

    def wait(self, *earlier):
        self.got = [after(got, *earlier) for got in self.got]

    def step(self):
        if self.done == self.bits - 1:
            return
        self.done += 1
        half = self.kept[0].shape[0] // 2
        sents = [
            (kept[half:] + got[half:].astype(f32)).astype(bf16)
            for kept, got in zip(self.kept, self.got)
        ]
        self.kept = [kept[:half] + got[:half].astype(f32) for kept, got in zip(self.kept, self.got)]
        if self.done == 2:
            sents = [jnp.concatenate(sents, 1)]
            self.kept = [jnp.concatenate(self.kept, 1)]
        self.start(sents)

    def total(self):
        while self.done < self.bits - 1:
            self.step()
        totals = [kept + got.astype(f32) for kept, got in zip(self.kept, self.got)]
        return jnp.concatenate(totals, 1)


def in_order(first, second, parity, axis=0):
    return jnp.where(
        parity == 0,
        jnp.concatenate([first, second], axis),
        jnp.concatenate([second, first], axis),
    )


def turned_pairs(block):
    first = [(2 * a + b, 2 * b + a) for a in range(2) for b in range(2)]
    second = [(2 * a + b, 2 * (1 - b) + a) for a in range(2) for b in range(2)]
    return lax.ppermute(block, "col", first), lax.ppermute(block, "col", second)


def from_pairs(same, other):
    first = [(2 * a + b, 2 * b + a) for a in range(2) for b in range(2)]
    second = [(2 * a + b, 2 * b + 1 - a) for a in range(2) for b in range(2)]
    return lax.ppermute(same, "col", first), lax.ppermute(other, "col", second)


def cuts(width):
    first = min(512, width)
    return [(0, first), (first, width)] if first < width else [(0, width)]


def shards(
    layer_input,
    gain_attn,
    qkv_weight,
    qkv_bias,
    out_weight,
    gain_mlp,
    gate_weight,
    up_weight,
    down_weight,
    cotangent,
):
    row = lax.axis_index("row")
    column = lax.axis_index("col")
    row_count = lax.axis_size("row")
    bits = row_count.bit_length() - 1
    core = column % 2
    sequence = column // 2
    parity = core.astype(jnp.int32).reshape(1)
    tok_local, model_width = layer_input.shape
    length = tok_local * 2
    deep = model_width // row_count
    ff_cols = gate_weight.shape[1]
    qkv_cols = qkv_weight.shape[1]
    out_cols = out_weight.shape[0]
    group_width = 2 * qkv_cols
    query_width = group_width - 2 * HD

    qkv_gather = Gather(qkv_weight, bits)
    out_gather = Gather(out_weight.T, bits)

    def both(block):
        first, second = turned_pairs(block)
        return in_order(first, second, sequence, 1)

    down_flipped = down_weight.T
    mlp_gathers = []
    for start, stop in cuts(ff_cols):
        padded = -(-(stop - start) // 256) * 256
        pieces = [
            jnp.pad(part[:, start:stop], ((0, 0), (0, padded - (stop - start))))
            for part in (gate_weight, up_weight, down_flipped)
        ]
        mlp_gathers.append(Gather(jnp.concatenate(pieces, 1), bits))
    place = jnp.arange(model_width, dtype=jnp.int32)
    masks = jnp.array([bit_reversed(p, bits) for p in range(row_count)], jnp.int32)
    source = jnp.repeat(masks ^ row, deep) * deep + place % deep
    to_stored = (place[:, None] == source[None, :]).astype(bf16)
    from_stored = (source[:, None] == place[None, :]).astype(bf16)

    def stored(block):
        return jnp.dot(block, to_stored, preferred_element_type=f32)

    def unstored(block):
        return jnp.dot(block, from_stored, preferred_element_type=f32).astype(bf16)

    def unstored_row(vector):
        blocks = vector.reshape(row_count, deep)
        blocks = jnp.concatenate(
            [blocks[bit_reversed(m, bits)][None] for m in range(row_count)], 0
        )
        for bit in range(bits):
            wide = blocks.reshape(-1, 2, 1 << bit, deep)
            turned = jnp.concatenate([wide[:, 1:], wide[:, :1]], 1).reshape(row_count, deep)
            blocks = jnp.where((row >> bit) % 2 == 1, turned, blocks)
        return blocks.reshape(model_width)

    input_rows = stored(layer_input)
    grad_out = stored(cotangent)
    gain_one = stored(gain_attn[None, :])
    gain_two = stored(gain_mlp[None, :])

    scale_one = lax.rsqrt(jnp.mean(input_rows * input_rows, axis=1) + eps)
    normed_own = (input_rows * scale_one[:, None] * gain_one).astype(bf16)
    normed_other = flip(normed_own, "col", 0)
    cosine, sine_part = rope_tables(length)
    grad_blocks = [grad_out.astype(bf16)]

    near, far = mlp_gathers
    a_four = qkv_gather.double()
    n_four = near.double(a_four)
    a_two = qkv_gather.double_all()
    a_rows = jnp.concatenate(qkv_gather.pieces, 0)
    a_beside = qkv_gather.catch_up()
    bias_rows = jnp.pad(qkv_bias[None, :], ((0, 15), (0, 0)))
    a_first = both(jnp.concatenate([a_rows, bias_rows], 0))
    bias_full = a_first[-16:-15].astype(f32)
    across = flip(grad_blocks[0], "col", 1)
    a_last = both(after(a_beside, across))
    qkv_pieces = [a_first[:-16], a_last]
    o_four = out_gather.double(a_beside)
    n_own = near.send(a_beside)
    o_two = out_gather.double_all()
    o_beside = out_gather.catch_up(n_own)
    o_rows = jnp.concatenate([*out_gather.pieces, o_beside], 0)
    n_two = near.double(o_two)
    n_beside = near.send(n_own)
    far.ready(a_last, n_four, o_four)
    f_four = far.double()
    out_full = jnp.pad(both(after(o_rows, a_last)), ((0, 0), (0, HD)))
    out_pieces = [out_full]
    split = -(-(query_width + HD) // 256)
    qk_rows, value_rows, att_first, log_first = attend(
        parity, normed_own, normed_other, qkv_pieces, bias_full, cosine, sine_part, split
    )
    n_last = near.send(n_beside, att_first)
    att_last, log_last = attend_rest(parity, after(qk_rows, n_beside, n_two), value_rows, split)
    log_totals = log_first + log_last
    att_own, att_other = project(att_first, after(att_last, f_four), out_pieces)
    att_got = flip(att_other, "col", 0)
    grad_blocks.append(flip(after(grad_blocks[0], att_got), "col", 0))
    grad_blocks += [across, flip(after(across, att_got), "col", 0)]
    middle = input_rows + att_own + att_got.astype(f32)
    scale_two = lax.rsqrt(jnp.mean(middle * middle, axis=1) + eps)
    blocks = [(middle * scale_two[:, None] * gain_two).astype(bf16)]
    across = flip(blocks[0], "col", 1)
    blocks.append(flip(after(blocks[0], n_last), "col", 0))
    blocks += [across, flip(across, "col", 0)]

    f_beside = far.catch_up(n_last)
    f_two = far.double(blocks[0])
    f_last = far.send(f_beside)
    first_pieces, second_pieces = (gather.all() for gather in mlp_gathers)
    act_own, *sums_own = mlp(blocks[:2], grad_blocks[:2], first_pieces)
    act_far, *sums_far = mlp(blocks[2:], grad_blocks[2:], first_pieces)
    sent_one, kept_one, sent_two, kept_two = outer(blocks, grad_blocks, [act_own, act_far])
    first_scatter = Scatter([(sent_one, kept_one), (sent_two, kept_two)], bits)
    start_far = after(blocks[2], kept_one)
    act_far, near_far, far_far = mlp(
        [start_far, blocks[3]], grad_blocks[2:], second_pieces, sums_far
    )
    far_far = after(far_far, *first_scatter.got)
    across = near_far.astype(f32) + flip(far_far, "col", 0).astype(f32)
    across = across.astype(bf16)
    normed_back = flip(across[0], "col", 1)
    act_own, near_own, far_own = mlp(
        [after(blocks[0], across), blocks[1]],
        grad_blocks[:2],
        second_pieces,
        sums_own,
    )
    first_scatter.step()
    far_own = after(far_own, normed_back, *first_scatter.got)
    beside = [flip(far_own[0], "col", 0)]
    beside.append(flip(after(far_own[1], beside[0]), "col", 0))
    first_scatter.step()
    down_back = flip(after(across[1], normed_back), "col", 1)

    def summed(k, back):
        return near_own[k].astype(f32) + beside[k].astype(f32) + back.astype(f32)

    grad_normed_two = summed(0, normed_back)
    scaled_two = gain_two * grad_normed_two
    inner_two = jnp.sum(scaled_two * middle, axis=1)
    grad_middle = (
        grad_out
        + scale_two[:, None] * scaled_two
        - middle * (scale_two**3 * inner_two / model_width)[:, None]
    )
    gain_two_grad = jnp.sum(grad_normed_two * middle * scale_two[:, None], axis=0)
    branch_own = grad_middle.astype(bf16)
    branch_other = flip(branch_own, "col", 0)
    out_scatter = Scatter([outer_one([branch_own, branch_other], jnp.concatenate([att_first, att_last], 1))], bits)
    sent_one, kept_one, sent_two, kept_two = outer(
        [after(blocks[0], out_scatter.kept[0], *first_scatter.kept), *blocks[1:]],
        grad_blocks,
        [act_own, act_far],
    )
    second_scatter = Scatter([(sent_one, kept_one), (sent_two, kept_two)], bits)
    out_scatter.wait(kept_one)
    out_scatter.step()
    mixed_first, bias_first, *carry = attend_back(
        parity,
        after(branch_own, kept_one, out_scatter.kept[0]),
        branch_other,
        out_pieces,
        qk_rows,
        value_rows,
        log_totals,
        cosine,
        sine_part,
        0,
        split,
    )
    out_scatter.wait(mixed_first)
    mixed_last, bias_last = attend_back(
        parity,
        after(branch_own, mixed_first),
        branch_other,
        out_pieces,
        qk_rows,
        value_rows,
        log_totals,
        cosine,
        sine_part,
        split,
        qk_rows.shape[1] // 128,
        carry,
    )
    bias_grad = jnp.concatenate([bias_first, bias_last], 1)[0]
    first_scatter.wait(mixed_last)
    grad_mixed = jnp.concatenate([mixed_first, mixed_last], 1)
    qkv_scatter = Scatter([outer_one([normed_own, normed_other], grad_mixed)], bits)
    passed = qkv_scatter.kept[0]
    first_scatter.wait(passed)
    second_scatter.wait(passed)
    out_scatter.wait(passed)
    second_scatter.step()
    layer_output = unstored((middle + summed(1, after(down_back, passed))).astype(bf16))
    qkv_full = jnp.concatenate(qkv_pieces, 0)
    grad_mixed = after(grad_mixed, passed, *second_scatter.kept)
    out_scatter.step()
    partial = jnp.einsum("tc,dc->td", grad_mixed, qkv_full, preferred_element_type=f32)
    grad_normed_one = partial[:tok_local] + flip(
        partial[tok_local:].astype(bf16), "col", 0
    ).astype(f32)
    scaled_one = gain_one * grad_normed_one
    inner_one = jnp.sum(scaled_one * input_rows, axis=1)
    input_grad = unstored(
        (
            grad_middle
            + scale_one[:, None] * scaled_one
            - input_rows * (scale_one**3 * inner_one / model_width)[:, None]
        ).astype(bf16)
    )
    gain_one_grad = jnp.sum(grad_normed_one * input_rows * scale_one[:, None], axis=0)

    def to_columns(total, width):
        low, high = total[:, :width].astype(bf16), total[:, width : 2 * width].astype(bf16)
        first, second = from_pairs(
            jnp.where(sequence == 0, low, high), jnp.where(sequence == 0, high, low)
        )
        return first.astype(f32) + second.astype(f32)

    bias_row = lax.dynamic_update_slice_in_dim(
        jnp.zeros((group_width * 2,), f32), bias_grad, core * group_width, 0
    )
    small = jnp.concatenate([unstored_row(gain_one_grad), unstored_row(gain_two_grad), bias_row])
    small = jnp.pad(small, (0, -small.shape[0] % 128)).reshape(-1, 128)
    small = after(small, *second_scatter.got)
    second_scatter.step()
    for bit in range(2):
        small = small + flip(small, "col", bit)
    for bit in range(bits):
        small = small + flip(small, "row", bit)
    qkv_scatter.step()
    qkv_scatter.step()
    qkv_scatter.wait(small)
    qkv_total = to_columns(qkv_scatter.total(), qkv_cols)
    out_total = to_columns(out_scatter.total(), out_cols)
    mlp_totals = []
    for scatter, (start, stop) in zip((first_scatter, second_scatter), cuts(ff_cols)):
        total = scatter.total()
        padded = total.shape[1] // 3
        mlp_totals.append(
            [total[:, k * padded : k * padded + stop - start] for k in range(3)]
        )
    gate_total, up_total, down_total = (jnp.concatenate(parts, 1) for parts in zip(*mlp_totals))
    small = small.reshape(-1)
    gain_one_total = small[:model_width]
    gain_two_total = small[model_width : 2 * model_width]
    bias_total = lax.dynamic_slice_in_dim(small, 2 * model_width + column * qkv_cols, qkv_cols, 0)
    return (
        layer_output,
        input_grad,
        gain_one_total,
        qkv_total,
        bias_total,
        out_total.T,
        gain_two_total,
        gate_total,
        up_total,
        down_total.T,
    )


def solution(mesh):
    in_specs = (
        P(("row", "col"), None),
        P(),
        P("row", "col"),
        P("col"),
        P("col", "row"),
        P(),
        P("row", "col"),
        P("row", "col"),
        P("col", "row"),
        P(("row", "col"), None),
    )
    out_specs = (
        P(("row", "col"), None),
        P(("row", "col"), None),
        P(),
        P("row", "col"),
        P("col"),
        P("col", "row"),
        P(),
        P("row", "col"),
        P("row", "col"),
        P("col", "row"),
    )
    return jax.shard_map(shards, mesh=mesh, in_specs=in_specs, out_specs=out_specs, check_vma=False)
```

```python
import functools
import math

import jax
import jax.numpy as jnp
from jax import lax
from jax.experimental import pallas as pl
from jax.experimental.pallas import tpu as pltpu
from jax.sharding import PartitionSpec as P

HD = 64
eps = 1e-06
theta_base = 1000000.0
bf16 = jnp.bfloat16
f32 = jnp.float32
NT = (((1,), (1,)), ((), ()))
TN = (((0,), (0,)), ((), ()))
MIB = 1024 * 1024


def flip(block, axis, bit):
    count = lax.axis_size(axis)
    return lax.ppermute(block, axis, [(i, i ^ 1 << bit) for i in range(count)])


def bit_reversed(value, bits):
    return sum((value >> b & 1) << (bits - 1 - b) for b in range(bits))


def after(value, *earlier):
    return lax.optimization_barrier((value, *earlier))[0]


def kernel_params(mib):
    return pltpu.CompilerParams(vmem_limit_bytes=mib * MIB)


def cost(flops, nbytes, exps=0):
    return pl.CostEstimate(
        flops=int(flops), bytes_accessed=int(nbytes), transcendentals=int(exps)
    )


def whole(array):
    return pl.BlockSpec(array.shape, lambda *_: (0,) * len(array.shape))


def in_place(block):
    return pl.BlockSpec(memory_space=pl.ANY)


def assemble(pieces, held, sems):
    copies = []
    at = 0
    for i, piece in enumerate(pieces):
        rows = piece.shape[0]
        copies.append(pltpu.make_async_copy(piece, held.at[pl.ds(at, rows)], sems.at[i]))
        at += rows
    for copy in copies:
        copy.start()
    for copy in copies:
        copy.wait()


def halves_turned(block):
    lane = lax.broadcasted_iota(jnp.int32, block.shape, 1)
    up = pltpu.roll(block, 128 - HD // 2, 1)
    return jnp.where(lane % HD < HD // 2, up, pltpu.roll(block, HD // 2, 1))


def side_rows(r, block, half, parity):
    side = (r // half) ^ parity
    return pl.ds(pl.multiple_of(side * half + r % half, block), block)


def pad_heads(key_value, rows, value, last):
    lane = lax.broadcasted_iota(jnp.int32, (1, 128), 1)
    kpad, vpad = key_value
    zero = jnp.zeros_like(value)
    vpad[0, rows, :] = jnp.concatenate([value, zero], 1).astype(bf16)
    vpad[1, rows, :] = jnp.concatenate([zero, value], 1).astype(bf16)
    kpad[1, rows, :] = jnp.where(lane >= HD, last, 0.0).astype(bf16)
    kpad[0, rows, :] = jnp.where(lane < HD, pltpu.roll(last, HD, 1), 0.0).astype(bf16)


def attend_kernel(parity_ref, own_ref, other_ref, bias_ref, cos_ref, sin_ref, *rest, block, count):
    pieces = rest[:count]
    qk_ref, v_ref, att_ref, lse_ref, held, kpad, vpad, lse_cols, sems = rest[count:]
    step = pl.program_id(0)
    half = own_ref.shape[0]
    length = 2 * half
    wide = qk_ref.shape[1]
    pairs = wide // 128
    parity = parity_ref[0]

    @pl.when(step == 0)
    def _():
        assemble(pieces, held, sems)
        for side, rows_ref in enumerate((own_ref, other_ref)):
            for r in range(0, half, block):
                at = pl.multiple_of((side ^ parity) * half + r, block)
                rows = pl.ds(at, block)
                mixed = jnp.dot(rows_ref[r : r + block, :], held[...], preferred_element_type=f32)
                mixed = (mixed + bias_ref[...]).astype(bf16).astype(f32)
                cos, sin = cos_ref[rows, :], sin_ref[rows, :]
                for p in range(pairs):
                    u = mixed[:, p * 128 : (p + 1) * 128]
                    turned = (u * cos + halves_turned(u) * sin).astype(bf16)
                    qk_ref[rows, p * 128 : (p + 1) * 128] = turned
                v_ref[rows, :] = mixed[:, wide:].astype(bf16)
                pad_heads((kpad, vpad), rows, mixed[:, wide:], turned.astype(f32))
        lse_cols[...] = jnp.zeros_like(lse_cols)

    factor = HD**-0.5 * math.log2(math.e)
    cols = pl.ds(pl.multiple_of(step * 128, 128), 128)
    row_i = lax.broadcasted_iota(jnp.int32, (block, block), 0)
    col_i = lax.broadcasted_iota(jnp.int32, (block, block), 1)
    for r in range(0, length, block):
        rows = pl.ds(r, block)
        to = side_rows(r, block, half, parity)
        q = qk_ref[rows, cols]

        def head(odd):
            keys = kpad[odd, : r + block, :]
            scores = lax.dot_general(q, keys, NT, preferred_element_type=f32)
            diag = jnp.where(col_i <= row_i, scores[:, r:], -1e30)
            scores = jnp.concatenate([scores[:, :r], diag], 1) if r else diag
            top = jnp.max(scores, 1, keepdims=True)
            e = jnp.exp2((scores - top) * factor)
            total = jnp.sum(e, 1, keepdims=True)
            out = jnp.dot(e.astype(bf16), vpad[odd, : r + block, :], preferred_element_type=f32)
            lse = top * factor + jnp.log2(total)
            at = lax.broadcasted_iota(jnp.int32, (1, 128), 1) == 2 * step + odd
            lse_cols[rows, :] = jnp.where(at, lse, lse_cols[rows, :])
            return out / total

        even = head(0)

        @pl.when(step < pairs - 1)
        def _():
            att_ref[to, :] = (even + head(1)).astype(bf16)

        @pl.when(step == pairs - 1)
        def _():
            att_ref[to, :] = even.astype(bf16)

    @pl.when(step == pairs - 1)
    def _():
        lse_ref[...] = lse_cols[...].T[: lse_ref.shape[0], :]


def attend(parity, own, other, pieces, bias, cos, sin):
    half, depth = own.shape
    length = 2 * half
    group = bias.shape[1]
    wide = group - HD
    pairs = wide // 128
    block = min(256, half)
    return pl.pallas_call(
        functools.partial(attend_kernel, block=block, count=len(pieces)),
        grid=(pairs,),
        in_specs=[pl.BlockSpec(memory_space=pltpu.SMEM)]
        + [whole(a) for a in (own, other, bias, cos, sin)]
        + [in_place(piece) for piece in pieces],
        out_specs=[
            pl.BlockSpec((length, wide), lambda p: (0, 0)),
            pl.BlockSpec((length, HD), lambda p: (0, 0)),
            pl.BlockSpec((length, 128), lambda p: (0, p)),
            pl.BlockSpec((8, length), lambda p: (0, 0)),
        ],
        out_shape=[
            jax.ShapeDtypeStruct((length, wide), bf16),
            jax.ShapeDtypeStruct((length, HD), bf16),
            jax.ShapeDtypeStruct((length, wide), bf16),
            jax.ShapeDtypeStruct((8, length), f32),
        ],
        scratch_shapes=[
            pltpu.VMEM((depth, group), bf16),
            pltpu.VMEM((2, length, 128), bf16),
            pltpu.VMEM((2, length, 128), bf16),
            pltpu.VMEM((length, 128), f32),
            pltpu.SemaphoreType.DMA((len(pieces),)),
        ],
        compiler_params=kernel_params(40),
        cost_estimate=cost(12e9, 8e6, 5e6),
    )(parity, own, other, bias, cos, sin, *pieces)


def project_kernel(att_ref, *rest, count):
    pieces = rest[:count]
    own_ref, other_ref, held, sems = rest[count:]
    half = own_ref.shape[0]
    assemble(pieces, held, sems)
    for side, ref in enumerate((own_ref, other_ref)):
        rows = att_ref[side * half : (side + 1) * half, :]
        ref[...] = lax.dot_general(rows, held[...], NT, preferred_element_type=f32).astype(ref.dtype)


def project(att, pieces):
    length, wide = att.shape
    depth = sum(piece.shape[0] for piece in pieces)
    return pl.pallas_call(
        functools.partial(project_kernel, count=len(pieces)),
        in_specs=[pl.BlockSpec(memory_space=pltpu.VMEM)] + [in_place(piece) for piece in pieces],
        out_specs=[pl.BlockSpec(memory_space=pltpu.VMEM)] * 2,
        out_shape=[
            jax.ShapeDtypeStruct((length // 2, depth), f32),
            jax.ShapeDtypeStruct((length // 2, depth), bf16),
        ],
        scratch_shapes=[
            pltpu.VMEM((depth, wide), bf16),
            pltpu.SemaphoreType.DMA((len(pieces),)),
        ],
        compiler_params=kernel_params(40),
        cost_estimate=cost(2 * length * depth * wide, 6e6),
    )(att, *pieces)


def attend_back_kernel(
    parity_ref,
    own_ref,
    other_ref,
    qk_ref,
    v_ref,
    lse_ref,
    cos_ref,
    sin_ref,
    *rest,
    block,
    count,
    first,
    last,
):
    pieces = rest[:count]
    if first == 0:
        mixed_ref, bias_ref, dk, dv, held, kpad, vpad, gatt, dq_acc, sems = rest[count:]
    else:
        dk_in, dv_in, mixed_ref, bias_ref, held, kpad, vpad, gatt, dq_acc, dk, dv, sems = rest[count:]
    step = pl.program_id(0) + first
    half_rows = own_ref.shape[0]
    length = 2 * half_rows
    wide = qk_ref.shape[1]
    pairs = wide // 128
    used = slice(first * 128, last * 128)
    parity = parity_ref[0]
    lane = lax.broadcasted_iota(jnp.int32, (1, 128), 1)

    @pl.when(step == first)
    def _():
        assemble(pieces, held, sems)
        for side, rows_ref in enumerate((own_ref, other_ref)):
            for r in range(0, half_rows, block):
                rows = pl.ds(pl.multiple_of((side ^ parity) * half_rows + r, block), block)
                got = jnp.dot(
                    rows_ref[r : r + block, :], held[:, used], preferred_element_type=f32
                )
                gatt[rows, :] = got.astype(bf16)
        for r in range(0, length, block):
            rows = pl.ds(r, block)
            keys = qk_ref[rows, wide - 128 :].astype(f32)
            pad_heads((kpad, vpad), rows, v_ref[rows, :].astype(f32), keys)
        dk[...] = dk_in[...] if first else jnp.zeros_like(dk)
        dv[...] = dv_in[...] if first else jnp.zeros_like(dv)

    factor = HD**-0.5 * math.log2(math.e)
    cols = pl.ds(pl.multiple_of(step * 128, 128), 128)
    here = pl.ds(pl.multiple_of((step - first) * 128, 128), 128)
    key_i = lax.broadcasted_iota(jnp.int32, (block, block), 0)
    query_i = lax.broadcasted_iota(jnp.int32, (block, block), 1)
    for r in range(0, length, block):
        rows = pl.ds(r, block)
        q = qk_ref[rows, cols]
        g = gatt[rows, here]

        def head(odd):
            lse = lse_ref[pl.ds(2 * step + odd, 1), rows]
            probs, grads = [], []
            inner = jnp.zeros((1, block), f32)
            for c in range(0, r + block, block):
                scores = lax.dot_general(
                    kpad[odd, c : c + block, :], q, NT, preferred_element_type=f32
                )
                p = jnp.exp2(scores * factor - lse)
                if c == r:
                    p = jnp.where(key_i <= query_i, p, 0.0)
                dp = lax.dot_general(vpad[odd, c : c + block, :], g, NT, preferred_element_type=f32)
                inner = inner + jnp.sum(p * dp, 0, keepdims=True)
                probs.append(p)
                grads.append(dp)
            dq = 0.0
            half = lane >= HD if odd else lane < HD
            for i, c in enumerate(range(0, r + block, block)):
                keys = pl.ds(c, block)
                ds = (probs[i] * (grads[i] - inner)).astype(bf16)
                p = probs[i].astype(bf16)
                dk[keys, :] += jnp.where(half, jnp.dot(ds, q, preferred_element_type=f32), 0.0)
                dv[keys, :] += jnp.where(half, jnp.dot(p, g, preferred_element_type=f32), 0.0)
                dq = dq + lax.dot_general(
                    ds, kpad[odd, c : c + block, :], TN, preferred_element_type=f32
                )
            return dq

        dq_acc[rows, :] = head(0)

        @pl.when(step < pairs - 1)
        def _():
            dq_acc[rows, :] += head(1)

    def back(u, rows):
        return u * cos_ref[rows, :] - halves_turned(u) * sin_ref[rows, :]

    scale = HD**-0.5
    for r in range(0, length, block):
        rows = pl.ds(r, block)
        to = side_rows(r, block, half_rows, parity)

        @pl.when(step < pairs - 1)
        def _():
            mixed_ref[to, here] = back(dq_acc[rows, :] * scale, rows).astype(bf16)

        if last == pairs:
            end = (last - first) * 128

            @pl.when(step == pairs - 1)
            def _():
                k = dk[rows, :]
                k = jnp.where(lane >= HD, k + pltpu.roll(k, HD, 1), dq_acc[rows, :]) * scale
                mixed_ref[to, end - 128 : end] = back(k, rows).astype(bf16)
                v = dv[rows, :]
                v = v + pltpu.roll(v, HD, 1)
                mixed_ref[to, end:] = v[:, :HD].astype(bf16)

    @pl.when(step == last - 1)
    def _():
        total = jnp.zeros((1, mixed_ref.shape[1]), f32)
        for r in range(0, length, block):
            part = mixed_ref[pl.ds(r, block), :].astype(f32)
            total = total + jnp.sum(part, 0, keepdims=True)
        bias_ref[...] = total


def attend_back(parity, own, other, pieces, qk, v, lse, cos, sin, first, last, earlier=()):
    half, depth = own.shape
    length = 2 * half
    wide = qk.shape[1]
    pairs = wide // 128
    group = (last - first) * 128 + (HD if last == pairs else 0)
    block = min(256, half)
    ins = (own, other, qk, v, lse, cos, sin)
    carried = pl.BlockSpec((length, 128), lambda p: (0, 0))
    carry = [jax.ShapeDtypeStruct((length, 128), f32)] * 2
    return pl.pallas_call(
        functools.partial(
            attend_back_kernel, block=block, count=len(pieces), first=first, last=last
        ),
        grid=(last - first,),
        in_specs=[pl.BlockSpec(memory_space=pltpu.SMEM)]
        + [whole(a) for a in ins]
        + [in_place(piece) for piece in pieces]
        + [carried] * len(earlier),
        out_specs=[
            pl.BlockSpec((length, group), lambda p: (0, 0)),
            pl.BlockSpec((1, group), lambda p: (0, 0)),
        ]
        + ([] if first else [carried] * 2),
        out_shape=[
            jax.ShapeDtypeStruct((length, group), bf16),
            jax.ShapeDtypeStruct((1, group), f32),
        ]
        + ([] if first else carry),
        scratch_shapes=[
            pltpu.VMEM((depth, wide), bf16),
            pltpu.VMEM((2, length, 128), bf16),
            pltpu.VMEM((2, length, 128), bf16),
            pltpu.VMEM((length, (last - first) * 128), bf16),
            pltpu.VMEM((length, 128), f32),
        ]
        + ([pltpu.VMEM((length, 128), f32)] * 2 if first else [])
        + [pltpu.SemaphoreType.DMA((len(pieces),))],
        compiler_params=kernel_params(50),
        cost_estimate=cost(12e9, 6e6, 3e6),
    )(parity, *ins, *pieces, *earlier)


def mlp_kernel(x0_ref, x1_ref, g0_ref, g1_ref, *rest, count, add):
    pieces = rest[:count]
    rest = rest[count:]
    if add:
        near_in, far_in, act_ref, near_ref, far_ref, held, sems = rest
    else:
        act_ref, near_ref, far_ref, held, sems = rest
    n = held.shape[1] // 3
    step = pl.program_id(0)

    @pl.when(step == 0)
    def _():
        assemble(pieces, held, sems)

    wg, wu, wd = (held[:, k * n : (k + 1) * n] for k in range(3))
    x = jnp.where(step == 0, x0_ref[...], x1_ref[...])
    g = jnp.where(step == 0, g0_ref[...], g1_ref[...])
    gate = jnp.dot(x, wg, preferred_element_type=f32)
    up = jnp.dot(x, wu, preferred_element_type=f32)
    gh = jnp.dot(g, wd, preferred_element_type=f32)
    sig = 1.0 / (1.0 + jnp.exp(-gate))
    silu = gate * sig
    hid = (silu * up).astype(bf16)
    ghs = gh * sig
    gg = (ghs * up * (1.0 + gate - silu)).astype(bf16)
    gu = (ghs * gate).astype(bf16)
    act_ref[:, :n] = gg
    act_ref[:, n : 2 * n] = gu
    act_ref[:, 2 * n :] = hid
    ngrad = lax.dot_general(gg, wg, NT, preferred_element_type=f32)
    ngrad = ngrad + lax.dot_general(gu, wu, NT, preferred_element_type=f32)
    down = lax.dot_general(hid, wd, NT, preferred_element_type=f32)

    @pl.when(step == 0)
    def _():
        near_ref[0] = (ngrad + near_in[0].astype(f32) if add else ngrad).astype(bf16)
        near_ref[1] = (down + near_in[1].astype(f32) if add else down).astype(bf16)

    @pl.when(step == 1)
    def _():
        far_ref[0] = (ngrad + far_in[0].astype(f32) if add else ngrad).astype(bf16)
        far_ref[1] = (down + far_in[1].astype(f32) if add else down).astype(bf16)


def mlp(rows, grads, pieces, sums=None):
    t, d = rows[0].shape
    columns = pieces[0].shape[1]
    add = sums is not None
    ins = (*rows, *grads)
    sums = tuple(sums or ())
    both = pl.BlockSpec((2, t, d), lambda i: (0, 0, 0))
    return pl.pallas_call(
        functools.partial(mlp_kernel, count=len(pieces), add=add),
        grid=(2,),
        in_specs=[whole(a) for a in ins] + [in_place(p) for p in pieces] + [both] * len(sums),
        out_specs=[pl.BlockSpec((t, columns), lambda i: (i, 0)), both, both],
        out_shape=[
            jax.ShapeDtypeStruct((2 * t, columns), bf16),
            jax.ShapeDtypeStruct((2, t, d), bf16),
            jax.ShapeDtypeStruct((2, t, d), bf16),
        ],
        scratch_shapes=[
            pltpu.VMEM((d, columns), bf16),
            pltpu.SemaphoreType.DMA((len(pieces),)),
        ],
        compiler_params=kernel_params(58),
        cost_estimate=cost(8 * t * d * columns, 30 * MIB, 2 * t * columns),
    )(*ins, *pieces, *sums)


def fill(sent_ref, kept_ref, lefts, rights, second, columns=None, start_at=0):
    half = kept_ref.shape[0]
    t = lefts[0].shape[0]
    q = half // 2
    low, high = columns or (0, rights[0].shape[1])
    if second:
        parts = ((sent_ref, 0, q), (sent_ref, q, 3 * q), (kept_ref, 0, 0), (kept_ref, q, 2 * q))
        size = q
    else:
        parts = ((sent_ref, 0, half), (kept_ref, 0, 0))
        size = half
    for ref, to, start in parts:
        total = 0.0
        for i, left in enumerate(lefts):
            right = rights[i * t // rights[0].shape[0]]
            at = i * t % right.shape[0]
            total = total + lax.dot_general(
                left[:, start : start + size],
                right[at : at + t, low:high],
                TN,
                preferred_element_type=f32,
            )
        ref[to : to + size, start_at : start_at + high - low] = total.astype(ref.dtype)


def outer_kernel(*refs, blocks):
    rows, grads, rights = refs[:blocks], refs[blocks : 2 * blocks], refs[2 * blocks : -4]
    sent_one, kept_one, sent_two, kept_two = refs[-4:]
    n = rights[0].shape[1]
    step = pl.program_id(0)

    @pl.when(step == 0)
    def _():
        fill(sent_one, kept_one, rows, rights, False)

    @pl.when(step == 1)
    def _():
        fill(sent_one, kept_one, rows, rights, False, (0, n // 2), n)
        fill(sent_two, kept_two, rows, rights, True, (n // 2, n), 0)

    @pl.when(step == 2)
    def _():
        fill(sent_two, kept_two, grads, rights, True, (0, n), n // 2)


def outer(rows, grads, acts):
    t, d = rows[0].shape
    tall, columns = acts[0].shape
    n = columns // 3
    flat = [*rows, *grads]
    out = pl.BlockSpec((d // 2, columns // 2), lambda k: (0, 0))
    return pl.pallas_call(
        functools.partial(outer_kernel, blocks=len(rows)),
        grid=(3,),
        in_specs=[whole(left) for left in flat]
        + [pl.BlockSpec((tall, n), lambda k: (0, k)) for _ in acts],
        out_specs=[out] * 4,
        out_shape=[
            jax.ShapeDtypeStruct((d // 2, columns // 2), bf16),
            jax.ShapeDtypeStruct((d // 2, columns // 2), f32),
            jax.ShapeDtypeStruct((d // 2, columns // 2), bf16),
            jax.ShapeDtypeStruct((d // 2, columns // 2), f32),
        ],
        compiler_params=kernel_params(58),
        cost_estimate=cost(2 * t * len(rows) * d * columns, 20 * MIB),
    )(*flat, *acts)


def outer_one_kernel(*refs):
    fill(refs[-2], refs[-1], refs[:-3], refs[-3:-2], False)


def outer_one(lefts, right):
    t, d = lefts[0].shape
    columns = right.shape[1]
    vmem = pl.BlockSpec(memory_space=pltpu.VMEM)
    return pl.pallas_call(
        outer_one_kernel,
        in_specs=[vmem] * (len(lefts) + 1),
        out_specs=[vmem] * 2,
        out_shape=[
            jax.ShapeDtypeStruct((d // 2, columns), bf16),
            jax.ShapeDtypeStruct((d // 2, columns), f32),
        ],
        compiler_params=kernel_params(40),
        cost_estimate=cost(2 * t * len(lefts) * d * columns, 6 * MIB),
    )(*lefts, right)


def rope_tables(length):
    inverse = theta_base ** (-(jnp.arange(HD // 2, dtype=f32) * 2.0 / HD))
    angles = jnp.arange(length, dtype=f32)[:, None] * inverse[None, :]
    c, s = jnp.cos(angles), jnp.sin(angles)
    return jnp.concatenate([c] * 4, 1), jnp.concatenate([-s, s, -s, s], 1)


class Gather:
    def __init__(self, block, bits):
        self.bits = bits
        self.left = bits - 1
        self.pieces = [block]
        self.sent = 0
        self.beside = []

    def ready(self, *earlier):
        self.pieces[-1] = after(self.pieces[-1], *earlier)

    def double(self, *earlier):
        held = jnp.concatenate(self.pieces, 0) if len(self.pieces) > 1 else self.pieces[0]
        self.pieces.append(flip(after(held, *earlier) if earlier else held, "row", self.left))
        self.left -= 1
        return self.pieces[-1]

    def send(self, *earlier):
        piece = self.pieces[self.sent]
        self.sent += 1
        self.beside.append(flip(after(piece, *earlier) if earlier else piece, "row", 0))
        return self.beside[-1]

    def catch_up(self, *earlier):
        rest = jnp.concatenate(self.pieces[self.sent :], 0)
        self.sent = len(self.pieces)
        self.beside.append(flip(after(rest, *earlier), "row", 0))
        return self.beside[-1]

    def finish(self, *earlier):
        while self.left > 0:
            self.double()
        self.catch_up(*earlier)
        out = self.pieces + self.beside
        return out if out[0].shape[0] % 16 == 0 else [jnp.concatenate(out, 0)]

    def all(self):
        while self.left > 0:
            self.double()
        while self.sent < len(self.pieces):
            self.send()
        out = self.pieces + self.beside
        return out if out[0].shape[0] % 16 == 0 else [jnp.concatenate(out, 0)]


class Scatter:
    def __init__(self, parts, bits):
        self.bits = bits
        self.orders = [[0, 1], [1, 0]][: len(parts)]
        self.kept = [kept for _, kept in parts]
        self.done = 0
        self.start([sent for sent, _ in parts])

    def start(self, sents):
        bits = [order[self.done] if self.done < 2 else self.done for order in self.orders]
        self.got = [flip(sent, "row", bit) for sent, bit in zip(sents, bits)]

    def wait(self, *earlier):
        self.got = [after(got, *earlier) for got in self.got]

    def step(self):
        if self.done == self.bits - 1:
            return
        self.done += 1
        half = self.kept[0].shape[0] // 2
        sents = [
            (kept[half:] + got[half:].astype(f32)).astype(bf16)
            for kept, got in zip(self.kept, self.got)
        ]
        self.kept = [kept[:half] + got[:half].astype(f32) for kept, got in zip(self.kept, self.got)]
        if self.done == 2:
            sents = [jnp.concatenate(sents, 1)]
            self.kept = [jnp.concatenate(self.kept, 1)]
        self.start(sents)

    def total(self):
        while self.done < self.bits - 1:
            self.step()
        totals = [kept + got.astype(f32) for kept, got in zip(self.kept, self.got)]
        return jnp.concatenate(totals, 1)


def turned_pairs(block):
    first = [(2 * a + b, 2 * b + a) for a in range(2) for b in range(2)]
    second = [(2 * a + b, 2 * (1 - b) + a) for a in range(2) for b in range(2)]
    return lax.ppermute(block, "col", first), lax.ppermute(block, "col", second)


def from_pairs(same, other):
    first = [(2 * a + b, 2 * b + a) for a in range(2) for b in range(2)]
    second = [(2 * a + b, 2 * b + 1 - a) for a in range(2) for b in range(2)]
    return lax.ppermute(same, "col", first), lax.ppermute(other, "col", second)


def cuts(width):
    first = min(512, width)
    return [(0, first), (first, width)] if first < width else [(0, width)]


def shards(
    layer_input,
    gain_attn,
    qkv_weight,
    qkv_bias,
    out_weight,
    gain_mlp,
    gate_weight,
    up_weight,
    down_weight,
    cotangent,
):
    row = lax.axis_index("row")
    column = lax.axis_index("col")
    row_count = lax.axis_size("row")
    bits = row_count.bit_length() - 1
    core = column % 2
    sequence = column // 2
    parity = core.astype(jnp.int32).reshape(1)
    tok_local, model_width = layer_input.shape
    length = tok_local * 2
    deep = model_width // row_count
    ff_cols = gate_weight.shape[1]
    qkv_cols = qkv_weight.shape[1]
    out_cols = out_weight.shape[0]
    group_width = 2 * qkv_cols
    query_width = group_width - 2 * HD

    bias_rows = jnp.pad(qkv_bias[None, :], ((0, 15), (0, 0)))
    first, second = turned_pairs(
        jnp.concatenate(
            [
                jnp.concatenate([qkv_weight, bias_rows], 0),
                jnp.pad(out_weight.T, ((0, 16), (0, 0))),
            ],
            1,
        )
    )
    low = jnp.where(sequence == 0, first, second)
    high = jnp.where(sequence == 0, second, first)
    qkv_own = jnp.concatenate([low[:, :qkv_cols], high[:, :qkv_cols]], 1)
    bias_full = qkv_own[deep : deep + 1].astype(f32)
    out_own = jnp.concatenate([low[:deep, qkv_cols:], high[:deep, qkv_cols:]], 1)
    out_own = jnp.pad(out_own, ((0, 0), (0, HD)))
    qkv_gather = Gather(qkv_own[:deep], bits)
    out_gather = Gather(out_own, bits)
    down_flipped = down_weight.T
    mlp_gathers = []
    for start, stop in cuts(ff_cols):
        padded = -(-(stop - start) // 256) * 256
        pieces = [
            jnp.pad(part[:, start:stop], ((0, 0), (0, padded - (stop - start))))
            for part in (gate_weight, up_weight, down_flipped)
        ]
        mlp_gathers.append(Gather(jnp.concatenate(pieces, 1), bits))
    place = jnp.arange(model_width, dtype=jnp.int32)
    masks = jnp.array([bit_reversed(p, bits) for p in range(row_count)], jnp.int32)
    source = jnp.repeat(masks ^ row, deep) * deep + place % deep
    to_stored = (place[:, None] == source[None, :]).astype(bf16)
    from_stored = (source[:, None] == place[None, :]).astype(bf16)

    def stored(block):
        return jnp.dot(block, to_stored, preferred_element_type=f32)

    def unstored(block):
        return jnp.dot(block, from_stored, preferred_element_type=f32).astype(bf16)

    def unstored_row(vector):
        blocks = vector.reshape(row_count, deep)
        blocks = jnp.concatenate(
            [blocks[bit_reversed(m, bits)][None] for m in range(row_count)], 0
        )
        for bit in range(bits):
            wide = blocks.reshape(-1, 2, 1 << bit, deep)
            turned = jnp.concatenate([wide[:, 1:], wide[:, :1]], 1).reshape(row_count, deep)
            blocks = jnp.where((row >> bit) % 2 == 1, turned, blocks)
        return blocks.reshape(model_width)

    input_rows = stored(after(layer_input, first, second))
    gain_one = stored(gain_attn[None, :])
    gain_two = stored(gain_mlp[None, :])

    scale_one = lax.rsqrt(jnp.mean(input_rows * input_rows, axis=1) + eps)
    normed_own = (input_rows * scale_one[:, None] * gain_one).astype(bf16)
    normed_other = flip(normed_own, "col", 0)
    cosine, sine_part = rope_tables(length)

    near, far = mlp_gathers
    a_own = qkv_gather.send()
    a_four = qkv_gather.double()
    near.ready(a_four)
    n_four = near.double()
    n_own = near.send()
    a_two = qkv_gather.double(a_own)
    a_beside = qkv_gather.send(a_own)
    o_four = out_gather.double(a_four)
    a_last = qkv_gather.send(a_beside)
    qkv_pieces = qkv_gather.all()
    far.ready(a_two, o_four)
    f_four = far.double()
    o_two = out_gather.double(a_two)
    grad_out = stored(after(cotangent, a_four))
    grad_blocks = [grad_out.astype(bf16)]
    across = flip(grad_blocks[0], "col", 1)
    out_pieces = out_gather.finish(a_last, o_two)
    n_two = near.double(o_two, a_last)
    n_beside = near.send(a_last)
    qk_rows, value_rows, att_rows, log_totals = attend(
        parity,
        normed_own,
        normed_other,
        qkv_pieces,
        bias_full,
        cosine,
        sine_part,
    )
    n_last = near.send(att_rows)
    att_own, att_other = project(after(att_rows, n_beside, n_two, across, f_four), out_pieces)
    att_got = flip(att_other, "col", 0)
    grad_blocks.append(flip(after(grad_blocks[0], att_got), "col", 0))
    grad_blocks += [across, flip(after(across, att_got), "col", 0)]
    middle = input_rows + att_own + att_got.astype(f32)
    scale_two = lax.rsqrt(jnp.mean(middle * middle, axis=1) + eps)
    blocks = [(middle * scale_two[:, None] * gain_two).astype(bf16)]
    across = flip(blocks[0], "col", 1)
    blocks.append(flip(after(blocks[0], n_last), "col", 0))
    blocks += [across, flip(across, "col", 0)]

    f_beside = far.catch_up(n_last)
    f_two = far.double(blocks[2])
    f_last = far.send(f_beside)
    first_pieces, second_pieces = (gather.all() for gather in mlp_gathers)
    act_own, *sums_own = mlp([after(blocks[0], blocks[2]), blocks[1]], grad_blocks[:2], first_pieces)
    act_far, *sums_far = mlp(blocks[2:], grad_blocks[2:], first_pieces)
    sent_one, kept_one, sent_two, kept_two = outer(blocks, grad_blocks, [act_own, act_far])
    first_scatter = Scatter([(sent_one, kept_one), (sent_two, kept_two)], bits)
    start_far = after(blocks[2], kept_one)
    act_far, near_far, far_far = mlp(
        [start_far, blocks[3]], grad_blocks[2:], second_pieces, sums_far
    )
    far_far = after(far_far, *first_scatter.got)
    across = near_far.astype(f32) + flip(far_far, "col", 0).astype(f32)
    across = across.astype(bf16)
    normed_back = flip(across[0], "col", 1)
    act_own, near_own, far_own = mlp(
        [after(blocks[0], across), blocks[1]],
        grad_blocks[:2],
        second_pieces,
        sums_own,
    )
    first_scatter.step()
    beside = flip(after(far_own, normed_back, *first_scatter.got), "col", 0)
    first_scatter.step()
    down_back = flip(after(across[1], normed_back), "col", 1)

    def summed(k, back):
        return near_own[k].astype(f32) + beside[k].astype(f32) + back.astype(f32)

    grad_normed_two = summed(0, normed_back)
    scaled_two = gain_two * grad_normed_two
    inner_two = jnp.sum(scaled_two * middle, axis=1)
    grad_middle = (
        grad_out
        + scale_two[:, None] * scaled_two
        - middle * (scale_two**3 * inner_two / model_width)[:, None]
    )
    gain_two_grad = jnp.sum(grad_normed_two * middle * scale_two[:, None], axis=0)
    branch_own = grad_middle.astype(bf16)
    branch_other = flip(branch_own, "col", 0)
    out_scatter = Scatter([outer_one([branch_own, branch_other], att_rows)], bits)
    sent_one, kept_one, sent_two, kept_two = outer(
        [after(blocks[0], out_scatter.kept[0], *first_scatter.kept), *blocks[1:]],
        grad_blocks,
        [act_own, act_far],
    )
    second_scatter = Scatter([(sent_one, kept_one), (sent_two, kept_two)], bits)
    out_scatter.wait(kept_one)
    out_scatter.step()
    layer_output = unstored((middle + summed(1, down_back)).astype(bf16))
    split = qk_rows.shape[1] // 256
    mixed_first, bias_first, *carry = attend_back(
        parity,
        after(branch_own, kept_one, out_scatter.kept[0], layer_output),
        branch_other,
        out_pieces,
        qk_rows,
        value_rows,
        log_totals,
        cosine,
        sine_part,
        0,
        split,
    )
    second_scatter.wait(mixed_first)
    out_scatter.wait(mixed_first)
    second_scatter.step()
    out_scatter.step()
    mixed_last, bias_last = attend_back(
        parity,
        after(branch_own, *second_scatter.kept, out_scatter.kept[0]),
        branch_other,
        out_pieces,
        qk_rows,
        value_rows,
        log_totals,
        cosine,
        sine_part,
        split,
        2 * split,
        carry,
    )
    bias_grad = jnp.concatenate([bias_first, bias_last], 1)[0]
    grad_mixed = jnp.concatenate([mixed_first, mixed_last], 1)
    qkv_scatter = Scatter(
        [outer_one([normed_own, normed_other], after(grad_mixed, *second_scatter.got))], bits
    )
    passed = qkv_scatter.kept[0]
    first_scatter.wait(passed)
    out_scatter.wait(passed)
    second_scatter.wait(passed)
    second_scatter.step()
    grad_mixed = after(grad_mixed, passed, second_scatter.kept[0])
    qkv_full = jnp.concatenate(qkv_pieces, 0)
    partial = jnp.einsum("tc,dc->td", grad_mixed, qkv_full, preferred_element_type=f32)
    grad_normed_one = partial[:tok_local] + flip(
        partial[tok_local:].astype(bf16), "col", 0
    ).astype(f32)
    scaled_one = gain_one * grad_normed_one
    inner_one = jnp.sum(scaled_one * input_rows, axis=1)
    input_grad = unstored(
        (
            grad_middle
            + scale_one[:, None] * scaled_one
            - input_rows * (scale_one**3 * inner_one / model_width)[:, None]
        ).astype(bf16)
    )
    gain_one_grad = jnp.sum(grad_normed_one * input_rows * scale_one[:, None], axis=0)

    def to_columns(total, width):
        low, high = total[:, :width].astype(bf16), total[:, width : 2 * width].astype(bf16)
        first, second = from_pairs(
            jnp.where(sequence == 0, low, high), jnp.where(sequence == 0, high, low)
        )
        return first.astype(f32) + second.astype(f32)

    bias_row = lax.dynamic_update_slice_in_dim(
        jnp.zeros((group_width * 2,), f32), bias_grad, core * group_width, 0
    )
    small = jnp.concatenate([unstored_row(gain_one_grad), unstored_row(gain_two_grad), bias_row])
    small = jnp.pad(small, (0, -small.shape[0] % 128)).reshape(-1, 128)
    for bit in range(2):
        small = small + flip(small, "col", bit)
    second_scatter.wait(small)
    small = after(small, *second_scatter.got)
    for bit in range(bits):
        small = small + flip(small, "row", bit)
    qkv_total = to_columns(qkv_scatter.total(), qkv_cols)
    out_total = to_columns(out_scatter.total(), out_cols)
    mlp_totals = []
    for scatter, (start, stop) in zip((first_scatter, second_scatter), cuts(ff_cols)):
        total = scatter.total()
        padded = total.shape[1] // 3
        mlp_totals.append(
            [total[:, k * padded : k * padded + stop - start] for k in range(3)]
        )
    gate_total, up_total, down_total = (jnp.concatenate(parts, 1) for parts in zip(*mlp_totals))
    small = small.reshape(-1)
    gain_one_total = small[:model_width]
    gain_two_total = small[model_width : 2 * model_width]
    bias_total = lax.dynamic_slice_in_dim(small, 2 * model_width + column * qkv_cols, qkv_cols, 0)
    return (
        layer_output,
        input_grad,
        gain_one_total,
        qkv_total,
        bias_total,
        out_total.T,
        gain_two_total,
        gate_total,
        up_total,
        down_total.T,
    )


def solution(mesh):
    in_specs = (
        P(("row", "col"), None),
        P(),
        P("row", "col"),
        P("col"),
        P("col", "row"),
        P(),
        P("row", "col"),
        P("row", "col"),
        P("col", "row"),
        P(("row", "col"), None),
    )
    out_specs = (
        P(("row", "col"), None),
        P(("row", "col"), None),
        P(),
        P("row", "col"),
        P("col"),
        P("col", "row"),
        P(),
        P("row", "col"),
        P("row", "col"),
        P("col", "row"),
    )
    return jax.shard_map(shards, mesh=mesh, in_specs=in_specs, out_specs=out_specs, check_vma=False)
```

```python
import functools
import math

import jax
import jax.numpy as jnp
from jax import lax
from jax.experimental import pallas as pl
from jax.experimental.pallas import tpu as pltpu
from jax.sharding import PartitionSpec as P

HD = 64
eps = 1e-06
theta_base = 1000000.0
bf16 = jnp.bfloat16
f32 = jnp.float32
NT = (((1,), (1,)), ((), ()))
TN = (((0,), (0,)), ((), ()))
MIB = 1024 * 1024


def flip(block, axis, bit):
    count = lax.axis_size(axis)
    return lax.ppermute(block, axis, [(i, i ^ 1 << bit) for i in range(count)])


def bit_reversed(value, bits):
    return sum((value >> b & 1) << (bits - 1 - b) for b in range(bits))


def after(value, *earlier):
    return lax.optimization_barrier((value, *earlier))[0]


def kernel_params(mib):
    return pltpu.CompilerParams(vmem_limit_bytes=mib * MIB)


def cost(flops, nbytes, exps=0):
    return pl.CostEstimate(
        flops=int(flops), bytes_accessed=int(nbytes), transcendentals=int(exps)
    )


def whole(array):
    return pl.BlockSpec(array.shape, lambda *_: (0,) * len(array.shape))


def in_place(block):
    return pl.BlockSpec(memory_space=pl.ANY)


def assemble(pieces, held, sems):
    copies = []
    at = 0
    for i, piece in enumerate(pieces):
        rows = piece.shape[0]
        copies.append(pltpu.make_async_copy(piece, held.at[pl.ds(at, rows)], sems.at[i]))
        at += rows
    for copy in copies:
        copy.start()
    for copy in copies:
        copy.wait()


def halves_turned(block):
    lane = lax.broadcasted_iota(jnp.int32, block.shape, 1)
    up = pltpu.roll(block, 128 - HD // 2, 1)
    return jnp.where(lane % HD < HD // 2, up, pltpu.roll(block, HD // 2, 1))


def side_rows(r, block, half, parity):
    side = (r // half) ^ parity
    return pl.ds(pl.multiple_of(side * half + r % half, block), block)


def pad_heads(key_value, rows, value, last):
    lane = lax.broadcasted_iota(jnp.int32, (1, 128), 1)
    kpad, vpad = key_value
    zero = jnp.zeros_like(value)
    vpad[0, rows, :] = jnp.concatenate([value, zero], 1).astype(bf16)
    vpad[1, rows, :] = jnp.concatenate([zero, value], 1).astype(bf16)
    kpad[1, rows, :] = jnp.where(lane >= HD, last, 0.0).astype(bf16)
    kpad[0, rows, :] = jnp.where(lane < HD, pltpu.roll(last, HD, 1), 0.0).astype(bf16)


def attend_kernel(parity_ref, *rest, block, count, first, last):
    if first == 0:
        own_ref, other_ref, bias_ref, cos_ref, sin_ref = rest[:5]
        pieces = rest[5 : 5 + count]
        qk_ref, v_ref, att_ref, lse_ref, held, kpad, vpad, lse_cols, sems = rest[5 + count :]
    else:
        qk_ref, v_ref, att_ref, lse_ref, kpad, vpad, lse_cols = rest
    step = pl.program_id(0) + first
    length, wide = qk_ref.shape
    half = length // 2
    pairs = wide // 128
    parity = parity_ref[0]

    @pl.when(step == first)
    def _():
        lse_cols[...] = jnp.zeros_like(lse_cols)
        if first:
            for r in range(0, length, block):
                rows = pl.ds(r, block)
                keys = qk_ref[rows, wide - 128 :].astype(f32)
                pad_heads((kpad, vpad), rows, v_ref[rows, :].astype(f32), keys)
            return
        assemble(pieces, held, sems)
        for side, rows_ref in enumerate((own_ref, other_ref)):
            for r in range(0, half, block):
                at = pl.multiple_of((side ^ parity) * half + r, block)
                rows = pl.ds(at, block)
                mixed = jnp.dot(rows_ref[r : r + block, :], held[...], preferred_element_type=f32)
                mixed = (mixed + bias_ref[...]).astype(bf16).astype(f32)
                cos, sin = cos_ref[rows, :], sin_ref[rows, :]
                for p in range(pairs):
                    u = mixed[:, p * 128 : (p + 1) * 128]
                    turned = (u * cos + halves_turned(u) * sin).astype(bf16)
                    qk_ref[rows, p * 128 : (p + 1) * 128] = turned
                v_ref[rows, :] = mixed[:, wide:].astype(bf16)
                pad_heads((kpad, vpad), rows, mixed[:, wide:], turned.astype(f32))

    factor = HD**-0.5 * math.log2(math.e)
    cols = pl.ds(pl.multiple_of(step * 128, 128), 128)
    row_i = lax.broadcasted_iota(jnp.int32, (block, block), 0)
    col_i = lax.broadcasted_iota(jnp.int32, (block, block), 1)
    for r in range(0, length, block):
        rows = pl.ds(r, block)
        to = side_rows(r, block, half, parity)
        q = qk_ref[rows, cols]

        def head(odd):
            keys = kpad[odd, : r + block, :]
            scores = lax.dot_general(q, keys, NT, preferred_element_type=f32)
            diag = jnp.where(col_i <= row_i, scores[:, r:], -1e30)
            scores = jnp.concatenate([scores[:, :r], diag], 1) if r else diag
            top = jnp.max(scores, 1, keepdims=True)
            e = jnp.exp2((scores - top) * factor)
            total = jnp.sum(e, 1, keepdims=True)
            out = jnp.dot(e.astype(bf16), vpad[odd, : r + block, :], preferred_element_type=f32)
            lse = top * factor + jnp.log2(total)
            at = lax.broadcasted_iota(jnp.int32, (1, 128), 1) == 2 * step + odd
            lse_cols[rows, :] = jnp.where(at, lse, lse_cols[rows, :])
            return out / total

        even = head(0)

        @pl.when(step < pairs - 1)
        def _():
            att_ref[to, :] = (even + head(1)).astype(bf16)

        @pl.when(step == pairs - 1)
        def _():
            att_ref[to, :] = even.astype(bf16)

    @pl.when(step == last - 1)
    def _():
        lse_ref[...] = lse_cols[...].T[: lse_ref.shape[0], :]


def attend(parity, own, other, pieces, bias, cos, sin, last):
    half, depth = own.shape
    length = 2 * half
    group = bias.shape[1]
    wide = group - HD
    block = min(256, half)
    return pl.pallas_call(
        functools.partial(attend_kernel, block=block, count=len(pieces), first=0, last=last),
        grid=(last,),
        in_specs=[pl.BlockSpec(memory_space=pltpu.SMEM)]
        + [whole(a) for a in (own, other, bias, cos, sin)]
        + [in_place(piece) for piece in pieces],
        out_specs=[
            pl.BlockSpec((length, wide), lambda p: (0, 0)),
            pl.BlockSpec((length, HD), lambda p: (0, 0)),
            pl.BlockSpec((length, 128), lambda p: (0, p)),
            pl.BlockSpec((8, length), lambda p: (0, 0)),
        ],
        out_shape=[
            jax.ShapeDtypeStruct((length, wide), bf16),
            jax.ShapeDtypeStruct((length, HD), bf16),
            jax.ShapeDtypeStruct((length, last * 128), bf16),
            jax.ShapeDtypeStruct((8, length), f32),
        ],
        scratch_shapes=[
            pltpu.VMEM((depth, group), bf16),
            pltpu.VMEM((2, length, 128), bf16),
            pltpu.VMEM((2, length, 128), bf16),
            pltpu.VMEM((length, 128), f32),
            pltpu.SemaphoreType.DMA((len(pieces),)),
        ],
        compiler_params=kernel_params(40),
        cost_estimate=cost(8e9, 6e6, 3e6),
    )(parity, own, other, bias, cos, sin, *pieces)


def attend_rest(parity, qk, v, first):
    length, wide = qk.shape
    pairs = wide // 128
    block = min(256, length // 2)
    return pl.pallas_call(
        functools.partial(attend_kernel, block=block, count=0, first=first, last=pairs),
        grid=(pairs - first,),
        in_specs=[pl.BlockSpec(memory_space=pltpu.SMEM), whole(qk), whole(v)],
        out_specs=[
            pl.BlockSpec((length, 128), lambda p: (0, p)),
            pl.BlockSpec((8, length), lambda p: (0, 0)),
        ],
        out_shape=[
            jax.ShapeDtypeStruct((length, (pairs - first) * 128), bf16),
            jax.ShapeDtypeStruct((8, length), f32),
        ],
        scratch_shapes=[
            pltpu.VMEM((2, length, 128), bf16),
            pltpu.VMEM((2, length, 128), bf16),
            pltpu.VMEM((length, 128), f32),
        ],
        compiler_params=kernel_params(40),
        cost_estimate=cost(6e9, 4e6, 3e6),
    )(parity, qk, v)


def project_kernel(first_ref, last_ref, *rest, count):
    pieces = rest[:count]
    own_ref, other_ref, held, sems = rest[count:]
    half = own_ref.shape[0]
    assemble(pieces, held, sems)
    for side, ref in enumerate((own_ref, other_ref)):
        total = 0.0
        at = 0
        for part_ref in (first_ref, last_ref):
            rows = part_ref[side * half : (side + 1) * half, :]
            weight = held[:, at : at + rows.shape[1]]
            total = total + lax.dot_general(rows, weight, NT, preferred_element_type=f32)
            at += rows.shape[1]
        ref[...] = total.astype(ref.dtype)


def project(first, last, pieces):
    length = first.shape[0]
    wide = first.shape[1] + last.shape[1]
    depth = sum(piece.shape[0] for piece in pieces)
    return pl.pallas_call(
        functools.partial(project_kernel, count=len(pieces)),
        in_specs=[pl.BlockSpec(memory_space=pltpu.VMEM)] * 2
        + [in_place(piece) for piece in pieces],
        out_specs=[pl.BlockSpec(memory_space=pltpu.VMEM)] * 2,
        out_shape=[
            jax.ShapeDtypeStruct((length // 2, depth), f32),
            jax.ShapeDtypeStruct((length // 2, depth), bf16),
        ],
        scratch_shapes=[
            pltpu.VMEM((depth, wide), bf16),
            pltpu.SemaphoreType.DMA((len(pieces),)),
        ],
        compiler_params=kernel_params(40),
        cost_estimate=cost(2 * length * depth * wide, 6e6),
    )(first, last, *pieces)


def attend_back_kernel(
    parity_ref,
    own_ref,
    other_ref,
    qk_ref,
    v_ref,
    lse_ref,
    cos_ref,
    sin_ref,
    *rest,
    block,
    count,
    first,
    last,
):
    pieces = rest[:count]
    if first == 0:
        mixed_ref, bias_ref, dk, dv, held, kpad, vpad, gatt, dq_acc, sems = rest[count:]
    else:
        dk_in, dv_in, mixed_ref, bias_ref, held, kpad, vpad, gatt, dq_acc, dk, dv, sems = rest[count:]
    step = pl.program_id(0) + first
    half_rows = own_ref.shape[0]
    length = 2 * half_rows
    wide = qk_ref.shape[1]
    pairs = wide // 128
    used = slice(first * 128, last * 128)
    parity = parity_ref[0]
    lane = lax.broadcasted_iota(jnp.int32, (1, 128), 1)

    @pl.when(step == first)
    def _():
        assemble(pieces, held, sems)
        for side, rows_ref in enumerate((own_ref, other_ref)):
            for r in range(0, half_rows, block):
                rows = pl.ds(pl.multiple_of((side ^ parity) * half_rows + r, block), block)
                got = jnp.dot(
                    rows_ref[r : r + block, :], held[:, used], preferred_element_type=f32
                )
                gatt[rows, :] = got.astype(bf16)
        for r in range(0, length, block):
            rows = pl.ds(r, block)
            keys = qk_ref[rows, wide - 128 :].astype(f32)
            pad_heads((kpad, vpad), rows, v_ref[rows, :].astype(f32), keys)
        dk[...] = dk_in[...] if first else jnp.zeros_like(dk)
        dv[...] = dv_in[...] if first else jnp.zeros_like(dv)

    factor = HD**-0.5 * math.log2(math.e)
    cols = pl.ds(pl.multiple_of(step * 128, 128), 128)
    here = pl.ds(pl.multiple_of((step - first) * 128, 128), 128)
    key_i = lax.broadcasted_iota(jnp.int32, (block, block), 0)
    query_i = lax.broadcasted_iota(jnp.int32, (block, block), 1)
    for r in range(0, length, block):
        rows = pl.ds(r, block)
        q = qk_ref[rows, cols]
        g = gatt[rows, here]

        def head(odd):
            lse = lse_ref[pl.ds(2 * step + odd, 1), rows]
            probs, grads = [], []
            inner = jnp.zeros((1, block), f32)
            for c in range(0, r + block, block):
                scores = lax.dot_general(
                    kpad[odd, c : c + block, :], q, NT, preferred_element_type=f32
                )
                p = jnp.exp2(scores * factor - lse)
                if c == r:
                    p = jnp.where(key_i <= query_i, p, 0.0)
                dp = lax.dot_general(vpad[odd, c : c + block, :], g, NT, preferred_element_type=f32)
                inner = inner + jnp.sum(p * dp, 0, keepdims=True)
                probs.append(p)
                grads.append(dp)
            dq = 0.0
            half = lane >= HD if odd else lane < HD
            for i, c in enumerate(range(0, r + block, block)):
                keys = pl.ds(c, block)
                ds = (probs[i] * (grads[i] - inner)).astype(bf16)
                p = probs[i].astype(bf16)
                dk[keys, :] += jnp.where(half, jnp.dot(ds, q, preferred_element_type=f32), 0.0)
                dv[keys, :] += jnp.where(half, jnp.dot(p, g, preferred_element_type=f32), 0.0)
                dq = dq + lax.dot_general(
                    ds, kpad[odd, c : c + block, :], TN, preferred_element_type=f32
                )
            return dq

        dq_acc[rows, :] = head(0)

        @pl.when(step < pairs - 1)
        def _():
            dq_acc[rows, :] += head(1)

    def back(u, rows):
        return u * cos_ref[rows, :] - halves_turned(u) * sin_ref[rows, :]

    scale = HD**-0.5
    for r in range(0, length, block):
        rows = pl.ds(r, block)
        to = side_rows(r, block, half_rows, parity)

        @pl.when(step < pairs - 1)
        def _():
            mixed_ref[to, here] = back(dq_acc[rows, :] * scale, rows).astype(bf16)

        if last == pairs:
            end = (last - first) * 128

            @pl.when(step == pairs - 1)
            def _():
                k = dk[rows, :]
                k = jnp.where(lane >= HD, k + pltpu.roll(k, HD, 1), dq_acc[rows, :]) * scale
                mixed_ref[to, end - 128 : end] = back(k, rows).astype(bf16)
                v = dv[rows, :]
                v = v + pltpu.roll(v, HD, 1)
                mixed_ref[to, end:] = v[:, :HD].astype(bf16)

    @pl.when(step == last - 1)
    def _():
        total = jnp.zeros((1, mixed_ref.shape[1]), f32)
        for r in range(0, length, block):
            part = mixed_ref[pl.ds(r, block), :].astype(f32)
            total = total + jnp.sum(part, 0, keepdims=True)
        bias_ref[...] = total


def attend_back(parity, own, other, pieces, qk, v, lse, cos, sin, first, last, earlier=()):
    half, depth = own.shape
    length = 2 * half
    wide = qk.shape[1]
    pairs = wide // 128
    group = (last - first) * 128 + (HD if last == pairs else 0)
    block = min(256, half)
    ins = (own, other, qk, v, lse, cos, sin)
    carried = pl.BlockSpec((length, 128), lambda p: (0, 0))
    carry = [jax.ShapeDtypeStruct((length, 128), f32)] * 2
    return pl.pallas_call(
        functools.partial(
            attend_back_kernel, block=block, count=len(pieces), first=first, last=last
        ),
        grid=(last - first,),
        in_specs=[pl.BlockSpec(memory_space=pltpu.SMEM)]
        + [whole(a) for a in ins]
        + [in_place(piece) for piece in pieces]
        + [carried] * len(earlier),
        out_specs=[
            pl.BlockSpec((length, group), lambda p: (0, 0)),
            pl.BlockSpec((1, group), lambda p: (0, 0)),
        ]
        + ([] if first else [carried] * 2),
        out_shape=[
            jax.ShapeDtypeStruct((length, group), bf16),
            jax.ShapeDtypeStruct((1, group), f32),
        ]
        + ([] if first else carry),
        scratch_shapes=[
            pltpu.VMEM((depth, wide), bf16),
            pltpu.VMEM((2, length, 128), bf16),
            pltpu.VMEM((2, length, 128), bf16),
            pltpu.VMEM((length, (last - first) * 128), bf16),
            pltpu.VMEM((length, 128), f32),
        ]
        + ([pltpu.VMEM((length, 128), f32)] * 2 if first else [])
        + [pltpu.SemaphoreType.DMA((len(pieces),))],
        compiler_params=kernel_params(50),
        cost_estimate=cost(12e9, 6e6, 3e6),
    )(parity, *ins, *pieces, *earlier)


def mlp_kernel(x0_ref, x1_ref, g0_ref, g1_ref, *rest, count, add):
    pieces = rest[:count]
    rest = rest[count:]
    if add:
        near_in, far_in, act_ref, near_ref, far_ref, held, sems = rest
    else:
        act_ref, near_ref, far_ref, held, sems = rest
    n = held.shape[1] // 3
    step = pl.program_id(0)

    @pl.when(step == 0)
    def _():
        assemble(pieces, held, sems)

    wg, wu, wd = (held[:, k * n : (k + 1) * n] for k in range(3))
    x = jnp.where(step == 0, x0_ref[...], x1_ref[...])
    g = jnp.where(step == 0, g0_ref[...], g1_ref[...])
    gate = jnp.dot(x, wg, preferred_element_type=f32)
    up = jnp.dot(x, wu, preferred_element_type=f32)
    gh = jnp.dot(g, wd, preferred_element_type=f32)
    sig = 1.0 / (1.0 + jnp.exp(-gate))
    silu = gate * sig
    hid = (silu * up).astype(bf16)
    ghs = gh * sig
    gg = (ghs * up * (1.0 + gate - silu)).astype(bf16)
    gu = (ghs * gate).astype(bf16)
    act_ref[:, :n] = gg
    act_ref[:, n : 2 * n] = gu
    act_ref[:, 2 * n :] = hid
    ngrad = lax.dot_general(gg, wg, NT, preferred_element_type=f32)
    ngrad = ngrad + lax.dot_general(gu, wu, NT, preferred_element_type=f32)
    down = lax.dot_general(hid, wd, NT, preferred_element_type=f32)

    @pl.when(step == 0)
    def _():
        near_ref[0] = (ngrad + near_in[0].astype(f32) if add else ngrad).astype(bf16)
        near_ref[1] = (down + near_in[1].astype(f32) if add else down).astype(bf16)

    @pl.when(step == 1)
    def _():
        far_ref[0] = (ngrad + far_in[0].astype(f32) if add else ngrad).astype(bf16)
        far_ref[1] = (down + far_in[1].astype(f32) if add else down).astype(bf16)


def mlp(rows, grads, pieces, sums=None):
    t, d = rows[0].shape
    columns = pieces[0].shape[1]
    add = sums is not None
    ins = (*rows, *grads)
    sums = tuple(sums or ())
    both = pl.BlockSpec((2, t, d), lambda i: (0, 0, 0))
    return pl.pallas_call(
        functools.partial(mlp_kernel, count=len(pieces), add=add),
        grid=(2,),
        in_specs=[whole(a) for a in ins] + [in_place(p) for p in pieces] + [both] * len(sums),
        out_specs=[pl.BlockSpec((t, columns), lambda i: (i, 0)), both, both],
        out_shape=[
            jax.ShapeDtypeStruct((2 * t, columns), bf16),
            jax.ShapeDtypeStruct((2, t, d), bf16),
            jax.ShapeDtypeStruct((2, t, d), bf16),
        ],
        scratch_shapes=[
            pltpu.VMEM((d, columns), bf16),
            pltpu.SemaphoreType.DMA((len(pieces),)),
        ],
        compiler_params=kernel_params(58),
        cost_estimate=cost(8 * t * d * columns, 30 * MIB, 2 * t * columns),
    )(*ins, *pieces, *sums)


def fill(sent_ref, kept_ref, lefts, rights, second):
    half = kept_ref.shape[0]
    t = lefts[0].shape[0]
    q = half // 2
    if second:
        parts = ((sent_ref, 0, q), (sent_ref, q, 3 * q), (kept_ref, 0, 0), (kept_ref, q, 2 * q))
        size = q
    else:
        parts = ((sent_ref, 0, half), (kept_ref, 0, 0))
        size = half
    for ref, to, start in parts:
        total = 0.0
        for i, left in enumerate(lefts):
            right = rights[i * t // rights[0].shape[0]]
            at = i * t % right.shape[0]
            total = total + lax.dot_general(
                left[:, start : start + size],
                right[at : at + t, :],
                TN,
                preferred_element_type=f32,
            )
        ref[to : to + size, :] = total.astype(ref.dtype)


def outer_kernel(*refs, blocks):
    rows, grads, rights = refs[:blocks], refs[blocks : 2 * blocks], refs[2 * blocks : -4]
    sent_one, kept_one, sent_two, kept_two = refs[-4:]
    step = pl.program_id(0)

    @pl.when(step < 2)
    def _():
        fill(sent_one, kept_one, rows, rights, False)

    @pl.when(step == 2)
    def _():
        fill(sent_two, kept_two, grads, rights, True)


def outer(rows, grads, acts):
    t, d = rows[0].shape
    tall, columns = acts[0].shape
    n = columns // 3
    flat = [*rows, *grads]
    one = pl.BlockSpec((d // 2, n), lambda k: (0, jnp.minimum(k, 1)))
    two = pl.BlockSpec((d // 2, n), lambda k: (0, 0))
    return pl.pallas_call(
        functools.partial(outer_kernel, blocks=len(rows)),
        grid=(3,),
        in_specs=[whole(left) for left in flat]
        + [pl.BlockSpec((tall, n), lambda k: (0, k)) for _ in acts],
        out_specs=[one, one, two, two],
        out_shape=[
            jax.ShapeDtypeStruct((d // 2, 2 * n), bf16),
            jax.ShapeDtypeStruct((d // 2, 2 * n), f32),
            jax.ShapeDtypeStruct((d // 2, n), bf16),
            jax.ShapeDtypeStruct((d // 2, n), f32),
        ],
        compiler_params=kernel_params(58),
        cost_estimate=cost(2 * t * len(rows) * d * columns, 20 * MIB),
    )(*flat, *acts)


def outer_one_kernel(*refs):
    fill(refs[-2], refs[-1], refs[:-3], refs[-3:-2], False)


def outer_one(lefts, right):
    t, d = lefts[0].shape
    columns = right.shape[1]
    vmem = pl.BlockSpec(memory_space=pltpu.VMEM)
    return pl.pallas_call(
        outer_one_kernel,
        in_specs=[vmem] * (len(lefts) + 1),
        out_specs=[vmem] * 2,
        out_shape=[
            jax.ShapeDtypeStruct((d // 2, columns), bf16),
            jax.ShapeDtypeStruct((d // 2, columns), f32),
        ],
        compiler_params=kernel_params(40),
        cost_estimate=cost(2 * t * len(lefts) * d * columns, 6 * MIB),
    )(*lefts, right)


def rope_tables(length):
    inverse = theta_base ** (-(jnp.arange(HD // 2, dtype=f32) * 2.0 / HD))
    angles = jnp.arange(length, dtype=f32)[:, None] * inverse[None, :]
    c, s = jnp.cos(angles), jnp.sin(angles)
    return jnp.concatenate([c] * 4, 1), jnp.concatenate([-s, s, -s, s], 1)


class Gather:
    def __init__(self, block, bits):
        self.bits = bits
        self.left = bits - 1
        self.pieces = [block]
        self.sent = 0
        self.beside = []

    def ready(self, *earlier):
        self.pieces[-1] = after(self.pieces[-1], *earlier)

    def double(self, *earlier):
        held = jnp.concatenate(self.pieces, 0) if len(self.pieces) > 1 else self.pieces[0]
        self.pieces.append(flip(after(held, *earlier) if earlier else held, "row", self.left))
        self.left -= 1
        return self.pieces[-1]

    def send(self, *earlier):
        piece = self.pieces[self.sent]
        self.sent += 1
        self.beside.append(flip(after(piece, *earlier) if earlier else piece, "row", 0))
        return self.beside[-1]

    def catch_up(self, *earlier):
        rest = jnp.concatenate(self.pieces[self.sent :], 0)
        self.sent = len(self.pieces)
        self.beside.append(flip(after(rest, *earlier), "row", 0))
        return self.beside[-1]

    def finish(self, *earlier):
        while self.left > 0:
            self.double()
        self.catch_up(*earlier)
        out = self.pieces + self.beside
        return out if out[0].shape[0] % 16 == 0 else [jnp.concatenate(out, 0)]

    def all(self):
        while self.left > 0:
            self.double()
        while self.sent < len(self.pieces):
            self.send()
        out = self.pieces + self.beside
        return out if out[0].shape[0] % 16 == 0 else [jnp.concatenate(out, 0)]


class Scatter:
    def __init__(self, parts, bits):
        self.bits = bits
        self.orders = [[0, 1], [1, 0]][: len(parts)]
        self.kept = [kept for _, kept in parts]
        self.done = 0
        self.start([sent for sent, _ in parts])

    def start(self, sents):
        bits = [order[self.done] if self.done < 2 else self.done for order in self.orders]
        self.got = [flip(sent, "row", bit) for sent, bit in zip(sents, bits)]

    def wait(self, *earlier):
        self.got = [after(got, *earlier) for got in self.got]

    def step(self):
        if self.done == self.bits - 1:
            return
        self.done += 1
        half = self.kept[0].shape[0] // 2
        sents = [
            (kept[half:] + got[half:].astype(f32)).astype(bf16)
            for kept, got in zip(self.kept, self.got)
        ]
        self.kept = [kept[:half] + got[:half].astype(f32) for kept, got in zip(self.kept, self.got)]
        if self.done == 2:
            sents = [jnp.concatenate(sents, 1)]
            self.kept = [jnp.concatenate(self.kept, 1)]
        self.start(sents)

    def total(self):
        while self.done < self.bits - 1:
            self.step()
        totals = [kept + got.astype(f32) for kept, got in zip(self.kept, self.got)]
        return jnp.concatenate(totals, 1)


def turned_pairs(block):
    first = [(2 * a + b, 2 * b + a) for a in range(2) for b in range(2)]
    second = [(2 * a + b, 2 * (1 - b) + a) for a in range(2) for b in range(2)]
    return lax.ppermute(block, "col", first), lax.ppermute(block, "col", second)


def from_pairs(same, other):
    first = [(2 * a + b, 2 * b + a) for a in range(2) for b in range(2)]
    second = [(2 * a + b, 2 * b + 1 - a) for a in range(2) for b in range(2)]
    return lax.ppermute(same, "col", first), lax.ppermute(other, "col", second)


def cuts(width):
    first = min(512, width)
    return [(0, first), (first, width)] if first < width else [(0, width)]


def shards(
    layer_input,
    gain_attn,
    qkv_weight,
    qkv_bias,
    out_weight,
    gain_mlp,
    gate_weight,
    up_weight,
    down_weight,
    cotangent,
):
    row = lax.axis_index("row")
    column = lax.axis_index("col")
    row_count = lax.axis_size("row")
    bits = row_count.bit_length() - 1
    core = column % 2
    sequence = column // 2
    parity = core.astype(jnp.int32).reshape(1)
    tok_local, model_width = layer_input.shape
    length = tok_local * 2
    deep = model_width // row_count
    ff_cols = gate_weight.shape[1]
    qkv_cols = qkv_weight.shape[1]
    out_cols = out_weight.shape[0]
    group_width = 2 * qkv_cols
    query_width = group_width - 2 * HD

    bias_rows = jnp.pad(qkv_bias[None, :], ((0, 15), (0, 0)))
    first, second = turned_pairs(
        jnp.concatenate(
            [
                jnp.concatenate([qkv_weight, bias_rows], 0),
                jnp.pad(out_weight.T, ((0, 16), (0, 0))),
            ],
            1,
        )
    )
    low = jnp.where(sequence == 0, first, second)
    high = jnp.where(sequence == 0, second, first)
    qkv_own = jnp.concatenate([low[:, :qkv_cols], high[:, :qkv_cols]], 1)
    bias_full = qkv_own[deep : deep + 1].astype(f32)
    out_own = jnp.concatenate([low[:deep, qkv_cols:], high[:deep, qkv_cols:]], 1)
    out_own = jnp.pad(out_own, ((0, 0), (0, HD)))
    qkv_gather = Gather(qkv_own[:deep], bits)
    out_gather = Gather(out_own, bits)
    down_flipped = down_weight.T
    mlp_gathers = []
    for start, stop in cuts(ff_cols):
        padded = -(-(stop - start) // 256) * 256
        pieces = [
            jnp.pad(part[:, start:stop], ((0, 0), (0, padded - (stop - start))))
            for part in (gate_weight, up_weight, down_flipped)
        ]
        mlp_gathers.append(Gather(jnp.concatenate(pieces, 1), bits))
    place = jnp.arange(model_width, dtype=jnp.int32)
    masks = jnp.array([bit_reversed(p, bits) for p in range(row_count)], jnp.int32)
    source = jnp.repeat(masks ^ row, deep) * deep + place % deep
    to_stored = (place[:, None] == source[None, :]).astype(bf16)
    from_stored = (source[:, None] == place[None, :]).astype(bf16)

    def stored(block):
        return jnp.dot(block, to_stored, preferred_element_type=f32)

    def unstored(block):
        return jnp.dot(block, from_stored, preferred_element_type=f32).astype(bf16)

    def unstored_row(vector):
        blocks = vector.reshape(row_count, deep)
        blocks = jnp.concatenate(
            [blocks[bit_reversed(m, bits)][None] for m in range(row_count)], 0
        )
        for bit in range(bits):
            wide = blocks.reshape(-1, 2, 1 << bit, deep)
            turned = jnp.concatenate([wide[:, 1:], wide[:, :1]], 1).reshape(row_count, deep)
            blocks = jnp.where((row >> bit) % 2 == 1, turned, blocks)
        return blocks.reshape(model_width)

    input_rows = stored(after(layer_input, first, second))
    gain_one = stored(gain_attn[None, :])
    gain_two = stored(gain_mlp[None, :])

    scale_one = lax.rsqrt(jnp.mean(input_rows * input_rows, axis=1) + eps)
    normed_own = (input_rows * scale_one[:, None] * gain_one).astype(bf16)
    normed_other = flip(normed_own, "col", 0)
    cosine, sine_part = rope_tables(length)

    near, far = mlp_gathers
    a_own = qkv_gather.send()
    a_four = qkv_gather.double()
    a_two = qkv_gather.double(a_own)
    a_beside = qkv_gather.send(a_own)
    o_four = out_gather.double(a_two)
    a_last = qkv_gather.send(a_beside)
    qkv_pieces = qkv_gather.all()
    near.ready(a_two)
    n_four = near.double()
    n_own = near.send(a_last)
    o_two = out_gather.double()
    grad_out = stored(after(cotangent, a_four))
    grad_blocks = [grad_out.astype(bf16)]
    across = flip(grad_blocks[0], "col", 1)
    split = -(-(query_width + HD) // 256)
    qk_rows, value_rows, att_first, log_first = attend(
        parity, normed_own, normed_other, qkv_pieces, bias_full, cosine, sine_part, split
    )
    out_pieces = out_gather.finish(att_first, o_two)
    n_two = near.double(att_first)
    n_beside = near.send(n_own)
    att_last, log_last = attend_rest(parity, after(qk_rows, n_four, n_own), value_rows, split)
    log_totals = log_first + log_last
    far.ready(n_two)
    f_four = far.double()
    n_last = near.send(n_beside)
    att_own, att_other = project(att_first, after(att_last, n_beside, n_two, across), out_pieces)
    att_got = flip(att_other, "col", 0)
    grad_blocks.append(flip(after(grad_blocks[0], att_got), "col", 0))
    grad_blocks += [across, flip(after(across, att_got), "col", 0)]
    middle = input_rows + att_own + att_got.astype(f32)
    scale_two = lax.rsqrt(jnp.mean(middle * middle, axis=1) + eps)
    blocks = [(middle * scale_two[:, None] * gain_two).astype(bf16)]
    across = flip(blocks[0], "col", 1)
    blocks.append(flip(after(blocks[0], n_last), "col", 0))
    blocks += [across, flip(across, "col", 0)]

    f_beside = far.catch_up(n_last)
    f_two = far.double(blocks[2])
    f_last = far.send(f_beside)
    first_pieces, second_pieces = (gather.all() for gather in mlp_gathers)
    act_own, *sums_own = mlp([after(blocks[0], blocks[2]), blocks[1]], grad_blocks[:2], first_pieces)
    act_far, *sums_far = mlp(blocks[2:], grad_blocks[2:], first_pieces)
    sent_one, kept_one, sent_two, kept_two = outer(blocks, grad_blocks, [act_own, act_far])
    first_scatter = Scatter([(sent_one, kept_one), (sent_two, kept_two)], bits)
    start_far = after(blocks[2], kept_one)
    act_far, near_far, far_far = mlp(
        [start_far, blocks[3]], grad_blocks[2:], second_pieces, sums_far
    )
    far_far = after(far_far, *first_scatter.got)
    across = near_far.astype(f32) + flip(far_far, "col", 0).astype(f32)
    across = across.astype(bf16)
    normed_back = flip(across[0], "col", 1)
    act_own, near_own, far_own = mlp(
        [after(blocks[0], across), blocks[1]],
        grad_blocks[:2],
        second_pieces,
        sums_own,
    )
    first_scatter.step()
    beside = flip(after(far_own, normed_back, *first_scatter.got), "col", 0)
    first_scatter.step()
    down_back = flip(after(across[1], normed_back), "col", 1)

    def summed(k, back):
        return near_own[k].astype(f32) + beside[k].astype(f32) + back.astype(f32)

    grad_normed_two = summed(0, normed_back)
    scaled_two = gain_two * grad_normed_two
    inner_two = jnp.sum(scaled_two * middle, axis=1)
    grad_middle = (
        grad_out
        + scale_two[:, None] * scaled_two
        - middle * (scale_two**3 * inner_two / model_width)[:, None]
    )
    gain_two_grad = jnp.sum(grad_normed_two * middle * scale_two[:, None], axis=0)
    branch_own = grad_middle.astype(bf16)
    branch_other = flip(branch_own, "col", 0)
    out_scatter = Scatter([outer_one([branch_own, branch_other], jnp.concatenate([att_first, att_last], 1))], bits)
    sent_one, kept_one, sent_two, kept_two = outer(
        [after(blocks[0], out_scatter.kept[0], *first_scatter.kept), *blocks[1:]],
        grad_blocks,
        [act_own, act_far],
    )
    second_scatter = Scatter([(sent_one, kept_one), (sent_two, kept_two)], bits)
    out_scatter.wait(kept_one)
    out_scatter.step()
    mixed_first, bias_first, *carry = attend_back(
        parity,
        after(branch_own, kept_one, out_scatter.kept[0]),
        branch_other,
        out_pieces,
        qk_rows,
        value_rows,
        log_totals,
        cosine,
        sine_part,
        0,
        split,
    )
    out_scatter.wait(mixed_first)
    out_scatter.step()
    first_scatter.wait(mixed_first)
    first_total = first_scatter.total()
    layer_output = unstored((middle + summed(1, after(down_back, mixed_first))).astype(bf16))
    mixed_last, bias_last = attend_back(
        parity,
        after(branch_own, out_scatter.kept[0], first_total, layer_output),
        branch_other,
        out_pieces,
        qk_rows,
        value_rows,
        log_totals,
        cosine,
        sine_part,
        split,
        qk_rows.shape[1] // 128,
        carry,
    )
    bias_grad = jnp.concatenate([bias_first, bias_last], 1)[0]
    grad_mixed = jnp.concatenate([mixed_first, mixed_last], 1)
    qkv_scatter = Scatter([outer_one([normed_own, normed_other], grad_mixed)], bits)
    passed = qkv_scatter.kept[0]
    second_scatter.wait(passed)
    out_scatter.wait(passed)
    second_scatter.step()
    qkv_full = jnp.concatenate(qkv_pieces, 0)
    grad_mixed = after(grad_mixed, passed, *second_scatter.kept)
    partial = jnp.einsum("tc,dc->td", grad_mixed, qkv_full, preferred_element_type=f32)
    grad_normed_one = partial[:tok_local] + flip(
        partial[tok_local:].astype(bf16), "col", 0
    ).astype(f32)
    scaled_one = gain_one * grad_normed_one
    inner_one = jnp.sum(scaled_one * input_rows, axis=1)
    input_grad = unstored(
        (
            grad_middle
            + scale_one[:, None] * scaled_one
            - input_rows * (scale_one**3 * inner_one / model_width)[:, None]
        ).astype(bf16)
    )
    gain_one_grad = jnp.sum(grad_normed_one * input_rows * scale_one[:, None], axis=0)

    def to_columns(total, width):
        low, high = total[:, :width].astype(bf16), total[:, width : 2 * width].astype(bf16)
        first, second = from_pairs(
            jnp.where(sequence == 0, low, high), jnp.where(sequence == 0, high, low)
        )
        return first.astype(f32) + second.astype(f32)

    bias_row = lax.dynamic_update_slice_in_dim(
        jnp.zeros((group_width * 2,), f32), bias_grad, core * group_width, 0
    )
    small = jnp.concatenate([unstored_row(gain_one_grad), unstored_row(gain_two_grad), bias_row])
    small = jnp.pad(small, (0, -small.shape[0] % 128)).reshape(-1, 128)
    second_scatter.step()
    for bit in range(2):
        small = small + flip(small, "col", bit)
    for bit in range(bits):
        small = small + flip(small, "row", bit)
    qkv_scatter.step()
    qkv_scatter.step()
    qkv_scatter.wait(small)
    qkv_total = to_columns(qkv_scatter.total(), qkv_cols)
    out_total = to_columns(out_scatter.total(), out_cols)
    mlp_totals = []
    for scatter, (start, stop) in zip((first_scatter, second_scatter), cuts(ff_cols)):
        total = first_total if scatter is first_scatter else scatter.total()
        padded = total.shape[1] // 3
        mlp_totals.append(
            [total[:, k * padded : k * padded + stop - start] for k in range(3)]
        )
    gate_total, up_total, down_total = (jnp.concatenate(parts, 1) for parts in zip(*mlp_totals))
    small = small.reshape(-1)
    gain_one_total = small[:model_width]
    gain_two_total = small[model_width : 2 * model_width]
    bias_total = lax.dynamic_slice_in_dim(small, 2 * model_width + column * qkv_cols, qkv_cols, 0)
    return (
        layer_output,
        input_grad,
        gain_one_total,
        qkv_total,
        bias_total,
        out_total.T,
        gain_two_total,
        gate_total,
        up_total,
        down_total.T,
    )


def solution(mesh):
    in_specs = (
        P(("row", "col"), None),
        P(),
        P("row", "col"),
        P("col"),
        P("col", "row"),
        P(),
        P("row", "col"),
        P("row", "col"),
        P("col", "row"),
        P(("row", "col"), None),
    )
    out_specs = (
        P(("row", "col"), None),
        P(("row", "col"), None),
        P(),
        P("row", "col"),
        P("col"),
        P("col", "row"),
        P(),
        P("row", "col"),
        P("row", "col"),
        P("col", "row"),
    )
    return jax.shard_map(shards, mesh=mesh, in_specs=in_specs, out_specs=out_specs, check_vma=False)
```

```python
import functools
import math

import jax
import jax.numpy as jnp
from jax import lax
from jax.experimental import pallas as pl
from jax.experimental.pallas import tpu as pltpu
from jax.sharding import PartitionSpec as P

HD = 64
eps = 1e-06
theta_base = 1000000.0
bf16 = jnp.bfloat16
f32 = jnp.float32
NT = (((1,), (1,)), ((), ()))
TN = (((0,), (0,)), ((), ()))
MIB = 1024 * 1024


def flip(block, axis, bit):
    count = lax.axis_size(axis)
    return lax.ppermute(block, axis, [(i, i ^ 1 << bit) for i in range(count)])


def bit_reversed(value, bits):
    return sum((value >> b & 1) << (bits - 1 - b) for b in range(bits))


def after(value, *earlier):
    return lax.optimization_barrier((value, *earlier))[0]


def kernel_params(mib):
    return pltpu.CompilerParams(vmem_limit_bytes=mib * MIB)


def cost(flops, nbytes, exps=0):
    return pl.CostEstimate(
        flops=int(flops), bytes_accessed=int(nbytes), transcendentals=int(exps)
    )


def whole(array):
    return pl.BlockSpec(array.shape, lambda *_: (0,) * len(array.shape))


def in_place(block):
    return pl.BlockSpec(memory_space=pl.ANY)


def assemble(pieces, held, sems):
    copies = []
    at = 0
    for i, piece in enumerate(pieces):
        rows = piece.shape[0]
        copies.append(pltpu.make_async_copy(piece, held.at[pl.ds(at, rows)], sems.at[i]))
        at += rows
    for copy in copies:
        copy.start()
    for copy in copies:
        copy.wait()


def halves_turned(block):
    lane = lax.broadcasted_iota(jnp.int32, block.shape, 1)
    up = pltpu.roll(block, 128 - HD // 2, 1)
    return jnp.where(lane % HD < HD // 2, up, pltpu.roll(block, HD // 2, 1))


def side_rows(r, block, half, parity):
    side = (r // half) ^ parity
    return pl.ds(pl.multiple_of(side * half + r % half, block), block)


def pad_heads(key_value, rows, value, last):
    lane = lax.broadcasted_iota(jnp.int32, (1, 128), 1)
    kpad, vpad = key_value
    zero = jnp.zeros_like(value)
    vpad[0, rows, :] = jnp.concatenate([value, zero], 1).astype(bf16)
    vpad[1, rows, :] = jnp.concatenate([zero, value], 1).astype(bf16)
    kpad[1, rows, :] = jnp.where(lane >= HD, last, 0.0).astype(bf16)
    kpad[0, rows, :] = jnp.where(lane < HD, pltpu.roll(last, HD, 1), 0.0).astype(bf16)


def attend_kernel(parity_ref, own_ref, other_ref, bias_ref, cos_ref, sin_ref, *rest, block, count):
    pieces = rest[:count]
    qk_ref, v_ref, att_ref, lse_ref, held, kpad, vpad, lse_cols, sems = rest[count:]
    step = pl.program_id(0)
    half = own_ref.shape[0]
    length = 2 * half
    wide = qk_ref.shape[1]
    pairs = wide // 128
    parity = parity_ref[0]

    @pl.when(step == 0)
    def _():
        assemble(pieces, held, sems)
        for side, rows_ref in enumerate((own_ref, other_ref)):
            for r in range(0, half, block):
                at = pl.multiple_of((side ^ parity) * half + r, block)
                rows = pl.ds(at, block)
                mixed = jnp.dot(rows_ref[r : r + block, :], held[...], preferred_element_type=f32)
                mixed = (mixed + bias_ref[...]).astype(bf16).astype(f32)
                cos, sin = cos_ref[rows, :], sin_ref[rows, :]
                for p in range(pairs):
                    u = mixed[:, p * 128 : (p + 1) * 128]
                    turned = (u * cos + halves_turned(u) * sin).astype(bf16)
                    qk_ref[rows, p * 128 : (p + 1) * 128] = turned
                v_ref[rows, :] = mixed[:, wide:].astype(bf16)
                pad_heads((kpad, vpad), rows, mixed[:, wide:], turned.astype(f32))
        lse_cols[...] = jnp.zeros_like(lse_cols)

    factor = HD**-0.5 * math.log2(math.e)
    cols = pl.ds(pl.multiple_of(step * 128, 128), 128)
    row_i = lax.broadcasted_iota(jnp.int32, (block, block), 0)
    col_i = lax.broadcasted_iota(jnp.int32, (block, block), 1)
    for r in range(0, length, block):
        rows = pl.ds(r, block)
        to = side_rows(r, block, half, parity)
        q = qk_ref[rows, cols]

        def head(odd):
            keys = kpad[odd, : r + block, :]
            scores = lax.dot_general(q, keys, NT, preferred_element_type=f32)
            diag = jnp.where(col_i <= row_i, scores[:, r:], -1e30)
            scores = jnp.concatenate([scores[:, :r], diag], 1) if r else diag
            top = jnp.max(scores, 1, keepdims=True)
            e = jnp.exp2((scores - top) * factor)
            total = jnp.sum(e, 1, keepdims=True)
            out = jnp.dot(e.astype(bf16), vpad[odd, : r + block, :], preferred_element_type=f32)
            lse = top * factor + jnp.log2(total)
            at = lax.broadcasted_iota(jnp.int32, (1, 128), 1) == 2 * step + odd
            lse_cols[rows, :] = jnp.where(at, lse, lse_cols[rows, :])
            return out / total

        even = head(0)

        @pl.when(step < pairs - 1)
        def _():
            att_ref[to, :] = (even + head(1)).astype(bf16)

        @pl.when(step == pairs - 1)
        def _():
            att_ref[to, :] = even.astype(bf16)

    @pl.when(step == pairs - 1)
    def _():
        lse_ref[...] = lse_cols[...].T[: lse_ref.shape[0], :]


def attend(parity, own, other, pieces, bias, cos, sin):
    half, depth = own.shape
    length = 2 * half
    group = bias.shape[1]
    wide = group - HD
    pairs = wide // 128
    block = min(256, half)
    return pl.pallas_call(
        functools.partial(attend_kernel, block=block, count=len(pieces)),
        grid=(pairs,),
        in_specs=[pl.BlockSpec(memory_space=pltpu.SMEM)]
        + [whole(a) for a in (own, other, bias, cos, sin)]
        + [in_place(piece) for piece in pieces],
        out_specs=[
            pl.BlockSpec((length, wide), lambda p: (0, 0)),
            pl.BlockSpec((length, HD), lambda p: (0, 0)),
            pl.BlockSpec((length, 128), lambda p: (0, p)),
            pl.BlockSpec((8, length), lambda p: (0, 0)),
        ],
        out_shape=[
            jax.ShapeDtypeStruct((length, wide), bf16),
            jax.ShapeDtypeStruct((length, HD), bf16),
            jax.ShapeDtypeStruct((length, wide), bf16),
            jax.ShapeDtypeStruct((8, length), f32),
        ],
        scratch_shapes=[
            pltpu.VMEM((depth, group), bf16),
            pltpu.VMEM((2, length, 128), bf16),
            pltpu.VMEM((2, length, 128), bf16),
            pltpu.VMEM((length, 128), f32),
            pltpu.SemaphoreType.DMA((len(pieces),)),
        ],
        compiler_params=kernel_params(40),
        cost_estimate=cost(12e9, 8e6, 5e6),
    )(parity, own, other, bias, cos, sin, *pieces)


def project_kernel(att_ref, *rest, count):
    pieces = rest[:count]
    own_ref, other_ref, held, sems = rest[count:]
    half = own_ref.shape[0]
    assemble(pieces, held, sems)
    for side, ref in enumerate((own_ref, other_ref)):
        rows = att_ref[side * half : (side + 1) * half, :]
        ref[...] = lax.dot_general(rows, held[...], NT, preferred_element_type=f32).astype(ref.dtype)


def project(att, pieces):
    length, wide = att.shape
    depth = sum(piece.shape[0] for piece in pieces)
    return pl.pallas_call(
        functools.partial(project_kernel, count=len(pieces)),
        in_specs=[pl.BlockSpec(memory_space=pltpu.VMEM)] + [in_place(piece) for piece in pieces],
        out_specs=[pl.BlockSpec(memory_space=pltpu.VMEM)] * 2,
        out_shape=[
            jax.ShapeDtypeStruct((length // 2, depth), f32),
            jax.ShapeDtypeStruct((length // 2, depth), bf16),
        ],
        scratch_shapes=[
            pltpu.VMEM((depth, wide), bf16),
            pltpu.SemaphoreType.DMA((len(pieces),)),
        ],
        compiler_params=kernel_params(40),
        cost_estimate=cost(2 * length * depth * wide, 6e6),
    )(att, *pieces)


def attend_back_kernel(
    parity_ref,
    own_ref,
    other_ref,
    qk_ref,
    v_ref,
    lse_ref,
    cos_ref,
    sin_ref,
    *rest,
    block,
    count,
    first,
    last,
):
    pieces = rest[:count]
    if first == 0:
        mixed_ref, bias_ref, dk, dv, held, kpad, vpad, gatt, dq_acc, sems = rest[count:]
    else:
        dk_in, dv_in, mixed_ref, bias_ref, held, kpad, vpad, gatt, dq_acc, dk, dv, sems = rest[count:]
    step = pl.program_id(0) + first
    half_rows = own_ref.shape[0]
    length = 2 * half_rows
    wide = qk_ref.shape[1]
    pairs = wide // 128
    used = slice(first * 128, last * 128)
    parity = parity_ref[0]
    lane = lax.broadcasted_iota(jnp.int32, (1, 128), 1)

    @pl.when(step == first)
    def _():
        assemble(pieces, held, sems)
        for side, rows_ref in enumerate((own_ref, other_ref)):
            for r in range(0, half_rows, block):
                rows = pl.ds(pl.multiple_of((side ^ parity) * half_rows + r, block), block)
                got = jnp.dot(
                    rows_ref[r : r + block, :], held[:, used], preferred_element_type=f32
                )
                gatt[rows, :] = got.astype(bf16)
        for r in range(0, length, block):
            rows = pl.ds(r, block)
            keys = qk_ref[rows, wide - 128 :].astype(f32)
            pad_heads((kpad, vpad), rows, v_ref[rows, :].astype(f32), keys)
        dk[...] = dk_in[...] if first else jnp.zeros_like(dk)
        dv[...] = dv_in[...] if first else jnp.zeros_like(dv)

    factor = HD**-0.5 * math.log2(math.e)
    cols = pl.ds(pl.multiple_of(step * 128, 128), 128)
    here = pl.ds(pl.multiple_of((step - first) * 128, 128), 128)
    key_i = lax.broadcasted_iota(jnp.int32, (block, block), 0)
    query_i = lax.broadcasted_iota(jnp.int32, (block, block), 1)
    for r in range(0, length, block):
        rows = pl.ds(r, block)
        q = qk_ref[rows, cols]
        g = gatt[rows, here]

        def head(odd):
            lse = lse_ref[pl.ds(2 * step + odd, 1), rows]
            probs, grads = [], []
            inner = jnp.zeros((1, block), f32)
            for c in range(0, r + block, block):
                scores = lax.dot_general(
                    kpad[odd, c : c + block, :], q, NT, preferred_element_type=f32
                )
                p = jnp.exp2(scores * factor - lse)
                if c == r:
                    p = jnp.where(key_i <= query_i, p, 0.0)
                dp = lax.dot_general(vpad[odd, c : c + block, :], g, NT, preferred_element_type=f32)
                inner = inner + jnp.sum(p * dp, 0, keepdims=True)
                probs.append(p)
                grads.append(dp)
            dq = 0.0
            half = lane >= HD if odd else lane < HD
            for i, c in enumerate(range(0, r + block, block)):
                keys = pl.ds(c, block)
                ds = (probs[i] * (grads[i] - inner)).astype(bf16)
                p = probs[i].astype(bf16)
                dk[keys, :] += jnp.where(half, jnp.dot(ds, q, preferred_element_type=f32), 0.0)
                dv[keys, :] += jnp.where(half, jnp.dot(p, g, preferred_element_type=f32), 0.0)
                dq = dq + lax.dot_general(
                    ds, kpad[odd, c : c + block, :], TN, preferred_element_type=f32
                )
            return dq

        dq_acc[rows, :] = head(0)

        @pl.when(step < pairs - 1)
        def _():
            dq_acc[rows, :] += head(1)

    def back(u, rows):
        return u * cos_ref[rows, :] - halves_turned(u) * sin_ref[rows, :]

    scale = HD**-0.5
    for r in range(0, length, block):
        rows = pl.ds(r, block)
        to = side_rows(r, block, half_rows, parity)

        @pl.when(step < pairs - 1)
        def _():
            mixed_ref[to, here] = back(dq_acc[rows, :] * scale, rows).astype(bf16)

        if last == pairs:
            end = (last - first) * 128

            @pl.when(step == pairs - 1)
            def _():
                k = dk[rows, :]
                k = jnp.where(lane >= HD, k + pltpu.roll(k, HD, 1), dq_acc[rows, :]) * scale
                mixed_ref[to, end - 128 : end] = back(k, rows).astype(bf16)
                v = dv[rows, :]
                v = v + pltpu.roll(v, HD, 1)
                mixed_ref[to, end:] = v[:, :HD].astype(bf16)

    @pl.when(step == last - 1)
    def _():
        total = jnp.zeros((1, mixed_ref.shape[1]), f32)
        for r in range(0, length, block):
            part = mixed_ref[pl.ds(r, block), :].astype(f32)
            total = total + jnp.sum(part, 0, keepdims=True)
        bias_ref[...] = total


def attend_back(parity, own, other, pieces, qk, v, lse, cos, sin, first, last, earlier=()):
    half, depth = own.shape
    length = 2 * half
    wide = qk.shape[1]
    pairs = wide // 128
    group = (last - first) * 128 + (HD if last == pairs else 0)
    block = min(256, half)
    ins = (own, other, qk, v, lse, cos, sin)
    carried = pl.BlockSpec((length, 128), lambda p: (0, 0))
    carry = [jax.ShapeDtypeStruct((length, 128), f32)] * 2
    return pl.pallas_call(
        functools.partial(
            attend_back_kernel, block=block, count=len(pieces), first=first, last=last
        ),
        grid=(last - first,),
        in_specs=[pl.BlockSpec(memory_space=pltpu.SMEM)]
        + [whole(a) for a in ins]
        + [in_place(piece) for piece in pieces]
        + [carried] * len(earlier),
        out_specs=[
            pl.BlockSpec((length, group), lambda p: (0, 0)),
            pl.BlockSpec((1, group), lambda p: (0, 0)),
        ]
        + ([] if first else [carried] * 2),
        out_shape=[
            jax.ShapeDtypeStruct((length, group), bf16),
            jax.ShapeDtypeStruct((1, group), f32),
        ]
        + ([] if first else carry),
        scratch_shapes=[
            pltpu.VMEM((depth, wide), bf16),
            pltpu.VMEM((2, length, 128), bf16),
            pltpu.VMEM((2, length, 128), bf16),
            pltpu.VMEM((length, (last - first) * 128), bf16),
            pltpu.VMEM((length, 128), f32),
        ]
        + ([pltpu.VMEM((length, 128), f32)] * 2 if first else [])
        + [pltpu.SemaphoreType.DMA((len(pieces),))],
        compiler_params=kernel_params(50),
        cost_estimate=cost(12e9, 6e6, 3e6),
    )(parity, *ins, *pieces, *earlier)


def mlp_kernel(x0_ref, x1_ref, g0_ref, g1_ref, *rest, count, add):
    pieces = rest[:count]
    rest = rest[count:]
    if add:
        near_in, far_in, act_ref, near_ref, far_ref, held, sems = rest
    else:
        act_ref, near_ref, far_ref, held, sems = rest
    n = held.shape[1] // 3
    step = pl.program_id(0)

    @pl.when(step == 0)
    def _():
        assemble(pieces, held, sems)

    wg, wu, wd = (held[:, k * n : (k + 1) * n] for k in range(3))
    x = jnp.where(step == 0, x0_ref[...], x1_ref[...])
    g = jnp.where(step == 0, g0_ref[...], g1_ref[...])
    gate = jnp.dot(x, wg, preferred_element_type=f32)
    up = jnp.dot(x, wu, preferred_element_type=f32)
    gh = jnp.dot(g, wd, preferred_element_type=f32)
    sig = 1.0 / (1.0 + jnp.exp(-gate))
    silu = gate * sig
    hid = (silu * up).astype(bf16)
    ghs = gh * sig
    gg = (ghs * up * (1.0 + gate - silu)).astype(bf16)
    gu = (ghs * gate).astype(bf16)
    act_ref[:, :n] = gg
    act_ref[:, n : 2 * n] = gu
    act_ref[:, 2 * n :] = hid
    ngrad = lax.dot_general(gg, wg, NT, preferred_element_type=f32)
    ngrad = ngrad + lax.dot_general(gu, wu, NT, preferred_element_type=f32)
    down = lax.dot_general(hid, wd, NT, preferred_element_type=f32)

    @pl.when(step == 0)
    def _():
        near_ref[0] = (ngrad + near_in[0].astype(f32) if add else ngrad).astype(bf16)
        near_ref[1] = (down + near_in[1].astype(f32) if add else down).astype(bf16)

    @pl.when(step == 1)
    def _():
        far_ref[0] = (ngrad + far_in[0].astype(f32) if add else ngrad).astype(bf16)
        far_ref[1] = (down + far_in[1].astype(f32) if add else down).astype(bf16)


def mlp(rows, grads, pieces, sums=None):
    t, d = rows[0].shape
    columns = pieces[0].shape[1]
    add = sums is not None
    ins = (*rows, *grads)
    sums = tuple(sums or ())
    both = pl.BlockSpec((2, t, d), lambda i: (0, 0, 0))
    return pl.pallas_call(
        functools.partial(mlp_kernel, count=len(pieces), add=add),
        grid=(2,),
        in_specs=[whole(a) for a in ins] + [in_place(p) for p in pieces] + [both] * len(sums),
        out_specs=[pl.BlockSpec((t, columns), lambda i: (i, 0)), both, both],
        out_shape=[
            jax.ShapeDtypeStruct((2 * t, columns), bf16),
            jax.ShapeDtypeStruct((2, t, d), bf16),
            jax.ShapeDtypeStruct((2, t, d), bf16),
        ],
        scratch_shapes=[
            pltpu.VMEM((d, columns), bf16),
            pltpu.SemaphoreType.DMA((len(pieces),)),
        ],
        compiler_params=kernel_params(58),
        cost_estimate=cost(8 * t * d * columns, 30 * MIB, 2 * t * columns),
    )(*ins, *pieces, *sums)


def fill(sent_ref, kept_ref, lefts, rights, second):
    half = kept_ref.shape[0]
    t = lefts[0].shape[0]
    q = half // 2
    if second:
        parts = ((sent_ref, 0, q), (sent_ref, q, 3 * q), (kept_ref, 0, 0), (kept_ref, q, 2 * q))
        size = q
    else:
        parts = ((sent_ref, 0, half), (kept_ref, 0, 0))
        size = half
    for ref, to, start in parts:
        total = 0.0
        for i, left in enumerate(lefts):
            right = rights[i * t // rights[0].shape[0]]
            at = i * t % right.shape[0]
            total = total + lax.dot_general(
                left[:, start : start + size],
                right[at : at + t, :],
                TN,
                preferred_element_type=f32,
            )
        ref[to : to + size, :] = total.astype(ref.dtype)


def outer_kernel(*refs, blocks):
    rows, grads, rights = refs[:blocks], refs[blocks : 2 * blocks], refs[2 * blocks : -4]
    sent_one, kept_one, sent_two, kept_two = refs[-4:]
    step = pl.program_id(0)

    @pl.when(step < 2)
    def _():
        fill(sent_one, kept_one, rows, rights, False)

    @pl.when(step == 2)
    def _():
        fill(sent_two, kept_two, grads, rights, True)


def outer(rows, grads, acts):
    t, d = rows[0].shape
    tall, columns = acts[0].shape
    n = columns // 3
    flat = [*rows, *grads]
    one = pl.BlockSpec((d // 2, n), lambda k: (0, jnp.minimum(k, 1)))
    two = pl.BlockSpec((d // 2, n), lambda k: (0, 0))
    return pl.pallas_call(
        functools.partial(outer_kernel, blocks=len(rows)),
        grid=(3,),
        in_specs=[whole(left) for left in flat]
        + [pl.BlockSpec((tall, n), lambda k: (0, k)) for _ in acts],
        out_specs=[one, one, two, two],
        out_shape=[
            jax.ShapeDtypeStruct((d // 2, 2 * n), bf16),
            jax.ShapeDtypeStruct((d // 2, 2 * n), f32),
            jax.ShapeDtypeStruct((d // 2, n), bf16),
            jax.ShapeDtypeStruct((d // 2, n), f32),
        ],
        compiler_params=kernel_params(58),
        cost_estimate=cost(2 * t * len(rows) * d * columns, 20 * MIB),
    )(*flat, *acts)


def outer_whole_kernel(row_ref, *refs, blocks, count, moved):
    rows, grads, rights, out_ref = refs[:blocks], refs[blocks : 2 * blocks], refs[2 * blocks : -1], refs[-1]
    step = pl.program_id(0)
    t, d = rows[0].shape
    deep = d // count
    bits = count.bit_length() - 1

    def product(lefts):
        for part in range(2):
            start = part * (d // 2)
            total = 0.0
            for i, left in enumerate(lefts):
                right = rights[i * t // rights[0].shape[0]]
                at = i * t % right.shape[0]
                total = total + lax.dot_general(
                    left[:, start : start + d // 2],
                    right[at : at + t, :],
                    TN,
                    preferred_element_type=f32,
                )
            total = total.astype(bf16)
            if not moved:
                out_ref[start : start + d // 2, :] = total
                continue
            for p in range(part * count // 2, (part + 1) * count // 2):
                to = (row_ref[0] ^ bit_reversed(p, bits)) * deep
                here = p * deep - start
                out_ref[pl.ds(pl.multiple_of(to, 16), deep), :] = total[here : here + deep]

    @pl.when(step < 2)
    def _():
        product(rows)

    @pl.when(step == 2)
    def _():
        product(grads)


def outer_whole(row, rows, grads, acts, count):
    t, d = rows[0].shape
    tall, columns = acts[0].shape
    n = columns // 3
    flat = [*rows, *grads]
    deep = d // count
    bits = count.bit_length() - 1
    moved = deep % 16 == 0
    out = pl.pallas_call(
        functools.partial(outer_whole_kernel, blocks=len(rows), count=count, moved=moved),
        grid=(3,),
        in_specs=[pl.BlockSpec(memory_space=pltpu.SMEM)]
        + [whole(left) for left in flat]
        + [pl.BlockSpec((tall, n), lambda k: (0, k)) for _ in acts],
        out_specs=pl.BlockSpec((d, n), lambda k: (0, k)),
        out_shape=jax.ShapeDtypeStruct((d, columns), bf16),
        compiler_params=kernel_params(58),
        cost_estimate=cost(2 * t * len(rows) * d * columns, 20 * MIB),
    )(row, *flat, *acts)
    if moved:
        return out
    places = jnp.array([bit_reversed(m, bits) for m in range(count)], jnp.int32)
    order = places[jnp.arange(count, dtype=jnp.int32) ^ row[0]]
    return out.reshape(count, deep, columns)[order].reshape(d, columns)


def outer_one_kernel(*refs):
    fill(refs[-2], refs[-1], refs[:-3], refs[-3:-2], False)


def outer_one(lefts, right):
    t, d = lefts[0].shape
    columns = right.shape[1]
    vmem = pl.BlockSpec(memory_space=pltpu.VMEM)
    return pl.pallas_call(
        outer_one_kernel,
        in_specs=[vmem] * (len(lefts) + 1),
        out_specs=[vmem] * 2,
        out_shape=[
            jax.ShapeDtypeStruct((d // 2, columns), bf16),
            jax.ShapeDtypeStruct((d // 2, columns), f32),
        ],
        compiler_params=kernel_params(40),
        cost_estimate=cost(2 * t * len(lefts) * d * columns, 6 * MIB),
    )(*lefts, right)


def rope_tables(length):
    inverse = theta_base ** (-(jnp.arange(HD // 2, dtype=f32) * 2.0 / HD))
    angles = jnp.arange(length, dtype=f32)[:, None] * inverse[None, :]
    c, s = jnp.cos(angles), jnp.sin(angles)
    return jnp.concatenate([c] * 4, 1), jnp.concatenate([-s, s, -s, s], 1)


class Gather:
    def __init__(self, block, bits):
        self.bits = bits
        self.left = bits - 1
        self.pieces = [block]
        self.sent = 0
        self.beside = []

    def ready(self, *earlier):
        self.pieces[-1] = after(self.pieces[-1], *earlier)

    def double(self, *earlier):
        held = jnp.concatenate(self.pieces, 0) if len(self.pieces) > 1 else self.pieces[0]
        self.pieces.append(flip(after(held, *earlier) if earlier else held, "row", self.left))
        self.left -= 1
        return self.pieces[-1]

    def send(self, *earlier):
        piece = self.pieces[self.sent]
        self.sent += 1
        self.beside.append(flip(after(piece, *earlier) if earlier else piece, "row", 0))
        return self.beside[-1]

    def catch_up(self, *earlier):
        rest = jnp.concatenate(self.pieces[self.sent :], 0)
        self.sent = len(self.pieces)
        self.beside.append(flip(after(rest, *earlier), "row", 0))
        return self.beside[-1]

    def finish(self, *earlier):
        while self.left > 0:
            self.double()
        self.catch_up(*earlier)
        out = self.pieces + self.beside
        return out if out[0].shape[0] % 16 == 0 else [jnp.concatenate(out, 0)]

    def all(self):
        while self.left > 0:
            self.double()
        while self.sent < len(self.pieces):
            self.send()
        out = self.pieces + self.beside
        return out if out[0].shape[0] % 16 == 0 else [jnp.concatenate(out, 0)]


class Scatter:
    def __init__(self, parts, bits):
        self.bits = bits
        self.orders = [[0, 1], [1, 0]][: len(parts)]
        self.kept = [kept for _, kept in parts]
        self.done = 0
        self.start([sent for sent, _ in parts])

    def start(self, sents):
        bits = [order[self.done] if self.done < 2 else self.done for order in self.orders]
        self.got = [flip(sent, "row", bit) for sent, bit in zip(sents, bits)]

    def wait(self, *earlier):
        self.got = [after(got, *earlier) for got in self.got]

    def step(self):
        if self.done == self.bits - 1:
            return
        self.done += 1
        half = self.kept[0].shape[0] // 2
        sents = [
            (kept[half:] + got[half:].astype(f32)).astype(bf16)
            for kept, got in zip(self.kept, self.got)
        ]
        self.kept = [kept[:half] + got[:half].astype(f32) for kept, got in zip(self.kept, self.got)]
        if self.done == 2:
            sents = [jnp.concatenate(sents, 1)]
            self.kept = [jnp.concatenate(self.kept, 1)]
        self.start(sents)

    def total(self):
        while self.done < self.bits - 1:
            self.step()
        totals = [kept + got.astype(f32) for kept, got in zip(self.kept, self.got)]
        return jnp.concatenate(totals, 1)


def turned_pairs(block):
    first = [(2 * a + b, 2 * b + a) for a in range(2) for b in range(2)]
    second = [(2 * a + b, 2 * (1 - b) + a) for a in range(2) for b in range(2)]
    return lax.ppermute(block, "col", first), lax.ppermute(block, "col", second)


def from_pairs(same, other):
    first = [(2 * a + b, 2 * b + a) for a in range(2) for b in range(2)]
    second = [(2 * a + b, 2 * b + 1 - a) for a in range(2) for b in range(2)]
    return lax.ppermute(same, "col", first), lax.ppermute(other, "col", second)


def cuts(width):
    first = min(512, width)
    return [(0, first), (first, width)] if first < width else [(0, width)]


def shards(
    layer_input,
    gain_attn,
    qkv_weight,
    qkv_bias,
    out_weight,
    gain_mlp,
    gate_weight,
    up_weight,
    down_weight,
    cotangent,
):
    row = lax.axis_index("row")
    column = lax.axis_index("col")
    row_count = lax.axis_size("row")
    bits = row_count.bit_length() - 1
    core = column % 2
    sequence = column // 2
    parity = core.astype(jnp.int32).reshape(1)
    tok_local, model_width = layer_input.shape
    length = tok_local * 2
    deep = model_width // row_count
    ff_cols = gate_weight.shape[1]
    qkv_cols = qkv_weight.shape[1]
    out_cols = out_weight.shape[0]
    group_width = 2 * qkv_cols
    query_width = group_width - 2 * HD

    bias_rows = jnp.pad(qkv_bias[None, :], ((0, 15), (0, 0)))
    first, second = turned_pairs(
        jnp.concatenate(
            [
                jnp.concatenate([qkv_weight, bias_rows], 0),
                jnp.pad(out_weight.T, ((0, 16), (0, 0))),
            ],
            1,
        )
    )
    low = jnp.where(sequence == 0, first, second)
    high = jnp.where(sequence == 0, second, first)
    qkv_own = jnp.concatenate([low[:, :qkv_cols], high[:, :qkv_cols]], 1)
    bias_full = qkv_own[deep : deep + 1].astype(f32)
    out_own = jnp.concatenate([low[:deep, qkv_cols:], high[:deep, qkv_cols:]], 1)
    out_own = jnp.pad(out_own, ((0, 0), (0, HD)))
    qkv_gather = Gather(qkv_own[:deep], bits)
    out_gather = Gather(out_own, bits)
    down_flipped = down_weight.T
    mlp_gathers = []
    for start, stop in cuts(ff_cols):
        padded = -(-(stop - start) // 256) * 256
        pieces = [
            jnp.pad(part[:, start:stop], ((0, 0), (0, padded - (stop - start))))
            for part in (gate_weight, up_weight, down_flipped)
        ]
        mlp_gathers.append(Gather(jnp.concatenate(pieces, 1), bits))
    place = jnp.arange(model_width, dtype=jnp.int32)
    masks = jnp.array([bit_reversed(p, bits) for p in range(row_count)], jnp.int32)
    source = jnp.repeat(masks ^ row, deep) * deep + place % deep
    to_stored = (place[:, None] == source[None, :]).astype(bf16)
    from_stored = (source[:, None] == place[None, :]).astype(bf16)

    def stored(block):
        return jnp.dot(block, to_stored, preferred_element_type=f32)

    def unstored(block):
        return jnp.dot(block, from_stored, preferred_element_type=f32).astype(bf16)

    def unstored_row(vector):
        blocks = vector.reshape(row_count, deep)
        blocks = jnp.concatenate(
            [blocks[bit_reversed(m, bits)][None] for m in range(row_count)], 0
        )
        for bit in range(bits):
            wide = blocks.reshape(-1, 2, 1 << bit, deep)
            turned = jnp.concatenate([wide[:, 1:], wide[:, :1]], 1).reshape(row_count, deep)
            blocks = jnp.where((row >> bit) % 2 == 1, turned, blocks)
        return blocks.reshape(model_width)

    input_rows = stored(after(layer_input, first, second))
    grad_out = stored(cotangent)
    gain_one = stored(gain_attn[None, :])
    gain_two = stored(gain_mlp[None, :])

    scale_one = lax.rsqrt(jnp.mean(input_rows * input_rows, axis=1) + eps)
    normed_own = (input_rows * scale_one[:, None] * gain_one).astype(bf16)
    normed_other = flip(normed_own, "col", 0)
    cosine, sine_part = rope_tables(length)
    grad_blocks = [grad_out.astype(bf16)]

    near, far = mlp_gathers
    n_four = near.double()
    n_own = near.send()
    a_own = qkv_gather.send()
    a_four = qkv_gather.double()
    a_two = qkv_gather.double(a_own)
    a_beside = qkv_gather.send(a_own)
    o_four = out_gather.double(a_four)
    a_last = qkv_gather.send(a_beside, n_own)
    qkv_pieces = qkv_gather.all()
    far.ready(a_two, o_four)
    f_four = far.double()
    o_two = out_gather.double(a_two)
    across = flip(after(grad_blocks[0], a_four), "col", 1)
    out_pieces = out_gather.finish(a_last, o_two)
    n_two = near.double(o_two)
    n_beside = near.send(a_last)
    qk_rows, value_rows, att_rows, log_totals = attend(
        parity,
        normed_own,
        normed_other,
        qkv_pieces,
        bias_full,
        cosine,
        sine_part,
    )
    n_last = near.send(att_rows)
    att_own, att_other = project(after(att_rows, n_beside, n_two, across, f_four), out_pieces)
    att_got = flip(att_other, "col", 0)
    grad_blocks.append(flip(after(grad_blocks[0], att_got), "col", 0))
    grad_blocks += [across, flip(after(across, att_got), "col", 0)]
    middle = input_rows + att_own + att_got.astype(f32)
    scale_two = lax.rsqrt(jnp.mean(middle * middle, axis=1) + eps)
    blocks = [(middle * scale_two[:, None] * gain_two).astype(bf16)]
    across = flip(blocks[0], "col", 1)
    blocks.append(flip(after(blocks[0], n_last), "col", 0))
    blocks += [across, flip(across, "col", 0)]

    f_beside = far.catch_up(n_last)
    f_two = far.double(blocks[2])
    f_last = far.send(f_beside)
    first_pieces, second_pieces = (gather.all() for gather in mlp_gathers)
    act_own, *sums_own = mlp([after(blocks[0], blocks[2]), blocks[1]], grad_blocks[:2], first_pieces)
    act_far, *sums_far = mlp(blocks[2:], grad_blocks[2:], first_pieces)
    sent_one, kept_one, sent_two, kept_two = outer(blocks, grad_blocks, [act_own, act_far])
    first_scatter = Scatter([(sent_one, kept_one), (sent_two, kept_two)], bits)
    start_far = after(blocks[2], kept_one)
    act_far, near_far, far_far = mlp(
        [start_far, blocks[3]], grad_blocks[2:], second_pieces, sums_far
    )
    far_far = after(far_far, *first_scatter.got)
    across = near_far.astype(f32) + flip(far_far, "col", 0).astype(f32)
    across = across.astype(bf16)
    normed_back = flip(across[0], "col", 1)
    act_own, near_own, far_own = mlp(
        [after(blocks[0], across), blocks[1]],
        grad_blocks[:2],
        second_pieces,
        sums_own,
    )
    first_scatter.step()
    beside = flip(after(far_own, normed_back, *first_scatter.got), "col", 0)
    first_scatter.step()
    down_back = flip(after(across[1], normed_back), "col", 1)

    def summed(k, back):
        return near_own[k].astype(f32) + beside[k].astype(f32) + back.astype(f32)

    second_whole = outer_whole(
        row.astype(jnp.int32).reshape(1),
        [after(blocks[0], near_own, *first_scatter.kept), *blocks[1:]],
        grad_blocks,
        [act_own, act_far],
        row_count,
    )
    second_total = lax.psum_scatter(second_whole, "row", scatter_dimension=0, tiled=True)
    grad_normed_two = summed(0, after(normed_back, second_whole))
    scaled_two = gain_two * grad_normed_two
    inner_two = jnp.sum(scaled_two * middle, axis=1)
    grad_middle = (
        grad_out
        + scale_two[:, None] * scaled_two
        - middle * (scale_two**3 * inner_two / model_width)[:, None]
    )
    gain_two_grad = jnp.sum(grad_normed_two * middle * scale_two[:, None], axis=0)
    branch_own = grad_middle.astype(bf16)
    branch_other = flip(branch_own, "col", 0)
    out_scatter = Scatter([outer_one([branch_own, branch_other], att_rows)], bits)
    split = qk_rows.shape[1] // 256
    mixed_first, bias_first, *carry = attend_back(
        parity,
        after(branch_own, out_scatter.kept[0]),
        branch_other,
        out_pieces,
        qk_rows,
        value_rows,
        log_totals,
        cosine,
        sine_part,
        0,
        split,
    )
    out_scatter.wait(mixed_first)
    out_scatter.step()
    mixed_last, bias_last = attend_back(
        parity,
        after(branch_own, out_scatter.kept[0]),
        branch_other,
        out_pieces,
        qk_rows,
        value_rows,
        log_totals,
        cosine,
        sine_part,
        split,
        2 * split,
        carry,
    )
    bias_grad = jnp.concatenate([bias_first, bias_last], 1)[0]
    grad_mixed = jnp.concatenate([mixed_first, mixed_last], 1)
    qkv_scatter = Scatter([outer_one([normed_own, normed_other], grad_mixed)], bits)
    passed = qkv_scatter.kept[0]
    out_scatter.wait(passed)
    first_scatter.wait(passed)
    first_total = first_scatter.total()
    layer_output = unstored((middle + summed(1, after(down_back, passed))).astype(bf16))
    qkv_full = jnp.concatenate(qkv_pieces, 0)
    grad_mixed = after(grad_mixed, passed)
    out_scatter.step()
    partial = jnp.einsum("tc,dc->td", grad_mixed, qkv_full, preferred_element_type=f32)
    grad_normed_one = partial[:tok_local] + flip(
        partial[tok_local:].astype(bf16), "col", 0
    ).astype(f32)
    scaled_one = gain_one * grad_normed_one
    inner_one = jnp.sum(scaled_one * input_rows, axis=1)
    input_grad = unstored(
        (
            grad_middle
            + scale_one[:, None] * scaled_one
            - input_rows * (scale_one**3 * inner_one / model_width)[:, None]
        ).astype(bf16)
    )
    gain_one_grad = jnp.sum(grad_normed_one * input_rows * scale_one[:, None], axis=0)

    def to_columns(total, width):
        low, high = total[:, :width].astype(bf16), total[:, width : 2 * width].astype(bf16)
        first, second = from_pairs(
            jnp.where(sequence == 0, low, high), jnp.where(sequence == 0, high, low)
        )
        return first.astype(f32) + second.astype(f32)

    bias_row = lax.dynamic_update_slice_in_dim(
        jnp.zeros((group_width * 2,), f32), bias_grad, core * group_width, 0
    )
    small = jnp.concatenate([unstored_row(gain_one_grad), unstored_row(gain_two_grad), bias_row])
    small = jnp.pad(small, (0, -small.shape[0] % 128)).reshape(-1, 128)
    for bit in range(2):
        small = small + flip(small, "col", bit)
    for bit in range(bits):
        small = small + flip(small, "row", bit)
    qkv_scatter.step()
    qkv_scatter.step()
    qkv_scatter.wait(small)
    qkv_total = to_columns(qkv_scatter.total(), qkv_cols)
    out_total = to_columns(out_scatter.total(), out_cols)
    mlp_totals = []
    for total, (start, stop) in zip(
        (first_total, after(second_total, small).astype(f32)), cuts(ff_cols)
    ):
        padded = total.shape[1] // 3
        mlp_totals.append(
            [total[:, k * padded : k * padded + stop - start] for k in range(3)]
        )
    gate_total, up_total, down_total = (jnp.concatenate(parts, 1) for parts in zip(*mlp_totals))
    small = small.reshape(-1)
    gain_one_total = small[:model_width]
    gain_two_total = small[model_width : 2 * model_width]
    bias_total = lax.dynamic_slice_in_dim(small, 2 * model_width + column * qkv_cols, qkv_cols, 0)
    return (
        layer_output,
        input_grad,
        gain_one_total,
        qkv_total,
        bias_total,
        out_total.T,
        gain_two_total,
        gate_total,
        up_total,
        down_total.T,
    )


def solution(mesh):
    in_specs = (
        P(("row", "col"), None),
        P(),
        P("row", "col"),
        P("col"),
        P("col", "row"),
        P(),
        P("row", "col"),
        P("row", "col"),
        P("col", "row"),
        P(("row", "col"), None),
    )
    out_specs = (
        P(("row", "col"), None),
        P(("row", "col"), None),
        P(),
        P("row", "col"),
        P("col"),
        P("col", "row"),
        P(),
        P("row", "col"),
        P("row", "col"),
        P("col", "row"),
    )
    return jax.shard_map(shards, mesh=mesh, in_specs=in_specs, out_specs=out_specs, check_vma=False)
```

```python
import functools
import math

import jax
import jax.numpy as jnp
from jax import lax
from jax.experimental import pallas as pl
from jax.experimental.pallas import tpu as pltpu
from jax.sharding import PartitionSpec as P

HD = 64
eps = 1e-06
theta_base = 1000000.0
bf16 = jnp.bfloat16
f32 = jnp.float32
NT = (((1,), (1,)), ((), ()))
TN = (((0,), (0,)), ((), ()))
MIB = 1024 * 1024


def flip(block, axis, bit):
    count = lax.axis_size(axis)
    return lax.ppermute(block, axis, [(i, i ^ 1 << bit) for i in range(count)])


def bit_reversed(value, bits):
    return sum((value >> b & 1) << (bits - 1 - b) for b in range(bits))


def after(value, *earlier):
    return lax.optimization_barrier((value, *earlier))[0]


def kernel_params(mib):
    return pltpu.CompilerParams(vmem_limit_bytes=mib * MIB)


def cost(flops, nbytes, exps=0):
    return pl.CostEstimate(
        flops=int(flops), bytes_accessed=int(nbytes), transcendentals=int(exps)
    )


def whole(array):
    return pl.BlockSpec(array.shape, lambda *_: (0,) * len(array.shape))


def in_place(block):
    return pl.BlockSpec(memory_space=pl.ANY)


def assemble(pieces, held, sems):
    copies = []
    at = 0
    for i, piece in enumerate(pieces):
        rows = piece.shape[0]
        copies.append(pltpu.make_async_copy(piece, held.at[pl.ds(at, rows)], sems.at[i]))
        at += rows
    for copy in copies:
        copy.start()
    for copy in copies:
        copy.wait()


def halves_turned(block):
    lane = lax.broadcasted_iota(jnp.int32, block.shape, 1)
    up = pltpu.roll(block, 128 - HD // 2, 1)
    return jnp.where(lane % HD < HD // 2, up, pltpu.roll(block, HD // 2, 1))


def side_rows(r, block, half, parity):
    side = (r // half) ^ parity
    return pl.ds(pl.multiple_of(side * half + r % half, block), block)


def pad_heads(key_value, rows, value, last):
    lane = lax.broadcasted_iota(jnp.int32, (1, 128), 1)
    kpad, vpad = key_value
    zero = jnp.zeros_like(value)
    vpad[0, rows, :] = jnp.concatenate([value, zero], 1).astype(bf16)
    vpad[1, rows, :] = jnp.concatenate([zero, value], 1).astype(bf16)
    kpad[1, rows, :] = jnp.where(lane >= HD, last, 0.0).astype(bf16)
    kpad[0, rows, :] = jnp.where(lane < HD, pltpu.roll(last, HD, 1), 0.0).astype(bf16)


def attend_kernel(parity_ref, own_ref, other_ref, bias_ref, cos_ref, sin_ref, *rest, block, count):
    pieces = rest[:count]
    qk_ref, v_ref, att_ref, lse_ref, held, kpad, vpad, lse_cols, sems = rest[count:]
    step = pl.program_id(0)
    half = own_ref.shape[0]
    length = 2 * half
    wide = qk_ref.shape[1]
    pairs = wide // 128
    parity = parity_ref[0]

    @pl.when(step == 0)
    def _():
        assemble(pieces, held, sems)
        for side, rows_ref in enumerate((own_ref, other_ref)):
            for r in range(0, half, block):
                at = pl.multiple_of((side ^ parity) * half + r, block)
                rows = pl.ds(at, block)
                mixed = jnp.dot(rows_ref[r : r + block, :], held[...], preferred_element_type=f32)
                mixed = (mixed + bias_ref[...]).astype(bf16).astype(f32)
                cos, sin = cos_ref[rows, :], sin_ref[rows, :]
                for p in range(pairs):
                    u = mixed[:, p * 128 : (p + 1) * 128]
                    turned = (u * cos + halves_turned(u) * sin).astype(bf16)
                    qk_ref[rows, p * 128 : (p + 1) * 128] = turned
                v_ref[rows, :] = mixed[:, wide:].astype(bf16)
                pad_heads((kpad, vpad), rows, mixed[:, wide:], turned.astype(f32))
        lse_cols[...] = jnp.zeros_like(lse_cols)

    factor = HD**-0.5 * math.log2(math.e)
    cols = pl.ds(pl.multiple_of(step * 128, 128), 128)
    row_i = lax.broadcasted_iota(jnp.int32, (block, block), 0)
    col_i = lax.broadcasted_iota(jnp.int32, (block, block), 1)
    for r in range(0, length, block):
        rows = pl.ds(r, block)
        to = side_rows(r, block, half, parity)
        q = qk_ref[rows, cols]

        def head(odd):
            keys = kpad[odd, : r + block, :]
            scores = lax.dot_general(q, keys, NT, preferred_element_type=f32)
            diag = jnp.where(col_i <= row_i, scores[:, r:], -1e30)
            scores = jnp.concatenate([scores[:, :r], diag], 1) if r else diag
            top = jnp.max(scores, 1, keepdims=True)
            e = jnp.exp2((scores - top) * factor)
            total = jnp.sum(e, 1, keepdims=True)
            out = jnp.dot(e.astype(bf16), vpad[odd, : r + block, :], preferred_element_type=f32)
            lse = top * factor + jnp.log2(total)
            at = lax.broadcasted_iota(jnp.int32, (1, 128), 1) == 2 * step + odd
            lse_cols[rows, :] = jnp.where(at, lse, lse_cols[rows, :])
            return out / total

        even = head(0)

        @pl.when(step < pairs - 1)
        def _():
            att_ref[to, :] = (even + head(1)).astype(bf16)

        @pl.when(step == pairs - 1)
        def _():
            att_ref[to, :] = even.astype(bf16)

    @pl.when(step == pairs - 1)
    def _():
        lse_ref[...] = lse_cols[...].T[: lse_ref.shape[0], :]


def attend(parity, own, other, pieces, bias, cos, sin):
    half, depth = own.shape
    length = 2 * half
    group = bias.shape[1]
    wide = group - HD
    pairs = wide // 128
    block = min(256, half)
    return pl.pallas_call(
        functools.partial(attend_kernel, block=block, count=len(pieces)),
        grid=(pairs,),
        in_specs=[pl.BlockSpec(memory_space=pltpu.SMEM)]
        + [whole(a) for a in (own, other, bias, cos, sin)]
        + [in_place(piece) for piece in pieces],
        out_specs=[
            pl.BlockSpec((length, wide), lambda p: (0, 0)),
            pl.BlockSpec((length, HD), lambda p: (0, 0)),
            pl.BlockSpec((length, 128), lambda p: (0, p)),
            pl.BlockSpec((8, length), lambda p: (0, 0)),
        ],
        out_shape=[
            jax.ShapeDtypeStruct((length, wide), bf16),
            jax.ShapeDtypeStruct((length, HD), bf16),
            jax.ShapeDtypeStruct((length, wide), bf16),
            jax.ShapeDtypeStruct((8, length), f32),
        ],
        scratch_shapes=[
            pltpu.VMEM((depth, group), bf16),
            pltpu.VMEM((2, length, 128), bf16),
            pltpu.VMEM((2, length, 128), bf16),
            pltpu.VMEM((length, 128), f32),
            pltpu.SemaphoreType.DMA((len(pieces),)),
        ],
        compiler_params=kernel_params(40),
        cost_estimate=cost(12e9, 8e6, 5e6),
    )(parity, own, other, bias, cos, sin, *pieces)


def project_kernel(att_ref, *rest, count):
    pieces = rest[:count]
    own_ref, other_ref, held, sems = rest[count:]
    half = own_ref.shape[0]
    assemble(pieces, held, sems)
    for side, ref in enumerate((own_ref, other_ref)):
        rows = att_ref[side * half : (side + 1) * half, :]
        ref[...] = lax.dot_general(rows, held[...], NT, preferred_element_type=f32).astype(ref.dtype)


def project(att, pieces):
    length, wide = att.shape
    depth = sum(piece.shape[0] for piece in pieces)
    return pl.pallas_call(
        functools.partial(project_kernel, count=len(pieces)),
        in_specs=[pl.BlockSpec(memory_space=pltpu.VMEM)] + [in_place(piece) for piece in pieces],
        out_specs=[pl.BlockSpec(memory_space=pltpu.VMEM)] * 2,
        out_shape=[
            jax.ShapeDtypeStruct((length // 2, depth), f32),
            jax.ShapeDtypeStruct((length // 2, depth), bf16),
        ],
        scratch_shapes=[
            pltpu.VMEM((depth, wide), bf16),
            pltpu.SemaphoreType.DMA((len(pieces),)),
        ],
        compiler_params=kernel_params(40),
        cost_estimate=cost(2 * length * depth * wide, 6e6),
    )(att, *pieces)


def attend_back_kernel(
    parity_ref,
    own_ref,
    other_ref,
    qk_ref,
    v_ref,
    lse_ref,
    cos_ref,
    sin_ref,
    *rest,
    block,
    count,
    first,
    last,
):
    pieces = rest[:count]
    if first == 0:
        mixed_ref, bias_ref, dk, dv, held, kpad, vpad, gatt, dq_acc, sems = rest[count:]
    else:
        dk_in, dv_in, mixed_ref, bias_ref, held, kpad, vpad, gatt, dq_acc, dk, dv, sems = rest[count:]
    step = pl.program_id(0) + first
    half_rows = own_ref.shape[0]
    length = 2 * half_rows
    wide = qk_ref.shape[1]
    pairs = wide // 128
    used = slice(first * 128, last * 128)
    parity = parity_ref[0]
    lane = lax.broadcasted_iota(jnp.int32, (1, 128), 1)

    @pl.when(step == first)
    def _():
        assemble(pieces, held, sems)
        for side, rows_ref in enumerate((own_ref, other_ref)):
            for r in range(0, half_rows, block):
                rows = pl.ds(pl.multiple_of((side ^ parity) * half_rows + r, block), block)
                got = jnp.dot(
                    rows_ref[r : r + block, :], held[:, used], preferred_element_type=f32
                )
                gatt[rows, :] = got.astype(bf16)
        for r in range(0, length, block):
            rows = pl.ds(r, block)
            keys = qk_ref[rows, wide - 128 :].astype(f32)
            pad_heads((kpad, vpad), rows, v_ref[rows, :].astype(f32), keys)
        dk[...] = dk_in[...] if first else jnp.zeros_like(dk)
        dv[...] = dv_in[...] if first else jnp.zeros_like(dv)

    factor = HD**-0.5 * math.log2(math.e)
    cols = pl.ds(pl.multiple_of(step * 128, 128), 128)
    here = pl.ds(pl.multiple_of((step - first) * 128, 128), 128)
    key_i = lax.broadcasted_iota(jnp.int32, (block, block), 0)
    query_i = lax.broadcasted_iota(jnp.int32, (block, block), 1)
    for r in range(0, length, block):
        rows = pl.ds(r, block)
        q = qk_ref[rows, cols]
        g = gatt[rows, here]

        def head(odd):
            lse = lse_ref[pl.ds(2 * step + odd, 1), rows]
            probs, grads = [], []
            inner = jnp.zeros((1, block), f32)
            for c in range(0, r + block, block):
                scores = lax.dot_general(
                    kpad[odd, c : c + block, :], q, NT, preferred_element_type=f32
                )
                p = jnp.exp2(scores * factor - lse)
                if c == r:
                    p = jnp.where(key_i <= query_i, p, 0.0)
                dp = lax.dot_general(vpad[odd, c : c + block, :], g, NT, preferred_element_type=f32)
                inner = inner + jnp.sum(p * dp, 0, keepdims=True)
                probs.append(p)
                grads.append(dp)
            dq = 0.0
            half = lane >= HD if odd else lane < HD
            for i, c in enumerate(range(0, r + block, block)):
                keys = pl.ds(c, block)
                ds = (probs[i] * (grads[i] - inner)).astype(bf16)
                p = probs[i].astype(bf16)
                dk[keys, :] += jnp.where(half, jnp.dot(ds, q, preferred_element_type=f32), 0.0)
                dv[keys, :] += jnp.where(half, jnp.dot(p, g, preferred_element_type=f32), 0.0)
                dq = dq + lax.dot_general(
                    ds, kpad[odd, c : c + block, :], TN, preferred_element_type=f32
                )
            return dq

        dq_acc[rows, :] = head(0)

        @pl.when(step < pairs - 1)
        def _():
            dq_acc[rows, :] += head(1)

    def back(u, rows):
        return u * cos_ref[rows, :] - halves_turned(u) * sin_ref[rows, :]

    scale = HD**-0.5
    for r in range(0, length, block):
        rows = pl.ds(r, block)
        to = side_rows(r, block, half_rows, parity)

        @pl.when(step < pairs - 1)
        def _():
            mixed_ref[to, here] = back(dq_acc[rows, :] * scale, rows).astype(bf16)

        if last == pairs:
            end = (last - first) * 128

            @pl.when(step == pairs - 1)
            def _():
                k = dk[rows, :]
                k = jnp.where(lane >= HD, k + pltpu.roll(k, HD, 1), dq_acc[rows, :]) * scale
                mixed_ref[to, end - 128 : end] = back(k, rows).astype(bf16)
                v = dv[rows, :]
                v = v + pltpu.roll(v, HD, 1)
                mixed_ref[to, end:] = v[:, :HD].astype(bf16)

    @pl.when(step == last - 1)
    def _():
        total = jnp.zeros((1, mixed_ref.shape[1]), f32)
        for r in range(0, length, block):
            part = mixed_ref[pl.ds(r, block), :].astype(f32)
            total = total + jnp.sum(part, 0, keepdims=True)
        bias_ref[...] = total


def attend_back(parity, own, other, pieces, qk, v, lse, cos, sin, first, last, earlier=()):
    half, depth = own.shape
    length = 2 * half
    wide = qk.shape[1]
    pairs = wide // 128
    group = (last - first) * 128 + (HD if last == pairs else 0)
    block = min(256, half)
    ins = (own, other, qk, v, lse, cos, sin)
    carried = pl.BlockSpec((length, 128), lambda p: (0, 0))
    carry = [jax.ShapeDtypeStruct((length, 128), f32)] * 2
    return pl.pallas_call(
        functools.partial(
            attend_back_kernel, block=block, count=len(pieces), first=first, last=last
        ),
        grid=(last - first,),
        in_specs=[pl.BlockSpec(memory_space=pltpu.SMEM)]
        + [whole(a) for a in ins]
        + [in_place(piece) for piece in pieces]
        + [carried] * len(earlier),
        out_specs=[
            pl.BlockSpec((length, group), lambda p: (0, 0)),
            pl.BlockSpec((1, group), lambda p: (0, 0)),
        ]
        + ([] if first else [carried] * 2),
        out_shape=[
            jax.ShapeDtypeStruct((length, group), bf16),
            jax.ShapeDtypeStruct((1, group), f32),
        ]
        + ([] if first else carry),
        scratch_shapes=[
            pltpu.VMEM((depth, wide), bf16),
            pltpu.VMEM((2, length, 128), bf16),
            pltpu.VMEM((2, length, 128), bf16),
            pltpu.VMEM((length, (last - first) * 128), bf16),
            pltpu.VMEM((length, 128), f32),
        ]
        + ([pltpu.VMEM((length, 128), f32)] * 2 if first else [])
        + [pltpu.SemaphoreType.DMA((len(pieces),))],
        compiler_params=kernel_params(50),
        cost_estimate=cost(12e9, 6e6, 3e6),
    )(parity, *ins, *pieces, *earlier)


def mlp_kernel(x0_ref, x1_ref, g0_ref, g1_ref, *rest, count, add):
    pieces = rest[:count]
    rest = rest[count:]
    if add:
        near_in, far_in, act_ref, near_ref, far_ref, held, sems = rest
    else:
        act_ref, near_ref, far_ref, held, sems = rest
    n = held.shape[1] // 3
    step = pl.program_id(0)

    @pl.when(step == 0)
    def _():
        assemble(pieces, held, sems)

    wg, wu, wd = (held[:, k * n : (k + 1) * n] for k in range(3))
    x = jnp.where(step == 0, x0_ref[...], x1_ref[...])
    g = jnp.where(step == 0, g0_ref[...], g1_ref[...])
    gate = jnp.dot(x, wg, preferred_element_type=f32)
    up = jnp.dot(x, wu, preferred_element_type=f32)
    gh = jnp.dot(g, wd, preferred_element_type=f32)
    sig = 1.0 / (1.0 + jnp.exp(-gate))
    silu = gate * sig
    hid = (silu * up).astype(bf16)
    ghs = gh * sig
    gg = (ghs * up * (1.0 + gate - silu)).astype(bf16)
    gu = (ghs * gate).astype(bf16)
    act_ref[:, :n] = gg
    act_ref[:, n : 2 * n] = gu
    act_ref[:, 2 * n :] = hid
    ngrad = lax.dot_general(gg, wg, NT, preferred_element_type=f32)
    ngrad = ngrad + lax.dot_general(gu, wu, NT, preferred_element_type=f32)
    down = lax.dot_general(hid, wd, NT, preferred_element_type=f32)

    @pl.when(step == 0)
    def _():
        near_ref[0] = (ngrad + near_in[0].astype(f32) if add else ngrad).astype(bf16)
        near_ref[1] = (down + near_in[1].astype(f32) if add else down).astype(bf16)

    @pl.when(step == 1)
    def _():
        far_ref[0] = (ngrad + far_in[0].astype(f32) if add else ngrad).astype(bf16)
        far_ref[1] = (down + far_in[1].astype(f32) if add else down).astype(bf16)


def mlp(rows, grads, pieces, sums=None):
    t, d = rows[0].shape
    columns = pieces[0].shape[1]
    add = sums is not None
    ins = (*rows, *grads)
    sums = tuple(sums or ())
    both = pl.BlockSpec((2, t, d), lambda i: (0, 0, 0))
    return pl.pallas_call(
        functools.partial(mlp_kernel, count=len(pieces), add=add),
        grid=(2,),
        in_specs=[whole(a) for a in ins] + [in_place(p) for p in pieces] + [both] * len(sums),
        out_specs=[pl.BlockSpec((t, columns), lambda i: (i, 0)), both, both],
        out_shape=[
            jax.ShapeDtypeStruct((2 * t, columns), bf16),
            jax.ShapeDtypeStruct((2, t, d), bf16),
            jax.ShapeDtypeStruct((2, t, d), bf16),
        ],
        scratch_shapes=[
            pltpu.VMEM((d, columns), bf16),
            pltpu.SemaphoreType.DMA((len(pieces),)),
        ],
        compiler_params=kernel_params(58),
        cost_estimate=cost(8 * t * d * columns, 30 * MIB, 2 * t * columns),
    )(*ins, *pieces, *sums)


def fill(sent_ref, kept_ref, lefts, rights, second):
    half = kept_ref.shape[0]
    t = lefts[0].shape[0]
    q = half // 2
    if second:
        parts = ((sent_ref, 0, q), (sent_ref, q, 3 * q), (kept_ref, 0, 0), (kept_ref, q, 2 * q))
        size = q
    else:
        parts = ((sent_ref, 0, half), (kept_ref, 0, 0))
        size = half
    for ref, to, start in parts:
        total = 0.0
        for i, left in enumerate(lefts):
            right = rights[i * t // rights[0].shape[0]]
            at = i * t % right.shape[0]
            total = total + lax.dot_general(
                left[:, start : start + size],
                right[at : at + t, :],
                TN,
                preferred_element_type=f32,
            )
        ref[to : to + size, :] = total.astype(ref.dtype)


def outer_kernel(*refs, blocks):
    rows, grads, rights = refs[:blocks], refs[blocks : 2 * blocks], refs[2 * blocks : -4]
    sent_one, kept_one, sent_two, kept_two = refs[-4:]
    step = pl.program_id(0)

    @pl.when(step < 2)
    def _():
        fill(sent_one, kept_one, rows, rights, False)

    @pl.when(step == 2)
    def _():
        fill(sent_two, kept_two, grads, rights, True)


def outer(rows, grads, acts):
    t, d = rows[0].shape
    tall, columns = acts[0].shape
    n = columns // 3
    flat = [*rows, *grads]
    one = pl.BlockSpec((d // 2, n), lambda k: (0, jnp.minimum(k, 1)))
    two = pl.BlockSpec((d // 2, n), lambda k: (0, 0))
    return pl.pallas_call(
        functools.partial(outer_kernel, blocks=len(rows)),
        grid=(3,),
        in_specs=[whole(left) for left in flat]
        + [pl.BlockSpec((tall, n), lambda k: (0, k)) for _ in acts],
        out_specs=[one, one, two, two],
        out_shape=[
            jax.ShapeDtypeStruct((d // 2, 2 * n), bf16),
            jax.ShapeDtypeStruct((d // 2, 2 * n), f32),
            jax.ShapeDtypeStruct((d // 2, n), bf16),
            jax.ShapeDtypeStruct((d // 2, n), f32),
        ],
        compiler_params=kernel_params(58),
        cost_estimate=cost(2 * t * len(rows) * d * columns, 20 * MIB),
    )(*flat, *acts)


def outer_whole_kernel(row_ref, *refs, blocks, count, moved):
    rows, grads, rights, out_ref = refs[:blocks], refs[blocks : 2 * blocks], refs[2 * blocks : -1], refs[-1]
    step = pl.program_id(0)
    t, d = rows[0].shape
    deep = d // count
    bits = count.bit_length() - 1

    def product(lefts):
        for part in range(2):
            start = part * (d // 2)
            total = 0.0
            for i, left in enumerate(lefts):
                right = rights[i * t // rights[0].shape[0]]
                at = i * t % right.shape[0]
                total = total + lax.dot_general(
                    left[:, start : start + d // 2],
                    right[at : at + t, :],
                    TN,
                    preferred_element_type=f32,
                )
            total = total.astype(bf16)
            if not moved:
                out_ref[start : start + d // 2, :] = total
                continue
            for p in range(part * count // 2, (part + 1) * count // 2):
                to = (row_ref[0] ^ bit_reversed(p, bits)) * deep
                here = p * deep - start
                out_ref[pl.ds(pl.multiple_of(to, 16), deep), :] = total[here : here + deep]

    @pl.when(step < 2)
    def _():
        product(rows)

    @pl.when(step == 2)
    def _():
        product(grads)


def outer_whole(row, rows, grads, acts, count):
    t, d = rows[0].shape
    tall, columns = acts[0].shape
    n = columns // 3
    flat = [*rows, *grads]
    deep = d // count
    bits = count.bit_length() - 1
    moved = deep % 16 == 0
    out = pl.pallas_call(
        functools.partial(outer_whole_kernel, blocks=len(rows), count=count, moved=moved),
        grid=(3,),
        in_specs=[pl.BlockSpec(memory_space=pltpu.SMEM)]
        + [whole(left) for left in flat]
        + [pl.BlockSpec((tall, n), lambda k: (0, k)) for _ in acts],
        out_specs=pl.BlockSpec((d, n), lambda k: (0, k)),
        out_shape=jax.ShapeDtypeStruct((d, columns), bf16),
        compiler_params=kernel_params(58),
        cost_estimate=cost(2 * t * len(rows) * d * columns, 20 * MIB),
    )(row, *flat, *acts)
    if moved:
        return out
    places = jnp.array([bit_reversed(m, bits) for m in range(count)], jnp.int32)
    order = places[jnp.arange(count, dtype=jnp.int32) ^ row[0]]
    return out.reshape(count, deep, columns)[order].reshape(d, columns)


def outer_one_kernel(*refs):
    fill(refs[-2], refs[-1], refs[:-3], refs[-3:-2], False)


def outer_one(lefts, right):
    t, d = lefts[0].shape
    columns = right.shape[1]
    vmem = pl.BlockSpec(memory_space=pltpu.VMEM)
    return pl.pallas_call(
        outer_one_kernel,
        in_specs=[vmem] * (len(lefts) + 1),
        out_specs=[vmem] * 2,
        out_shape=[
            jax.ShapeDtypeStruct((d // 2, columns), bf16),
            jax.ShapeDtypeStruct((d // 2, columns), f32),
        ],
        compiler_params=kernel_params(40),
        cost_estimate=cost(2 * t * len(lefts) * d * columns, 6 * MIB),
    )(*lefts, right)


def rope_tables(length):
    inverse = theta_base ** (-(jnp.arange(HD // 2, dtype=f32) * 2.0 / HD))
    angles = jnp.arange(length, dtype=f32)[:, None] * inverse[None, :]
    c, s = jnp.cos(angles), jnp.sin(angles)
    return jnp.concatenate([c] * 4, 1), jnp.concatenate([-s, s, -s, s], 1)


class Gather:
    def __init__(self, block, bits):
        self.bits = bits
        self.left = bits - 1
        self.pieces = [block]
        self.sent = 0
        self.beside = []

    def ready(self, *earlier):
        self.pieces[-1] = after(self.pieces[-1], *earlier)

    def double(self, *earlier):
        held = jnp.concatenate(self.pieces, 0) if len(self.pieces) > 1 else self.pieces[0]
        self.pieces.append(flip(after(held, *earlier) if earlier else held, "row", self.left))
        self.left -= 1
        return self.pieces[-1]

    def send(self, *earlier):
        piece = self.pieces[self.sent]
        self.sent += 1
        self.beside.append(flip(after(piece, *earlier) if earlier else piece, "row", 0))
        return self.beside[-1]

    def catch_up(self, *earlier):
        rest = jnp.concatenate(self.pieces[self.sent :], 0)
        self.sent = len(self.pieces)
        self.beside.append(flip(after(rest, *earlier), "row", 0))
        return self.beside[-1]

    def finish(self, *earlier):
        while self.left > 0:
            self.double()
        self.catch_up(*earlier)
        out = self.pieces + self.beside
        return out if out[0].shape[0] % 16 == 0 else [jnp.concatenate(out, 0)]

    def all(self):
        while self.left > 0:
            self.double()
        while self.sent < len(self.pieces):
            self.send()
        out = self.pieces + self.beside
        return out if out[0].shape[0] % 16 == 0 else [jnp.concatenate(out, 0)]


class Scatter:
    def __init__(self, parts, bits):
        self.bits = bits
        self.orders = [[0, 1], [1, 0]][: len(parts)]
        self.kept = [kept for _, kept in parts]
        self.done = 0
        self.start([sent for sent, _ in parts])

    def start(self, sents):
        bits = [order[self.done] if self.done < 2 else self.done for order in self.orders]
        self.got = [flip(sent, "row", bit) for sent, bit in zip(sents, bits)]

    def wait(self, *earlier):
        self.got = [after(got, *earlier) for got in self.got]

    def step(self):
        if self.done == self.bits - 1:
            return
        self.done += 1
        half = self.kept[0].shape[0] // 2
        sents = [
            (kept[half:] + got[half:].astype(f32)).astype(bf16)
            for kept, got in zip(self.kept, self.got)
        ]
        self.kept = [kept[:half] + got[:half].astype(f32) for kept, got in zip(self.kept, self.got)]
        if self.done == 2:
            sents = [jnp.concatenate(sents, 1)]
            self.kept = [jnp.concatenate(self.kept, 1)]
        self.start(sents)

    def total(self):
        while self.done < self.bits - 1:
            self.step()
        totals = [kept + got.astype(f32) for kept, got in zip(self.kept, self.got)]
        return jnp.concatenate(totals, 1)


def turned_pairs(block):
    first = [(2 * a + b, 2 * b + a) for a in range(2) for b in range(2)]
    second = [(2 * a + b, 2 * (1 - b) + a) for a in range(2) for b in range(2)]
    return lax.ppermute(block, "col", first), lax.ppermute(block, "col", second)


def from_pairs(same, other):
    first = [(2 * a + b, 2 * b + a) for a in range(2) for b in range(2)]
    second = [(2 * a + b, 2 * b + 1 - a) for a in range(2) for b in range(2)]
    return lax.ppermute(same, "col", first), lax.ppermute(other, "col", second)


def cuts(width):
    first = min(512, width)
    return [(0, first), (first, width)] if first < width else [(0, width)]


def shards(
    layer_input,
    gain_attn,
    qkv_weight,
    qkv_bias,
    out_weight,
    gain_mlp,
    gate_weight,
    up_weight,
    down_weight,
    cotangent,
):
    row = lax.axis_index("row")
    column = lax.axis_index("col")
    row_count = lax.axis_size("row")
    bits = row_count.bit_length() - 1
    core = column % 2
    sequence = column // 2
    parity = core.astype(jnp.int32).reshape(1)
    tok_local, model_width = layer_input.shape
    length = tok_local * 2
    deep = model_width // row_count
    ff_cols = gate_weight.shape[1]
    qkv_cols = qkv_weight.shape[1]
    out_cols = out_weight.shape[0]
    group_width = 2 * qkv_cols
    query_width = group_width - 2 * HD

    bias_rows = jnp.pad(qkv_bias[None, :], ((0, 15), (0, 0)))
    first, second = turned_pairs(
        jnp.concatenate(
            [
                jnp.concatenate([qkv_weight, bias_rows], 0),
                jnp.pad(out_weight.T, ((0, 16), (0, 0))),
            ],
            1,
        )
    )
    low = jnp.where(sequence == 0, first, second)
    high = jnp.where(sequence == 0, second, first)
    qkv_own = jnp.concatenate([low[:, :qkv_cols], high[:, :qkv_cols]], 1)
    bias_full = qkv_own[deep : deep + 1].astype(f32)
    out_own = jnp.concatenate([low[:deep, qkv_cols:], high[:deep, qkv_cols:]], 1)
    out_own = jnp.pad(out_own, ((0, 0), (0, HD)))
    qkv_gather = Gather(qkv_own[:deep], bits)
    out_gather = Gather(out_own, bits)
    down_flipped = down_weight.T
    mlp_gathers = []
    for start, stop in cuts(ff_cols):
        padded = -(-(stop - start) // 256) * 256
        pieces = [
            jnp.pad(part[:, start:stop], ((0, 0), (0, padded - (stop - start))))
            for part in (gate_weight, up_weight, down_flipped)
        ]
        mlp_gathers.append(Gather(jnp.concatenate(pieces, 1), bits))
    place = jnp.arange(model_width, dtype=jnp.int32)
    masks = jnp.array([bit_reversed(p, bits) for p in range(row_count)], jnp.int32)
    source = jnp.repeat(masks ^ row, deep) * deep + place % deep
    to_stored = (place[:, None] == source[None, :]).astype(bf16)
    from_stored = (source[:, None] == place[None, :]).astype(bf16)

    def stored(block):
        return jnp.dot(block, to_stored, preferred_element_type=f32)

    def unstored(block):
        return jnp.dot(block, from_stored, preferred_element_type=f32).astype(bf16)

    def unstored_row(vector):
        blocks = vector.reshape(row_count, deep)
        blocks = jnp.concatenate(
            [blocks[bit_reversed(m, bits)][None] for m in range(row_count)], 0
        )
        for bit in range(bits):
            wide = blocks.reshape(-1, 2, 1 << bit, deep)
            turned = jnp.concatenate([wide[:, 1:], wide[:, :1]], 1).reshape(row_count, deep)
            blocks = jnp.where((row >> bit) % 2 == 1, turned, blocks)
        return blocks.reshape(model_width)

    input_rows = stored(after(layer_input, first, second))
    gain_one = stored(gain_attn[None, :])
    gain_two = stored(gain_mlp[None, :])

    scale_one = lax.rsqrt(jnp.mean(input_rows * input_rows, axis=1) + eps)
    normed_own = (input_rows * scale_one[:, None] * gain_one).astype(bf16)
    normed_other = flip(normed_own, "col", 0)
    cosine, sine_part = rope_tables(length)

    near, far = mlp_gathers
    n_four = near.double()
    n_own = near.send()
    a_own = qkv_gather.send()
    a_four = qkv_gather.double()
    a_two = qkv_gather.double(a_own)
    a_beside = qkv_gather.send(a_own)
    o_four = out_gather.double(a_two)
    a_last = qkv_gather.send(a_beside, n_own)
    qkv_pieces = qkv_gather.all()
    far.ready(a_two, o_four)
    f_four = far.double()
    o_two = out_gather.double(a_two)
    grad_out = stored(after(cotangent, a_four))
    grad_blocks = [grad_out.astype(bf16)]
    across = flip(grad_blocks[0], "col", 1)
    out_pieces = out_gather.finish(a_last, o_two)
    n_two = near.double(o_two)
    n_beside = near.send(a_last)
    qk_rows, value_rows, att_rows, log_totals = attend(
        parity,
        normed_own,
        normed_other,
        qkv_pieces,
        bias_full,
        cosine,
        sine_part,
    )
    n_last = near.send(att_rows)
    att_own, att_other = project(after(att_rows, n_beside, n_two, across, f_four), out_pieces)
    att_got = flip(att_other, "col", 0)
    grad_blocks.append(flip(after(grad_blocks[0], att_got), "col", 0))
    grad_blocks += [across, flip(after(across, att_got), "col", 0)]
    middle = input_rows + att_own + att_got.astype(f32)
    scale_two = lax.rsqrt(jnp.mean(middle * middle, axis=1) + eps)
    blocks = [(middle * scale_two[:, None] * gain_two).astype(bf16)]
    across = flip(blocks[0], "col", 1)
    blocks.append(flip(after(blocks[0], n_last), "col", 0))
    blocks += [across, flip(across, "col", 0)]

    f_beside = far.catch_up(n_last)
    f_two = far.double(blocks[2])
    f_last = far.send(f_beside)
    first_pieces, second_pieces = (gather.all() for gather in mlp_gathers)
    act_own, *sums_own = mlp([after(blocks[0], blocks[2]), blocks[1]], grad_blocks[:2], first_pieces)
    act_far, *sums_far = mlp(blocks[2:], grad_blocks[2:], first_pieces)
    sent_one, kept_one, sent_two, kept_two = outer(blocks, grad_blocks, [act_own, act_far])
    first_scatter = Scatter([(sent_one, kept_one), (sent_two, kept_two)], bits)
    start_far = after(blocks[2], kept_one)
    act_far, near_far, far_far = mlp(
        [start_far, blocks[3]], grad_blocks[2:], second_pieces, sums_far
    )
    far_far = after(far_far, *first_scatter.got)
    across = near_far.astype(f32) + flip(far_far, "col", 0).astype(f32)
    across = across.astype(bf16)
    normed_back = flip(across[0], "col", 1)
    act_own, near_own, far_own = mlp(
        [after(blocks[0], across), blocks[1]],
        grad_blocks[:2],
        second_pieces,
        sums_own,
    )
    first_scatter.step()
    beside = flip(after(far_own, normed_back, *first_scatter.got), "col", 0)
    first_scatter.step()
    down_back = flip(after(across[1], normed_back), "col", 1)

    def summed(k, back):
        return near_own[k].astype(f32) + beside[k].astype(f32) + back.astype(f32)

    second_whole = outer_whole(
        row.astype(jnp.int32).reshape(1),
        [after(blocks[0], near_own, *first_scatter.kept), *blocks[1:]],
        grad_blocks,
        [act_own, act_far],
        row_count,
    )
    second_total = lax.psum_scatter(second_whole, "row", scatter_dimension=0, tiled=True)
    grad_normed_two = summed(0, after(normed_back, second_whole))
    scaled_two = gain_two * grad_normed_two
    inner_two = jnp.sum(scaled_two * middle, axis=1)
    grad_middle = (
        grad_out
        + scale_two[:, None] * scaled_two
        - middle * (scale_two**3 * inner_two / model_width)[:, None]
    )
    gain_two_grad = jnp.sum(grad_normed_two * middle * scale_two[:, None], axis=0)
    branch_own = grad_middle.astype(bf16)
    branch_other = flip(branch_own, "col", 0)
    out_scatter = Scatter([outer_one([branch_own, branch_other], att_rows)], bits)
    split = qk_rows.shape[1] // 256
    mixed_first, bias_first, *carry = attend_back(
        parity,
        after(branch_own, out_scatter.kept[0]),
        branch_other,
        out_pieces,
        qk_rows,
        value_rows,
        log_totals,
        cosine,
        sine_part,
        0,
        split,
    )
    out_scatter.wait(mixed_first)
    out_scatter.step()
    mixed_last, bias_last = attend_back(
        parity,
        after(branch_own, out_scatter.kept[0]),
        branch_other,
        out_pieces,
        qk_rows,
        value_rows,
        log_totals,
        cosine,
        sine_part,
        split,
        2 * split,
        carry,
    )
    bias_grad = jnp.concatenate([bias_first, bias_last], 1)[0]
    grad_mixed = jnp.concatenate([mixed_first, mixed_last], 1)
    qkv_scatter = Scatter([outer_one([normed_own, normed_other], grad_mixed)], bits)
    passed = qkv_scatter.kept[0]
    out_scatter.wait(passed)
    first_scatter.wait(passed)
    first_total = first_scatter.total()
    layer_output = unstored((middle + summed(1, after(down_back, passed))).astype(bf16))
    qkv_full = jnp.concatenate(qkv_pieces, 0)
    grad_mixed = after(grad_mixed, passed)
    partial = jnp.einsum("tc,dc->td", grad_mixed, qkv_full, preferred_element_type=f32)
    grad_normed_one = partial[:tok_local] + flip(
        partial[tok_local:].astype(bf16), "col", 0
    ).astype(f32)
    scaled_one = gain_one * grad_normed_one
    inner_one = jnp.sum(scaled_one * input_rows, axis=1)
    input_grad = unstored(
        (
            grad_middle
            + scale_one[:, None] * scaled_one
            - input_rows * (scale_one**3 * inner_one / model_width)[:, None]
        ).astype(bf16)
    )
    gain_one_grad = jnp.sum(grad_normed_one * input_rows * scale_one[:, None], axis=0)

    def to_columns(total, width):
        low, high = total[:, :width].astype(bf16), total[:, width : 2 * width].astype(bf16)
        first, second = from_pairs(
            jnp.where(sequence == 0, low, high), jnp.where(sequence == 0, high, low)
        )
        return first.astype(f32) + second.astype(f32)

    bias_row = lax.dynamic_update_slice_in_dim(
        jnp.zeros((group_width * 2,), f32), bias_grad, core * group_width, 0
    )
    small = jnp.concatenate([unstored_row(gain_one_grad), unstored_row(gain_two_grad), bias_row])
    small = jnp.pad(small, (0, -small.shape[0] % 128)).reshape(-1, 128)
    for bit in range(2):
        small = small + flip(small, "col", bit)
    for bit in range(bits):
        small = small + flip(small, "row", bit)
    out_scatter.wait(*qkv_scatter.got)
    out_scatter.step()
    qkv_scatter.step()
    out_total = to_columns(out_scatter.total(), out_cols)
    qkv_scatter.step()
    qkv_scatter.wait(small)
    qkv_total = to_columns(qkv_scatter.total(), qkv_cols)
    mlp_totals = []
    for total, (start, stop) in zip(
        (first_total, after(second_total, small).astype(f32)), cuts(ff_cols)
    ):
        padded = total.shape[1] // 3
        mlp_totals.append(
            [total[:, k * padded : k * padded + stop - start] for k in range(3)]
        )
    gate_total, up_total, down_total = (jnp.concatenate(parts, 1) for parts in zip(*mlp_totals))
    small = small.reshape(-1)
    gain_one_total = small[:model_width]
    gain_two_total = small[model_width : 2 * model_width]
    bias_total = lax.dynamic_slice_in_dim(small, 2 * model_width + column * qkv_cols, qkv_cols, 0)
    return (
        layer_output,
        input_grad,
        gain_one_total,
        qkv_total,
        bias_total,
        out_total.T,
        gain_two_total,
        gate_total,
        up_total,
        down_total.T,
    )


def solution(mesh):
    in_specs = (
        P(("row", "col"), None),
        P(),
        P("row", "col"),
        P("col"),
        P("col", "row"),
        P(),
        P("row", "col"),
        P("row", "col"),
        P("col", "row"),
        P(("row", "col"), None),
    )
    out_specs = (
        P(("row", "col"), None),
        P(("row", "col"), None),
        P(),
        P("row", "col"),
        P("col"),
        P("col", "row"),
        P(),
        P("row", "col"),
        P("row", "col"),
        P("col", "row"),
    )
    return jax.shard_map(shards, mesh=mesh, in_specs=in_specs, out_specs=out_specs, check_vma=False)
```

```python
import functools
import math

import jax
import jax.numpy as jnp
from jax import lax
from jax.experimental import pallas as pl
from jax.experimental.pallas import tpu as pltpu
from jax.sharding import PartitionSpec as P

HD = 64
eps = 1e-06
theta_base = 1000000.0
bf16 = jnp.bfloat16
f32 = jnp.float32
NT = (((1,), (1,)), ((), ()))
TN = (((0,), (0,)), ((), ()))
MIB = 1024 * 1024


def flip(block, axis, bit):
    count = lax.axis_size(axis)
    return lax.ppermute(block, axis, [(i, i ^ 1 << bit) for i in range(count)])


def bit_reversed(value, bits):
    return sum((value >> b & 1) << (bits - 1 - b) for b in range(bits))


def after(value, *earlier):
    return lax.optimization_barrier((value, *earlier))[0]


def kernel_params(mib):
    return pltpu.CompilerParams(vmem_limit_bytes=mib * MIB)


def cost(flops, nbytes, exps=0):
    return pl.CostEstimate(
        flops=int(flops), bytes_accessed=int(nbytes), transcendentals=int(exps)
    )


def whole(array):
    return pl.BlockSpec(array.shape, lambda *_: (0,) * len(array.shape))


def in_place(block):
    return pl.BlockSpec(memory_space=pl.ANY)


def assemble(pieces, held, sems):
    copies = []
    at = 0
    for i, piece in enumerate(pieces):
        rows = piece.shape[0]
        copies.append(pltpu.make_async_copy(piece, held.at[pl.ds(at, rows)], sems.at[i]))
        at += rows
    for copy in copies:
        copy.start()
    for copy in copies:
        copy.wait()


def halves_turned(block):
    lane = lax.broadcasted_iota(jnp.int32, block.shape, 1)
    up = pltpu.roll(block, 128 - HD // 2, 1)
    return jnp.where(lane % HD < HD // 2, up, pltpu.roll(block, HD // 2, 1))


def side_rows(r, block, half, parity):
    side = (r // half) ^ parity
    return pl.ds(pl.multiple_of(side * half + r % half, block), block)


def pad_heads(key_value, rows, value, last):
    lane = lax.broadcasted_iota(jnp.int32, (1, 128), 1)
    kpad, vpad = key_value
    zero = jnp.zeros_like(value)
    vpad[0, rows, :] = jnp.concatenate([value, zero], 1).astype(bf16)
    vpad[1, rows, :] = jnp.concatenate([zero, value], 1).astype(bf16)
    kpad[1, rows, :] = jnp.where(lane >= HD, last, 0.0).astype(bf16)
    kpad[0, rows, :] = jnp.where(lane < HD, pltpu.roll(last, HD, 1), 0.0).astype(bf16)


def attend_kernel(parity_ref, own_ref, other_ref, bias_ref, cos_ref, sin_ref, *rest, block, count):
    pieces = rest[:count]
    qk_ref, v_ref, att_ref, lse_ref, held, kpad, vpad, lse_cols, sems = rest[count:]
    step = pl.program_id(0)
    half = own_ref.shape[0]
    length = 2 * half
    wide = qk_ref.shape[1]
    pairs = wide // 128
    parity = parity_ref[0]

    @pl.when(step == 0)
    def _():
        assemble(pieces, held, sems)
        for side, rows_ref in enumerate((own_ref, other_ref)):
            for r in range(0, half, block):
                at = pl.multiple_of((side ^ parity) * half + r, block)
                rows = pl.ds(at, block)
                mixed = jnp.dot(rows_ref[r : r + block, :], held[...], preferred_element_type=f32)
                mixed = (mixed + bias_ref[...]).astype(bf16).astype(f32)
                cos, sin = cos_ref[rows, :], sin_ref[rows, :]
                for p in range(pairs):
                    u = mixed[:, p * 128 : (p + 1) * 128]
                    turned = (u * cos + halves_turned(u) * sin).astype(bf16)
                    qk_ref[rows, p * 128 : (p + 1) * 128] = turned
                v_ref[rows, :] = mixed[:, wide:].astype(bf16)
                pad_heads((kpad, vpad), rows, mixed[:, wide:], turned.astype(f32))
        lse_cols[...] = jnp.zeros_like(lse_cols)

    factor = HD**-0.5 * math.log2(math.e)
    cols = pl.ds(pl.multiple_of(step * 128, 128), 128)
    row_i = lax.broadcasted_iota(jnp.int32, (block, block), 0)
    col_i = lax.broadcasted_iota(jnp.int32, (block, block), 1)
    for r in range(0, length, block):
        rows = pl.ds(r, block)
        to = side_rows(r, block, half, parity)
        q = qk_ref[rows, cols]

        def head(odd):
            keys = kpad[odd, : r + block, :]
            scores = lax.dot_general(q, keys, NT, preferred_element_type=f32)
            diag = jnp.where(col_i <= row_i, scores[:, r:], -1e30)
            scores = jnp.concatenate([scores[:, :r], diag], 1) if r else diag
            top = jnp.max(scores, 1, keepdims=True)
            e = jnp.exp2((scores - top) * factor)
            total = jnp.sum(e, 1, keepdims=True)
            out = jnp.dot(e.astype(bf16), vpad[odd, : r + block, :], preferred_element_type=f32)
            lse = top * factor + jnp.log2(total)
            at = lax.broadcasted_iota(jnp.int32, (1, 128), 1) == 2 * step + odd
            lse_cols[rows, :] = jnp.where(at, lse, lse_cols[rows, :])
            return out / total

        even = head(0)

        @pl.when(step < pairs - 1)
        def _():
            att_ref[to, :] = (even + head(1)).astype(bf16)

        @pl.when(step == pairs - 1)
        def _():
            att_ref[to, :] = even.astype(bf16)

    @pl.when(step == pairs - 1)
    def _():
        lse_ref[...] = lse_cols[...].T[: lse_ref.shape[0], :]


def attend(parity, own, other, pieces, bias, cos, sin):
    half, depth = own.shape
    length = 2 * half
    group = bias.shape[1]
    wide = group - HD
    pairs = wide // 128
    block = min(256, half)
    return pl.pallas_call(
        functools.partial(attend_kernel, block=block, count=len(pieces)),
        grid=(pairs,),
        in_specs=[pl.BlockSpec(memory_space=pltpu.SMEM)]
        + [whole(a) for a in (own, other, bias, cos, sin)]
        + [in_place(piece) for piece in pieces],
        out_specs=[
            pl.BlockSpec((length, wide), lambda p: (0, 0)),
            pl.BlockSpec((length, HD), lambda p: (0, 0)),
            pl.BlockSpec((length, 128), lambda p: (0, p)),
            pl.BlockSpec((8, length), lambda p: (0, 0)),
        ],
        out_shape=[
            jax.ShapeDtypeStruct((length, wide), bf16),
            jax.ShapeDtypeStruct((length, HD), bf16),
            jax.ShapeDtypeStruct((length, wide), bf16),
            jax.ShapeDtypeStruct((8, length), f32),
        ],
        scratch_shapes=[
            pltpu.VMEM((depth, group), bf16),
            pltpu.VMEM((2, length, 128), bf16),
            pltpu.VMEM((2, length, 128), bf16),
            pltpu.VMEM((length, 128), f32),
            pltpu.SemaphoreType.DMA((len(pieces),)),
        ],
        compiler_params=kernel_params(40),
        cost_estimate=cost(12e9, 8e6, 5e6),
    )(parity, own, other, bias, cos, sin, *pieces)


def project_kernel(att_ref, *rest, count):
    pieces = rest[:count]
    own_ref, other_ref, held, sems = rest[count:]
    half = own_ref.shape[0]
    assemble(pieces, held, sems)
    for side, ref in enumerate((own_ref, other_ref)):
        rows = att_ref[side * half : (side + 1) * half, :]
        ref[...] = lax.dot_general(rows, held[...], NT, preferred_element_type=f32).astype(ref.dtype)


def project(att, pieces):
    length, wide = att.shape
    depth = sum(piece.shape[0] for piece in pieces)
    return pl.pallas_call(
        functools.partial(project_kernel, count=len(pieces)),
        in_specs=[pl.BlockSpec(memory_space=pltpu.VMEM)] + [in_place(piece) for piece in pieces],
        out_specs=[pl.BlockSpec(memory_space=pltpu.VMEM)] * 2,
        out_shape=[
            jax.ShapeDtypeStruct((length // 2, depth), f32),
            jax.ShapeDtypeStruct((length // 2, depth), bf16),
        ],
        scratch_shapes=[
            pltpu.VMEM((depth, wide), bf16),
            pltpu.SemaphoreType.DMA((len(pieces),)),
        ],
        compiler_params=kernel_params(40),
        cost_estimate=cost(2 * length * depth * wide, 6e6),
    )(att, *pieces)


def attend_back_kernel(
    parity_ref,
    own_ref,
    other_ref,
    qk_ref,
    v_ref,
    lse_ref,
    cos_ref,
    sin_ref,
    *rest,
    block,
    count,
    first,
    last,
):
    pieces = rest[:count]
    if first == 0:
        mixed_ref, bias_ref, dk, dv, held, kpad, vpad, gatt, dq_acc, sems = rest[count:]
    else:
        dk_in, dv_in, mixed_ref, bias_ref, held, kpad, vpad, gatt, dq_acc, dk, dv, sems = rest[count:]
    step = pl.program_id(0) + first
    half_rows = own_ref.shape[0]
    length = 2 * half_rows
    wide = qk_ref.shape[1]
    pairs = wide // 128
    used = slice(first * 128, last * 128)
    parity = parity_ref[0]
    lane = lax.broadcasted_iota(jnp.int32, (1, 128), 1)

    @pl.when(step == first)
    def _():
        assemble(pieces, held, sems)
        for side, rows_ref in enumerate((own_ref, other_ref)):
            for r in range(0, half_rows, block):
                rows = pl.ds(pl.multiple_of((side ^ parity) * half_rows + r, block), block)
                got = jnp.dot(
                    rows_ref[r : r + block, :], held[:, used], preferred_element_type=f32
                )
                gatt[rows, :] = got.astype(bf16)
        for r in range(0, length, block):
            rows = pl.ds(r, block)
            keys = qk_ref[rows, wide - 128 :].astype(f32)
            pad_heads((kpad, vpad), rows, v_ref[rows, :].astype(f32), keys)
        dk[...] = dk_in[...] if first else jnp.zeros_like(dk)
        dv[...] = dv_in[...] if first else jnp.zeros_like(dv)

    factor = HD**-0.5 * math.log2(math.e)
    cols = pl.ds(pl.multiple_of(step * 128, 128), 128)
    here = pl.ds(pl.multiple_of((step - first) * 128, 128), 128)
    key_i = lax.broadcasted_iota(jnp.int32, (block, block), 0)
    query_i = lax.broadcasted_iota(jnp.int32, (block, block), 1)
    for r in range(0, length, block):
        rows = pl.ds(r, block)
        q = qk_ref[rows, cols]
        g = gatt[rows, here]

        def head(odd):
            lse = lse_ref[pl.ds(2 * step + odd, 1), rows]
            probs, grads = [], []
            inner = jnp.zeros((1, block), f32)
            for c in range(0, r + block, block):
                scores = lax.dot_general(
                    kpad[odd, c : c + block, :], q, NT, preferred_element_type=f32
                )
                p = jnp.exp2(scores * factor - lse)
                if c == r:
                    p = jnp.where(key_i <= query_i, p, 0.0)
                dp = lax.dot_general(vpad[odd, c : c + block, :], g, NT, preferred_element_type=f32)
                inner = inner + jnp.sum(p * dp, 0, keepdims=True)
                probs.append(p)
                grads.append(dp)
            dq = 0.0
            half = lane >= HD if odd else lane < HD
            for i, c in enumerate(range(0, r + block, block)):
                keys = pl.ds(c, block)
                ds = (probs[i] * (grads[i] - inner)).astype(bf16)
                p = probs[i].astype(bf16)
                dk[keys, :] += jnp.where(half, jnp.dot(ds, q, preferred_element_type=f32), 0.0)
                dv[keys, :] += jnp.where(half, jnp.dot(p, g, preferred_element_type=f32), 0.0)
                dq = dq + lax.dot_general(
                    ds, kpad[odd, c : c + block, :], TN, preferred_element_type=f32
                )
            return dq

        dq_acc[rows, :] = head(0)

        @pl.when(step < pairs - 1)
        def _():
            dq_acc[rows, :] += head(1)

    def back(u, rows):
        return u * cos_ref[rows, :] - halves_turned(u) * sin_ref[rows, :]

    scale = HD**-0.5
    for r in range(0, length, block):
        rows = pl.ds(r, block)
        to = side_rows(r, block, half_rows, parity)

        @pl.when(step < pairs - 1)
        def _():
            mixed_ref[to, here] = back(dq_acc[rows, :] * scale, rows).astype(bf16)

        if last == pairs:
            end = (last - first) * 128

            @pl.when(step == pairs - 1)
            def _():
                k = dk[rows, :]
                k = jnp.where(lane >= HD, k + pltpu.roll(k, HD, 1), dq_acc[rows, :]) * scale
                mixed_ref[to, end - 128 : end] = back(k, rows).astype(bf16)
                v = dv[rows, :]
                v = v + pltpu.roll(v, HD, 1)
                mixed_ref[to, end:] = v[:, :HD].astype(bf16)

    @pl.when(step == last - 1)
    def _():
        total = jnp.zeros((1, mixed_ref.shape[1]), f32)
        for r in range(0, length, block):
            part = mixed_ref[pl.ds(r, block), :].astype(f32)
            total = total + jnp.sum(part, 0, keepdims=True)
        bias_ref[...] = total


def attend_back(parity, own, other, pieces, qk, v, lse, cos, sin, first, last, earlier=()):
    half, depth = own.shape
    length = 2 * half
    wide = qk.shape[1]
    pairs = wide // 128
    group = (last - first) * 128 + (HD if last == pairs else 0)
    block = min(256, half)
    ins = (own, other, qk, v, lse, cos, sin)
    carried = pl.BlockSpec((length, 128), lambda p: (0, 0))
    carry = [jax.ShapeDtypeStruct((length, 128), f32)] * 2
    return pl.pallas_call(
        functools.partial(
            attend_back_kernel, block=block, count=len(pieces), first=first, last=last
        ),
        grid=(last - first,),
        in_specs=[pl.BlockSpec(memory_space=pltpu.SMEM)]
        + [whole(a) for a in ins]
        + [in_place(piece) for piece in pieces]
        + [carried] * len(earlier),
        out_specs=[
            pl.BlockSpec((length, group), lambda p: (0, 0)),
            pl.BlockSpec((1, group), lambda p: (0, 0)),
        ]
        + ([] if first else [carried] * 2),
        out_shape=[
            jax.ShapeDtypeStruct((length, group), bf16),
            jax.ShapeDtypeStruct((1, group), f32),
        ]
        + ([] if first else carry),
        scratch_shapes=[
            pltpu.VMEM((depth, wide), bf16),
            pltpu.VMEM((2, length, 128), bf16),
            pltpu.VMEM((2, length, 128), bf16),
            pltpu.VMEM((length, (last - first) * 128), bf16),
            pltpu.VMEM((length, 128), f32),
        ]
        + ([pltpu.VMEM((length, 128), f32)] * 2 if first else [])
        + [pltpu.SemaphoreType.DMA((len(pieces),))],
        compiler_params=kernel_params(50),
        cost_estimate=cost(12e9, 6e6, 3e6),
    )(parity, *ins, *pieces, *earlier)


def mlp_kernel(*refs, blocks, count, add):
    rows, grads, rest = refs[:blocks], refs[blocks : 2 * blocks], refs[2 * blocks :]
    pieces, rest = rest[:count], rest[count:]
    earlier, rest = rest[: blocks * add], rest[blocks * add :]
    act_ref, outs = rest[0], rest[1 : 1 + blocks]
    held, sems = rest[1 + blocks :]
    n = held.shape[1] // 3
    step = pl.program_id(0)

    @pl.when(step == 0)
    def _():
        assemble(pieces, held, sems)

    def chosen(parts):
        block = parts[0][...]
        for k in range(1, blocks):
            block = jnp.where(step == k, parts[k][...], block)
        return block

    wg, wu, wd = (held[:, k * n : (k + 1) * n] for k in range(3))
    x = chosen(rows)
    g = chosen(grads)
    gate = jnp.dot(x, wg, preferred_element_type=f32)
    up = jnp.dot(x, wu, preferred_element_type=f32)
    gh = jnp.dot(g, wd, preferred_element_type=f32)
    sig = 1.0 / (1.0 + jnp.exp(-gate))
    silu = gate * sig
    hid = (silu * up).astype(bf16)
    ghs = gh * sig
    gg = (ghs * up * (1.0 + gate - silu)).astype(bf16)
    gu = (ghs * gate).astype(bf16)
    act_ref[:, :n] = gg
    act_ref[:, n : 2 * n] = gu
    act_ref[:, 2 * n :] = hid
    ngrad = lax.dot_general(gg, wg, NT, preferred_element_type=f32)
    ngrad = ngrad + lax.dot_general(gu, wu, NT, preferred_element_type=f32)
    down = lax.dot_general(hid, wd, NT, preferred_element_type=f32)
    for k in range(blocks):

        @pl.when(step == k)
        def _():
            for part, value in enumerate((ngrad, down)):
                if add:
                    value = value + earlier[k][part].astype(f32)
                outs[k][part] = value.astype(bf16)


def mlp(rows, grads, pieces, sums=None):
    t, d = rows[0].shape
    blocks = len(rows)
    columns = pieces[0].shape[1]
    ins = (*rows, *grads)
    sums = tuple(sums or ())
    both = pl.BlockSpec((2, t, d), lambda i: (0, 0, 0))
    return pl.pallas_call(
        functools.partial(mlp_kernel, blocks=blocks, count=len(pieces), add=bool(sums)),
        grid=(blocks,),
        in_specs=[whole(a) for a in ins] + [in_place(p) for p in pieces] + [both] * len(sums),
        out_specs=[pl.BlockSpec((t, columns), lambda i: (i, 0))] + [both] * blocks,
        out_shape=[jax.ShapeDtypeStruct((blocks * t, columns), bf16)]
        + [jax.ShapeDtypeStruct((2, t, d), bf16)] * blocks,
        scratch_shapes=[
            pltpu.VMEM((d, columns), bf16),
            pltpu.SemaphoreType.DMA((len(pieces),)),
        ],
        compiler_params=kernel_params(58),
        cost_estimate=cost(6 * blocks * t * d * columns, 15 * blocks * MIB, blocks * t * columns),
    )(*ins, *pieces, *sums)


def fill(sent_ref, kept_ref, lefts, rights, second):
    half = kept_ref.shape[0]
    t = lefts[0].shape[0]
    q = half // 2
    if second:
        parts = ((sent_ref, 0, q), (sent_ref, q, 3 * q), (kept_ref, 0, 0), (kept_ref, q, 2 * q))
        size = q
    else:
        parts = ((sent_ref, 0, half), (kept_ref, 0, 0))
        size = half
    for ref, to, start in parts:
        total = 0.0
        for i, left in enumerate(lefts):
            right = rights[i * t // rights[0].shape[0]]
            at = i * t % right.shape[0]
            total = total + lax.dot_general(
                left[:, start : start + size],
                right[at : at + t, :],
                TN,
                preferred_element_type=f32,
            )
        ref[to : to + size, :] = total.astype(ref.dtype)


def outer_kernel(*refs, blocks):
    rows, grads, rights = refs[:blocks], refs[blocks : 2 * blocks], refs[2 * blocks : -4]
    sent_one, kept_one, sent_two, kept_two = refs[-4:]
    step = pl.program_id(0)

    @pl.when(step < 2)
    def _():
        fill(sent_one, kept_one, rows, rights, False)

    @pl.when(step == 2)
    def _():
        fill(sent_two, kept_two, grads, rights, True)


def outer(rows, grads, acts):
    t, d = rows[0].shape
    tall, columns = acts[0].shape
    n = columns // 3
    flat = [*rows, *grads]
    one = pl.BlockSpec((d // 2, n), lambda k: (0, jnp.minimum(k, 1)))
    two = pl.BlockSpec((d // 2, n), lambda k: (0, 0))
    return pl.pallas_call(
        functools.partial(outer_kernel, blocks=len(rows)),
        grid=(3,),
        in_specs=[whole(left) for left in flat]
        + [pl.BlockSpec((tall, n), lambda k: (0, k)) for _ in acts],
        out_specs=[one, one, two, two],
        out_shape=[
            jax.ShapeDtypeStruct((d // 2, 2 * n), bf16),
            jax.ShapeDtypeStruct((d // 2, 2 * n), f32),
            jax.ShapeDtypeStruct((d // 2, n), bf16),
            jax.ShapeDtypeStruct((d // 2, n), f32),
        ],
        compiler_params=kernel_params(58),
        cost_estimate=cost(2 * t * len(rows) * d * columns, 20 * MIB),
    )(*flat, *acts)


def outer_whole_kernel(row_ref, *refs, blocks, count, moved):
    rows, grads, rights, out_ref = refs[:blocks], refs[blocks : 2 * blocks], refs[2 * blocks : -1], refs[-1]
    step = pl.program_id(0)
    t, d = rows[0].shape
    deep = d // count
    bits = count.bit_length() - 1

    def product(lefts):
        for part in range(2):
            start = part * (d // 2)
            total = 0.0
            for i, left in enumerate(lefts):
                right = rights[i * t // rights[0].shape[0]]
                at = i * t % right.shape[0]
                total = total + lax.dot_general(
                    left[:, start : start + d // 2],
                    right[at : at + t, :],
                    TN,
                    preferred_element_type=f32,
                )
            total = total.astype(bf16)
            if not moved:
                out_ref[start : start + d // 2, :] = total
                continue
            for p in range(part * count // 2, (part + 1) * count // 2):
                to = (row_ref[0] ^ bit_reversed(p, bits)) * deep
                here = p * deep - start
                out_ref[pl.ds(pl.multiple_of(to, 16), deep), :] = total[here : here + deep]

    @pl.when(step < 2)
    def _():
        product(rows)

    @pl.when(step == 2)
    def _():
        product(grads)


def outer_whole(row, rows, grads, acts, count):
    t, d = rows[0].shape
    tall, columns = acts[0].shape
    n = columns // 3
    flat = [*rows, *grads]
    deep = d // count
    bits = count.bit_length() - 1
    moved = deep % 16 == 0
    out = pl.pallas_call(
        functools.partial(outer_whole_kernel, blocks=len(rows), count=count, moved=moved),
        grid=(3,),
        in_specs=[pl.BlockSpec(memory_space=pltpu.SMEM)]
        + [whole(left) for left in flat]
        + [pl.BlockSpec((tall, n), lambda k: (0, k)) for _ in acts],
        out_specs=pl.BlockSpec((d, n), lambda k: (0, k)),
        out_shape=jax.ShapeDtypeStruct((d, columns), bf16),
        compiler_params=kernel_params(58),
        cost_estimate=cost(2 * t * len(rows) * d * columns, 20 * MIB),
    )(row, *flat, *acts)
    if moved:
        return out
    places = jnp.array([bit_reversed(m, bits) for m in range(count)], jnp.int32)
    order = places[jnp.arange(count, dtype=jnp.int32) ^ row[0]]
    return out.reshape(count, deep, columns)[order].reshape(d, columns)


def outer_one_kernel(*refs):
    fill(refs[-2], refs[-1], refs[:-3], refs[-3:-2], False)


def outer_one(lefts, right):
    t, d = lefts[0].shape
    columns = right.shape[1]
    vmem = pl.BlockSpec(memory_space=pltpu.VMEM)
    return pl.pallas_call(
        outer_one_kernel,
        in_specs=[vmem] * (len(lefts) + 1),
        out_specs=[vmem] * 2,
        out_shape=[
            jax.ShapeDtypeStruct((d // 2, columns), bf16),
            jax.ShapeDtypeStruct((d // 2, columns), f32),
        ],
        compiler_params=kernel_params(40),
        cost_estimate=cost(2 * t * len(lefts) * d * columns, 6 * MIB),
    )(*lefts, right)


def rope_tables(length):
    inverse = theta_base ** (-(jnp.arange(HD // 2, dtype=f32) * 2.0 / HD))
    angles = jnp.arange(length, dtype=f32)[:, None] * inverse[None, :]
    c, s = jnp.cos(angles), jnp.sin(angles)
    return jnp.concatenate([c] * 4, 1), jnp.concatenate([-s, s, -s, s], 1)


class Gather:
    def __init__(self, block, bits):
        self.bits = bits
        self.left = bits - 1
        self.pieces = [block]
        self.sent = 0
        self.beside = []

    def ready(self, *earlier):
        self.pieces[-1] = after(self.pieces[-1], *earlier)

    def double(self, *earlier):
        held = jnp.concatenate(self.pieces, 0) if len(self.pieces) > 1 else self.pieces[0]
        self.pieces.append(flip(after(held, *earlier) if earlier else held, "row", self.left))
        self.left -= 1
        return self.pieces[-1]

    def send(self, *earlier):
        piece = self.pieces[self.sent]
        self.sent += 1
        self.beside.append(flip(after(piece, *earlier) if earlier else piece, "row", 0))
        return self.beside[-1]

    def catch_up(self, *earlier):
        rest = jnp.concatenate(self.pieces[self.sent :], 0)
        self.sent = len(self.pieces)
        self.beside.append(flip(after(rest, *earlier), "row", 0))
        return self.beside[-1]

    def finish(self, *earlier):
        while self.left > 0:
            self.double()
        self.catch_up(*earlier)
        out = self.pieces + self.beside
        return out if out[0].shape[0] % 16 == 0 else [jnp.concatenate(out, 0)]

    def all(self):
        while self.left > 0:
            self.double()
        while self.sent < len(self.pieces):
            self.send()
        out = self.pieces + self.beside
        return out if out[0].shape[0] % 16 == 0 else [jnp.concatenate(out, 0)]


class Scatter:
    def __init__(self, parts, bits):
        self.bits = bits
        self.orders = [[0, 1], [1, 0]][: len(parts)]
        self.kept = [kept for _, kept in parts]
        self.done = 0
        self.start([sent for sent, _ in parts])

    def start(self, sents):
        bits = [order[self.done] if self.done < 2 else self.done for order in self.orders]
        self.got = [flip(sent, "row", bit) for sent, bit in zip(sents, bits)]

    def wait(self, *earlier):
        self.got = [after(got, *earlier) for got in self.got]

    def step(self):
        if self.done == self.bits - 1:
            return
        self.done += 1
        half = self.kept[0].shape[0] // 2
        sents = [
            (kept[half:] + got[half:].astype(f32)).astype(bf16)
            for kept, got in zip(self.kept, self.got)
        ]
        self.kept = [kept[:half] + got[:half].astype(f32) for kept, got in zip(self.kept, self.got)]
        if self.done == 2:
            sents = [jnp.concatenate(sents, 1)]
            self.kept = [jnp.concatenate(self.kept, 1)]
        self.start(sents)

    def total(self):
        while self.done < self.bits - 1:
            self.step()
        totals = [kept + got.astype(f32) for kept, got in zip(self.kept, self.got)]
        return jnp.concatenate(totals, 1)


def turned_pairs(block):
    first = [(2 * a + b, 2 * b + a) for a in range(2) for b in range(2)]
    second = [(2 * a + b, 2 * (1 - b) + a) for a in range(2) for b in range(2)]
    return lax.ppermute(block, "col", first), lax.ppermute(block, "col", second)


def from_pairs(same, other):
    first = [(2 * a + b, 2 * b + a) for a in range(2) for b in range(2)]
    second = [(2 * a + b, 2 * b + 1 - a) for a in range(2) for b in range(2)]
    return lax.ppermute(same, "col", first), lax.ppermute(other, "col", second)


def cuts(width):
    first = min(512, width)
    return [(0, first), (first, width)] if first < width else [(0, width)]


def shards(
    layer_input,
    gain_attn,
    qkv_weight,
    qkv_bias,
    out_weight,
    gain_mlp,
    gate_weight,
    up_weight,
    down_weight,
    cotangent,
):
    row = lax.axis_index("row")
    column = lax.axis_index("col")
    row_count = lax.axis_size("row")
    bits = row_count.bit_length() - 1
    core = column % 2
    sequence = column // 2
    parity = core.astype(jnp.int32).reshape(1)
    tok_local, model_width = layer_input.shape
    length = tok_local * 2
    deep = model_width // row_count
    ff_cols = gate_weight.shape[1]
    qkv_cols = qkv_weight.shape[1]
    out_cols = out_weight.shape[0]
    group_width = 2 * qkv_cols
    query_width = group_width - 2 * HD

    bias_rows = jnp.pad(qkv_bias[None, :], ((0, 15), (0, 0)))
    first, second = turned_pairs(
        jnp.concatenate(
            [
                jnp.concatenate([qkv_weight, bias_rows], 0),
                jnp.pad(out_weight.T, ((0, 16), (0, 0))),
            ],
            1,
        )
    )
    low = jnp.where(sequence == 0, first, second)
    high = jnp.where(sequence == 0, second, first)
    qkv_own = jnp.concatenate([low[:, :qkv_cols], high[:, :qkv_cols]], 1)
    bias_full = qkv_own[deep : deep + 1].astype(f32)
    out_own = jnp.concatenate([low[:deep, qkv_cols:], high[:deep, qkv_cols:]], 1)
    out_own = jnp.pad(out_own, ((0, 0), (0, HD)))
    qkv_gather = Gather(qkv_own[:deep], bits)
    out_gather = Gather(out_own, bits)
    down_flipped = down_weight.T
    mlp_gathers = []
    for start, stop in cuts(ff_cols):
        padded = -(-(stop - start) // 256) * 256
        pieces = [
            jnp.pad(part[:, start:stop], ((0, 0), (0, padded - (stop - start))))
            for part in (gate_weight, up_weight, down_flipped)
        ]
        mlp_gathers.append(Gather(jnp.concatenate(pieces, 1), bits))
    place = jnp.arange(model_width, dtype=jnp.int32)
    masks = jnp.array([bit_reversed(p, bits) for p in range(row_count)], jnp.int32)
    source = jnp.repeat(masks ^ row, deep) * deep + place % deep
    to_stored = (place[:, None] == source[None, :]).astype(bf16)
    from_stored = (source[:, None] == place[None, :]).astype(bf16)

    def stored(block):
        return jnp.dot(block, to_stored, preferred_element_type=f32)

    def unstored(block):
        return jnp.dot(block, from_stored, preferred_element_type=f32).astype(bf16)

    def unstored_row(vector):
        blocks = vector.reshape(row_count, deep)
        blocks = jnp.concatenate(
            [blocks[bit_reversed(m, bits)][None] for m in range(row_count)], 0
        )
        for bit in range(bits):
            wide = blocks.reshape(-1, 2, 1 << bit, deep)
            turned = jnp.concatenate([wide[:, 1:], wide[:, :1]], 1).reshape(row_count, deep)
            blocks = jnp.where((row >> bit) % 2 == 1, turned, blocks)
        return blocks.reshape(model_width)

    input_rows = stored(after(layer_input, first, second))
    grad_out = stored(cotangent)
    gain_one = stored(gain_attn[None, :])
    gain_two = stored(gain_mlp[None, :])

    scale_one = lax.rsqrt(jnp.mean(input_rows * input_rows, axis=1) + eps)
    normed_own = (input_rows * scale_one[:, None] * gain_one).astype(bf16)
    normed_other = flip(normed_own, "col", 0)
    cosine, sine_part = rope_tables(length)
    grad_blocks = [grad_out.astype(bf16)]

    near, far = mlp_gathers
    n_four = near.double()
    n_own = near.send()
    a_own = qkv_gather.send()
    a_four = qkv_gather.double()
    a_two = qkv_gather.double(a_own)
    a_beside = qkv_gather.send(a_own)
    o_four = out_gather.double(a_four)
    a_last = qkv_gather.send(a_beside, n_own)
    qkv_pieces = qkv_gather.all()
    far.ready(a_two, o_four)
    f_four = far.double()
    o_two = out_gather.double(a_two)
    across = flip(after(grad_blocks[0], a_four), "col", 1)
    out_pieces = out_gather.finish(a_last, o_two)
    n_two = near.double(o_two)
    n_beside = near.send(a_last)
    qk_rows, value_rows, att_rows, log_totals = attend(
        parity,
        normed_own,
        normed_other,
        qkv_pieces,
        bias_full,
        cosine,
        sine_part,
    )
    n_last = near.send(att_rows)
    att_own, att_other = project(after(att_rows, n_beside, n_two, across, f_four), out_pieces)
    att_got = flip(att_other, "col", 0)
    grad_blocks.append(flip(after(grad_blocks[0], att_got), "col", 0))
    grad_blocks += [across, flip(after(across, att_got), "col", 0)]
    middle = input_rows + att_own + att_got.astype(f32)
    scale_two = lax.rsqrt(jnp.mean(middle * middle, axis=1) + eps)
    blocks = [(middle * scale_two[:, None] * gain_two).astype(bf16)]
    across = flip(blocks[0], "col", 1)
    blocks.append(flip(after(blocks[0], n_last), "col", 0))
    blocks += [across, flip(across, "col", 0)]

    f_beside = far.catch_up(n_last)
    f_two = far.double(blocks[2])
    first_pieces = near.all()
    act_all, *sums = mlp(blocks, grad_blocks, first_pieces)
    sums_own, sums_far = sums[:2], sums[2:]
    f_last = far.send(f_beside, act_all)
    second_pieces = far.all()
    sent_one, kept_one, sent_two, kept_two = outer(blocks, grad_blocks, [act_all])
    first_scatter = Scatter([(sent_one, kept_one), (sent_two, kept_two)], bits)
    start_far = after(blocks[2], kept_one)
    act_far, near_far, far_far = mlp(
        [start_far, blocks[3]], grad_blocks[2:], second_pieces, sums_far
    )
    far_far = after(far_far, *first_scatter.got)
    across = near_far.astype(f32) + flip(far_far, "col", 0).astype(f32)
    across = across.astype(bf16)
    normed_back = flip(across[0], "col", 1)
    act_own, near_own, far_own = mlp(
        [after(blocks[0], across), blocks[1]],
        grad_blocks[:2],
        second_pieces,
        sums_own,
    )
    first_scatter.step()
    beside = flip(after(far_own, normed_back, *first_scatter.got), "col", 0)
    first_scatter.step()
    down_back = flip(after(across[1], normed_back), "col", 1)

    def summed(k, back):
        return near_own[k].astype(f32) + beside[k].astype(f32) + back.astype(f32)

    second_whole = outer_whole(
        row.astype(jnp.int32).reshape(1),
        [after(blocks[0], near_own, *first_scatter.kept), *blocks[1:]],
        grad_blocks,
        [act_own, act_far],
        row_count,
    )
    second_total = lax.psum_scatter(second_whole, "row", scatter_dimension=0, tiled=True)
    grad_normed_two = summed(0, after(normed_back, second_whole))
    scaled_two = gain_two * grad_normed_two
    inner_two = jnp.sum(scaled_two * middle, axis=1)
    grad_middle = (
        grad_out
        + scale_two[:, None] * scaled_two
        - middle * (scale_two**3 * inner_two / model_width)[:, None]
    )
    gain_two_grad = jnp.sum(grad_normed_two * middle * scale_two[:, None], axis=0)
    branch_own = grad_middle.astype(bf16)
    branch_other = flip(branch_own, "col", 0)
    out_scatter = Scatter([outer_one([branch_own, branch_other], att_rows)], bits)
    split = qk_rows.shape[1] // 256
    mixed_first, bias_first, *carry = attend_back(
        parity,
        after(branch_own, out_scatter.kept[0]),
        branch_other,
        out_pieces,
        qk_rows,
        value_rows,
        log_totals,
        cosine,
        sine_part,
        0,
        split,
    )
    out_scatter.wait(mixed_first)
    out_scatter.step()
    mixed_last, bias_last = attend_back(
        parity,
        after(branch_own, out_scatter.kept[0]),
        branch_other,
        out_pieces,
        qk_rows,
        value_rows,
        log_totals,
        cosine,
        sine_part,
        split,
        2 * split,
        carry,
    )
    bias_grad = jnp.concatenate([bias_first, bias_last], 1)[0]
    grad_mixed = jnp.concatenate([mixed_first, mixed_last], 1)
    qkv_scatter = Scatter([outer_one([normed_own, normed_other], grad_mixed)], bits)
    passed = qkv_scatter.kept[0]
    out_scatter.wait(passed)
    first_scatter.wait(passed)
    first_total = first_scatter.total()
    layer_output = unstored((middle + summed(1, after(down_back, passed))).astype(bf16))
    qkv_full = jnp.concatenate(qkv_pieces, 0)
    grad_mixed = after(grad_mixed, passed)
    out_scatter.step()

    def back_to_normed(rows):
        return jnp.einsum("tc,dc->td", rows, qkv_full, preferred_element_type=f32)

    other = flip(back_to_normed(grad_mixed[tok_local:]).astype(bf16), "col", 0)
    grad_normed_one = back_to_normed(grad_mixed[:tok_local]) + other.astype(f32)
    scaled_one = gain_one * grad_normed_one
    inner_one = jnp.sum(scaled_one * input_rows, axis=1)
    input_grad = unstored(
        (
            grad_middle
            + scale_one[:, None] * scaled_one
            - input_rows * (scale_one**3 * inner_one / model_width)[:, None]
        ).astype(bf16)
    )
    gain_one_grad = jnp.sum(grad_normed_one * input_rows * scale_one[:, None], axis=0)

    def to_columns(total, width):
        low, high = total[:, :width].astype(bf16), total[:, width : 2 * width].astype(bf16)
        first, second = from_pairs(
            jnp.where(sequence == 0, low, high), jnp.where(sequence == 0, high, low)
        )
        return first.astype(f32) + second.astype(f32)

    bias_row = lax.dynamic_update_slice_in_dim(
        jnp.zeros((group_width * 2,), f32), bias_grad, core * group_width, 0
    )
    small = jnp.concatenate([unstored_row(gain_one_grad), unstored_row(gain_two_grad), bias_row])
    small = jnp.pad(small, (0, -small.shape[0] % 128)).reshape(-1, 128)
    for bit in range(2):
        small = small + flip(small, "col", bit)
    for bit in range(bits):
        small = small + flip(small, "row", bit)
    qkv_scatter.step()
    qkv_scatter.step()
    qkv_scatter.wait(small)
    qkv_total = to_columns(qkv_scatter.total(), qkv_cols)
    out_total = to_columns(out_scatter.total(), out_cols)
    mlp_totals = []
    for total, (start, stop) in zip(
        (first_total, after(second_total, small).astype(f32)), cuts(ff_cols)
    ):
        padded = total.shape[1] // 3
        mlp_totals.append(
            [total[:, k * padded : k * padded + stop - start] for k in range(3)]
        )
    gate_total, up_total, down_total = (jnp.concatenate(parts, 1) for parts in zip(*mlp_totals))
    small = small.reshape(-1)
    gain_one_total = small[:model_width]
    gain_two_total = small[model_width : 2 * model_width]
    bias_total = lax.dynamic_slice_in_dim(small, 2 * model_width + column * qkv_cols, qkv_cols, 0)
    return (
        layer_output,
        input_grad,
        gain_one_total,
        qkv_total,
        bias_total,
        out_total.T,
        gain_two_total,
        gate_total,
        up_total,
        down_total.T,
    )


def solution(mesh):
    in_specs = (
        P(("row", "col"), None),
        P(),
        P("row", "col"),
        P("col"),
        P("col", "row"),
        P(),
        P("row", "col"),
        P("row", "col"),
        P("col", "row"),
        P(("row", "col"), None),
    )
    out_specs = (
        P(("row", "col"), None),
        P(("row", "col"), None),
        P(),
        P("row", "col"),
        P("col"),
        P("col", "row"),
        P(),
        P("row", "col"),
        P("row", "col"),
        P("col", "row"),
    )
    return jax.shard_map(shards, mesh=mesh, in_specs=in_specs, out_specs=out_specs, check_vma=False)
```

```python
import functools
import math

import jax
import jax.numpy as jnp
from jax import lax
from jax.experimental import pallas as pl
from jax.experimental.pallas import tpu as pltpu
from jax.sharding import PartitionSpec as P

HD = 64
eps = 1e-06
theta_base = 1000000.0
bf16 = jnp.bfloat16
f32 = jnp.float32
NT = (((1,), (1,)), ((), ()))
TN = (((0,), (0,)), ((), ()))
MIB = 1024 * 1024


def flip(block, axis, bit):
    count = lax.axis_size(axis)
    return lax.ppermute(block, axis, [(i, i ^ 1 << bit) for i in range(count)])


def bit_reversed(value, bits):
    return sum((value >> b & 1) << (bits - 1 - b) for b in range(bits))


def after(value, *earlier):
    return lax.optimization_barrier((value, *earlier))[0]


def kernel_params(mib):
    return pltpu.CompilerParams(vmem_limit_bytes=mib * MIB)


def cost(flops, nbytes, exps=0):
    return pl.CostEstimate(
        flops=int(flops), bytes_accessed=int(nbytes), transcendentals=int(exps)
    )


def whole(array):
    return pl.BlockSpec(array.shape, lambda *_: (0,) * len(array.shape))


def in_place(block):
    return pl.BlockSpec(memory_space=pl.ANY)


def assemble(pieces, held, sems):
    copies = []
    at = 0
    for i, piece in enumerate(pieces):
        rows = piece.shape[0]
        copies.append(pltpu.make_async_copy(piece, held.at[pl.ds(at, rows)], sems.at[i]))
        at += rows
    for copy in copies:
        copy.start()
    for copy in copies:
        copy.wait()


def halves_turned(block):
    lane = lax.broadcasted_iota(jnp.int32, block.shape, 1)
    up = pltpu.roll(block, 128 - HD // 2, 1)
    return jnp.where(lane % HD < HD // 2, up, pltpu.roll(block, HD // 2, 1))


def side_rows(r, block, half, parity):
    side = (r // half) ^ parity
    return pl.ds(pl.multiple_of(side * half + r % half, block), block)


def pad_heads(key_value, rows, value, last):
    lane = lax.broadcasted_iota(jnp.int32, (1, 128), 1)
    kpad, vpad = key_value
    zero = jnp.zeros_like(value)
    vpad[0, rows, :] = jnp.concatenate([value, zero], 1).astype(bf16)
    vpad[1, rows, :] = jnp.concatenate([zero, value], 1).astype(bf16)
    kpad[1, rows, :] = jnp.where(lane >= HD, last, 0.0).astype(bf16)
    kpad[0, rows, :] = jnp.where(lane < HD, pltpu.roll(last, HD, 1), 0.0).astype(bf16)


def attend_kernel(parity_ref, own_ref, other_ref, bias_ref, cos_ref, sin_ref, *rest, block, count):
    pieces = rest[:count]
    qk_ref, v_ref, att_ref, lse_ref, held, kpad, vpad, lse_cols, sems = rest[count:]
    step = pl.program_id(0)
    half = own_ref.shape[0]
    length = 2 * half
    wide = qk_ref.shape[1]
    pairs = wide // 128
    parity = parity_ref[0]

    @pl.when(step == 0)
    def _():
        assemble(pieces, held, sems)
        for side, rows_ref in enumerate((own_ref, other_ref)):
            for r in range(0, half, block):
                at = pl.multiple_of((side ^ parity) * half + r, block)
                rows = pl.ds(at, block)
                mixed = jnp.dot(rows_ref[r : r + block, :], held[...], preferred_element_type=f32)
                mixed = (mixed + bias_ref[...]).astype(bf16).astype(f32)
                cos, sin = cos_ref[rows, :], sin_ref[rows, :]
                for p in range(pairs):
                    u = mixed[:, p * 128 : (p + 1) * 128]
                    turned = (u * cos + halves_turned(u) * sin).astype(bf16)
                    qk_ref[rows, p * 128 : (p + 1) * 128] = turned
                v_ref[rows, :] = mixed[:, wide:].astype(bf16)
                pad_heads((kpad, vpad), rows, mixed[:, wide:], turned.astype(f32))
        lse_cols[...] = jnp.zeros_like(lse_cols)

    factor = HD**-0.5 * math.log2(math.e)
    cols = pl.ds(pl.multiple_of(step * 128, 128), 128)
    row_i = lax.broadcasted_iota(jnp.int32, (block, block), 0)
    col_i = lax.broadcasted_iota(jnp.int32, (block, block), 1)
    for r in range(0, length, block):
        rows = pl.ds(r, block)
        to = side_rows(r, block, half, parity)
        q = qk_ref[rows, cols]

        def head(odd):
            keys = kpad[odd, : r + block, :]
            scores = lax.dot_general(q, keys, NT, preferred_element_type=f32)
            diag = jnp.where(col_i <= row_i, scores[:, r:], -1e30)
            scores = jnp.concatenate([scores[:, :r], diag], 1) if r else diag
            top = jnp.max(scores, 1, keepdims=True)
            e = jnp.exp2((scores - top) * factor)
            total = jnp.sum(e, 1, keepdims=True)
            out = jnp.dot(e.astype(bf16), vpad[odd, : r + block, :], preferred_element_type=f32)
            lse = top * factor + jnp.log2(total)
            at = lax.broadcasted_iota(jnp.int32, (1, 128), 1) == 2 * step + odd
            lse_cols[rows, :] = jnp.where(at, lse, lse_cols[rows, :])
            return out / total

        even = head(0)

        @pl.when(step < pairs - 1)
        def _():
            att_ref[to, :] = (even + head(1)).astype(bf16)

        @pl.when(step == pairs - 1)
        def _():
            att_ref[to, :] = even.astype(bf16)

    @pl.when(step == pairs - 1)
    def _():
        lse_ref[...] = lse_cols[...].T[: lse_ref.shape[0], :]


def attend(parity, own, other, pieces, bias, cos, sin):
    half, depth = own.shape
    length = 2 * half
    group = bias.shape[1]
    wide = group - HD
    pairs = wide // 128
    block = min(256, half)
    return pl.pallas_call(
        functools.partial(attend_kernel, block=block, count=len(pieces)),
        grid=(pairs,),
        in_specs=[pl.BlockSpec(memory_space=pltpu.SMEM)]
        + [whole(a) for a in (own, other, bias, cos, sin)]
        + [in_place(piece) for piece in pieces],
        out_specs=[
            pl.BlockSpec((length, wide), lambda p: (0, 0)),
            pl.BlockSpec((length, HD), lambda p: (0, 0)),
            pl.BlockSpec((length, 128), lambda p: (0, p)),
            pl.BlockSpec((8, length), lambda p: (0, 0)),
        ],
        out_shape=[
            jax.ShapeDtypeStruct((length, wide), bf16),
            jax.ShapeDtypeStruct((length, HD), bf16),
            jax.ShapeDtypeStruct((length, wide), bf16),
            jax.ShapeDtypeStruct((8, length), f32),
        ],
        scratch_shapes=[
            pltpu.VMEM((depth, group), bf16),
            pltpu.VMEM((2, length, 128), bf16),
            pltpu.VMEM((2, length, 128), bf16),
            pltpu.VMEM((length, 128), f32),
            pltpu.SemaphoreType.DMA((len(pieces),)),
        ],
        compiler_params=kernel_params(40),
        cost_estimate=cost(12e9, 8e6, 5e6),
    )(parity, own, other, bias, cos, sin, *pieces)


def project_kernel(att_ref, *rest, count):
    pieces = rest[:count]
    own_ref, other_ref, held, sems = rest[count:]
    half = own_ref.shape[0]
    assemble(pieces, held, sems)
    for side, ref in enumerate((own_ref, other_ref)):
        rows = att_ref[side * half : (side + 1) * half, :]
        ref[...] = lax.dot_general(rows, held[...], NT, preferred_element_type=f32).astype(ref.dtype)


def project(att, pieces):
    length, wide = att.shape
    depth = sum(piece.shape[0] for piece in pieces)
    return pl.pallas_call(
        functools.partial(project_kernel, count=len(pieces)),
        in_specs=[pl.BlockSpec(memory_space=pltpu.VMEM)] + [in_place(piece) for piece in pieces],
        out_specs=[pl.BlockSpec(memory_space=pltpu.VMEM)] * 2,
        out_shape=[
            jax.ShapeDtypeStruct((length // 2, depth), f32),
            jax.ShapeDtypeStruct((length // 2, depth), bf16),
        ],
        scratch_shapes=[
            pltpu.VMEM((depth, wide), bf16),
            pltpu.SemaphoreType.DMA((len(pieces),)),
        ],
        compiler_params=kernel_params(40),
        cost_estimate=cost(2 * length * depth * wide, 6e6),
    )(att, *pieces)


def attend_back_kernel(
    parity_ref,
    own_ref,
    other_ref,
    qk_ref,
    v_ref,
    lse_ref,
    cos_ref,
    sin_ref,
    *rest,
    block,
    count,
    first,
    last,
):
    pieces = rest[:count]
    if first == 0:
        mixed_ref, bias_ref, dk, dv, held, kpad, vpad, gatt, dq_acc, sems = rest[count:]
    else:
        dk_in, dv_in, mixed_ref, bias_ref, held, kpad, vpad, gatt, dq_acc, dk, dv, sems = rest[count:]
    step = pl.program_id(0) + first
    half_rows = own_ref.shape[0]
    length = 2 * half_rows
    wide = qk_ref.shape[1]
    pairs = wide // 128
    used = slice(first * 128, last * 128)
    parity = parity_ref[0]
    lane = lax.broadcasted_iota(jnp.int32, (1, 128), 1)

    @pl.when(step == first)
    def _():
        assemble(pieces, held, sems)
        for side, rows_ref in enumerate((own_ref, other_ref)):
            for r in range(0, half_rows, block):
                rows = pl.ds(pl.multiple_of((side ^ parity) * half_rows + r, block), block)
                got = jnp.dot(
                    rows_ref[r : r + block, :], held[:, used], preferred_element_type=f32
                )
                gatt[rows, :] = got.astype(bf16)
        for r in range(0, length, block):
            rows = pl.ds(r, block)
            keys = qk_ref[rows, wide - 128 :].astype(f32)
            pad_heads((kpad, vpad), rows, v_ref[rows, :].astype(f32), keys)
        dk[...] = dk_in[...] if first else jnp.zeros_like(dk)
        dv[...] = dv_in[...] if first else jnp.zeros_like(dv)

    factor = HD**-0.5 * math.log2(math.e)
    cols = pl.ds(pl.multiple_of(step * 128, 128), 128)
    here = pl.ds(pl.multiple_of((step - first) * 128, 128), 128)
    key_i = lax.broadcasted_iota(jnp.int32, (block, block), 0)
    query_i = lax.broadcasted_iota(jnp.int32, (block, block), 1)
    for r in range(0, length, block):
        rows = pl.ds(r, block)
        q = qk_ref[rows, cols]
        g = gatt[rows, here]

        def head(odd):
            lse = lse_ref[pl.ds(2 * step + odd, 1), rows]
            probs, grads = [], []
            inner = jnp.zeros((1, block), f32)
            for c in range(0, r + block, block):
                scores = lax.dot_general(
                    kpad[odd, c : c + block, :], q, NT, preferred_element_type=f32
                )
                p = jnp.exp2(scores * factor - lse)
                if c == r:
                    p = jnp.where(key_i <= query_i, p, 0.0)
                dp = lax.dot_general(vpad[odd, c : c + block, :], g, NT, preferred_element_type=f32)
                inner = inner + jnp.sum(p * dp, 0, keepdims=True)
                probs.append(p)
                grads.append(dp)
            dq = 0.0
            half = lane >= HD if odd else lane < HD
            for i, c in enumerate(range(0, r + block, block)):
                keys = pl.ds(c, block)
                ds = (probs[i] * (grads[i] - inner)).astype(bf16)
                p = probs[i].astype(bf16)
                dk[keys, :] += jnp.where(half, jnp.dot(ds, q, preferred_element_type=f32), 0.0)
                dv[keys, :] += jnp.where(half, jnp.dot(p, g, preferred_element_type=f32), 0.0)
                dq = dq + lax.dot_general(
                    ds, kpad[odd, c : c + block, :], TN, preferred_element_type=f32
                )
            return dq

        dq_acc[rows, :] = head(0)

        @pl.when(step < pairs - 1)
        def _():
            dq_acc[rows, :] += head(1)

    def back(u, rows):
        return u * cos_ref[rows, :] - halves_turned(u) * sin_ref[rows, :]

    scale = HD**-0.5
    for r in range(0, length, block):
        rows = pl.ds(r, block)
        to = side_rows(r, block, half_rows, parity)

        @pl.when(step < pairs - 1)
        def _():
            mixed_ref[to, here] = back(dq_acc[rows, :] * scale, rows).astype(bf16)

        if last == pairs:
            end = (last - first) * 128

            @pl.when(step == pairs - 1)
            def _():
                k = dk[rows, :]
                k = jnp.where(lane >= HD, k + pltpu.roll(k, HD, 1), dq_acc[rows, :]) * scale
                mixed_ref[to, end - 128 : end] = back(k, rows).astype(bf16)
                v = dv[rows, :]
                v = v + pltpu.roll(v, HD, 1)
                mixed_ref[to, end:] = v[:, :HD].astype(bf16)

    @pl.when(step == last - 1)
    def _():
        total = jnp.zeros((1, mixed_ref.shape[1]), f32)
        for r in range(0, length, block):
            part = mixed_ref[pl.ds(r, block), :].astype(f32)
            total = total + jnp.sum(part, 0, keepdims=True)
        bias_ref[...] = total


def attend_back(parity, own, other, pieces, qk, v, lse, cos, sin, first, last, earlier=()):
    half, depth = own.shape
    length = 2 * half
    wide = qk.shape[1]
    pairs = wide // 128
    group = (last - first) * 128 + (HD if last == pairs else 0)
    block = min(256, half)
    ins = (own, other, qk, v, lse, cos, sin)
    carried = pl.BlockSpec((length, 128), lambda p: (0, 0))
    carry = [jax.ShapeDtypeStruct((length, 128), f32)] * 2
    return pl.pallas_call(
        functools.partial(
            attend_back_kernel, block=block, count=len(pieces), first=first, last=last
        ),
        grid=(last - first,),
        in_specs=[pl.BlockSpec(memory_space=pltpu.SMEM)]
        + [whole(a) for a in ins]
        + [in_place(piece) for piece in pieces]
        + [carried] * len(earlier),
        out_specs=[
            pl.BlockSpec((length, group), lambda p: (0, 0)),
            pl.BlockSpec((1, group), lambda p: (0, 0)),
        ]
        + ([] if first else [carried] * 2),
        out_shape=[
            jax.ShapeDtypeStruct((length, group), bf16),
            jax.ShapeDtypeStruct((1, group), f32),
        ]
        + ([] if first else carry),
        scratch_shapes=[
            pltpu.VMEM((depth, wide), bf16),
            pltpu.VMEM((2, length, 128), bf16),
            pltpu.VMEM((2, length, 128), bf16),
            pltpu.VMEM((length, (last - first) * 128), bf16),
            pltpu.VMEM((length, 128), f32),
        ]
        + ([pltpu.VMEM((length, 128), f32)] * 2 if first else [])
        + [pltpu.SemaphoreType.DMA((len(pieces),))],
        compiler_params=kernel_params(50),
        cost_estimate=cost(12e9, 6e6, 3e6),
    )(parity, *ins, *pieces, *earlier)


def mlp_kernel(*refs, blocks, count, add):
    rows, grads, rest = refs[:blocks], refs[blocks : 2 * blocks], refs[2 * blocks :]
    pieces, rest = rest[:count], rest[count:]
    earlier, rest = rest[: blocks * add], rest[blocks * add :]
    act_ref, outs = rest[0], rest[1 : 1 + blocks]
    held, sems = rest[1 + blocks :]
    n = held.shape[1] // 3
    step = pl.program_id(0)

    @pl.when(step == 0)
    def _():
        assemble(pieces, held, sems)

    def chosen(parts):
        block = parts[0][...]
        for k in range(1, blocks):
            block = jnp.where(step == k, parts[k][...], block)
        return block

    wg, wu, wd = (held[:, k * n : (k + 1) * n] for k in range(3))
    x = chosen(rows)
    g = chosen(grads)
    gate = jnp.dot(x, wg, preferred_element_type=f32)
    up = jnp.dot(x, wu, preferred_element_type=f32)
    gh = jnp.dot(g, wd, preferred_element_type=f32)
    sig = 1.0 / (1.0 + jnp.exp(-gate))
    silu = gate * sig
    hid = (silu * up).astype(bf16)
    ghs = gh * sig
    gg = (ghs * up * (1.0 + gate - silu)).astype(bf16)
    gu = (ghs * gate).astype(bf16)
    act_ref[:, :n] = gg
    act_ref[:, n : 2 * n] = gu
    act_ref[:, 2 * n :] = hid
    ngrad = lax.dot_general(gg, wg, NT, preferred_element_type=f32)
    ngrad = ngrad + lax.dot_general(gu, wu, NT, preferred_element_type=f32)
    down = lax.dot_general(hid, wd, NT, preferred_element_type=f32)
    for k in range(blocks):

        @pl.when(step == k)
        def _():
            for part, value in enumerate((ngrad, down)):
                if add:
                    value = value + earlier[k][part].astype(f32)
                outs[k][part] = value.astype(bf16)


def mlp(rows, grads, pieces, sums=None):
    t, d = rows[0].shape
    blocks = len(rows)
    columns = pieces[0].shape[1]
    ins = (*rows, *grads)
    sums = tuple(sums or ())
    both = pl.BlockSpec((2, t, d), lambda i: (0, 0, 0))
    return pl.pallas_call(
        functools.partial(mlp_kernel, blocks=blocks, count=len(pieces), add=bool(sums)),
        grid=(blocks,),
        in_specs=[whole(a) for a in ins] + [in_place(p) for p in pieces] + [both] * len(sums),
        out_specs=[pl.BlockSpec((t, columns), lambda i: (i, 0))] + [both] * blocks,
        out_shape=[jax.ShapeDtypeStruct((blocks * t, columns), bf16)]
        + [jax.ShapeDtypeStruct((2, t, d), bf16)] * blocks,
        scratch_shapes=[
            pltpu.VMEM((d, columns), bf16),
            pltpu.SemaphoreType.DMA((len(pieces),)),
        ],
        compiler_params=kernel_params(58),
        cost_estimate=cost(6 * blocks * t * d * columns, 15 * blocks * MIB, blocks * t * columns),
    )(*ins, *pieces, *sums)


def fill(sent_ref, kept_ref, lefts, rights, second):
    half = kept_ref.shape[0]
    t = lefts[0].shape[0]
    q = half // 2
    if second:
        parts = ((sent_ref, 0, q), (sent_ref, q, 3 * q), (kept_ref, 0, 0), (kept_ref, q, 2 * q))
        size = q
    else:
        parts = ((sent_ref, 0, half), (kept_ref, 0, 0))
        size = half
    for ref, to, start in parts:
        total = 0.0
        for i, left in enumerate(lefts):
            right = rights[i * t // rights[0].shape[0]]
            at = i * t % right.shape[0]
            total = total + lax.dot_general(
                left[:, start : start + size],
                right[at : at + t, :],
                TN,
                preferred_element_type=f32,
            )
        ref[to : to + size, :] = total.astype(ref.dtype)


def outer_kernel(*refs, blocks):
    rows, grads, rights = refs[:blocks], refs[blocks : 2 * blocks], refs[2 * blocks : -4]
    sent_one, kept_one, sent_two, kept_two = refs[-4:]
    step = pl.program_id(0)

    @pl.when(step < 2)
    def _():
        fill(sent_one, kept_one, rows, rights, False)

    @pl.when(step == 2)
    def _():
        fill(sent_two, kept_two, grads, rights, True)


def outer(rows, grads, acts):
    t, d = rows[0].shape
    tall, columns = acts[0].shape
    n = columns // 3
    flat = [*rows, *grads]
    one = pl.BlockSpec((d // 2, n), lambda k: (0, jnp.minimum(k, 1)))
    two = pl.BlockSpec((d // 2, n), lambda k: (0, 0))
    return pl.pallas_call(
        functools.partial(outer_kernel, blocks=len(rows)),
        grid=(3,),
        in_specs=[whole(left) for left in flat]
        + [pl.BlockSpec((tall, n), lambda k: (0, k)) for _ in acts],
        out_specs=[one, one, two, two],
        out_shape=[
            jax.ShapeDtypeStruct((d // 2, 2 * n), bf16),
            jax.ShapeDtypeStruct((d // 2, 2 * n), f32),
            jax.ShapeDtypeStruct((d // 2, n), bf16),
            jax.ShapeDtypeStruct((d // 2, n), f32),
        ],
        compiler_params=kernel_params(58),
        cost_estimate=cost(2 * t * len(rows) * d * columns, 20 * MIB),
    )(*flat, *acts)


def outer_whole_kernel(row_ref, *refs, blocks, count, moved):
    rows, grads, rights, out_ref = refs[:blocks], refs[blocks : 2 * blocks], refs[2 * blocks : -1], refs[-1]
    step = pl.program_id(0)
    t, d = rows[0].shape
    deep = d // count
    bits = count.bit_length() - 1

    def product(lefts):
        for part in range(2):
            start = part * (d // 2)
            total = 0.0
            for i, left in enumerate(lefts):
                right = rights[i * t // rights[0].shape[0]]
                at = i * t % right.shape[0]
                total = total + lax.dot_general(
                    left[:, start : start + d // 2],
                    right[at : at + t, :],
                    TN,
                    preferred_element_type=f32,
                )
            total = total.astype(bf16)
            if not moved:
                out_ref[start : start + d // 2, :] = total
                continue
            for p in range(part * count // 2, (part + 1) * count // 2):
                to = (row_ref[0] ^ bit_reversed(p, bits)) * deep
                here = p * deep - start
                out_ref[pl.ds(pl.multiple_of(to, 16), deep), :] = total[here : here + deep]

    @pl.when(step < 2)
    def _():
        product(rows)

    @pl.when(step == 2)
    def _():
        product(grads)


def outer_whole(row, rows, grads, acts, count):
    t, d = rows[0].shape
    tall, columns = acts[0].shape
    n = columns // 3
    flat = [*rows, *grads]
    deep = d // count
    bits = count.bit_length() - 1
    moved = deep % 16 == 0
    out = pl.pallas_call(
        functools.partial(outer_whole_kernel, blocks=len(rows), count=count, moved=moved),
        grid=(3,),
        in_specs=[pl.BlockSpec(memory_space=pltpu.SMEM)]
        + [whole(left) for left in flat]
        + [pl.BlockSpec((tall, n), lambda k: (0, k)) for _ in acts],
        out_specs=pl.BlockSpec((d, n), lambda k: (0, k)),
        out_shape=jax.ShapeDtypeStruct((d, columns), bf16),
        compiler_params=kernel_params(58),
        cost_estimate=cost(2 * t * len(rows) * d * columns, 20 * MIB),
    )(row, *flat, *acts)
    if moved:
        return out
    places = jnp.array([bit_reversed(m, bits) for m in range(count)], jnp.int32)
    order = places[jnp.arange(count, dtype=jnp.int32) ^ row[0]]
    return out.reshape(count, deep, columns)[order].reshape(d, columns)


def outer_one_kernel(*refs):
    fill(refs[-2], refs[-1], refs[:-3], refs[-3:-2], False)


def outer_one(lefts, right):
    t, d = lefts[0].shape
    columns = right.shape[1]
    vmem = pl.BlockSpec(memory_space=pltpu.VMEM)
    return pl.pallas_call(
        outer_one_kernel,
        in_specs=[vmem] * (len(lefts) + 1),
        out_specs=[vmem] * 2,
        out_shape=[
            jax.ShapeDtypeStruct((d // 2, columns), bf16),
            jax.ShapeDtypeStruct((d // 2, columns), f32),
        ],
        compiler_params=kernel_params(40),
        cost_estimate=cost(2 * t * len(lefts) * d * columns, 6 * MIB),
    )(*lefts, right)


def rope_tables(length):
    inverse = theta_base ** (-(jnp.arange(HD // 2, dtype=f32) * 2.0 / HD))
    angles = jnp.arange(length, dtype=f32)[:, None] * inverse[None, :]
    c, s = jnp.cos(angles), jnp.sin(angles)
    return jnp.concatenate([c] * 4, 1), jnp.concatenate([-s, s, -s, s], 1)


class Gather:
    def __init__(self, block, bits):
        self.bits = bits
        self.left = bits - 1
        self.pieces = [block]
        self.sent = 0
        self.beside = []

    def ready(self, *earlier):
        self.pieces[-1] = after(self.pieces[-1], *earlier)

    def double(self, *earlier):
        held = jnp.concatenate(self.pieces, 0) if len(self.pieces) > 1 else self.pieces[0]
        self.pieces.append(flip(after(held, *earlier) if earlier else held, "row", self.left))
        self.left -= 1
        return self.pieces[-1]

    def send(self, *earlier):
        piece = self.pieces[self.sent]
        self.sent += 1
        self.beside.append(flip(after(piece, *earlier) if earlier else piece, "row", 0))
        return self.beside[-1]

    def catch_up(self, *earlier):
        rest = jnp.concatenate(self.pieces[self.sent :], 0)
        self.sent = len(self.pieces)
        self.beside.append(flip(after(rest, *earlier), "row", 0))
        return self.beside[-1]

    def finish(self, *earlier):
        while self.left > 0:
            self.double()
        self.catch_up(*earlier)
        out = self.pieces + self.beside
        return out if out[0].shape[0] % 16 == 0 else [jnp.concatenate(out, 0)]

    def all(self):
        while self.left > 0:
            self.double()
        while self.sent < len(self.pieces):
            self.send()
        out = self.pieces + self.beside
        return out if out[0].shape[0] % 16 == 0 else [jnp.concatenate(out, 0)]


class Scatter:
    def __init__(self, parts, bits):
        self.bits = bits
        self.orders = [[0, 1], [1, 0]][: len(parts)]
        self.kept = [kept for _, kept in parts]
        self.done = 0
        self.start([sent for sent, _ in parts])

    def start(self, sents):
        bits = [order[self.done] if self.done < 2 else self.done for order in self.orders]
        self.got = [flip(sent, "row", bit) for sent, bit in zip(sents, bits)]

    def wait(self, *earlier):
        self.got = [after(got, *earlier) for got in self.got]

    def step(self):
        if self.done == self.bits - 1:
            return
        self.done += 1
        half = self.kept[0].shape[0] // 2
        sents = [
            (kept[half:] + got[half:].astype(f32)).astype(bf16)
            for kept, got in zip(self.kept, self.got)
        ]
        self.kept = [kept[:half] + got[:half].astype(f32) for kept, got in zip(self.kept, self.got)]
        if self.done == 2:
            sents = [jnp.concatenate(sents, 1)]
            self.kept = [jnp.concatenate(self.kept, 1)]
        self.start(sents)

    def total(self):
        while self.done < self.bits - 1:
            self.step()
        totals = [kept + got.astype(f32) for kept, got in zip(self.kept, self.got)]
        return jnp.concatenate(totals, 1)


def turned_pairs(block):
    first = [(2 * a + b, 2 * b + a) for a in range(2) for b in range(2)]
    second = [(2 * a + b, 2 * (1 - b) + a) for a in range(2) for b in range(2)]
    return lax.ppermute(block, "col", first), lax.ppermute(block, "col", second)


def from_pairs(same, other):
    first = [(2 * a + b, 2 * b + a) for a in range(2) for b in range(2)]
    second = [(2 * a + b, 2 * b + 1 - a) for a in range(2) for b in range(2)]
    return lax.ppermute(same, "col", first), lax.ppermute(other, "col", second)


def cuts(width):
    first = min(512, width)
    return [(0, first), (first, width)] if first < width else [(0, width)]


def shards(
    layer_input,
    gain_attn,
    qkv_weight,
    qkv_bias,
    out_weight,
    gain_mlp,
    gate_weight,
    up_weight,
    down_weight,
    cotangent,
):
    row = lax.axis_index("row")
    column = lax.axis_index("col")
    row_count = lax.axis_size("row")
    bits = row_count.bit_length() - 1
    core = column % 2
    sequence = column // 2
    parity = core.astype(jnp.int32).reshape(1)
    tok_local, model_width = layer_input.shape
    length = tok_local * 2
    deep = model_width // row_count
    ff_cols = gate_weight.shape[1]
    qkv_cols = qkv_weight.shape[1]
    out_cols = out_weight.shape[0]
    group_width = 2 * qkv_cols
    query_width = group_width - 2 * HD

    bias_rows = jnp.pad(qkv_bias[None, :], ((0, 15), (0, 0)))
    first, second = turned_pairs(
        jnp.concatenate(
            [
                jnp.concatenate([qkv_weight, bias_rows], 0),
                jnp.pad(out_weight.T, ((0, 16), (0, 0))),
            ],
            1,
        )
    )
    low = jnp.where(sequence == 0, first, second)
    high = jnp.where(sequence == 0, second, first)
    qkv_own = jnp.concatenate([low[:, :qkv_cols], high[:, :qkv_cols]], 1)
    bias_full = qkv_own[deep : deep + 1].astype(f32)
    out_own = jnp.concatenate([low[:deep, qkv_cols:], high[:deep, qkv_cols:]], 1)
    out_own = jnp.pad(out_own, ((0, 0), (0, HD)))
    qkv_gather = Gather(qkv_own[:deep], bits)
    out_gather = Gather(out_own, bits)
    down_flipped = down_weight.T
    mlp_gathers = []
    for start, stop in cuts(ff_cols):
        padded = -(-(stop - start) // 256) * 256
        pieces = [
            jnp.pad(part[:, start:stop], ((0, 0), (0, padded - (stop - start))))
            for part in (gate_weight, up_weight, down_flipped)
        ]
        mlp_gathers.append(Gather(jnp.concatenate(pieces, 1), bits))
    place = jnp.arange(model_width, dtype=jnp.int32)
    masks = jnp.array([bit_reversed(p, bits) for p in range(row_count)], jnp.int32)
    source = jnp.repeat(masks ^ row, deep) * deep + place % deep
    to_stored = (place[:, None] == source[None, :]).astype(bf16)
    from_stored = (source[:, None] == place[None, :]).astype(bf16)

    def stored(block):
        return jnp.dot(block, to_stored, preferred_element_type=f32)

    def unstored(block):
        return jnp.dot(block, from_stored, preferred_element_type=f32).astype(bf16)

    def unstored_row(vector):
        blocks = vector.reshape(row_count, deep)
        blocks = jnp.concatenate(
            [blocks[bit_reversed(m, bits)][None] for m in range(row_count)], 0
        )
        for bit in range(bits):
            wide = blocks.reshape(-1, 2, 1 << bit, deep)
            turned = jnp.concatenate([wide[:, 1:], wide[:, :1]], 1).reshape(row_count, deep)
            blocks = jnp.where((row >> bit) % 2 == 1, turned, blocks)
        return blocks.reshape(model_width)

    input_rows = stored(after(layer_input, first, second))
    grad_out = stored(cotangent)
    gain_one = stored(gain_attn[None, :])
    gain_two = stored(gain_mlp[None, :])

    scale_one = lax.rsqrt(jnp.mean(input_rows * input_rows, axis=1) + eps)
    normed_own = (input_rows * scale_one[:, None] * gain_one).astype(bf16)
    normed_other = flip(normed_own, "col", 0)
    cosine, sine_part = rope_tables(length)
    grad_blocks = [grad_out.astype(bf16)]

    near, far = mlp_gathers
    n_four = near.double()
    n_own = near.send()
    a_own = qkv_gather.send()
    a_four = qkv_gather.double()
    a_two = qkv_gather.double(a_own)
    a_beside = qkv_gather.send(a_own)
    o_four = out_gather.double(a_four)
    a_last = qkv_gather.send(a_beside, n_own)
    qkv_pieces = qkv_gather.all()
    far.ready(a_two, o_four)
    f_four = far.double()
    o_two = out_gather.double(a_two)
    across = flip(after(grad_blocks[0], a_four), "col", 1)
    out_pieces = out_gather.finish(a_last, o_two)
    n_two = near.double(o_two)
    n_beside = near.send(a_last)
    qk_rows, value_rows, att_rows, log_totals = attend(
        parity,
        normed_own,
        normed_other,
        qkv_pieces,
        bias_full,
        cosine,
        sine_part,
    )
    n_last = near.send(att_rows)
    att_own, att_other = project(after(att_rows, n_beside, n_two, across, f_four), out_pieces)
    att_got = flip(att_other, "col", 0)
    grad_blocks.append(flip(after(grad_blocks[0], att_got), "col", 0))
    grad_blocks += [across, flip(after(across, att_got), "col", 0)]
    middle = input_rows + att_own + att_got.astype(f32)
    scale_two = lax.rsqrt(jnp.mean(middle * middle, axis=1) + eps)
    blocks = [(middle * scale_two[:, None] * gain_two).astype(bf16)]
    across = flip(blocks[0], "col", 1)
    blocks.append(flip(after(blocks[0], n_last), "col", 0))
    blocks += [across, flip(across, "col", 0)]

    f_beside = far.catch_up(n_last)
    f_two = far.double(blocks[2])
    first_pieces = near.all()
    act_all, *sums = mlp(blocks, grad_blocks, first_pieces)
    sums_own, sums_far = sums[:2], sums[2:]
    f_last = far.send(f_beside, act_all)
    second_pieces = far.all()
    sent_one, kept_one, sent_two, kept_two = outer(blocks, grad_blocks, [act_all])
    first_scatter = Scatter([(sent_one, kept_one), (sent_two, kept_two)], bits)
    start_far = after(blocks[2], kept_one)
    act_far, near_far, far_far = mlp(
        [start_far, blocks[3]], grad_blocks[2:], second_pieces, sums_far
    )
    far_far = after(far_far, *first_scatter.got)
    across = near_far.astype(f32) + flip(far_far, "col", 0).astype(f32)
    across = across.astype(bf16)
    normed_back = flip(across[0], "col", 1)
    act_own, near_own, far_own = mlp(
        [after(blocks[0], across), blocks[1]],
        grad_blocks[:2],
        second_pieces,
        sums_own,
    )
    first_scatter.step()
    beside = flip(after(far_own, normed_back, *first_scatter.got), "col", 0)
    first_scatter.step()
    down_back = flip(after(across[1], normed_back), "col", 1)

    def summed(k, back):
        return near_own[k].astype(f32) + beside[k].astype(f32) + back.astype(f32)

    second_whole = outer_whole(
        row.astype(jnp.int32).reshape(1),
        [after(blocks[0], near_own, *first_scatter.kept), *blocks[1:]],
        grad_blocks,
        [act_own, act_far],
        row_count,
    )
    second_total = lax.psum_scatter(second_whole, "row", scatter_dimension=0, tiled=True)
    grad_normed_two = summed(0, after(normed_back, second_whole))
    scaled_two = gain_two * grad_normed_two
    inner_two = jnp.sum(scaled_two * middle, axis=1)
    grad_middle = (
        grad_out
        + scale_two[:, None] * scaled_two
        - middle * (scale_two**3 * inner_two / model_width)[:, None]
    )
    gain_two_grad = jnp.sum(grad_normed_two * middle * scale_two[:, None], axis=0)
    branch_own = grad_middle.astype(bf16)
    branch_other = flip(branch_own, "col", 0)
    out_scatter = Scatter([outer_one([branch_own, branch_other], att_rows)], bits)
    split = qk_rows.shape[1] // 256
    mixed_first, bias_first, *carry = attend_back(
        parity,
        after(branch_own, out_scatter.kept[0]),
        branch_other,
        out_pieces,
        qk_rows,
        value_rows,
        log_totals,
        cosine,
        sine_part,
        0,
        split,
    )
    out_scatter.wait(mixed_first)
    out_scatter.step()
    mixed_last, bias_last = attend_back(
        parity,
        after(branch_own, out_scatter.kept[0]),
        branch_other,
        out_pieces,
        qk_rows,
        value_rows,
        log_totals,
        cosine,
        sine_part,
        split,
        2 * split,
        carry,
    )
    bias_grad = jnp.concatenate([bias_first, bias_last], 1)[0]
    grad_mixed = jnp.concatenate([mixed_first, mixed_last], 1)
    qkv_scatter = Scatter([outer_one([normed_own, normed_other], grad_mixed)], bits)
    passed = qkv_scatter.kept[0]
    out_scatter.wait(passed)
    first_scatter.wait(passed)
    first_total = first_scatter.total()
    layer_output = unstored((middle + summed(1, after(down_back, passed))).astype(bf16))
    qkv_full = jnp.concatenate(qkv_pieces, 0)
    grad_mixed = after(grad_mixed, passed)

    def back_to_normed(rows):
        return jnp.einsum("tc,dc->td", rows, qkv_full, preferred_element_type=f32)

    other = flip(back_to_normed(grad_mixed[tok_local:]).astype(bf16), "col", 0)
    grad_normed_one = back_to_normed(grad_mixed[:tok_local]) + other.astype(f32)
    scaled_one = gain_one * grad_normed_one
    inner_one = jnp.sum(scaled_one * input_rows, axis=1)
    input_grad = unstored(
        (
            grad_middle
            + scale_one[:, None] * scaled_one
            - input_rows * (scale_one**3 * inner_one / model_width)[:, None]
        ).astype(bf16)
    )
    gain_one_grad = jnp.sum(grad_normed_one * input_rows * scale_one[:, None], axis=0)

    bias_row = lax.dynamic_update_slice_in_dim(
        jnp.zeros((group_width * 2,), f32), bias_grad, core * group_width, 0
    )
    small = jnp.concatenate([unstored_row(gain_one_grad), unstored_row(gain_two_grad), bias_row])
    small = jnp.pad(small, (0, -small.shape[0] % 128)).reshape(-1, 128)
    for bit in range(2):
        small = small + flip(small, "col", bit)
    for bit in range(bits):
        small = small + flip(small, "row", bit)
    qkv_scatter.step()
    qkv_scatter.kept = [jnp.concatenate([qkv_scatter.kept[0], out_scatter.kept[0]], 1)]
    qkv_scatter.got = [jnp.concatenate([qkv_scatter.got[0], out_scatter.got[0]], 1)]
    qkv_scatter.step()
    qkv_scatter.wait(small)
    total = qkv_scatter.total().astype(bf16)
    ends = (0, qkv_cols, group_width, group_width + out_cols, group_width + 2 * out_cols)
    parts = [total[:, start:stop] for start, stop in zip(ends, ends[1:])]
    low = jnp.concatenate([parts[0], parts[2]], 1)
    high = jnp.concatenate([parts[1], parts[3]], 1)
    first, second = from_pairs(
        jnp.where(sequence == 0, low, high), jnp.where(sequence == 0, high, low)
    )
    both_totals = first.astype(f32) + second.astype(f32)
    qkv_total, out_total = both_totals[:, :qkv_cols], both_totals[:, qkv_cols:]
    mlp_totals = []
    for total, (start, stop) in zip(
        (first_total, after(second_total, small).astype(f32)), cuts(ff_cols)
    ):
        padded = total.shape[1] // 3
        mlp_totals.append(
            [total[:, k * padded : k * padded + stop - start] for k in range(3)]
        )
    gate_total, up_total, down_total = (jnp.concatenate(parts, 1) for parts in zip(*mlp_totals))
    small = small.reshape(-1)
    gain_one_total = small[:model_width]
    gain_two_total = small[model_width : 2 * model_width]
    bias_total = lax.dynamic_slice_in_dim(small, 2 * model_width + column * qkv_cols, qkv_cols, 0)
    return (
        layer_output,
        input_grad,
        gain_one_total,
        qkv_total,
        bias_total,
        out_total.T,
        gain_two_total,
        gate_total,
        up_total,
        down_total.T,
    )


def solution(mesh):
    in_specs = (
        P(("row", "col"), None),
        P(),
        P("row", "col"),
        P("col"),
        P("col", "row"),
        P(),
        P("row", "col"),
        P("row", "col"),
        P("col", "row"),
        P(("row", "col"), None),
    )
    out_specs = (
        P(("row", "col"), None),
        P(("row", "col"), None),
        P(),
        P("row", "col"),
        P("col"),
        P("col", "row"),
        P(),
        P("row", "col"),
        P("row", "col"),
        P("col", "row"),
    )
    return jax.shard_map(shards, mesh=mesh, in_specs=in_specs, out_specs=out_specs, check_vma=False)
```
